128 devices in a mesh: batch: 16 (over y, x), seq: 8 (over z, core).
Axes of the slice: x: 4, y: 4, z: 4, core: 2. Of those that a mesh axis runs over, the one named last changes fastest.
Arguments:
- block_input: bfloat16 [64, 1024, 768], P('batch', 'seq'), may hold values from -6 to 6
- token_ids: int32 [64, 1024], P('batch', 'seq'), may hold values from 0 to 8007, as said below
- hash_table: int32 [8008], replicated, may hold values from 0 to 15
- doc_lengths: int32 [64, 8], P('batch'), may hold values from 1 to 256, 1024 in all within a row
- turn_mask: int32 [64, 1024], P('batch', 'seq'), may hold values 0 or 1
- attn_norm_gain: float32 [768], replicated, may hold values from 0.5 to 1.5
- attn_norm_bias: float32 [768], replicated, may hold values from -3 to 3
- qkv_weight: bfloat16 [768, 2304], replicated, may hold values from -0.21875 to 0.21875
- proj_weight: bfloat16 [768, 768], replicated, may hold values from -1.75 to 1.75
- ffn_norm_gain: float32 [768], replicated, may hold values from 0.5 to 1.5
- ffn_norm_bias: float32 [768], replicated, may hold values from -3 to 3
- expert_up: bfloat16 [16, 768, 3072], P('batch'), may hold values from -0.21875 to 0.21875
- expert_down: bfloat16 [16, 3072, 768], P('batch'), may hold values from -0.109375 to 0.109375
- out_grad: bfloat16 [64, 1024, 768], P('batch', 'seq'), may hold values from -6 to 6
Outputs:
- block_output: bfloat16 [64, 1024, 768], P('batch', 'seq')
- input_grad: float32 [64, 1024, 768], P('batch', 'seq')
- attn_gain_grad: float32 [768], replicated
- attn_bias_grad: float32 [768], replicated
- qkv_grad: float32 [768, 2304], replicated
- proj_grad: float32 [768, 768], replicated
- ffn_gain_grad: float32 [768], replicated
- ffn_bias_grad: float32 [768], replicated
- up_grad: float32 [16, 768, 3072], P('batch', None, 'seq')
- down_grad: float32 [16, 3072, 768], P('batch', 'seq')
- expert_counts: int32 [16], replicated
- received_counts: int32 [16, 8, 16], P('batch', 'seq')
The draws below stay inside these ranges and needn't reach their ends.
Inputs may be any that keep to these rules, and one draw needn't show every extreme that they name: `token_ids`: among the 512 tokens of one device (4 rows by 128 positions), at most 64 have an expert (by hash_table) equal to any one expert; in every draw one expert gets exactly 64 from every device. `doc_lengths`: the 8 lengths of a row sum to 1024; the longest of each row is exactly 256.
All inputs are finite; a program needn't handle non-finite values. No bound on the sum of `turn_mask` on one device may be relied on, other than what follows from the above.
Results may differ from the reference program's by a relative error of at most 0.0098.
Values may be sent and summed in bfloat16 or wider, within the bound.
No kernel may reach another device: no remote copies, remote signals or barrier semaphores. Data moves between devices by JAX's collectives and lax.ppermute only.
A program may use at most 192 MiB of HBM per device.

```python
import math
import jax
import jax.numpy as jnp
import numpy as np
from jax import lax

D = 768
HEADS = 12
HEAD_DIM = 64
FF = 3072
VOCAB = 8008
SEQ_LEN = 1024
MAXLEN = 256
NSEG = 8
ROWS_DEV = 4
ROWS = 64
EXPERTS = 16
SHARD = 128
TOK_DEV = 512
CAP = 64
N_BATCH = 16
N_SEQ = 8


def shuffled_vocab(key):
    return jax.random.permutation(key, VOCAB).astype(jnp.int32)


def draw_hash_table(key, part):
    vocab_order = shuffled_vocab(key)
    labels = (jnp.arange(VOCAB, dtype=jnp.int32) % EXPERTS).astype(jnp.int32)
    return jnp.zeros((VOCAB,), jnp.int32).at[vocab_order].set(labels)


def draw_token_ids(key, part):
    vocab_order = shuffled_vocab(key)
    key = jax.random.fold_in(key, 7)
    favoured_key, device_key = jax.random.split(key)
    favoured = jax.random.randint(favoured_key, (), 0, EXPERTS).astype(jnp.int32)
    seq_shards = SEQ_LEN // SHARD

    def one_device(device_seed):
        key_one, key_two, key_three = jax.random.split(device_seed, 3)
        rest_slots = CAP + jax.random.permutation(key_one, EXPERTS * CAP - CAP)[:TOK_DEV - CAP].astype(jnp.int32)
        picked = jnp.concatenate([jnp.arange(CAP, dtype=jnp.int32), rest_slots])
        owners_of = (picked // CAP + favoured) % EXPERTS
        owners_of = jax.random.permutation(key_two, owners_of)
        within = jax.random.randint(key_three, (TOK_DEV,), 0, VOCAB // EXPERTS).astype(jnp.int32)
        return vocab_order[owners_of + EXPERTS * within]
    token_table = jax.vmap(one_device)(jax.random.split(device_key, EXPERTS * seq_shards))
    token_table = token_table.reshape(EXPERTS, seq_shards, ROWS_DEV, SHARD).transpose(0, 2, 1, 3)
    return token_table.reshape(EXPERTS * ROWS_DEV, SEQ_LEN).astype(jnp.int32)


def touch_ends(entries, rng, low, top_value):
    shape = entries.shape
    spot = [jax.random.randint(jax.random.fold_in(rng, axis), (), 0, shape[axis]) for axis in range(len(shape))]
    entries = entries.at[tuple(spot)].set(low)
    longest = shape.index(max(shape))
    spot[longest] = (spot[longest] + 1) % shape[longest]
    return entries.at[tuple(spot)].set(top_value)


def levels(rng, dims, shards, low, largest):
    def one(dim, shards_of):
        draws = jax.random.uniform(jax.random.fold_in(jax.random.fold_in(rng, 6), dim), (shards_of,), jnp.float32, low / len(shards), largest / len(shards))
        return jnp.repeat(jnp.exp(draws), dims[dim] // shards_of).reshape((-1,) + (1,) * (len(dims) - dim - 1))

    level = one(*shards[0])
    for cut in shards[1:]:
        level = level * one(*cut)
    return level


def profile(amount, total, reach, lean):
    portions = [(1 << 20) // math.isqrt(standing ** lean) + 1 for standing in range(2, amount + 1)]
    rest, counts = total - reach - (amount - 1), [1] * (amount - 1)
    while rest > 0:
        free = [i for i in range(amount - 1) if counts[i] < reach]
        mass, budget = sum([portions[i] for i in free]), rest
        for i in free:
            addition = min(reach - counts[i], max(1, budget * portions[i] // mass), rest)
            counts[i] = counts[i] + addition
            rest = rest - addition
    return np.array([reach] + counts)


def ragged_sizes(rng, count, total, bound, skew):
    if count == 2:
        one = jax.random.randint(rng, (), max(1, total - bound), min(bound, total - 1) + 1)
        return jnp.stack([one, total - one])
    sizes = jnp.asarray(profile(count, total, bound, skew), jnp.int32)
    twos = (count - 1) // 2
    source_of, sink = sizes[1:1 + 2 * twos:2], sizes[2:2 + 2 * twos:2]
    slack = jnp.minimum(source_of - 1, bound - sink)
    passed = jax.random.randint(jax.random.fold_in(rng, 1), (twos,), 0, 1 << 20) % (slack + 1)
    sizes = sizes.at[1:1 + 2 * twos:2].set(source_of - passed).at[2:2 + 2 * twos:2].set(sink + passed)
    return sizes[jax.random.permutation(jax.random.fold_in(rng, 2), count)]


def scatter_about(own_key, extent, width, most, cuts=(), kind=jnp.bfloat16):
    array = width * jax.random.normal(own_key, extent, jnp.float32)
    if cuts:
        array = array * levels(own_key, extent, cuts, -0.22, 0.18)
    return jnp.clip(array, -most, most).astype(kind)


def setup_inputs(seed: int = 0) -> dict:
    keys = jax.random.split(jax.random.key(seed), 15)
    return {
        "block_input": scatter_about(keys[0], (ROWS, SEQ_LEN, D), 1.0, 6.0, ((0, 16), (1, 8))),
        "token_ids": draw_token_ids(jax.random.fold_in(keys[14], 71), 0),
        "hash_table": draw_hash_table(jax.random.fold_in(keys[14], 71), 0),
        "doc_lengths": jax.vmap(lambda own: ragged_sizes(own, NSEG, SEQ_LEN, MAXLEN, 2))(jax.random.split(keys[3], ROWS)).reshape((ROWS, NSEG)).astype(jnp.int32),
        "turn_mask": touch_ends((jax.random.randint(keys[4], (ROWS, SEQ_LEN), 0, 4) < 3).astype(jnp.int32), jax.random.fold_in(keys[4], 1), 0, 1),
        "attn_norm_gain": jnp.clip(1.0 + 0.1 * jax.random.normal(keys[5], (D,), jnp.float32), 0.5, 1.5),
        "attn_norm_bias": scatter_about(keys[6], (D,), 0.5, 3.0, (), jnp.float32),
        "qkv_weight": scatter_about(keys[7], (D, 3 * D), D ** -0.5, 0.21875),
        "proj_weight": scatter_about(keys[8], (D, D), (D // 64) ** -0.5, 1.75),
        "ffn_norm_gain": jnp.clip(1.0 + 0.1 * jax.random.normal(keys[9], (D,), jnp.float32), 0.5, 1.5),
        "ffn_norm_bias": scatter_about(keys[10], (D,), 0.5, 3.0, (), jnp.float32),
        "expert_up": scatter_about(keys[11], (EXPERTS, D, FF), D ** -0.5, 0.21875, ((0, 16),)),
        "expert_down": scatter_about(keys[12], (EXPERTS, FF, D), FF ** -0.5, 0.109375, ((0, 16),)),
        "out_grad": scatter_about(keys[13], (ROWS, SEQ_LEN, D), 1.0, 6.0, ((0, 16), (1, 8))),
    }


@jax.custom_vjp
def low(v):
    return lax.optimization_barrier(v.astype(jnp.bfloat16)).astype(jnp.float32)

@jax.custom_vjp
def low_back(v):
    return v

def low_keep(v):
    return (low(v), None)

def low_pass(kept, grad):
    return (grad,)

def back_keep(v):
    return (v, None)

def back_low(kept, grad):
    return (low(grad),)
low.defvjp(low_keep, low_pass)
low_back.defvjp(back_keep, back_low)
EPS = 1e-05
MASKED = -1e+30

def layer_norm(values, gain_vec, bias_vec):
    row_mean = lax.optimization_barrier(jnp.mean(values, axis=-1, keepdims=True))
    centred = values - row_mean
    spread = lax.optimization_barrier(jnp.mean(centred * centred, axis=-1, keepdims=True))
    return centred * lax.rsqrt(spread + EPS) * gain_vec + bias_vec

def gelu_curve(values):
    return jax.nn.gelu(values, approximate=True)

def row_attention(packed_args):
    packed_row, row_segments = packed_args
    query_part = packed_row[:, :D].reshape(SEQ_LEN, HEADS, HEAD_DIM)
    key_part = packed_row[:, D:2 * D].reshape(SEQ_LEN, HEADS, HEAD_DIM)
    value_part = packed_row[:, 2 * D:].reshape(SEQ_LEN, HEADS, HEAD_DIM)
    scores = jnp.einsum('qhd,khd->hqk', query_part, key_part, precision=lax.Precision.HIGHEST) * HEAD_DIM ** (-0.5)
    scores = low_back(scores)
    positions = jnp.arange(SEQ_LEN, dtype=jnp.int32)
    allowed = (row_segments[:, None] == row_segments[None, :]) & (positions[None, :] <= positions[:, None])
    scores = jnp.where(allowed[None], scores, MASKED)
    row_top = lax.optimization_barrier(jnp.max(scores, axis=-1, keepdims=True))
    weights = jnp.exp(scores - row_top)
    attention = weights / lax.optimization_barrier(jnp.sum(weights, axis=-1, keepdims=True))
    attended = jnp.einsum('hqk,khd->qhd', low(attention), value_part, precision=lax.Precision.HIGHEST)
    return attended.reshape(SEQ_LEN, D)

def reference(block_input, token_ids, hash_table, doc_lengths, turn_mask, attn_norm_gain, attn_norm_bias, qkv_weight, proj_weight, ffn_norm_gain, ffn_norm_bias, expert_up, expert_down, out_grad):
    positions = jnp.arange(SEQ_LEN, dtype=jnp.int32)
    doc_ends = jnp.cumsum(doc_lengths, axis=-1).astype(jnp.int32)
    segments = lax.optimization_barrier(jnp.sum((positions[None, :, None] >= doc_ends[:, None, :]).astype(jnp.int32), axis=-1)).astype(jnp.int32)
    chosen = hash_table[token_ids.reshape(-1)].astype(jnp.int32)
    row_limit = N_BATCH * N_SEQ * CAP

    def forward(inputs, gain_one, bias_one, qkv_mat, proj_mat, gain_two, bias_two, up_mats, down_mats):
        normed_one = low(layer_norm(inputs, gain_one, bias_one))
        projected = jnp.einsum('rsd,de->rse', normed_one, qkv_mat, precision=lax.Precision.HIGHEST)
        projected = low(low_back(projected))
        attended = lax.map(jax.checkpoint(row_attention), (projected, segments))
        attended = low(low_back(attended))
        mixed_out = low_back(jnp.einsum('rsd,de->rse', attended, proj_mat, precision=lax.Precision.HIGHEST))
        after_attn = inputs + mixed_out
        normed_two = low(low_back(layer_norm(after_attn, gain_two, bias_two))).reshape(-1, D)

        def expert_rows(packed_args):
            number, up_matrix, down_matrix = packed_args
            row_order = jnp.argsort((chosen != number).astype(jnp.int32), stable=True)[:row_limit].astype(jnp.int32)
            is_member = (chosen[row_order] == number).astype(jnp.float32)[:, None]
            rows_in = normed_two[row_order] * is_member
            hidden = low_back(jnp.dot(rows_in, up_matrix, preferred_element_type=jnp.float32, precision=lax.Precision.HIGHEST))
            active = low(gelu_curve(hidden))
            result = jnp.dot(active, down_matrix, preferred_element_type=jnp.float32, precision=lax.Precision.HIGHEST)
            result = low(low_back(result))
            return (result * is_member, row_order)
        expert_outs, row_orders = lax.map(jax.checkpoint(expert_rows), (jnp.arange(EXPERTS, dtype=jnp.int32), up_mats, down_mats))
        expert_mix = jnp.zeros_like(normed_two).at[row_orders.reshape(-1)].add(expert_outs.reshape(-1, D))
        return after_attn + expert_mix.reshape(after_attn.shape)
    as_floats = (block_input.astype(jnp.float32), attn_norm_gain.astype(jnp.float32), attn_norm_bias.astype(jnp.float32), qkv_weight.astype(jnp.float32), proj_weight.astype(jnp.float32), ffn_norm_gain.astype(jnp.float32), ffn_norm_bias.astype(jnp.float32), expert_up.astype(jnp.float32), expert_down.astype(jnp.float32))
    output, pull = jax.vjp(forward, as_floats[0], as_floats[1], as_floats[2], as_floats[3], as_floats[4], as_floats[5], as_floats[6], as_floats[7], as_floats[8])
    upstream = out_grad.astype(jnp.float32) * turn_mask.astype(jnp.float32)[..., None]
    gradients = pull(upstream)
    onehot = (chosen[:, None] == jnp.arange(EXPERTS, dtype=jnp.int32)[None, :]).astype(jnp.int32)
    expert_tally = lax.optimization_barrier(jnp.sum(onehot, axis=0)).astype(jnp.int32)
    blocked = onehot.reshape(N_BATCH, ROWS_DEV, N_SEQ, SHARD, EXPERTS)
    block_tally = lax.optimization_barrier(jnp.sum(blocked, axis=(1, 3))).astype(jnp.int32)
    received = jnp.transpose(block_tally, (2, 1, 0)).astype(jnp.int32)
    return (output.astype(jnp.bfloat16), gradients[0], gradients[1], gradients[2], gradients[3], gradients[4], gradients[5], gradients[6], gradients[7], gradients[8], expert_tally, received)
```

```python
import jax
import jax.numpy as jnp
from jax import lax
from jax.experimental import pallas as pl
from jax.experimental.pallas import tpu as pltpu
from jax.sharding import PartitionSpec as P

BF = jnp.bfloat16
F32 = jnp.float32
I32 = jnp.int32
EPS = 1e-05
MASKED = -1e30
HEADS = 12
HEAD_SIZE = 64
PAIRS = 6
CAP = 64
SWAP = [(i, i ^ 1) for i in range(8)]
UP_ONE = [(i, i + 1) for i in range(0, 8, 2)]
DOWN_ONE = [(i + 1, i) for i in range(0, 8, 2)]
AHEAD_TWO = [(i, i + 2) for i in range(6)]
BACK_TWO = [(i + 2, i) for i in range(6)]
PAY_ROWS = 10240
GEMM_ROWS = 9216
VM = pl.BlockSpec(memory_space=pltpu.VMEM)
SM = pl.BlockSpec(memory_space=pltpu.SMEM)


def shape(dims, kind=BF):
    return jax.ShapeDtypeStruct(dims, kind)


def kernel_call(body, outs, args, name, flops, grid=None, in_specs=None, out_specs=None, scratch=()):
    moved = sum(a.size * a.dtype.itemsize for a in args) + sum(
        o.size * o.dtype.itemsize for o in outs
    )
    extra = {} if grid is None else {"grid": grid}
    return pl.pallas_call(
        body,
        out_shape=outs,
        in_specs=in_specs or [VM] * len(args),
        out_specs=out_specs or [VM] * len(outs),
        scratch_shapes=list(scratch),
        compiler_params=pltpu.CompilerParams(vmem_limit_bytes=56 * 1024 * 1024),
        cost_estimate=pl.CostEstimate(flops=flops, bytes_accessed=moved, transcendentals=0),
        name=name,
        **extra,
    )(*args)


def nn(a, b):
    return jnp.dot(a, b, preferred_element_type=F32)


def nt(a, b):
    return lax.dot_general(a, b, (((1,), (1,)), ((), ())), preferred_element_type=F32)


def tn(a, b):
    return lax.dot_general(a, b, (((0,), (0,)), ((), ())), preferred_element_type=F32)


def iota(dims, axis):
    return lax.broadcasted_iota(I32, dims, axis)


def norm_parts(values):
    centred = values - jnp.mean(values, axis=-1, keepdims=True)
    inverse = lax.rsqrt(jnp.mean(centred * centred, axis=-1, keepdims=True) + EPS)
    return centred * inverse, inverse


def norm_back(grad, gain, unit, inverse):
    t = grad * gain
    return inverse * (
        t - jnp.mean(t, axis=-1, keepdims=True) - unit * jnp.mean(t * unit, axis=-1, keepdims=True)
    )


def route_kernel(tok, table, turn, grad, target_out, count_out, sent):
    ids = jnp.concatenate([tok[i : i + 1, :] for i in range(4)], axis=1)
    live = jnp.concatenate([turn[i : i + 1, :] for i in range(4)], axis=1).astype(F32)
    high, low = ids >> 7, ids & 127
    picked = nn(table[...], (iota((64, 512), 0) == high).astype(F32).astype(BF))
    chosen = jnp.sum(jnp.where(iota((128, 512), 0) == low, picked, 0.0), axis=0, keepdims=True)
    member = (iota((16, 512), 0) == chosen.astype(I32)).astype(F32)
    earlier = (iota((512, 512), 0) < iota((512, 512), 1)).astype(F32).astype(BF)
    before = nn(member.astype(BF), earlier)
    slot = jnp.sum(before * member, axis=0, keepdims=True)
    target = (chosen * CAP + slot).astype(I32)
    target_out[...] = jnp.broadcast_to(target, (8, 512))
    count_out[...] = jnp.broadcast_to(jnp.sum(member, axis=1, keepdims=True), (16, 128))
    for i in range(4):
        placing = jnp.where(iota((256, 512), 0) + 256 * i == target, live, 0.0).astype(BF)
        sent[256 * i : 256 * (i + 1), :] = nn(placing, grad[...]).astype(BF)


def own_kernel(x, gain, bias, weight, normed, query, keyval):
    unit, _ = norm_parts(x[...].astype(F32))
    rows = (unit * gain[...] + bias[...]).astype(BF)
    normed[...] = rows
    query[...] = nn(rows, weight[:, :768]).astype(BF)
    keyval[...] = nn(rows, weight[:, 768:]).astype(BF)


def head_masks(scale):
    lane = iota((1, 128), 1)
    first = jnp.where(lane < 64, scale, 0.0).astype(BF)
    second = jnp.where(lane >= 64, scale, 0.0).astype(BF)
    return first, second


def stack_heads(pair, masks):
    return jnp.concatenate([pair * masks[0], pair * masks[1]], axis=0)


def window_bias(start):
    key = iota((384, 128), 0)
    allowed = (key >= start) & (key <= iota((384, 128), 1) + 256)
    half = jnp.where(allowed, 0.0, MASKED)
    return jnp.concatenate([half, half], axis=1)


def join_heads(both):
    one = jnp.where(iota((128, 128), 0) < 64, both[:, :128], both[:, 128:])
    return one.T


def forward_kernel(
    behind_two, early, late, x, start, gain, bias, weight, query, keyval, proj, gain_two, bias_two,
    target, normed_halo, keyval_halo, attended, log_out, after_out, sent, context,
):
    scales = head_masks(HEAD_SIZE ** (-0.5))

    def one_row(r, carry):
        halo = jnp.concatenate([behind_two[r], early[r] + late[r]], axis=0).astype(F32)
        unit, _ = norm_parts(halo)
        rows = (unit * gain[...] + bias[...]).astype(BF)
        normed_halo[r] = rows
        fresh = nn(rows, weight[:, 768:]).astype(BF)
        keyval_halo[r] = fresh
        context[0:256, :] = fresh
        context[256:384, :] = keyval[r]
        mask = window_bias(start[r])
        for p in range(PAIRS):
            lo, hi = 128 * p, 128 * (p + 1)
            keys = context[:, lo:hi]
            values = context[:, 768 + lo : 768 + hi]
            stacked = stack_heads(query[r, :, lo:hi], scales)
            scores = nt(keys, stacked) + mask
            top = jnp.max(scores, axis=0, keepdims=True)
            weights = jnp.exp(scores - top)
            total = jnp.sum(weights, axis=0, keepdims=True)
            log_out[r, p : p + 1, :] = top + jnp.log(total)
            share = (weights * (1.0 / total)).astype(BF)
            attended[r, :, lo:hi] = join_heads(tn(values, share)).astype(BF)
        return carry

    lax.fori_loop(0, 4, one_row, 0)
    mixed = nn(attended[...].reshape(512, 768), proj[...])
    after = x[...].reshape(512, 768).astype(F32) + mixed
    after_out[...] = after
    unit, _ = norm_parts(after)
    rows = (unit * gain_two[...] + bias_two[...]).astype(BF)
    for i in range(4):
        placing = (iota((256, 512), 0) + 256 * i == target[0:1, :]).astype(F32).astype(BF)
        sent[256 * i : 256 * (i + 1), :] = nn(placing, rows).astype(BF)


def active_grad_kernel(grad, down, out):
    out[...] = nt(grad[...], down[...]).astype(BF)


def gelu_both(v):
    c = 0.7978845608028654
    square = v * v
    t = jnp.tanh(v * (c + (c * 0.044715) * square))
    half = 0.5 * v
    value = half + half * t
    slope = 0.5 + 0.5 * t + half * (1.0 - t * t) * (c + (3.0 * c * 0.044715) * square)
    return value, slope


def expert_kernel(x, up, raw, active, hidden_grad, back, total):
    step = pl.program_id(0)

    @pl.when(step == 0)
    def _():
        total[...] = jnp.zeros_like(total)

    for r in range(4):
        rows = slice(256 * r, 256 * (r + 1))
        value, slope = gelu_both(nn(x[rows, :], up[...]))
        active[rows, :] = value.astype(BF)
        low = (raw[rows, :].astype(F32) * slope).astype(BF)
        hidden_grad[rows, :] = low
        total[rows, :] += nt(low, up[...])

    @pl.when(step == pl.num_programs(0) - 1)
    def _():
        back[...] = total[...].astype(BF)


def weight_kernel(x, grad, active, hidden_grad, down, out, up_part, down_part, x_t, grad_t, total):
    step = pl.program_id(0)

    @pl.when(step == 0)
    def _():
        total[...] = jnp.zeros_like(total)
        x_t[...] = x[...].T
        grad_t[...] = grad[...].T

    total[...] += nn(active[...], down[...])
    one = nn(x_t[...], hidden_grad[...]).astype(BF)
    up_part[0] = one[:, :384]
    up_part[1] = one[:, 384:]
    two = nn(grad_t[...], active[...]).astype(BF)
    down_part[0] = two[:, :384]
    down_part[1] = two[:, 384:]

    @pl.when(step == pl.num_programs(0) - 1)
    def _():
        out[...] = total[...].astype(BF)


def output_kernel(after, target, returned, out):
    placing = (iota((512, 1024), 1) == target[...]).astype(F32).astype(BF)
    out[...] = (after[...] + nn(placing, returned[...])).astype(BF)


def middle_kernel(
    back, target, after, grad, turn, gain, proj, attended, after_grad, attended_grad, proj_part, terms
):
    placing = (iota((512, 1024), 1) == target[...]).astype(F32).astype(BF)
    normed_grad = nn(placing, back[...])
    unit, inverse = norm_parts(after[...])
    terms[0:1, :] = jnp.sum(normed_grad * unit, axis=0, keepdims=True)
    terms[1:2, :] = jnp.sum(normed_grad, axis=0, keepdims=True)
    upstream = grad[...].astype(F32) * turn[...]
    total = upstream + norm_back(normed_grad, gain[...], unit, inverse)
    after_grad[...] = total
    low = total.astype(BF)
    attended_grad[...] = nt(low, proj[...]).astype(BF)
    for i in range(3):
        proj_part[i] = tn(attended[...], low[:, 256 * i : 256 * (i + 1)]).astype(BF)


def backward_kernel(
    query, keyval, keyval_halo, attended_grad, log_total, start,
    query_grad, own_grad, halo_grad, context,
):
    scales = head_masks(HEAD_SIZE ** (-0.5))
    ones = head_masks(1.0)

    def one_row(r, carry):
        context[0:256, :] = keyval_halo[r]
        context[256:384, :] = keyval[r]
        mask = window_bias(start[r])
        for p in range(PAIRS):
            lo, hi = 128 * p, 128 * (p + 1)
            keys = context[:, lo:hi]
            values = context[:, 768 + lo : 768 + hi]
            stacked = stack_heads(query[r, :, lo:hi], scales)
            grads = stack_heads(attended_grad[r, :, lo:hi], ones)
            scores = nt(keys, stacked) + mask
            share = jnp.exp(scores - log_total[r, p : p + 1, :])
            share_grad = nt(values, grads)
            row_sum = jnp.sum(share * share_grad, axis=0, keepdims=True)
            score_grad = (share * (share_grad - row_sum)).astype(BF)
            key_grad = nn(score_grad, stacked).astype(BF)
            value_grad = nn(share.astype(BF), grads).astype(BF)
            halo_grad[r, :, lo:hi] = key_grad[:256]
            own_grad[r, :, lo:hi] = key_grad[256:]
            halo_grad[r, :, 768 + lo : 768 + hi] = value_grad[:256]
            own_grad[r, :, 768 + lo : 768 + hi] = value_grad[256:]
            turned = join_heads(tn(keys, score_grad))
            query_grad[r, :, lo:hi] = (turned * HEAD_SIZE ** (-0.5)).astype(BF)
        return carry

    lax.fori_loop(0, 4, one_row, 0)


def qkv_grad_kernel(normed, normed_halo, query_grad, own_grad, halo_grad, out, own_t, halo_t):
    step = pl.program_id(0)

    @pl.when(step == 0)
    def _():
        own_t[...] = normed[...].T
        halo_t[...] = normed_halo[...].T

    @pl.when(step < 3)
    def _():
        out[0] = nn(own_t[...], query_grad[...]).astype(BF)

    @pl.when(step >= 3)
    def _():
        out[0] = (nn(own_t[...], own_grad[...]) + nn(halo_t[...], halo_grad[...])).astype(BF)


def input_part_kernel(
    query_grad, own_grad, halo_grad, weight, x, behind_two, early, late, own_out, two_out, one_out, terms
):
    own = nt(query_grad[...], weight[:, :768]) + nt(own_grad[...], weight[:, 768:])
    own_out[...] = own
    unit, _ = norm_parts(x[...].astype(F32))
    gain_sum = jnp.sum(own * unit, axis=0, keepdims=True)
    bias_sum = jnp.sum(own, axis=0, keepdims=True)
    for r in range(4):
        part = nt(halo_grad[r], weight[:, 768:])
        two_out[r] = part[:128].astype(BF)
        one_out[r] = part[128:].astype(BF)
        halo = jnp.concatenate([behind_two[r], early[r] + late[r]], axis=0).astype(F32)
        unit, _ = norm_parts(halo)
        gain_sum += jnp.sum(part * unit, axis=0, keepdims=True)
        bias_sum += jnp.sum(part, axis=0, keepdims=True)
    terms[0:1, :] = gain_sum
    terms[1:2, :] = bias_sum


def input_grad_kernel(even, x, gain, own, from_one, from_two, after_grad, out):
    unit, inverse = norm_parts(x[...].astype(F32))
    total = own[...] + from_two[...].astype(F32) + even[0, 0] * from_one[...].astype(F32)
    out[...] = after_grad[...] + norm_back(total, gain[...], unit, inverse)


def along_x(d):
    return [(b, (b & 12) | ((b + d) & 3)) for b in range(16)]


def along_y(d):
    return [(b, (b + 4 * d) & 15) for b in range(16)]


def along_z(d):
    return [(s, (s + 2 * d) & 7) for s in range(8)]


def pick(array, index):
    return lax.dynamic_index_in_dim(array, index, 0, keepdims=False)


def meet(pieces, axis, route):
    got = [lax.ppermute(pieces[d], axis, route(d)) for d in (2, 1, 3)]
    total = pieces[0].astype(F32)
    for piece in got:
        total = total + piece.astype(F32)
    return total.astype(BF)


def gather(piece, axis, route, place):
    parts = [piece] + [lax.ppermute(piece, axis, route(d)) for d in (1, 2, 3)]
    stack = jnp.stack(parts)
    return jnp.stack([pick(stack, (place - p) % 4) for p in range(4)])


def sum_everywhere(payload):
    rows, lanes = payload.shape
    place = lax.axis_index("batch")
    x, y = place % 4, place // 4
    core = lax.axis_index("seq") % 2
    halves = payload.reshape(2, rows // 2, lanes)
    got = lax.ppermute(pick(halves, 1 - core), "seq", SWAP)
    dims = (2, 4, 4, rows // 64, lanes)
    kept, got = pick(halves, core).reshape(dims), got.reshape(dims)

    def parts(half, at):
        return [
            (pick(kept[half], (at + d) % 4).astype(F32) + pick(got[half], (at + d) % 4).astype(F32)).astype(BF)
            for d in range(4)
        ]

    one = meet(parts(0, x), "batch", along_x)
    two = meet(parts(1, y), "batch", along_y)
    one = meet([pick(one, (y + d) % 4) for d in range(4)], "batch", along_y)
    two = meet([pick(two, (x + d) % 4) for d in range(4)], "batch", along_x)
    both = meet([jnp.stack([one, two])] * 4, "seq", along_z)
    one = gather(both[0], "batch", along_y, y)
    two = gather(both[1], "batch", along_x, x)
    one = gather(one, "batch", along_x, x)
    two = gather(two, "batch", along_y, y)
    mine = jnp.stack([one, two]).reshape(rows // 2, lanes)
    other = lax.ppermute(mine, "seq", SWAP)
    joined = jnp.where(core == 0, jnp.stack([mine, other]), jnp.stack([other, mine]))
    return joined.reshape(rows, lanes)


def exchange(array):
    return lax.all_to_all(
        array.reshape(16, CAP, 768), "batch", split_axis=0, concat_axis=0, tiled=True
    ).reshape(1024, 768)


def local(
    block_input, token_ids, hash_table, doc_lengths, turn_mask, attn_norm_gain, attn_norm_bias,
    qkv_weight, proj_weight, ffn_norm_gain, ffn_norm_bias, expert_up, expert_down, out_grad,
):
    seq = lax.axis_index("seq")
    owner = lax.axis_index("batch")
    odd = seq % 2
    flat = (512, 768)
    rows3 = (4, 128, 768)
    gain_one, bias_one = attn_norm_gain.reshape(1, 768), attn_norm_bias.reshape(1, 768)
    gain_two, bias_two = ffn_norm_gain.reshape(1, 768), ffn_norm_bias.reshape(1, 768)
    up, down = expert_up[0], expert_down[0]

    behind_two = lax.ppermute(block_input, "seq", AHEAD_TWO)
    early = lax.ppermute(block_input, "seq", UP_ONE)
    late = lax.ppermute(behind_two, "seq", DOWN_ONE)

    ends = jnp.cumsum(doc_lengths, axis=-1)
    position = seq * 128 + jnp.arange(128, dtype=I32)
    start = jnp.max(
        jnp.where(ends[:, None, :] <= position[None, :, None], ends[:, None, :], 0), axis=-1
    )
    start = (start - (seq - 2) * 128).astype(I32).reshape(4, 1, 128)
    table = jnp.pad(hash_table, (0, 8192 - 8008)).reshape(64, 128).T.astype(BF)
    turn = turn_mask.reshape(512, 1).astype(F32)

    target, counts, grad_sent = kernel_call(
        route_kernel,
        [shape((8, 512), I32), shape((16, 128), F32), shape((1024, 768))],
        [token_ids, table, turn_mask, out_grad.reshape(flat)],
        "route", 10**9,
    )
    target_col = target[0].reshape(512, 1)
    grad_rows = exchange(grad_sent)

    normed, query, keyval = kernel_call(
        own_kernel,
        [shape(flat), shape(flat), shape((512, 1536))],
        [block_input.reshape(flat), gain_one, bias_one, qkv_weight],
        "own", 18 * 10**8,
    )
    query, keyval = query.reshape(rows3), keyval.reshape(4, 128, 1536)

    normed_halo, keyval_halo, attended, log_total, after, rows_sent = kernel_call(
        forward_kernel,
        [
            shape((4, 256, 768)), shape((4, 256, 1536)), shape(rows3), shape((4, 8, 256), F32),
            shape(flat, F32), shape((1024, 768)),
        ],
        [
            behind_two, early, late, block_input, start, gain_one, bias_one, qkv_weight, query, keyval,
            proj_weight, gain_two, bias_two, target,
        ],
        "forward", 8 * 10**9,
        scratch=[pltpu.VMEM((384, 1536), BF)],
    )
    rows = exchange(rows_sent)

    raw = kernel_call(
        active_grad_kernel,
        [shape((1024, 3072))],
        [grad_rows, down],
        "active_grad", 48 * 10**8,
        grid=(6,),
        in_specs=[
            pl.BlockSpec((1024, 768), lambda i: (0, 0)),
            pl.BlockSpec((512, 768), lambda i: (i, 0)),
        ],
        out_specs=[pl.BlockSpec((1024, 512), lambda i: (0, i))],
    )[0]

    active, hidden_grad, back_sent = kernel_call(
        expert_kernel,
        [shape((1024, 3072)), shape((1024, 3072)), shape((1024, 768))],
        [rows, up, raw],
        "expert", 97 * 10**8,
        grid=(6,),
        in_specs=[
            pl.BlockSpec((1024, 768), lambda i: (0, 0)),
            pl.BlockSpec((768, 512), lambda i: (0, i)),
            pl.BlockSpec((1024, 512), lambda i: (0, i)),
        ],
        out_specs=[
            pl.BlockSpec((1024, 512), lambda i: (0, i)),
            pl.BlockSpec((1024, 512), lambda i: (0, i)),
            pl.BlockSpec((1024, 768), lambda i: (0, 0)),
        ],
        scratch=[pltpu.VMEM((1024, 768), F32)],
    )
    back = exchange(back_sent)

    result, up_part, down_part = kernel_call(
        weight_kernel,
        [shape((1024, 768)), shape((8, 768, 384)), shape((8, 768, 384))],
        [rows, grad_rows, active, hidden_grad, down],
        "weights", 145 * 10**8,
        grid=(4,),
        in_specs=[
            pl.BlockSpec((1024, 768), lambda i: (0, 0)),
            pl.BlockSpec((1024, 768), lambda i: (0, 0)),
            pl.BlockSpec((1024, 768), lambda i: (0, i)),
            pl.BlockSpec((1024, 768), lambda i: (0, i)),
            pl.BlockSpec((768, 768), lambda i: (i, 0)),
        ],
        out_specs=[
            pl.BlockSpec((1024, 768), lambda i: (0, 0)),
            pl.BlockSpec((2, 768, 384), lambda i: (i, 0, 0)),
            pl.BlockSpec((2, 768, 384), lambda i: (i, 0, 0)),
        ],
        scratch=[pltpu.VMEM((768, 1024), BF), pltpu.VMEM((768, 1024), BF), pltpu.VMEM((1024, 768), F32)],
    )
    returned = exchange(result)
    up_sum = lax.psum_scatter(up_part, "seq", scatter_dimension=0, tiled=True)
    down_sum = lax.psum_scatter(down_part, "seq", scatter_dimension=0, tiled=True)

    after_grad, attended_grad, proj_part, terms_two = kernel_call(
        middle_kernel,
        [shape(flat, F32), shape(flat), shape((3, 768, 256)), shape((2, 768), F32)],
        [back, target_col, after, out_grad.reshape(flat), turn, gain_two, proj_weight, attended.reshape(flat)],
        "middle", 2 * 10**9,
    )

    query_grad, own_grad, halo_grad = kernel_call(
        backward_kernel,
        [shape(rows3), shape((4, 128, 1536)), shape((4, 256, 1536))],
        [query, keyval, keyval_halo, attended_grad.reshape(rows3), log_total, start],
        "backward", 6 * 10**9,
        scratch=[pltpu.VMEM((384, 1536), BF)],
    )
    query_grad, own_grad = query_grad.reshape(flat), own_grad.reshape(512, 1536)

    qkv_part = kernel_call(
        qkv_grad_kernel,
        [shape((9, 768, 256))],
        [normed, normed_halo.reshape(1024, 768), query_grad, own_grad, halo_grad.reshape(1024, 1536)],
        "qkv_grad", 42 * 10**8,
        grid=(9,),
        in_specs=[
            pl.BlockSpec((512, 768), lambda i: (0, 0)),
            pl.BlockSpec((1024, 768), lambda i: (0, 0)),
            pl.BlockSpec((512, 256), lambda i: (0, jnp.minimum(i, 2))),
            pl.BlockSpec((512, 256), lambda i: (0, jnp.maximum(i - 3, 0))),
            pl.BlockSpec((1024, 256), lambda i: (0, jnp.maximum(i - 3, 0))),
        ],
        out_specs=[pl.BlockSpec((1, 768, 256), lambda i: (i, 0, 0))],
        scratch=[pltpu.VMEM((768, 512), BF), pltpu.VMEM((768, 1024), BF)],
    )[0]

    input_own, input_two, input_one, terms_one = kernel_call(
        input_part_kernel,
        [shape(flat, F32), shape(rows3), shape(rows3), shape((2, 768), F32)],
        [query_grad, own_grad, halo_grad, qkv_weight, block_input.reshape(flat), behind_two, early, late],
        "input_part", 42 * 10**8,
    )
    from_one = lax.ppermute(input_one, "seq", SWAP)
    passed = jnp.where(odd == 1, input_two + from_one, input_two)
    from_two = lax.ppermute(passed, "seq", BACK_TWO)
    even = (1 - odd).astype(F32).reshape(1, 1)
    input_grad = kernel_call(
        input_grad_kernel,
        [shape(flat, F32)],
        [
            even, block_input.reshape(flat), gain_one, input_own, from_one.reshape(flat),
            from_two.reshape(flat), after_grad,
        ],
        "input_grad", 10**7,
        in_specs=[SM] + [VM] * 6,
    )[0]

    here = jnp.arange(128, dtype=I32) == seq * 16 + owner
    tally = jnp.where(here[None, :], counts, 0.0).reshape(2048)
    extra = jnp.concatenate([terms_one.reshape(-1), terms_two.reshape(-1), tally]).astype(BF)
    extra = jnp.pad(extra, (0, (PAY_ROWS - GEMM_ROWS) * 256 - extra.size)).reshape(-1, 256)
    payload = jnp.concatenate([qkv_part.reshape(-1, 256), proj_part.reshape(-1, 256), extra], axis=0)
    summed = sum_everywhere(payload)
    blocks = summed[:GEMM_ROWS].reshape(12, 768, 256).astype(F32)
    qkv_sum = jnp.transpose(blocks[:9], (1, 0, 2)).reshape(768, 2304)
    proj_sum = jnp.transpose(blocks[9:], (1, 0, 2)).reshape(768, 768)
    tail = summed[GEMM_ROWS:].reshape(-1).astype(F32)
    terms = tail[:3072].reshape(4, 768)
    every = tail[3072:5120].reshape(16, 8, 16).astype(I32)

    block_output = kernel_call(
        output_kernel, [shape(flat)], [after, target_col, returned], "output", 8 * 10**8
    )[0]
    return (
        block_output.reshape(rows3),
        input_grad.reshape(rows3),
        terms[0],
        terms[1],
        qkv_sum,
        proj_sum,
        terms[2],
        terms[3],
        up_sum.astype(F32),
        jnp.swapaxes(down_sum.astype(F32), 1, 2),
        jnp.sum(every, axis=(1, 2)),
        lax.dynamic_slice(every, (owner, seq, 0), (1, 1, 16)),
    )


def solution(mesh):
    placed = (
        P("batch", "seq", None),
        P("batch", "seq"),
        P(),
        P("batch", None),
        P("batch", "seq"),
        P(),
        P(),
        P(),
        P(),
        P(),
        P(),
        P("batch", None, None),
        P("batch", None, None),
        P("batch", "seq", None),
    )
    return jax.shard_map(
        local,
        mesh=mesh,
        in_specs=placed,
        out_specs=(
            P("batch", "seq", None),
            P("batch", "seq", None),
            P(),
            P(),
            P(),
            P(),
            P(),
            P(),
            P("batch", None, "seq"),
            P("batch", "seq", None),
            P(),
            P("batch", "seq", None),
        ),
        check_vma=False,
    )
```

```python
import jax
import jax.numpy as jnp
from jax import lax
from jax.experimental import pallas as pl
from jax.experimental.pallas import tpu as pltpu
from jax.sharding import PartitionSpec as P

BF = jnp.bfloat16
F32 = jnp.float32
I32 = jnp.int32
EPS = 1e-05
MASKED = -1e30
HEADS = 12
HEAD_SIZE = 64
PAIRS = 6
CAP = 64
SWAP = [(i, i ^ 1) for i in range(8)]
UP_ONE = [(i, i + 1) for i in range(0, 8, 2)]
DOWN_ONE = [(i + 1, i) for i in range(0, 8, 2)]
AHEAD_TWO = [(i, i + 2) for i in range(6)]
BACK_TWO = [(i + 2, i) for i in range(6)]
HALF_ROWS = 5120
GEMM_ROWS = 4608
VM = pl.BlockSpec(memory_space=pltpu.VMEM)
SM = pl.BlockSpec(memory_space=pltpu.SMEM)


def shape(dims, kind=BF):
    return jax.ShapeDtypeStruct(dims, kind)


def kernel_call(body, outs, args, name, flops, grid=None, in_specs=None, out_specs=None, scratch=(), aliases=None):
    moved = sum(a.size * a.dtype.itemsize for a in args) + sum(
        o.size * o.dtype.itemsize for o in outs
    )
    extra = {} if grid is None else {"grid": grid}
    return pl.pallas_call(
        body,
        out_shape=outs,
        in_specs=in_specs or [VM] * len(args),
        out_specs=out_specs or [VM] * len(outs),
        scratch_shapes=list(scratch),
        compiler_params=pltpu.CompilerParams(vmem_limit_bytes=58 * 1024 * 1024),
        cost_estimate=pl.CostEstimate(flops=flops, bytes_accessed=moved, transcendentals=0),
        name=name,
        input_output_aliases=aliases or {},
        **extra,
    )(*args)


def nn(a, b):
    return jnp.dot(a, b, preferred_element_type=F32)


def nt(a, b):
    return lax.dot_general(a, b, (((1,), (1,)), ((), ())), preferred_element_type=F32)


def tn(a, b):
    return lax.dot_general(a, b, (((0,), (0,)), ((), ())), preferred_element_type=F32)


def iota(dims, axis):
    return lax.broadcasted_iota(I32, dims, axis)


def row(ref):
    return ref[...].reshape(1, 768)


def column(line):
    return jnp.broadcast_to(line, (128, line.shape[1])).T[:, 0:1]


def flat_line(ref):
    return jnp.concatenate([ref[i : i + 1, :] for i in range(4)], axis=1).astype(F32)


def norm_parts(values):
    centred = values - jnp.mean(values, axis=-1, keepdims=True)
    inverse = lax.rsqrt(jnp.mean(centred * centred, axis=-1, keepdims=True) + EPS)
    return centred * inverse, inverse


def norm_back(grad, gain, unit, inverse):
    t = grad * gain
    return inverse * (
        t - jnp.mean(t, axis=-1, keepdims=True) - unit * jnp.mean(t * unit, axis=-1, keepdims=True)
    )


def route_kernel(place, tok, table, turn, grad, target_out, tally, sent):
    ids = jnp.concatenate([tok[i : i + 1, :] for i in range(4)], axis=1)
    live = flat_line(turn)
    high, low = ids >> 7, ids & 127
    picked = tn(table[...].astype(F32).astype(BF), (iota((64, 512), 0) == high).astype(F32).astype(BF))
    chosen = jnp.sum(jnp.where(iota((128, 512), 0) == low, picked, 0.0), axis=0, keepdims=True)
    member = (iota((16, 512), 0) == chosen.astype(I32)).astype(F32)
    earlier = (iota((512, 512), 0) < iota((512, 512), 1)).astype(F32).astype(BF)
    before = nn(member.astype(BF), earlier)
    slot = jnp.sum(before * member, axis=0, keepdims=True)
    target = (chosen * CAP + slot).astype(I32)
    target_out[...] = jnp.broadcast_to(target, (8, 512))
    counts = jnp.sum(member, axis=1, keepdims=True)
    tally[...] = jnp.where(iota((16, 128), 1) == place[0] * 16 + place[1], counts, 0.0)
    for i in range(4):
        placing = jnp.where(iota((256, 512), 0) + 256 * i == target, live, 0.0).astype(BF)
        sent[256 * i : 256 * (i + 1), :] = nn(placing, grad[...]).astype(BF)


def own_kernel(x, gain, bias, weight, unit_out, query, keyval):
    unit, _ = norm_parts(x[...].astype(F32))
    unit_out[...] = unit.astype(BF)
    rows = (unit * row(gain) + row(bias)).astype(BF)
    query[...] = nn(rows, weight[:, :768]).astype(BF)
    keyval[...] = nn(rows, weight[:, 768:]).astype(BF)


def head_masks(scale):
    lane = iota((1, 128), 1)
    first = jnp.where(lane < 64, scale, 0.0).astype(BF)
    second = jnp.where(lane >= 64, scale, 0.0).astype(BF)
    return first, second


def stack_heads(pair, masks):
    return jnp.concatenate([pair * masks[0], pair * masks[1]], axis=0)


def window_bias(place, lengths, r):
    lane = iota((1, 128), 1) + place[0] * 128
    end, start = jnp.int32(0), jnp.zeros((1, 128), I32)
    for j in range(8):
        end = end + lengths[r, j]
        start = jnp.where(end <= lane, end, start)
    start = start - (place[0] - 2) * 128
    key = iota((384, 128), 0)
    allowed = (key >= start) & (key <= iota((384, 128), 1) + 256)
    half = jnp.where(allowed, 0.0, MASKED)
    return jnp.concatenate([half, half], axis=1)


def join_heads(both):
    one = jnp.where(iota((128, 128), 0) < 64, both[:, :128], both[:, 128:])
    return one.T


def forward_kernel(
    place, lengths, behind_two, early, late, x, gain, bias, weight, query, keyval, proj, gain_two, bias_two,
    target, unit_halo, keyval_halo, attended, log_out, after_out, sent, context,
):
    scales = head_masks(HEAD_SIZE ** (-0.5))

    def one_row(r, carry):
        halo = jnp.concatenate([behind_two[r], early[r] + late[r]], axis=0).astype(F32)
        unit, _ = norm_parts(halo)
        unit_halo[r] = unit.astype(BF)
        rows = (unit * row(gain) + row(bias)).astype(BF)
        fresh = nn(rows, weight[:, 768:]).astype(BF)
        keyval_halo[r] = fresh
        context[0:256, :] = fresh
        context[256:384, :] = keyval[r]
        mask = window_bias(place, lengths, r)
        for p in range(PAIRS):
            lo, hi = 128 * p, 128 * (p + 1)
            keys = context[:, lo:hi]
            values = context[:, 768 + lo : 768 + hi]
            stacked = stack_heads(query[r, :, lo:hi], scales)
            scores = nt(keys, stacked) + mask
            top = jnp.max(scores, axis=0, keepdims=True)
            weights = jnp.exp(scores - top)
            total = jnp.sum(weights, axis=0, keepdims=True)
            log_out[r, p : p + 1, :] = top + jnp.log(total)
            share = (weights * (1.0 / total)).astype(BF)
            attended[r, :, lo:hi] = join_heads(tn(values, share)).astype(BF)
        return carry

    lax.fori_loop(0, 4, one_row, 0)
    mixed = nn(attended[...].reshape(512, 768), proj[...])
    after = x[...].reshape(512, 768).astype(F32) + mixed
    after_out[...] = after
    unit, _ = norm_parts(after)
    rows = (unit * row(gain_two) + row(bias_two)).astype(BF)
    for i in range(4):
        placing = (iota((256, 512), 0) + 256 * i == target[0:1, :]).astype(F32).astype(BF)
        sent[256 * i : 256 * (i + 1), :] = nn(placing, rows).astype(BF)


def active_grad_kernel(grad, down, out):
    out[...] = nt(grad[...], down[...]).astype(BF)


def gelu_both(v):
    c = 0.7978845608028654
    square = v * v
    t = jnp.tanh(v * (c + (c * 0.044715) * square))
    half = 0.5 * v
    value = half + half * t
    slope = 0.5 + 0.5 * t + half * (1.0 - t * t) * (c + (3.0 * c * 0.044715) * square)
    return value, slope


def expert_kernel(x, up, raw, active, hidden_grad, back, total):
    step = pl.program_id(0)

    @pl.when(step == 0)
    def _():
        total[...] = jnp.zeros_like(total)

    for r in range(4):
        rows = slice(256 * r, 256 * (r + 1))
        value, slope = gelu_both(nn(x[rows, :], up[...]))
        active[rows, :] = value.astype(BF)
        low = (raw[rows, :].astype(F32) * slope).astype(BF)
        hidden_grad[rows, :] = low
        total[rows, :] += nt(low, up[...])

    @pl.when(step == pl.num_programs(0) - 1)
    def _():
        back[...] = total[...].astype(BF)


def weight_kernel(x, grad, active, hidden_grad, down, out, parts, x_t, grad_t, total):
    step = pl.program_id(0)

    @pl.when(step == 0)
    def _():
        total[...] = jnp.zeros_like(total)
        x_t[...] = x[...].T
        grad_t[...] = grad[...].T

    total[...] += nn(active[...], down[...])
    one = nn(x_t[...], hidden_grad[...]).astype(BF)
    two = nn(grad_t[...], active[...]).astype(BF)
    for j in range(2):
        parts[j, :768, :] = one[:, 384 * j : 384 * (j + 1)]
        parts[j, 768:, :] = two[:, 384 * j : 384 * (j + 1)]

    @pl.when(step == pl.num_programs(0) - 1)
    def _():
        out[...] = total[...].astype(BF)


def output_kernel(after, target, returned, out):
    placing = (iota((512, 1024), 1).astype(F32) == column(target[0:1, :].astype(F32))).astype(F32).astype(BF)
    out[...] = (after[...] + nn(placing, returned[...])).astype(BF)


def middle_kernel(
    back, target, after, grad, turn, gain, proj, attended, after_grad, attended_grad, proj_part, terms
):
    placing = (iota((512, 1024), 1).astype(F32) == column(target[0:1, :].astype(F32))).astype(F32).astype(BF)
    normed_grad = nn(placing, back[...])
    unit, inverse = norm_parts(after[...])
    terms[0:1, :] = jnp.sum(normed_grad * unit, axis=0, keepdims=True)
    terms[1:2, :] = jnp.sum(normed_grad, axis=0, keepdims=True)
    upstream = grad[...].astype(F32) * column(flat_line(turn))
    total = upstream + norm_back(normed_grad, row(gain), unit, inverse)
    after_grad[...] = total
    low = total.astype(BF)
    attended_grad[...] = nt(low, proj[...]).astype(BF)
    for i in range(3):
        proj_part[i] = tn(attended[...], low[:, 256 * i : 256 * (i + 1)]).astype(BF)


def backward_kernel(
    place, lengths, query, keyval, keyval_halo, attended_grad, log_total,
    query_grad, own_grad, halo_grad, context,
):
    scales = head_masks(HEAD_SIZE ** (-0.5))
    ones = head_masks(1.0)

    def one_row(r, carry):
        context[0:256, :] = keyval_halo[r]
        context[256:384, :] = keyval[r]
        mask = window_bias(place, lengths, r)
        for p in range(PAIRS):
            lo, hi = 128 * p, 128 * (p + 1)
            keys = context[:, lo:hi]
            values = context[:, 768 + lo : 768 + hi]
            stacked = stack_heads(query[r, :, lo:hi], scales)
            grads = stack_heads(attended_grad[r, :, lo:hi], ones)
            scores = nt(keys, stacked) + mask
            share = jnp.exp(scores - log_total[r, p : p + 1, :])
            share_grad = nt(values, grads)
            row_sum = jnp.sum(share * share_grad, axis=0, keepdims=True)
            score_grad = (share * (share_grad - row_sum)).astype(BF)
            key_grad = nn(score_grad, stacked).astype(BF)
            value_grad = nn(share.astype(BF), grads).astype(BF)
            halo_grad[r, :, lo:hi] = key_grad[:256]
            own_grad[r, :, lo:hi] = key_grad[256:]
            halo_grad[r, :, 768 + lo : 768 + hi] = value_grad[:256]
            own_grad[r, :, 768 + lo : 768 + hi] = value_grad[256:]
            turned = join_heads(tn(keys, score_grad))
            query_grad[r, :, lo:hi] = (turned * HEAD_SIZE ** (-0.5)).astype(BF)
        return carry

    lax.fori_loop(0, 4, one_row, 0)


def qkv_grad_kernel(
    half, unit, unit_halo, query_grad, own_grad, halo_grad, weight, gain, bias, proj_part, terms_two, tally,
    out, own_t, halo_t, gain_sum, bias_sum, gain_wide, bias_wide,
):
    step = pl.program_id(0)
    block = half[0] * 6 + step

    @pl.when(step == 0)
    def _():
        own_t[0:768, :] = unit[...].T
        own_t[768:784, :] = jnp.ones((16, 512), BF)
        halo_t[0:768, :] = unit_halo[...].T
        halo_t[768:784, :] = jnp.ones((16, 1024), BF)
        gain_wide[...] = jnp.broadcast_to(row(gain), (256, 768)).T
        bias_wide[...] = jnp.broadcast_to(row(bias), (256, 768)).T
        gain_sum[...] = jnp.zeros_like(gain_sum)
        bias_sum[...] = jnp.zeros_like(bias_sum)

    def finish(both):
        body, sums = both[0:768], both[768:769]
        place = pl.ds(pl.multiple_of(step * 768, 768), 768)
        out[place, :] = (gain_wide[...] * body + bias_wide[...] * sums).astype(BF)
        wide = weight[...].astype(F32)
        gain_sum[...] += wide * body
        bias_sum[...] += wide * sums

    @pl.when(block < 3)
    def _():
        finish(nn(own_t[...], query_grad[...]))

    @pl.when((block >= 3) & (block < 9))
    def _():
        finish(nn(own_t[...], own_grad[...]) + nn(halo_t[...], halo_grad[...]))

    @pl.when(block >= 9)
    def _():
        out[pl.ds(pl.multiple_of(step * 768, 768), 768), :] = proj_part[0]

    @pl.when(step == 5)
    def _():
        columns = jnp.concatenate(
            [
                jnp.broadcast_to(jnp.sum(gain_sum[...], axis=1, keepdims=True), (768, 128)),
                jnp.broadcast_to(jnp.sum(bias_sum[...], axis=1, keepdims=True), (768, 128)),
            ],
            axis=1,
        ).T
        out[GEMM_ROWS:, :] = jnp.zeros((HALF_ROWS - GEMM_ROWS, 256), BF)
        first = (half[0] == 0).astype(F32)
        for t in range(3):
            lanes = slice(256 * t, 256 * (t + 1))
            block = jnp.concatenate(
                [columns[0:1, lanes], columns[128:129, lanes], terms_two[:, lanes] * first], axis=0
            )
            out[GEMM_ROWS + 16 * t : GEMM_ROWS + 16 * t + 16, :] = jnp.concatenate(
                [block, jnp.zeros((12, 256), F32)], axis=0
            ).astype(BF)
        out[GEMM_ROWS + 48 : GEMM_ROWS + 64, 0:128] = (tally[...] * first).astype(BF)


def place_half(half, data, qkv, proj, stage, sems):
    for j in range(6):
        lanes = slice(256 * (j % 3), 256 * (j % 3 + 1))
        stage[j // 3, :, lanes] = data[768 * j : 768 * (j + 1), :].astype(F32)

    @pl.when(half == 0)
    def _():
        one = pltpu.make_async_copy(stage.at[0], qkv.at[:, 0:768], sems.at[0])
        two = pltpu.make_async_copy(stage.at[1], qkv.at[:, 768:1536], sems.at[1])
        one.start()
        two.start()
        one.wait()
        two.wait()

    @pl.when(half == 1)
    def _():
        one = pltpu.make_async_copy(stage.at[0], qkv.at[:, 1536:2304], sems.at[0])
        two = pltpu.make_async_copy(stage.at[1], proj, sems.at[1])
        one.start()
        two.start()
        one.wait()
        two.wait()


def finish_mine_kernel(place, mine, qkv, proj, stage, sems):
    place_half(place[0] % 2, mine, qkv, proj, stage, sems)


def finish_other_kernel(
    place, other, tail, qkv_in, proj_in, qkv, proj, gain_one, bias_one, gain_two, bias_two, counts, received, stage, sems
):
    both = tail[...].astype(F32) + other[GEMM_ROWS:, :].astype(F32)
    for i, out in enumerate([gain_one, bias_one, gain_two, bias_two]):
        line = jnp.concatenate([both[16 * t + i : 16 * t + i + 1, :] for t in range(3)], axis=1)
        out[...] = line.reshape(768)
    every = both[48:64, 0:128]
    counts[...] = nt(jnp.ones((8, 128), BF), every.astype(BF))[0:1, :].astype(I32).reshape(16)
    chosen = (iota((16, 128), 0) == place[1]) & ((iota((16, 128), 1) >> 4) == place[0])
    mine = jnp.where(chosen, every, 0.0).astype(BF)
    fold = ((iota((128, 16), 0) & 15) == iota((128, 16), 1)).astype(F32).astype(BF)
    received[0] = jnp.sum(nn(mine, fold), axis=0, keepdims=True).astype(I32)
    place_half(1 - place[0] % 2, other, qkv, proj, stage, sems)


def expert_sum_kernel(parts, up, down):
    up[0] = parts[0, :768, :].astype(F32)
    down[0] = parts[0, 768:, :].astype(F32).T


def input_part_kernel(
    query_grad, own_grad, halo_grad, weight, own_out, two_out, one_out
):
    for r in range(4):
        part = nt(halo_grad[r], weight[:, 768:])
        two_out[r] = part[:128].astype(BF)
        one_out[r] = part[128:].astype(BF)
    own_out[...] = nt(query_grad[...], weight[:, :768]) + nt(own_grad[...], weight[:, 768:])


def input_grad_kernel(even, x, gain, own, from_one, from_two, after_grad, out):
    unit, inverse = norm_parts(x[...].astype(F32))
    total = own[...] + from_two[...].astype(F32) + even[0, 0] * from_one[...].astype(F32)
    out[...] = after_grad[...] + norm_back(total, row(gain), unit, inverse)


PAIR_ONE = [b ^ 1 for b in range(4)]
PAIR_TWO = [b ^ 3 for b in range(4)]


def x_route(pair):
    return [(b, (b & 12) | pair[b & 3]) for b in range(16)]


def y_route(pair):
    return [(b, (b & 3) | (pair[b >> 2] << 2)) for b in range(16)]


def along_x(d):
    return [(b, (b & 12) | ((b + d) & 3)) for b in range(16)]


def along_y(d):
    return [(b, (b + 4 * d) & 15) for b in range(16)]


def along_z(d):
    return [(s, (s + 2 * d) & 7) for s in range(8)]


def pick(array, index):
    return lax.dynamic_index_in_dim(array, index, 0, keepdims=False)


def part_of(array, index):
    return lax.dynamic_index_in_dim(array, index % 4, 1, keepdims=False)


def meet(array, route, place):
    total = part_of(array, place).astype(F32)
    for d in (2, 1, 3):
        total = total + lax.ppermute(part_of(array, place + d), "batch", route(d)).astype(F32)
    return total.astype(BF)


def gather(piece, route, place):
    parts = [piece] + [lax.ppermute(piece, "batch", route(d)) for d in (1, 2, 3)]
    stack = jnp.stack(parts, axis=1)
    return jnp.stack([part_of(stack, place - p + 4) for p in range(4)], axis=1)


def sum_everywhere(keep, got, beside):
    rows, lanes = keep.shape
    place = lax.axis_index("batch")
    x, y = place % 4, place // 4
    xs = [(x_route(PAIR_ONE), (x & 1) ^ (x >> 1)), (x_route(PAIR_TWO), x >> 1)]
    ys = [(y_route(PAIR_ONE), (y & 1) ^ (y >> 1)), (y_route(PAIR_TWO), y >> 1)]
    plans = [xs + ys, xs[::-1] + ys[::-1], ys + xs, ys[::-1] + xs[::-1]]
    kept, got = keep.reshape(4, rows // 4, lanes), got.reshape(4, rows // 4, lanes)
    streams = [(kept[i], got[i]) for i in range(4)]
    for stage in range(2):
        sent, stay = [], []
        for plan, pair in zip(plans, streams):
            bit = plan[stage][1]
            size = pair[0].shape[0] // 2
            halves = [a.reshape(2, size, lanes) for a in pair]
            sent.append(
                (pick(halves[0], 1 - bit).astype(F32) + pick(halves[1], 1 - bit).astype(F32)).astype(BF)
            )
            stay.append(
                (pick(halves[0], bit).astype(F32) + pick(halves[1], bit).astype(F32)).astype(BF)
            )
        moved = [
            lax.ppermute(data, "batch", plan[stage][0]) for plan, data in zip(plans, sent)
        ]
        if stage == 0:
            stay[0] = after_all(stay[0], beside[0])
        streams = list(zip(stay, moved))
    chunks = [(a.astype(F32) + b.astype(F32)).astype(BF) for a, b in streams]
    quarter = chunks[0].shape[0] // 4
    group = (2, 4, quarter, lanes)
    one = meet(jnp.stack(chunks[:2]).reshape(group), along_y, y)
    two = meet(jnp.stack(chunks[2:]).reshape(group), along_x, x)
    whole = jnp.stack([one, two])
    total = whole.astype(F32)
    for d in (2, 1, 3):
        total = total + lax.ppermute(whole, "seq", along_z(d)).astype(F32)
    total = after_all(total.astype(BF), beside[1])
    one = gather(total[0], along_y, y).reshape(2, 4 * quarter, lanes)
    two = gather(total[1], along_x, x).reshape(2, 4 * quarter, lanes)
    chunks = [one[0], one[1], two[0], two[1]]
    for stage in (1, 0):
        moved = [
            lax.ppermute(data, "batch", plan[stage][0]) for plan, data in zip(plans, chunks)
        ]
        chunks = [
            jnp.where(plan[stage][1] == 0, jnp.stack([a, b]), jnp.stack([b, a])).reshape(-1, lanes)
            for plan, a, b in zip(plans, chunks, moved)
        ]
    return jnp.concatenate(chunks, axis=0)


def after_all(value, *others):
    return lax.optimization_barrier((value, *others))[0]


def exchange(array):
    return lax.all_to_all(
        array.reshape(16, CAP, 768), "batch", split_axis=0, concat_axis=0, tiled=True
    ).reshape(1024, 768)


def local(
    block_input, token_ids, hash_table, doc_lengths, turn_mask, attn_norm_gain, attn_norm_bias,
    qkv_weight, proj_weight, ffn_norm_gain, ffn_norm_bias, expert_up, expert_down, out_grad,
):
    seq = lax.axis_index("seq")
    owner = lax.axis_index("batch")
    odd = seq % 2
    flat = (512, 768)
    rows3 = (4, 128, 768)
    place = jnp.stack([seq, owner]).astype(I32)
    up, down = expert_up[0], expert_down[0]

    behind_two = lax.ppermute(block_input, "seq", AHEAD_TWO)
    early = lax.ppermute(block_input, "seq", UP_ONE)

    table = jnp.pad(hash_table, (0, 8192 - 8008)).reshape(64, 128)
    target, tally, grad_sent = kernel_call(
        route_kernel,
        [shape((8, 512), I32), shape((16, 128), F32), shape((1024, 768))],
        [place, token_ids, table, turn_mask, out_grad.reshape(flat)],
        "route", 10**9,
        in_specs=[SM] + [VM] * 4,
    )
    grad_rows = exchange(grad_sent)

    unit, query, keyval = kernel_call(
        own_kernel,
        [shape(flat), shape(flat), shape((512, 1536))],
        [block_input.reshape(flat), attn_norm_gain, attn_norm_bias, qkv_weight],
        "own", 18 * 10**8,
    )
    late = lax.ppermute(after_all(behind_two, query, grad_sent), "seq", DOWN_ONE)
    query, keyval = query.reshape(rows3), keyval.reshape(4, 128, 1536)

    unit_halo, keyval_halo, attended, log_total, after, rows_sent = kernel_call(
        forward_kernel,
        [
            shape((4, 256, 768)), shape((4, 256, 1536)), shape(rows3), shape((4, 8, 256), F32),
            shape(flat, F32), shape((1024, 768)),
        ],
        [
            place, doc_lengths, behind_two, early, late, block_input, attn_norm_gain, attn_norm_bias,
            qkv_weight, query, keyval, proj_weight, ffn_norm_gain, ffn_norm_bias, target,
        ],
        "forward", 8 * 10**9,
        in_specs=[SM] * 2 + [VM] * 13,
        scratch=[pltpu.VMEM((384, 1536), BF)],
    )
    rows = exchange(rows_sent)

    raw = kernel_call(
        active_grad_kernel,
        [shape((1024, 3072))],
        [grad_rows, down],
        "active_grad", 48 * 10**8,
        grid=(6,),
        in_specs=[
            pl.BlockSpec((1024, 768), lambda i: (0, 0)),
            pl.BlockSpec((512, 768), lambda i: (i, 0)),
        ],
        out_specs=[pl.BlockSpec((1024, 512), lambda i: (0, i))],
    )[0]

    active, hidden_grad, back_sent = kernel_call(
        expert_kernel,
        [shape((1024, 3072)), shape((1024, 3072)), shape((1024, 768))],
        [rows, up, raw],
        "expert", 97 * 10**8,
        grid=(6,),
        in_specs=[
            pl.BlockSpec((1024, 768), lambda i: (0, 0)),
            pl.BlockSpec((768, 512), lambda i: (0, i)),
            pl.BlockSpec((1024, 512), lambda i: (0, i)),
        ],
        out_specs=[
            pl.BlockSpec((1024, 512), lambda i: (0, i)),
            pl.BlockSpec((1024, 512), lambda i: (0, i)),
            pl.BlockSpec((1024, 768), lambda i: (0, 0)),
        ],
        scratch=[pltpu.VMEM((1024, 768), F32)],
    )
    back = exchange(back_sent)

    result, parts = kernel_call(
        weight_kernel,
        [shape((1024, 768)), shape((8, 1536, 384))],
        [rows, grad_rows, active, hidden_grad, down],
        "weights", 145 * 10**8,
        grid=(4,),
        in_specs=[
            pl.BlockSpec((1024, 768), lambda i: (0, 0)),
            pl.BlockSpec((1024, 768), lambda i: (0, 0)),
            pl.BlockSpec((1024, 768), lambda i: (0, i)),
            pl.BlockSpec((1024, 768), lambda i: (0, i)),
            pl.BlockSpec((768, 768), lambda i: (i, 0)),
        ],
        out_specs=[
            pl.BlockSpec((1024, 768), lambda i: (0, 0)),
            pl.BlockSpec((2, 1536, 384), lambda i: (i, 0, 0)),
        ],
        scratch=[pltpu.VMEM((768, 1024), BF), pltpu.VMEM((768, 1024), BF), pltpu.VMEM((1024, 768), F32)],
    )
    returned = exchange(result)
    parts_sum = lax.psum_scatter(after_all(parts, back), "seq", scatter_dimension=0, tiled=True)

    after_grad, attended_grad, proj_part, terms_two = kernel_call(
        middle_kernel,
        [shape(flat, F32), shape(flat), shape((3, 768, 256)), shape((2, 768), F32)],
        [back, target, after, out_grad.reshape(flat), turn_mask, ffn_norm_gain, proj_weight, attended.reshape(flat)],
        "middle", 2 * 10**9,
    )

    query_grad, own_grad, halo_grad = kernel_call(
        backward_kernel,
        [shape(rows3), shape((4, 128, 1536)), shape((4, 256, 1536))],
        [place, doc_lengths, query, keyval, keyval_halo, attended_grad.reshape(rows3), log_total],
        "backward", 6 * 10**9,
        in_specs=[SM] * 2 + [VM] * 5,
        scratch=[pltpu.VMEM((384, 1536), BF)],
    )
    query_grad, own_grad = query_grad.reshape(flat), own_grad.reshape(512, 1536)

    def half_of(which, first):
        return pl.pallas_call(
            qkv_grad_kernel,
            out_shape=shape((HALF_ROWS, 256)),
            grid_spec=pltpu.PrefetchScalarGridSpec(
                num_scalar_prefetch=1,
                grid=(6,),
                in_specs=[
                    pl.BlockSpec((512, 768), lambda i, h: (0, 0)),
                    pl.BlockSpec((1024, 768), lambda i, h: (0, 0)),
                    pl.BlockSpec((512, 256), lambda i, h: (0, jnp.minimum(6 * h[0] + i, 2))),
                    pl.BlockSpec((512, 256), lambda i, h: (0, jnp.clip(6 * h[0] + i - 3, 0, 5))),
                    pl.BlockSpec((1024, 256), lambda i, h: (0, jnp.clip(6 * h[0] + i - 3, 0, 5))),
                    pl.BlockSpec((768, 256), lambda i, h: (0, jnp.minimum(6 * h[0] + i, 8))),
                    VM,
                    VM,
                    pl.BlockSpec((1, 768, 256), lambda i, h: (jnp.maximum(6 * h[0] + i - 9, 0), 0, 0)),
                    pl.BlockSpec((2, 768), lambda i, h: (0, 0)),
                    pl.BlockSpec((16, 128), lambda i, h: (0, 0)),
                ],
                out_specs=pl.BlockSpec((HALF_ROWS, 256), lambda i, h: (0, 0)),
                scratch_shapes=[
                    pltpu.VMEM((784, 512), BF),
                    pltpu.VMEM((784, 1024), BF),
                    pltpu.VMEM((768, 256), F32),
                    pltpu.VMEM((768, 256), F32),
                    pltpu.VMEM((768, 256), F32),
                    pltpu.VMEM((768, 256), F32),
                ],
            ),
            compiler_params=pltpu.CompilerParams(vmem_limit_bytes=58 * 1024 * 1024),
            cost_estimate=pl.CostEstimate(flops=3 * 10**9, bytes_accessed=12 * 10**6, transcendentals=0),
            name="qkv_grad",
        )(
            which.reshape(1), unit, unit_halo.reshape(1024, 768), first, own_grad,
            halo_grad.reshape(1024, 1536), qkv_weight, attn_norm_gain, attn_norm_bias, proj_part,
            terms_two, tally,
        )

    away = half_of(1 - odd, query_grad)
    got = lax.ppermute(away, "seq", SWAP)
    keep = half_of(odd, after_all(query_grad, returned))

    input_own, input_two, input_one = kernel_call(
        input_part_kernel,
        [shape(flat, F32), shape(rows3), shape(rows3)],
        [after_all(query_grad, keep), own_grad, halo_grad, qkv_weight],
        "input_part", 42 * 10**8,
    )
    from_one = lax.ppermute(input_one, "seq", SWAP)
    passed = jnp.where(odd == 1, input_two + from_one, input_two)
    from_two = lax.ppermute(passed, "seq", BACK_TWO)
    even = (1 - odd).astype(F32).reshape(1, 1)
    input_grad = kernel_call(
        input_grad_kernel,
        [shape(flat, F32)],
        [
            even, block_input.reshape(flat), attn_norm_gain, input_own, from_one.reshape(flat),
            from_two.reshape(flat), after_grad,
        ],
        "input_grad", 10**7,
        in_specs=[SM] + [VM] * 6,
    )[0]

    block_output = kernel_call(
        output_kernel, [shape(flat)], [after, target, returned], "output", 8 * 10**8
    )[0]
    mine = sum_everywhere(keep, got, (input_own, block_output))
    other = lax.ppermute(mine, "seq", SWAP)
    sums = [shape((768, 2304), F32), shape((768, 768), F32)]
    away_spec = [pl.BlockSpec(memory_space=pl.ANY)] * 2
    landing = [pltpu.VMEM((2, 768, 768), F32), pltpu.SemaphoreType.DMA((2,))]
    qkv_half, proj_half = kernel_call(
        finish_mine_kernel, sums, [place, mine], "finish_mine", 10**6,
        in_specs=[SM, VM], out_specs=away_spec, scratch=landing,
    )
    line = shape((768,), F32)
    qkv_sum, proj_sum, *rest = kernel_call(
        finish_other_kernel,
        sums + [line] * 4 + [shape((16,), I32), shape((1, 1, 16), I32)],
        [place, other, mine[GEMM_ROWS:], qkv_half, proj_half],
        "finish_other", 10**6,
        in_specs=[SM, VM, VM] + away_spec, out_specs=away_spec + [VM] * 6, scratch=landing,
        aliases={3: 0, 4: 1},
    )
    up_sum, down_sum = kernel_call(
        expert_sum_kernel,
        [shape((1, 768, 384), F32), shape((1, 384, 768), F32)],
        [parts_sum], "expert_sum", 10**6,
    )

    return (
        block_output.reshape(rows3),
        input_grad.reshape(rows3),
        rest[0],
        rest[1],
        qkv_sum,
        proj_sum,
        rest[2],
        rest[3],
        up_sum,
        down_sum,
        rest[4],
        rest[5],
    )


def solution(mesh):
    placed = (
        P("batch", "seq", None),
        P("batch", "seq"),
        P(),
        P("batch", None),
        P("batch", "seq"),
        P(),
        P(),
        P(),
        P(),
        P(),
        P(),
        P("batch", None, None),
        P("batch", None, None),
        P("batch", "seq", None),
    )
    return jax.shard_map(
        local,
        mesh=mesh,
        in_specs=placed,
        out_specs=(
            P("batch", "seq", None),
            P("batch", "seq", None),
            P(),
            P(),
            P(),
            P(),
            P(),
            P(),
            P("batch", None, "seq"),
            P("batch", "seq", None),
            P(),
            P("batch", "seq", None),
        ),
        check_vma=False,
    )
```

```python
import jax
import jax.numpy as jnp
from jax import lax
from jax.experimental import pallas as pl
from jax.experimental.pallas import tpu as pltpu
from jax.sharding import PartitionSpec as P

BF = jnp.bfloat16
F32 = jnp.float32
I32 = jnp.int32
EPS = 1e-05
MASKED = -1e30
HEADS = 12
HEAD_SIZE = 64
PAIRS = 6
CAP = 64
SWAP = [(i, i ^ 1) for i in range(8)]
UP_ONE = [(i, i + 1) for i in range(0, 8, 2)]
DOWN_ONE = [(i + 1, i) for i in range(0, 8, 2)]
AHEAD_TWO = [(i, i + 2) for i in range(6)]
BACK_TWO = [(i + 2, i) for i in range(6)]
HALF_ROWS = 5120
GEMM_ROWS = 4608
VM = pl.BlockSpec(memory_space=pltpu.VMEM)
SM = pl.BlockSpec(memory_space=pltpu.SMEM)


def shape(dims, kind=BF):
    return jax.ShapeDtypeStruct(dims, kind)


def kernel_call(body, outs, args, name, flops, grid=None, in_specs=None, out_specs=None, scratch=(), aliases=None):
    moved = sum(a.size * a.dtype.itemsize for a in args) + sum(
        o.size * o.dtype.itemsize for o in outs
    )
    extra = {} if grid is None else {"grid": grid}
    return pl.pallas_call(
        body,
        out_shape=outs,
        in_specs=in_specs or [VM] * len(args),
        out_specs=out_specs or [VM] * len(outs),
        scratch_shapes=list(scratch),
        compiler_params=pltpu.CompilerParams(vmem_limit_bytes=58 * 1024 * 1024),
        cost_estimate=pl.CostEstimate(flops=flops, bytes_accessed=moved, transcendentals=0),
        name=name,
        input_output_aliases=aliases or {},
        **extra,
    )(*args)


def nn(a, b):
    return jnp.dot(a, b, preferred_element_type=F32)


def nt(a, b):
    return lax.dot_general(a, b, (((1,), (1,)), ((), ())), preferred_element_type=F32)


def tn(a, b):
    return lax.dot_general(a, b, (((0,), (0,)), ((), ())), preferred_element_type=F32)


def iota(dims, axis):
    return lax.broadcasted_iota(I32, dims, axis)


def row(ref):
    return ref[...].reshape(1, 768)


def column(line):
    return jnp.broadcast_to(line, (128, line.shape[1])).T[:, 0:1]


def flat_line(ref):
    return jnp.concatenate([ref[i : i + 1, :] for i in range(4)], axis=1).astype(F32)


def norm_parts(values):
    centred = values - jnp.mean(values, axis=-1, keepdims=True)
    inverse = lax.rsqrt(jnp.mean(centred * centred, axis=-1, keepdims=True) + EPS)
    return centred * inverse, inverse


def norm_back(grad, gain, unit, inverse):
    t = grad * gain
    return inverse * (
        t - jnp.mean(t, axis=-1, keepdims=True) - unit * jnp.mean(t * unit, axis=-1, keepdims=True)
    )


def route_kernel(place, tok, table, turn, grad, target_out, tally, sent):
    ids = jnp.concatenate([tok[i : i + 1, :] for i in range(4)], axis=1)
    live = flat_line(turn)
    high, low = ids >> 7, ids & 127
    picked = tn(table[...].astype(F32).astype(BF), (iota((64, 512), 0) == high).astype(F32).astype(BF))
    chosen = jnp.sum(jnp.where(iota((128, 512), 0) == low, picked, 0.0), axis=0, keepdims=True)
    member = (iota((16, 512), 0) == chosen.astype(I32)).astype(F32)
    earlier = (iota((512, 512), 0) < iota((512, 512), 1)).astype(F32).astype(BF)
    before = nn(member.astype(BF), earlier)
    slot = jnp.sum(before * member, axis=0, keepdims=True)
    target = (chosen * CAP + slot).astype(I32)
    target_out[...] = jnp.broadcast_to(target, (8, 512))
    counts = jnp.sum(member, axis=1, keepdims=True)
    tally[...] = jnp.where(iota((16, 128), 1) == place[0] * 16 + place[1], counts, 0.0)
    for i in range(4):
        placing = jnp.where(iota((256, 512), 0) + 256 * i == target, live, 0.0).astype(BF)
        sent[256 * i : 256 * (i + 1), :] = nn(placing, grad[...]).astype(BF)


def own_kernel(x, gain, bias, weight, unit_out, query, keyval):
    unit, _ = norm_parts(x[...].astype(F32))
    unit_out[...] = unit.astype(BF)
    rows = (unit * row(gain) + row(bias)).astype(BF)
    query[...] = nn(rows, weight[:, :768]).astype(BF)
    keyval[...] = nn(rows, weight[:, 768:]).astype(BF)


def head_masks(scale):
    lane = iota((1, 128), 1)
    first = jnp.where(lane < 64, scale, 0.0).astype(BF)
    second = jnp.where(lane >= 64, scale, 0.0).astype(BF)
    return first, second


def stack_heads(pair, masks):
    return jnp.concatenate([pair * masks[0], pair * masks[1]], axis=0)


def window_bias(place, lengths, r):
    lane = iota((1, 128), 1) + place[0] * 128
    end, start = jnp.int32(0), jnp.zeros((1, 128), I32)
    for j in range(8):
        end = end + lengths[r, j]
        start = jnp.where(end <= lane, end, start)
    start = start - (place[0] - 2) * 128
    key = iota((384, 128), 0)
    allowed = (key >= start) & (key <= iota((384, 128), 1) + 256)
    half = jnp.where(allowed, 0.0, MASKED)
    return jnp.concatenate([half, half], axis=1)


def join_heads(both):
    one = jnp.where(iota((128, 128), 0) < 64, both[:, :128], both[:, 128:])
    return one.T


def forward_kernel(
    place, lengths, behind_two, early, late, x, gain, bias, weight, query, keyval, proj, gain_two, bias_two,
    target, unit_halo, keyval_halo, attended, log_out, after_out, sent, context,
):
    scales = head_masks(HEAD_SIZE ** (-0.5))

    def one_row(r, carry):
        halo = jnp.concatenate([behind_two[r], early[r] + late[r]], axis=0).astype(F32)
        unit, _ = norm_parts(halo)
        unit_halo[r] = unit.astype(BF)
        rows = (unit * row(gain) + row(bias)).astype(BF)
        fresh = nn(rows, weight[:, 768:]).astype(BF)
        keyval_halo[r] = fresh
        context[0:256, :] = fresh
        context[256:384, :] = keyval[r]
        mask = window_bias(place, lengths, r)
        for p in range(PAIRS):
            lo, hi = 128 * p, 128 * (p + 1)
            keys = context[:, lo:hi]
            values = context[:, 768 + lo : 768 + hi]
            stacked = stack_heads(query[r, :, lo:hi], scales)
            scores = nt(keys, stacked) + mask
            top = jnp.max(scores, axis=0, keepdims=True)
            weights = jnp.exp(scores - top)
            total = jnp.sum(weights, axis=0, keepdims=True)
            log_out[r, p : p + 1, :] = top + jnp.log(total)
            share = (weights * (1.0 / total)).astype(BF)
            attended[r, :, lo:hi] = join_heads(tn(values, share)).astype(BF)
        return carry

    lax.fori_loop(0, 4, one_row, 0)
    mixed = nn(attended[...].reshape(512, 768), proj[...])
    after = x[...].reshape(512, 768).astype(F32) + mixed
    after_out[...] = after
    unit, _ = norm_parts(after)
    rows = (unit * row(gain_two) + row(bias_two)).astype(BF)
    for i in range(4):
        placing = (iota((256, 512), 0) + 256 * i == target[0:1, :]).astype(F32).astype(BF)
        sent[256 * i : 256 * (i + 1), :] = nn(placing, rows).astype(BF)


def active_grad_kernel(grad, down, out):
    out[...] = nt(grad[...], down[...]).astype(BF)


def gelu_both(v):
    c = 0.7978845608028654
    square = v * v
    t = jnp.tanh(v * (c + (c * 0.044715) * square))
    half = 0.5 * v
    value = half + half * t
    slope = 0.5 + 0.5 * t + half * (1.0 - t * t) * (c + (3.0 * c * 0.044715) * square)
    return value, slope


def expert_kernel(x, up, raw, active, hidden_grad, back, total):
    step = pl.program_id(0)

    @pl.when(step == 0)
    def _():
        total[...] = jnp.zeros_like(total)

    for r in range(4):
        rows = slice(256 * r, 256 * (r + 1))
        value, slope = gelu_both(nn(x[rows, :], up[...]))
        active[rows, :] = value.astype(BF)
        low = (raw[rows, :].astype(F32) * slope).astype(BF)
        hidden_grad[rows, :] = low
        total[rows, :] += nt(low, up[...])

    @pl.when(step == pl.num_programs(0) - 1)
    def _():
        back[...] = total[...].astype(BF)


def weight_kernel(x, grad, active, hidden_grad, down, out, parts, x_t, grad_t, total):
    step = pl.program_id(0)

    @pl.when(step == 0)
    def _():
        total[...] = jnp.zeros_like(total)
        x_t[...] = x[...].T
        grad_t[...] = grad[...].T

    total[...] += nn(active[...], down[...])
    one = nn(x_t[...], hidden_grad[...]).astype(BF)
    two = nn(grad_t[...], active[...]).astype(BF)
    for j in range(2):
        parts[j, :768, :] = one[:, 384 * j : 384 * (j + 1)]
        parts[j, 768:, :] = two[:, 384 * j : 384 * (j + 1)]

    @pl.when(step == pl.num_programs(0) - 1)
    def _():
        out[...] = total[...].astype(BF)


def output_kernel(after, target, returned, out):
    placing = (iota((512, 1024), 1).astype(F32) == column(target[0:1, :].astype(F32))).astype(F32).astype(BF)
    out[...] = (after[...] + nn(placing, returned[...])).astype(BF)


def middle_kernel(
    back, target, after, grad, turn, gain, proj, attended, after_grad, attended_grad, proj_part, terms
):
    placing = (iota((512, 1024), 1).astype(F32) == column(target[0:1, :].astype(F32))).astype(F32).astype(BF)
    normed_grad = nn(placing, back[...])
    unit, inverse = norm_parts(after[...])
    terms[0:1, :] = jnp.sum(normed_grad * unit, axis=0, keepdims=True)
    terms[1:2, :] = jnp.sum(normed_grad, axis=0, keepdims=True)
    upstream = grad[...].astype(F32) * column(flat_line(turn))
    total = upstream + norm_back(normed_grad, row(gain), unit, inverse)
    after_grad[...] = total
    low = total.astype(BF)
    attended_grad[...] = nt(low, proj[...]).astype(BF)
    for i in range(3):
        proj_part[i] = tn(attended[...], low[:, 256 * i : 256 * (i + 1)]).astype(BF)


def backward_kernel(
    place, lengths, query, keyval, keyval_halo, attended_grad, log_total,
    query_grad, own_grad, halo_grad, context,
):
    scales = head_masks(HEAD_SIZE ** (-0.5))
    ones = head_masks(1.0)

    def one_row(r, carry):
        context[0:256, :] = keyval_halo[r]
        context[256:384, :] = keyval[r]
        mask = window_bias(place, lengths, r)
        for p in range(PAIRS):
            lo, hi = 128 * p, 128 * (p + 1)
            keys = context[:, lo:hi]
            values = context[:, 768 + lo : 768 + hi]
            stacked = stack_heads(query[r, :, lo:hi], scales)
            grads = stack_heads(attended_grad[r, :, lo:hi], ones)
            scores = nt(keys, stacked) + mask
            share = jnp.exp(scores - log_total[r, p : p + 1, :])
            share_grad = nt(values, grads)
            row_sum = jnp.sum(share * share_grad, axis=0, keepdims=True)
            score_grad = (share * (share_grad - row_sum)).astype(BF)
            key_grad = nn(score_grad, stacked).astype(BF)
            value_grad = nn(share.astype(BF), grads).astype(BF)
            halo_grad[r, :, lo:hi] = key_grad[:256]
            own_grad[r, :, lo:hi] = key_grad[256:]
            halo_grad[r, :, 768 + lo : 768 + hi] = value_grad[:256]
            own_grad[r, :, 768 + lo : 768 + hi] = value_grad[256:]
            turned = join_heads(tn(keys, score_grad))
            query_grad[r, :, lo:hi] = (turned * HEAD_SIZE ** (-0.5)).astype(BF)
        return carry

    lax.fori_loop(0, 4, one_row, 0)


def qkv_grad_kernel(
    half, unit, unit_halo, query_grad, own_grad, halo_grad, weight, gain, bias, proj_part, terms_two, tally,
    out, own_t, halo_t, gain_sum, bias_sum, gain_wide, bias_wide,
):
    step = pl.program_id(0)
    block = half[0] * 6 + step

    @pl.when(step == 0)
    def _():
        own_t[0:768, :] = unit[...].T
        own_t[768:784, :] = jnp.ones((16, 512), BF)
        halo_t[0:768, :] = unit_halo[...].T
        halo_t[768:784, :] = jnp.ones((16, 1024), BF)
        gain_wide[...] = jnp.broadcast_to(row(gain), (256, 768)).T
        bias_wide[...] = jnp.broadcast_to(row(bias), (256, 768)).T
        gain_sum[...] = jnp.zeros_like(gain_sum)
        bias_sum[...] = jnp.zeros_like(bias_sum)

    def finish(both):
        body, sums = both[0:768], both[768:769]
        place = pl.ds(pl.multiple_of(step * 768, 768), 768)
        out[place, :] = (gain_wide[...] * body + bias_wide[...] * sums).astype(BF)
        wide = weight[...].astype(F32)
        gain_sum[...] += wide * body
        bias_sum[...] += wide * sums

    @pl.when(block < 3)
    def _():
        finish(nn(own_t[...], query_grad[...]))

    @pl.when((block >= 3) & (block < 9))
    def _():
        finish(nn(own_t[...], own_grad[...]) + nn(halo_t[...], halo_grad[...]))

    @pl.when(block >= 9)
    def _():
        out[pl.ds(pl.multiple_of(step * 768, 768), 768), :] = proj_part[0]

    @pl.when(step == 5)
    def _():
        columns = jnp.concatenate(
            [
                jnp.broadcast_to(jnp.sum(gain_sum[...], axis=1, keepdims=True), (768, 128)),
                jnp.broadcast_to(jnp.sum(bias_sum[...], axis=1, keepdims=True), (768, 128)),
            ],
            axis=1,
        ).T
        out[GEMM_ROWS:, :] = jnp.zeros((HALF_ROWS - GEMM_ROWS, 256), BF)
        first = (half[0] == 0).astype(F32)
        for t in range(3):
            lanes = slice(256 * t, 256 * (t + 1))
            block = jnp.concatenate(
                [columns[0:1, lanes], columns[128:129, lanes], terms_two[:, lanes] * first], axis=0
            )
            out[GEMM_ROWS + 16 * t : GEMM_ROWS + 16 * t + 16, :] = jnp.concatenate(
                [block, jnp.zeros((12, 256), F32)], axis=0
            ).astype(BF)
        out[GEMM_ROWS + 48 : GEMM_ROWS + 64, 0:128] = (tally[...] * first).astype(BF)


def place_half(half, data, qkv, proj, stage, sems):
    for j in range(6):
        lanes = slice(256 * (j % 3), 256 * (j % 3 + 1))
        stage[j // 3, :, lanes] = data[768 * j : 768 * (j + 1), :].astype(F32)

    @pl.when(half == 0)
    def _():
        one = pltpu.make_async_copy(stage.at[0], qkv.at[:, 0:768], sems.at[0])
        two = pltpu.make_async_copy(stage.at[1], qkv.at[:, 768:1536], sems.at[1])
        one.start()
        two.start()
        one.wait()
        two.wait()

    @pl.when(half == 1)
    def _():
        one = pltpu.make_async_copy(stage.at[0], qkv.at[:, 1536:2304], sems.at[0])
        two = pltpu.make_async_copy(stage.at[1], proj, sems.at[1])
        one.start()
        two.start()
        one.wait()
        two.wait()


def finish_mine_kernel(place, mine, qkv, proj, stage, sems):
    place_half(place[0] % 2, mine, qkv, proj, stage, sems)


def finish_other_kernel(
    place, other, tail, qkv_in, proj_in, qkv, proj, gain_one, bias_one, gain_two, bias_two, counts, received, stage, sems
):
    both = tail[...].astype(F32) + other[GEMM_ROWS:, :].astype(F32)
    for i, out in enumerate([gain_one, bias_one, gain_two, bias_two]):
        line = jnp.concatenate([both[16 * t + i : 16 * t + i + 1, :] for t in range(3)], axis=1)
        out[...] = line.reshape(768)
    every = both[48:64, 0:128]
    counts[...] = nt(jnp.ones((8, 128), BF), every.astype(BF))[0:1, :].astype(I32).reshape(16)
    chosen = (iota((16, 128), 0) == place[1]) & ((iota((16, 128), 1) >> 4) == place[0])
    mine = jnp.where(chosen, every, 0.0).astype(BF)
    fold = ((iota((128, 16), 0) & 15) == iota((128, 16), 1)).astype(F32).astype(BF)
    received[0] = jnp.sum(nn(mine, fold), axis=0, keepdims=True).astype(I32)
    place_half(1 - place[0] % 2, other, qkv, proj, stage, sems)


def expert_sum_kernel(parts, up, down):
    up[0] = parts[0, :768, :].astype(F32)
    down[0] = parts[0, 768:, :].astype(F32).T


def input_part_kernel(
    query_grad, own_grad, halo_grad, weight, own_out, two_out, one_out
):
    for r in range(4):
        part = nt(halo_grad[r], weight[:, 768:])
        two_out[r] = part[:128].astype(BF)
        one_out[r] = part[128:].astype(BF)
    own_out[...] = nt(query_grad[...], weight[:, :768]) + nt(own_grad[...], weight[:, 768:])


def input_grad_kernel(even, x, gain, own, from_one, from_two, after_grad, out):
    unit, inverse = norm_parts(x[...].astype(F32))
    total = own[...] + from_two[...].astype(F32) + even[0, 0] * from_one[...].astype(F32)
    out[...] = after_grad[...] + norm_back(total, row(gain), unit, inverse)


PAIR_ONE = [b ^ 1 for b in range(4)]
PAIR_TWO = [b ^ 3 for b in range(4)]
BOTH = ("batch", "seq")


def by_core(even_move, odd_move):
    pairs = []
    for b in range(16):
        for s in range(8):
            x, y = (even_move, odd_move)[s % 2](b & 3, b >> 2)
            pairs.append((b * 8 + s, (y * 4 + x) * 8 + s))
    return pairs


def first_pairs(pair):
    return by_core(lambda x, y: (pair[x], y), lambda x, y: (x, pair[y]))


def second_step(d):
    return by_core(lambda x, y: (x, (y + d) & 3), lambda x, y: ((x + d) & 3, y))


def along_z(d):
    return [(s, (s + 2 * d) & 7) for s in range(8)]


def pick(array, index):
    return lax.dynamic_index_in_dim(array, index, 0, keepdims=False)


def part_of(array, index):
    return lax.dynamic_index_in_dim(array, index % 4, 1, keepdims=False)


def sum_start(keep, got):
    rows, lanes = keep.shape
    seq, place = lax.axis_index("seq"), lax.axis_index("batch")
    core, x, y = seq % 2, place % 4, place // 4
    one, two = jnp.where(core == 0, x, y), jnp.where(core == 0, y, x)
    bits = [(one & 1) ^ (one >> 1), one >> 1]
    routes = [first_pairs(PAIR_ONE), first_pairs(PAIR_TWO)]
    kept, got = keep.reshape(2, rows // 2, lanes), got.reshape(2, rows // 2, lanes)
    return bits, routes, two, pair_stage([(kept[i], got[i]) for i in range(2)], bits, routes)


def pair_stage(streams, bits, routes):
    sent, stay = [], []
    for pair, bit in zip(streams, bits):
        size, lanes = pair[0].shape[0] // 2, pair[0].shape[1]
        halves = [a.reshape(2, size, lanes) for a in pair]
        for where, index in ((sent, 1 - bit), (stay, bit)):
            where.append((pick(halves[0], index).astype(F32) + pick(halves[1], index).astype(F32)).astype(BF))
    moved = [lax.ppermute(data, BOTH, route) for route, data in zip(routes, sent)]
    return list(zip(stay, moved))


def pair_gather(chunks, bits, routes):
    moved = [lax.ppermute(data, BOTH, route) for route, data in zip(routes, chunks)]
    return [
        jnp.where(bit == 0, jnp.stack([a, b]), jnp.stack([b, a])).reshape(-1, a.shape[1])
        for bit, a, b in zip(bits, chunks, moved)
    ]


def sum_finish(bits, routes, place, streams, beside):
    streams = pair_stage(streams, bits[::-1], routes[::-1])
    chunks = [(a.astype(F32) + b.astype(F32)).astype(BF) for a, b in streams]
    size, lanes = chunks[0].shape
    grouped = jnp.stack(chunks).reshape(2, 4, size // 4, lanes)
    total = part_of(grouped, place).astype(F32)
    for d in (2, 1, 3):
        total = total + lax.ppermute(part_of(grouped, place + d), BOTH, second_step(d)).astype(F32)
    whole = after_all(total.astype(BF), beside[0])
    total = whole.astype(F32)
    for d in (2, 1, 3):
        total = total + lax.ppermute(whole, "seq", along_z(d)).astype(F32)
    piece = after_all(total.astype(BF), beside[1])
    parts = [piece] + [lax.ppermute(piece, BOTH, second_step(d)) for d in (1, 2, 3)]
    stack = jnp.stack(parts, axis=1)
    ordered = jnp.stack([part_of(stack, place - p + 4) for p in range(4)], axis=1).reshape(2, size, lanes)
    chunks = pair_gather([ordered[0], ordered[1]], bits[::-1], routes[::-1])
    chunks[0] = after_all(chunks[0], beside[2])
    chunks = pair_gather(chunks, bits, routes)
    return jnp.concatenate(chunks, axis=0)


def after_all(value, *others):
    return lax.optimization_barrier((value, *others))[0]


def exchange(array):
    return lax.all_to_all(
        array.reshape(16, CAP, 768), "batch", split_axis=0, concat_axis=0, tiled=True
    ).reshape(1024, 768)


def local(
    block_input, token_ids, hash_table, doc_lengths, turn_mask, attn_norm_gain, attn_norm_bias,
    qkv_weight, proj_weight, ffn_norm_gain, ffn_norm_bias, expert_up, expert_down, out_grad,
):
    seq = lax.axis_index("seq")
    owner = lax.axis_index("batch")
    odd = seq % 2
    flat = (512, 768)
    rows3 = (4, 128, 768)
    place = jnp.stack([seq, owner]).astype(I32)
    up, down = expert_up[0], expert_down[0]

    behind_two = lax.ppermute(block_input, "seq", AHEAD_TWO)
    early = lax.ppermute(block_input, "seq", UP_ONE)

    table = jnp.pad(hash_table, (0, 8192 - 8008)).reshape(64, 128)
    target, tally, grad_sent = kernel_call(
        route_kernel,
        [shape((8, 512), I32), shape((16, 128), F32), shape((1024, 768))],
        [place, token_ids, table, turn_mask, out_grad.reshape(flat)],
        "route", 10**9,
        in_specs=[SM] + [VM] * 4,
    )
    grad_rows = exchange(grad_sent)

    unit, query, keyval = kernel_call(
        own_kernel,
        [shape(flat), shape(flat), shape((512, 1536))],
        [block_input.reshape(flat), attn_norm_gain, attn_norm_bias, qkv_weight],
        "own", 18 * 10**8,
    )
    late = lax.ppermute(after_all(behind_two, query, grad_sent), "seq", DOWN_ONE)
    query, keyval = query.reshape(rows3), keyval.reshape(4, 128, 1536)

    unit_halo, keyval_halo, attended, log_total, after, rows_sent = kernel_call(
        forward_kernel,
        [
            shape((4, 256, 768)), shape((4, 256, 1536)), shape(rows3), shape((4, 8, 256), F32),
            shape(flat, F32), shape((1024, 768)),
        ],
        [
            place, doc_lengths, behind_two, early, late, block_input, attn_norm_gain, attn_norm_bias,
            qkv_weight, query, keyval, proj_weight, ffn_norm_gain, ffn_norm_bias, target,
        ],
        "forward", 8 * 10**9,
        in_specs=[SM] * 2 + [VM] * 13,
        scratch=[pltpu.VMEM((384, 1536), BF)],
    )
    rows = exchange(rows_sent)

    raw = kernel_call(
        active_grad_kernel,
        [shape((1024, 3072))],
        [grad_rows, down],
        "active_grad", 48 * 10**8,
        grid=(6,),
        in_specs=[
            pl.BlockSpec((1024, 768), lambda i: (0, 0)),
            pl.BlockSpec((512, 768), lambda i: (i, 0)),
        ],
        out_specs=[pl.BlockSpec((1024, 512), lambda i: (0, i))],
    )[0]

    active, hidden_grad, back_sent = kernel_call(
        expert_kernel,
        [shape((1024, 3072)), shape((1024, 3072)), shape((1024, 768))],
        [rows, up, raw],
        "expert", 97 * 10**8,
        grid=(6,),
        in_specs=[
            pl.BlockSpec((1024, 768), lambda i: (0, 0)),
            pl.BlockSpec((768, 512), lambda i: (0, i)),
            pl.BlockSpec((1024, 512), lambda i: (0, i)),
        ],
        out_specs=[
            pl.BlockSpec((1024, 512), lambda i: (0, i)),
            pl.BlockSpec((1024, 512), lambda i: (0, i)),
            pl.BlockSpec((1024, 768), lambda i: (0, 0)),
        ],
        scratch=[pltpu.VMEM((1024, 768), F32)],
    )
    back = exchange(back_sent)

    result, parts = kernel_call(
        weight_kernel,
        [shape((1024, 768)), shape((8, 1536, 384))],
        [rows, grad_rows, active, hidden_grad, down],
        "weights", 145 * 10**8,
        grid=(4,),
        in_specs=[
            pl.BlockSpec((1024, 768), lambda i: (0, 0)),
            pl.BlockSpec((1024, 768), lambda i: (0, 0)),
            pl.BlockSpec((1024, 768), lambda i: (0, i)),
            pl.BlockSpec((1024, 768), lambda i: (0, i)),
            pl.BlockSpec((768, 768), lambda i: (i, 0)),
        ],
        out_specs=[
            pl.BlockSpec((1024, 768), lambda i: (0, 0)),
            pl.BlockSpec((2, 1536, 384), lambda i: (i, 0, 0)),
        ],
        scratch=[pltpu.VMEM((768, 1024), BF), pltpu.VMEM((768, 1024), BF), pltpu.VMEM((1024, 768), F32)],
    )
    returned = exchange(result)
    parts_sum = lax.psum_scatter(after_all(parts, back), "seq", scatter_dimension=0, tiled=True)

    after_grad, attended_grad, proj_part, terms_two = kernel_call(
        middle_kernel,
        [shape(flat, F32), shape(flat), shape((3, 768, 256)), shape((2, 768), F32)],
        [back, target, after, out_grad.reshape(flat), turn_mask, ffn_norm_gain, proj_weight, attended.reshape(flat)],
        "middle", 2 * 10**9,
    )

    query_grad, own_grad, halo_grad = kernel_call(
        backward_kernel,
        [shape(rows3), shape((4, 128, 1536)), shape((4, 256, 1536))],
        [place, doc_lengths, query, keyval, keyval_halo, attended_grad.reshape(rows3), log_total],
        "backward", 6 * 10**9,
        in_specs=[SM] * 2 + [VM] * 5,
        scratch=[pltpu.VMEM((384, 1536), BF)],
    )
    query_grad, own_grad = query_grad.reshape(flat), own_grad.reshape(512, 1536)

    def half_of(which, first):
        return pl.pallas_call(
            qkv_grad_kernel,
            out_shape=shape((HALF_ROWS, 256)),
            grid_spec=pltpu.PrefetchScalarGridSpec(
                num_scalar_prefetch=1,
                grid=(6,),
                in_specs=[
                    pl.BlockSpec((512, 768), lambda i, h: (0, 0)),
                    pl.BlockSpec((1024, 768), lambda i, h: (0, 0)),
                    pl.BlockSpec((512, 256), lambda i, h: (0, jnp.minimum(6 * h[0] + i, 2))),
                    pl.BlockSpec((512, 256), lambda i, h: (0, jnp.clip(6 * h[0] + i - 3, 0, 5))),
                    pl.BlockSpec((1024, 256), lambda i, h: (0, jnp.clip(6 * h[0] + i - 3, 0, 5))),
                    pl.BlockSpec((768, 256), lambda i, h: (0, jnp.minimum(6 * h[0] + i, 8))),
                    VM,
                    VM,
                    pl.BlockSpec((1, 768, 256), lambda i, h: (jnp.maximum(6 * h[0] + i - 9, 0), 0, 0)),
                    pl.BlockSpec((2, 768), lambda i, h: (0, 0)),
                    pl.BlockSpec((16, 128), lambda i, h: (0, 0)),
                ],
                out_specs=pl.BlockSpec((HALF_ROWS, 256), lambda i, h: (0, 0)),
                scratch_shapes=[
                    pltpu.VMEM((784, 512), BF),
                    pltpu.VMEM((784, 1024), BF),
                    pltpu.VMEM((768, 256), F32),
                    pltpu.VMEM((768, 256), F32),
                    pltpu.VMEM((768, 256), F32),
                    pltpu.VMEM((768, 256), F32),
                ],
            ),
            compiler_params=pltpu.CompilerParams(vmem_limit_bytes=58 * 1024 * 1024),
            cost_estimate=pl.CostEstimate(flops=3 * 10**9, bytes_accessed=12 * 10**6, transcendentals=0),
            name="qkv_grad",
        )(
            which.reshape(1), unit, unit_halo.reshape(1024, 768), first, own_grad,
            halo_grad.reshape(1024, 1536), qkv_weight, attn_norm_gain, attn_norm_bias, proj_part,
            terms_two, tally,
        )

    away = half_of(1 - odd, query_grad)
    got = lax.ppermute(away, "seq", SWAP)
    keep = half_of(odd, after_all(query_grad, returned))

    bits, routes, turn, streams = sum_start(keep, got)

    input_own, input_two, input_one = kernel_call(
        input_part_kernel,
        [shape(flat, F32), shape(rows3), shape(rows3)],
        [after_all(query_grad, streams[0][1]), own_grad, halo_grad, qkv_weight],
        "input_part", 42 * 10**8,
    )
    from_one = lax.ppermute(input_one, "seq", SWAP)
    passed = jnp.where(odd == 1, input_two + from_one, input_two)
    from_two = lax.ppermute(passed, "seq", BACK_TWO)
    even = (1 - odd).astype(F32).reshape(1, 1)
    input_grad = kernel_call(
        input_grad_kernel,
        [shape(flat, F32)],
        [
            even, block_input.reshape(flat), attn_norm_gain, input_own, from_one.reshape(flat),
            from_two.reshape(flat), after_grad,
        ],
        "input_grad", 10**7,
        in_specs=[SM] + [VM] * 6,
    )[0]

    block_output = kernel_call(
        output_kernel, [shape(flat)], [after, target, returned], "output", 8 * 10**8
    )[0]
    up_sum, down_sum = kernel_call(
        expert_sum_kernel,
        [shape((1, 768, 384), F32), shape((1, 384, 768), F32)],
        [parts_sum], "expert_sum", 10**6,
    )
    mine = sum_finish(bits, routes, turn, streams, (passed, block_output, from_two))
    other = lax.ppermute(mine, "seq", SWAP)
    sums = [shape((768, 2304), F32), shape((768, 768), F32)]
    away_spec = [pl.BlockSpec(memory_space=pl.ANY)] * 2
    landing = [pltpu.VMEM((2, 768, 768), F32), pltpu.SemaphoreType.DMA((2,))]
    qkv_half, proj_half = kernel_call(
        finish_mine_kernel, sums, [place, mine], "finish_mine", 10**6,
        in_specs=[SM, VM], out_specs=away_spec, scratch=landing,
    )
    line = shape((768,), F32)
    qkv_sum, proj_sum, *rest = kernel_call(
        finish_other_kernel,
        sums + [line] * 4 + [shape((16,), I32), shape((1, 1, 16), I32)],
        [place, other, mine[GEMM_ROWS:], qkv_half, proj_half],
        "finish_other", 10**6,
        in_specs=[SM, VM, VM] + away_spec, out_specs=away_spec + [VM] * 6, scratch=landing,
        aliases={3: 0, 4: 1},
    )
    return (
        block_output.reshape(rows3),
        input_grad.reshape(rows3),
        rest[0],
        rest[1],
        qkv_sum,
        proj_sum,
        rest[2],
        rest[3],
        up_sum,
        down_sum,
        rest[4],
        rest[5],
    )


def solution(mesh):
    placed = (
        P("batch", "seq", None),
        P("batch", "seq"),
        P(),
        P("batch", None),
        P("batch", "seq"),
        P(),
        P(),
        P(),
        P(),
        P(),
        P(),
        P("batch", None, None),
        P("batch", None, None),
        P("batch", "seq", None),
    )
    return jax.shard_map(
        local,
        mesh=mesh,
        in_specs=placed,
        out_specs=(
            P("batch", "seq", None),
            P("batch", "seq", None),
            P(),
            P(),
            P(),
            P(),
            P(),
            P(),
            P("batch", None, "seq"),
            P("batch", "seq", None),
            P(),
            P("batch", "seq", None),
        ),
        check_vma=False,
    )
```

```python
import jax
import jax.numpy as jnp
from jax import lax
from jax.experimental import pallas as pl
from jax.experimental.pallas import tpu as pltpu
from jax.sharding import PartitionSpec as P

BF = jnp.bfloat16
F32 = jnp.float32
I32 = jnp.int32
EPS = 1e-05
MASKED = -1e30
HEADS = 12
HEAD_SIZE = 64
PAIRS = 6
CAP = 64
SWAP = [(i, i ^ 1) for i in range(8)]
UP_ONE = [(i, i + 1) for i in range(0, 8, 2)]
DOWN_ONE = [(i + 1, i) for i in range(0, 8, 2)]
AHEAD_TWO = [(i, i + 2) for i in range(6)]
BACK_TWO = [(i + 2, i) for i in range(6)]
HALF_ROWS = 5120
GEMM_ROWS = 4608
VM = pl.BlockSpec(memory_space=pltpu.VMEM)
HB = pl.BlockSpec(memory_space=pl.ANY)
SM = pl.BlockSpec(memory_space=pltpu.SMEM)


def shape(dims, kind=BF):
    return jax.ShapeDtypeStruct(dims, kind)


def kernel_call(body, outs, args, name, flops, grid=None, in_specs=None, out_specs=None, scratch=(), aliases=None):
    moved = sum(a.size * a.dtype.itemsize for a in args) + sum(
        o.size * o.dtype.itemsize for o in outs
    )
    extra = {} if grid is None else {"grid": grid}
    return pl.pallas_call(
        body,
        out_shape=outs,
        in_specs=in_specs or [VM] * len(args),
        out_specs=out_specs or [VM] * len(outs),
        scratch_shapes=list(scratch),
        compiler_params=pltpu.CompilerParams(vmem_limit_bytes=58 * 1024 * 1024),
        cost_estimate=pl.CostEstimate(flops=flops, bytes_accessed=moved, transcendentals=0),
        name=name,
        input_output_aliases=aliases or {},
        **extra,
    )(*args)


def nn(a, b):
    return jnp.dot(a, b, preferred_element_type=F32)


def nt(a, b):
    return lax.dot_general(a, b, (((1,), (1,)), ((), ())), preferred_element_type=F32)


def tn(a, b):
    return lax.dot_general(a, b, (((0,), (0,)), ((), ())), preferred_element_type=F32)


def iota(dims, axis):
    return lax.broadcasted_iota(I32, dims, axis)


def row(ref):
    return ref[...].reshape(1, 768)


def column(line):
    return jnp.broadcast_to(line, (128, line.shape[1])).T[:, 0:1]


def flat_line(ref):
    return jnp.concatenate([ref[i : i + 1, :] for i in range(4)], axis=1).astype(F32)


def norm_parts(values):
    centred = values - jnp.mean(values, axis=-1, keepdims=True)
    inverse = lax.rsqrt(jnp.mean(centred * centred, axis=-1, keepdims=True) + EPS)
    return centred * inverse, inverse


def norm_back(grad, gain, unit, inverse):
    t = grad * gain
    return inverse * (
        t - jnp.mean(t, axis=-1, keepdims=True) - unit * jnp.mean(t * unit, axis=-1, keepdims=True)
    )


def route_kernel(place, tok, table, turn, grad, target_out, tally, sent):
    ids = jnp.concatenate([tok[i : i + 1, :] for i in range(4)], axis=1)
    live = flat_line(turn)
    high, low = ids >> 7, ids & 127
    picked = tn(table[...].astype(F32).astype(BF), (iota((64, 512), 0) == high).astype(F32).astype(BF))
    chosen = jnp.sum(jnp.where(iota((128, 512), 0) == low, picked, 0.0), axis=0, keepdims=True)
    member = (iota((16, 512), 0) == chosen.astype(I32)).astype(F32)
    earlier = (iota((512, 512), 0) < iota((512, 512), 1)).astype(F32).astype(BF)
    before = nn(member.astype(BF), earlier)
    slot = jnp.sum(before * member, axis=0, keepdims=True)
    target = (chosen * CAP + slot).astype(I32)
    target_out[...] = jnp.broadcast_to(target, (8, 512))
    counts = jnp.sum(member, axis=1, keepdims=True)
    tally[...] = jnp.where(iota((16, 128), 1) == place[0] * 16 + place[1], counts, 0.0)
    for i in range(4):
        placing = jnp.where(iota((256, 512), 0) + 256 * i == target, live, 0.0).astype(BF)
        sent[256 * i : 256 * (i + 1), :] = nn(placing, grad[...]).astype(BF)


def own_kernel(x, gain, bias, weight, unit_out, query, keyval):
    unit, _ = norm_parts(x[...].astype(F32))
    unit_out[...] = unit.astype(BF)
    rows = (unit * row(gain) + row(bias)).astype(BF)
    query[...] = nn(rows, weight[:, :768]).astype(BF)
    keyval[...] = nn(rows, weight[:, 768:]).astype(BF)


def head_masks(scale):
    lane = iota((1, 128), 1)
    first = jnp.where(lane < 64, scale, 0.0).astype(BF)
    second = jnp.where(lane >= 64, scale, 0.0).astype(BF)
    return first, second


def stack_heads(pair, masks):
    return jnp.concatenate([pair * masks[0], pair * masks[1]], axis=0)


def window_bias(place, lengths, r):
    lane = iota((1, 128), 1) + place[0] * 128
    end, start = jnp.int32(0), jnp.zeros((1, 128), I32)
    for j in range(8):
        end = end + lengths[r, j]
        start = jnp.where(end <= lane, end, start)
    start = start - (place[0] - 2) * 128
    key = iota((384, 128), 0)
    allowed = (key >= start) & (key <= iota((384, 128), 1) + 256)
    half = jnp.where(allowed, 0.0, MASKED)
    return jnp.concatenate([half, half], axis=1)


def join_heads(both):
    one = jnp.where(iota((128, 128), 0) < 64, both[:, :128], both[:, 128:])
    return one.T


def copies(sources, targets, sems):
    out = [
        pltpu.make_async_copy(a, b, sems.at[i]) for i, (a, b) in enumerate(zip(sources, targets))
    ]
    for copy in out:
        copy.start()
    return out


def lanes_of(p, offset=0):
    return slice(offset + 128 * p, offset + 128 * (p + 1))


def forward_kernel(
    place, lengths, gain, bias, gain_two, bias_two, target,
    behind_two, early, late, weight, keyval, query, x, proj,
    unit_halo, context_out, attended, log_out, after_out, sent,
    b2, e1, l1, w, q, xv, wp, units, rows_in, context, att, aft, snd, in_sems, out_sems,
):
    loads = copies(
        [behind_two, early, late, weight, keyval, query, x, proj],
        [b2, e1, l1, w, context.at[:, 256:384, :], q, xv, wp],
        in_sems,
    )
    scales = head_masks(HEAD_SIZE ** (-0.5))
    for copy in loads[:3]:
        copy.wait()

    def norm_row(r, carry):
        halo = jnp.concatenate([b2[r], e1[r] + l1[r]], axis=0).astype(F32)
        unit, _ = norm_parts(halo)
        units[r] = unit.astype(BF)
        rows_in[r] = (unit * row(gain) + row(bias)).astype(BF)
        return carry

    lax.fori_loop(0, 4, norm_row, 0)
    unit_copy = pltpu.make_async_copy(units, unit_halo, out_sems.at[0])
    unit_copy.start()
    loads[3].wait()
    for j in range(3):
        cols = slice(512 * j, 512 * (j + 1))
        fresh = nn(rows_in[...].reshape(1024, 768), w[:, 768 + 512 * j : 768 + 512 * (j + 1)])
        context[:, 0:256, cols] = fresh.astype(BF).reshape(4, 256, 512)
    for copy in loads[4:6]:
        copy.wait()
    context_copy = pltpu.make_async_copy(context, context_out, out_sems.at[1])
    context_copy.start()

    def one_row(r, carry):
        mask = window_bias(place, lengths, r)
        pairs = range(PAIRS)
        stacked = [stack_heads(q[r, :, lanes_of(p)], scales) for p in pairs]
        scores = [nt(context[r, :, lanes_of(p)], stacked[p]) + mask for p in pairs]
        tops = [jnp.max(a, axis=0, keepdims=True) for a in scores]
        weights = [jnp.exp(a - t) for a, t in zip(scores, tops)]
        totals = [jnp.sum(a, axis=0, keepdims=True) for a in weights]
        shares = [(a * (1.0 / t)).astype(BF) for a, t in zip(weights, totals)]
        mixed = [tn(context[r, :, lanes_of(p, 768)], shares[p]) for p in pairs]
        for p in pairs:
            log_out[r, p : p + 1, :] = tops[p] + jnp.log(totals[p])
            att[r, :, lanes_of(p)] = join_heads(mixed[p]).astype(BF)
        return carry

    lax.fori_loop(0, 4, one_row, 0)
    att_copy = pltpu.make_async_copy(att, attended, out_sems.at[2])
    att_copy.start()
    loads[6].wait()
    loads[7].wait()
    after = xv[...].reshape(512, 768).astype(F32) + nn(att[...].reshape(512, 768), wp[...])
    aft[...] = after
    after_copy = pltpu.make_async_copy(aft, after_out, out_sems.at[3])
    after_copy.start()
    unit, _ = norm_parts(after)
    rows = (unit * row(gain_two) + row(bias_two)).astype(BF)
    sends = []
    for i in range(2):
        part = slice(512 * i, 512 * (i + 1))
        placing = (iota((512, 512), 0) + 512 * i == target[0:1, :]).astype(F32).astype(BF)
        snd[part, :] = nn(placing, rows).astype(BF)
        sends.append(pltpu.make_async_copy(snd.at[part], sent.at[part], out_sems.at[4 + i]))
        sends[-1].start()
    for copy in [unit_copy, context_copy, att_copy, after_copy] + sends:
        copy.wait()


def active_grad_kernel(grad, down, out):
    out[0] = nt(grad[...], down[...]).astype(BF)


def gelu_both(v):
    c = 0.7978845608028654
    square = v * v
    p = c + (c * 0.044715) * square
    gate = 0.5 + 0.5 * jnp.tanh(v * p)
    value = v * gate
    return value, gate + value * (1.0 - gate) * (6.0 * p - 4.0 * c)


def expert_kernel(x, up, raw, active, hidden_grad, back, total):
    step = pl.program_id(0)

    @pl.when(step == 0)
    def _():
        total[...] = jnp.zeros_like(total)

    parts = [slice(256 * r, 256 * (r + 1)) for r in range(4)]
    hidden = [nn(x[rows, :], up[...]) for rows in parts]
    lows = []
    for rows, v in zip(parts, hidden):
        value, slope = gelu_both(v)
        active[0, rows, :] = value.astype(BF)
        low = (raw[0, rows, :].astype(F32) * slope).astype(BF)
        hidden_grad[0, rows, :] = low
        lows.append(low)
    for rows, low in zip(parts, lows):
        total[rows, :] += nt(low, up[...])

    @pl.when(step == pl.num_programs(0) - 1)
    def _():
        back[...] = total[...].astype(BF)


def turn_kernel(unit, unit_halo, out):
    out[0:768, 0:512] = unit[...].T
    out[0:768, 512:1536] = unit_halo[...].T
    out[768:784, :] = jnp.ones((16, 1536), BF)


def weight_kernel(x, grad, active, hidden_grad, down, out, parts, x_t, grad_t, total):
    step = pl.program_id(0)

    @pl.when(step == 0)
    def _():
        total[...] = jnp.zeros_like(total)
        x_t[...] = x[...].T
        grad_t[...] = grad[...].T

    total[...] += nn(active[0], down[...])
    one = nn(x_t[...], hidden_grad[0]).astype(BF)
    two = nn(grad_t[...], active[0]).astype(BF)
    for j in range(2):
        parts[j, :768, :] = one[:, 384 * j : 384 * (j + 1)]
        parts[j, 768:, :] = two[:, 384 * j : 384 * (j + 1)]

    @pl.when(step == pl.num_programs(0) - 1)
    def _():
        out[...] = total[...].astype(BF)


def output_kernel(after, target, returned, out):
    placing = (iota((512, 1024), 1).astype(F32) == column(target[0:1, :].astype(F32))).astype(F32).astype(BF)
    out[...] = (after[...] + nn(placing, returned[...])).astype(BF)


def fill_half(
    half, turned, query_grad, context_grad, weight, gain, bias, proj_part, terms_two, tally,
    out, gain_wide, bias_wide, gain_sum, bias_sum, target, sems,
):
    gain_wide[...] = jnp.broadcast_to(row(gain), (256, 768)).T
    bias_wide[...] = jnp.broadcast_to(row(bias), (256, 768)).T
    gain_sum[...] = jnp.zeros_like(gain_sum)
    bias_sum[...] = jnp.zeros_like(bias_sum)

    def send(step, size=768):
        rows = slice(768 * step, 768 * step + size)
        return pltpu.make_async_copy(out.at[rows], target.at[rows], sems.at[step])

    def finish(step, both, block):
        body, sums = both[0:768], both[768:769]
        out[768 * step : 768 * (step + 1), :] = (gain_wide[...] * body + bias_wide[...] * sums).astype(BF)
        send(step).start()
        wide = weight[:, 256 * block : 256 * (block + 1)].astype(F32)
        gain_sum[...] += wide * body
        bias_sum[...] += wide * sums

    @pl.when(half == 0)
    def _():
        for j in range(3):
            cols = slice(256 * j, 256 * (j + 1))
            finish(j, nn(turned[:, 0:512], query_grad[:, cols]), j)
            finish(3 + j, nn(turned[...], context_grad[:, cols]), 3 + j)

    @pl.when(half == 1)
    def _():
        for j in range(3):
            finish(j, nn(turned[...], context_grad[:, 768 + 256 * j : 1024 + 256 * j]), 6 + j)
            out[768 * (3 + j) : 768 * (4 + j), :] = proj_part[j]
            send(3 + j).start()

    columns = jnp.concatenate(
        [
            jnp.broadcast_to(jnp.sum(gain_sum[...], axis=1, keepdims=True), (768, 128)),
            jnp.broadcast_to(jnp.sum(bias_sum[...], axis=1, keepdims=True), (768, 128)),
        ],
        axis=1,
    ).T
    out[GEMM_ROWS:, :] = jnp.zeros((HALF_ROWS - GEMM_ROWS, 256), BF)
    first = (half == 0).astype(F32)
    for t in range(3):
        lanes = slice(256 * t, 256 * (t + 1))
        block = jnp.concatenate(
            [columns[0:1, lanes], columns[128:129, lanes], terms_two[:, lanes] * first, jnp.zeros((12, 256), F32)],
            axis=0,
        )
        out[GEMM_ROWS + 16 * t : GEMM_ROWS + 16 * t + 16, :] = block.astype(BF)
    out[GEMM_ROWS + 48 : GEMM_ROWS + 64, 0:128] = (tally[...] * first).astype(BF)
    send(6, HALF_ROWS - GEMM_ROWS).start()
    for step in range(6):
        send(step).wait()
    send(6, HALF_ROWS - GEMM_ROWS).wait()


def backward_kernel(
    place, lengths, gain_two, gain, bias, target, turn, log_total, tally,
    back, after, grad, proj, attended, query, context, turned, weight,
    after_grad, query_grad, context_grad, proj_part, terms, payload,
    bk, af, gr, wp, att, q, ctx, tu, w, ag, do, dq, cg, pp, out,
    gain_wide, bias_wide, gain_sum, bias_sum, in_sems, out_sems, pay_sems,
):
    loads = copies(
        [back, after, grad, proj, attended, query, context, turned, weight],
        [bk, af, gr, wp, att, q, ctx, tu, w],
        in_sems,
    )
    scales = head_masks(HEAD_SIZE ** (-0.5))
    ones = head_masks(1.0)
    placing = (iota((512, 1024), 1).astype(F32) == column(target[0:1, :].astype(F32))).astype(F32).astype(BF)
    live = column(flat_line(turn))
    loads[0].wait()
    normed_grad = nn(placing, bk[...])
    loads[1].wait()
    unit, inverse = norm_parts(af[...])
    terms[0:1, :] = jnp.sum(normed_grad * unit, axis=0, keepdims=True)
    terms[1:2, :] = jnp.sum(normed_grad, axis=0, keepdims=True)
    loads[2].wait()
    total = gr[...].astype(F32) * live + norm_back(normed_grad, row(gain_two), unit, inverse)
    ag[...] = total
    stores = [pltpu.make_async_copy(ag, after_grad, out_sems.at[0])]
    stores[0].start()
    low = total.astype(BF)
    loads[3].wait()
    do[...] = nt(low, wp[...]).astype(BF).reshape(4, 128, 768)
    loads[4].wait()
    mixed = nn(att[...].T, low).astype(BF)
    for j in range(3):
        pp[j] = mixed[:, 256 * j : 256 * (j + 1)]
    loads[5].wait()
    loads[6].wait()

    def one_row(r, carry):
        mask = window_bias(place, lengths, r)
        pairs = range(PAIRS)
        stacked = [stack_heads(q[r, :, lanes_of(p)], scales) for p in pairs]
        grads = [stack_heads(do[r, :, lanes_of(p)], ones) for p in pairs]
        scores = [nt(ctx[r, :, lanes_of(p)], stacked[p]) for p in pairs]
        share_grads = [nt(ctx[r, :, lanes_of(p, 768)], grads[p]) for p in pairs]
        shares = [jnp.exp(scores[p] + mask - log_total[r, p : p + 1, :]) for p in pairs]
        sums = [jnp.sum(a * b, axis=0, keepdims=True) for a, b in zip(shares, share_grads)]
        score_grads = [(a * (b - c)).astype(BF) for a, b, c in zip(shares, share_grads, sums)]
        key_grads = [nn(score_grads[p], stacked[p]).astype(BF) for p in pairs]
        value_grads = [nn(shares[p].astype(BF), grads[p]).astype(BF) for p in pairs]
        turned_grads = [tn(ctx[r, :, lanes_of(p)], score_grads[p]) for p in pairs]
        halo = pl.ds(pl.multiple_of(512 + r * 256, 256), 256)
        own = pl.ds(pl.multiple_of(r * 128, 128), 128)
        for p in pairs:
            cg[halo, lanes_of(p)] = key_grads[p][:256]
            cg[own, lanes_of(p)] = key_grads[p][256:]
            cg[halo, lanes_of(p, 768)] = value_grads[p][:256]
            cg[own, lanes_of(p, 768)] = value_grads[p][256:]
            dq[own, lanes_of(p)] = (join_heads(turned_grads[p]) * HEAD_SIZE ** (-0.5)).astype(BF)
        return carry

    lax.fori_loop(0, 4, one_row, 0)
    for i, (a, b) in enumerate([(dq, query_grad), (cg, context_grad), (pp, proj_part)]):
        stores.append(pltpu.make_async_copy(a, b, out_sems.at[1 + i]))
        stores[-1].start()
    loads[7].wait()
    loads[8].wait()
    fill_half(
        1 - place[0] % 2, tu, dq, cg, w, gain, bias, pp, terms, tally,
        out, gain_wide, bias_wide, gain_sum, bias_sum, payload, pay_sems,
    )
    for copy in stores:
        copy.wait()


def keep_kernel(
    place, gain, bias, terms_two, tally, query_grad, context_grad, proj_part, turned, weight,
    payload, dq, cg, pp, tu, w, out, gain_wide, bias_wide, gain_sum, bias_sum, in_sems, pay_sems,
):
    for copy in copies([turned, query_grad, context_grad, weight, proj_part], [tu, dq, cg, w, pp], in_sems):
        copy.wait()
    fill_half(
        place[0] % 2, tu, dq, cg, w, gain, bias, pp, terms_two, tally,
        out, gain_wide, bias_wide, gain_sum, bias_sum, payload, pay_sems,
    )


def place_half(half, data, qkv, proj, stage, sems):
    for j in range(6):
        lanes = slice(256 * (j % 3), 256 * (j % 3 + 1))
        stage[j // 3, :, lanes] = data[768 * j : 768 * (j + 1), :].astype(F32)

    @pl.when(half == 0)
    def _():
        one = pltpu.make_async_copy(stage.at[0], qkv.at[:, 0:768], sems.at[0])
        two = pltpu.make_async_copy(stage.at[1], qkv.at[:, 768:1536], sems.at[1])
        one.start()
        two.start()
        one.wait()
        two.wait()

    @pl.when(half == 1)
    def _():
        one = pltpu.make_async_copy(stage.at[0], qkv.at[:, 1536:2304], sems.at[0])
        two = pltpu.make_async_copy(stage.at[1], proj, sems.at[1])
        one.start()
        two.start()
        one.wait()
        two.wait()


def finish_mine_kernel(place, mine, qkv, proj, stage, sems):
    place_half(place[0] % 2, mine, qkv, proj, stage, sems)


def finish_other_kernel(
    place, other, tail, qkv_in, proj_in, qkv, proj, gain_one, bias_one, gain_two, bias_two, counts, received, stage, sems
):
    both = tail[...].astype(F32) + other[GEMM_ROWS:, :].astype(F32)
    for i, out in enumerate([gain_one, bias_one, gain_two, bias_two]):
        line = jnp.concatenate([both[16 * t + i : 16 * t + i + 1, :] for t in range(3)], axis=1)
        out[...] = line.reshape(768)
    every = both[48:64, 0:128]
    counts[...] = nt(jnp.ones((8, 128), BF), every.astype(BF))[0:1, :].astype(I32).reshape(16)
    chosen = (iota((16, 128), 0) == place[1]) & ((iota((16, 128), 1) >> 4) == place[0])
    mine = jnp.where(chosen, every, 0.0).astype(BF)
    fold = ((iota((128, 16), 0) & 15) == iota((128, 16), 1)).astype(F32).astype(BF)
    received[0] = jnp.sum(nn(mine, fold), axis=0, keepdims=True).astype(I32)
    place_half(1 - place[0] % 2, other, qkv, proj, stage, sems)


def expert_sum_kernel(parts, up, down):
    up[0] = parts[0, :768, :].astype(F32)
    down[0] = parts[0, 768:, :].astype(F32).T


def input_part_kernel(query_grad, context_grad, weight, own_out, two_out, one_out, dq, cg, w, in_sems):
    loads = copies(
        [weight, context_grad.at[512:1536], context_grad.at[0:512], query_grad],
        [w, cg.at[512:1536], cg.at[0:512], dq],
        in_sems,
    )
    loads[0].wait()
    loads[1].wait()
    part = nt(cg[512:1536, :], w[:, 768:]).astype(BF).reshape(4, 256, 768)
    two_out[...] = part[:, :128]
    one_out[...] = part[:, 128:]
    loads[2].wait()
    loads[3].wait()
    own_out[...] = nt(dq[...], w[:, :768]) + nt(cg[0:512, :], w[:, 768:])


def input_grad_kernel(even, x, gain, own, from_one, from_two, after_grad, out):
    unit, inverse = norm_parts(x[...].astype(F32))
    total = own[...] + from_two[...].astype(F32) + even[0, 0] * from_one[...].astype(F32)
    out[...] = after_grad[...] + norm_back(total, row(gain), unit, inverse)


PAIR_ONE = [b ^ 1 for b in range(4)]
PAIR_TWO = [b ^ 3 for b in range(4)]
PAIRS_OF = [PAIR_ONE, PAIR_TWO]
BOTH = ("batch", "seq")


def by_core(even_move, odd_move):
    pairs = []
    for b in range(16):
        for s in range(8):
            x, y = (even_move, odd_move)[s % 2](b & 3, b >> 2)
            pairs.append((b * 8 + s, (y * 4 + x) * 8 + s))
    return pairs


def first_pairs(pair):
    return by_core(lambda x, y: (pair[x], y), lambda x, y: (x, pair[y]))


def second_step(d):
    return by_core(lambda x, y: (x, (y + d) & 3), lambda x, y: ((x + d) & 3, y))


def along_z(d):
    return [(s, (s + 2 * d) & 7) for s in range(8)]


def pick(array, index):
    return lax.dynamic_index_in_dim(array, index, 0, keepdims=False)


def part_of(array, index):
    return lax.dynamic_index_in_dim(array, index % 4, 1, keepdims=False)


def sum_start(keep, got):
    seq, place = lax.axis_index("seq"), lax.axis_index("batch")
    core, x, y = seq % 2, place % 4, place // 4
    one, two = jnp.where(core == 0, x, y), jnp.where(core == 0, y, x)
    bits = [(one & 1) ^ (one >> 1), one >> 1]
    size = HALF_ROWS // 4

    def part(stream, bit):
        at = (stream * 2 + bit) * size
        return rows_at(keep, at, size).astype(F32) + rows_at(got, at, size).astype(F32)

    moved = [
        lax.ppermute(part(i, 1 - bits[i]).astype(BF), BOTH, first_pairs(PAIRS_OF[i])) for i in range(2)
    ]
    return bits, two, part, moved


def rows_at(array, at, size):
    return lax.dynamic_slice(array, (at, 0), (size, array.shape[1]))


def pair_gather(chunks, bits, pairs):
    moved = [lax.ppermute(data, BOTH, first_pairs(pair)) for pair, data in zip(pairs, chunks)]
    return [
        jnp.where(bit == 0, jnp.stack([a, b]), jnp.stack([b, a])).reshape(-1, a.shape[1])
        for bit, a, b in zip(bits, chunks, moved)
    ]


def sum_finish(bits, place, part, moved, beside):
    size = HALF_ROWS // 8
    sums = [part(i, bits[i]) + moved[i].astype(F32) for i in range(2)]
    sent = [rows_at(sums[i], (1 - bits[1 - i]) * size, size).astype(BF) for i in range(2)]
    stay = [rows_at(sums[i], bits[1 - i] * size, size) for i in range(2)]
    moved = [lax.ppermute(sent[i], BOTH, first_pairs(PAIRS_OF[1 - i])) for i in range(2)]
    chunks = [(a + b.astype(F32)).astype(BF) for a, b in zip(stay, moved)]
    size, lanes = chunks[0].shape
    grouped = jnp.stack(chunks).reshape(2, 4, size // 4, lanes)
    total = part_of(grouped, place).astype(F32)
    for d in (2, 1, 3):
        total = total + lax.ppermute(part_of(grouped, place + d), BOTH, second_step(d)).astype(F32)
    whole = after_all(total.astype(BF), *beside[0])
    total = whole.astype(F32)
    for d in (2, 1, 3):
        total = total + lax.ppermute(whole, "seq", along_z(d)).astype(F32)
    piece = after_all(total.astype(BF), *beside[1])
    parts = [piece] + [lax.ppermute(piece, BOTH, second_step(d)) for d in (1, 2, 3)]
    stack = jnp.stack(parts, axis=1)
    ordered = jnp.stack([part_of(stack, place - p + 4) for p in range(4)], axis=1).reshape(2, size, lanes)
    chunks = pair_gather([ordered[0], ordered[1]], bits[::-1], PAIRS_OF[::-1])
    chunks[0] = after_all(chunks[0], *beside[2])
    chunks = pair_gather(chunks, bits, PAIRS_OF)
    return jnp.concatenate(chunks, axis=0)


def after_all(value, *others):
    return lax.optimization_barrier((value, *others))[0]


def exchange(array):
    return lax.all_to_all(
        array.reshape(16, CAP, 768), "batch", split_axis=0, concat_axis=0, tiled=True
    ).reshape(1024, 768)


def local(
    block_input, token_ids, hash_table, doc_lengths, turn_mask, attn_norm_gain, attn_norm_bias,
    qkv_weight, proj_weight, ffn_norm_gain, ffn_norm_bias, expert_up, expert_down, out_grad,
):
    seq = lax.axis_index("seq")
    owner = lax.axis_index("batch")
    odd = seq % 2
    flat = (512, 768)
    rows3 = (4, 128, 768)
    place = jnp.stack([seq, owner]).astype(I32)
    up, down = expert_up[0], expert_down[0]

    behind_two = lax.ppermute(block_input, "seq", AHEAD_TWO)
    early = lax.ppermute(block_input, "seq", UP_ONE)

    table = jnp.pad(hash_table, (0, 8192 - 8008)).reshape(64, 128)
    target, tally, grad_sent = kernel_call(
        route_kernel,
        [shape((8, 512), I32), shape((16, 128), F32), shape((1024, 768))],
        [place, token_ids, table, turn_mask, out_grad.reshape(flat)],
        "route", 10**9,
        in_specs=[SM] + [VM] * 4,
    )
    grad_rows = exchange(grad_sent)

    unit, query, keyval = kernel_call(
        own_kernel,
        [shape(flat), shape(flat), shape((512, 1536))],
        [block_input.reshape(flat), attn_norm_gain, attn_norm_bias, qkv_weight],
        "own", 18 * 10**8,
    )
    late = lax.ppermute(after_all(behind_two, query, grad_sent), "seq", DOWN_ONE)
    query, keyval = query.reshape(rows3), keyval.reshape(4, 128, 1536)

    unit_halo, context, attended, log_total, after, rows_sent = kernel_call(
        forward_kernel,
        [
            shape((4, 256, 768)), shape((4, 384, 1536)), shape(rows3), shape((4, 8, 256), F32),
            shape(flat, F32), shape((1024, 768)),
        ],
        [
            place, doc_lengths, attn_norm_gain, attn_norm_bias, ffn_norm_gain, ffn_norm_bias, target,
            behind_two, early, late, qkv_weight, keyval, query, block_input, proj_weight,
        ],
        "forward", 10**9,
        in_specs=[SM] * 2 + [VM] * 5 + [HB] * 8,
        out_specs=[HB] * 3 + [VM] + [HB] * 2,
        scratch=[
            pltpu.VMEM(rows3, BF), pltpu.VMEM(rows3, BF), pltpu.VMEM(rows3, BF), pltpu.VMEM((768, 2304), BF),
            pltpu.VMEM(rows3, BF), pltpu.VMEM(rows3, BF), pltpu.VMEM((768, 768), BF),
            pltpu.VMEM((4, 256, 768), BF), pltpu.VMEM((4, 256, 768), BF), pltpu.VMEM((4, 384, 1536), BF),
            pltpu.VMEM(rows3, BF), pltpu.VMEM(flat, F32), pltpu.VMEM((1024, 768), BF),
            pltpu.SemaphoreType.DMA((8,)), pltpu.SemaphoreType.DMA((6,)),
        ],
    )
    rows = exchange(rows_sent)

    turned = kernel_call(
        turn_kernel, [shape((784, 1536))], [unit, unit_halo.reshape(1024, 768)], "turn", 10**6
    )[0]
    tile = pl.BlockSpec((1, 1024, 768), lambda i: (i, 0, 0))
    tiled = shape((4, 1024, 768))
    whole = pl.BlockSpec((1024, 768), lambda i: (0, 0))
    raw = kernel_call(
        active_grad_kernel,
        [tiled],
        [after_all(grad_rows, turned), down],
        "active_grad", 48 * 10**8,
        grid=(4,),
        in_specs=[whole, pl.BlockSpec((768, 768), lambda i: (i, 0))],
        out_specs=[tile],
    )[0]

    active, hidden_grad, back_sent = kernel_call(
        expert_kernel,
        [tiled, tiled, shape((1024, 768))],
        [rows, up, raw],
        "expert", 97 * 10**8,
        grid=(4,),
        in_specs=[whole, pl.BlockSpec((768, 768), lambda i: (0, i)), tile],
        out_specs=[tile, tile, whole],
        scratch=[pltpu.VMEM((1024, 768), F32)],
    )
    back = exchange(back_sent)

    result, parts = kernel_call(
        weight_kernel,
        [shape((1024, 768)), shape((8, 1536, 384))],
        [rows, grad_rows, active, hidden_grad, down],
        "weights", 145 * 10**8,
        grid=(4,),
        in_specs=[
            whole,
            whole,
            tile,
            tile,
            pl.BlockSpec((768, 768), lambda i: (i, 0)),
        ],
        out_specs=[
            pl.BlockSpec((1024, 768), lambda i: (0, 0)),
            pl.BlockSpec((2, 1536, 384), lambda i: (i, 0, 0)),
        ],
        scratch=[pltpu.VMEM((768, 1024), BF), pltpu.VMEM((768, 1024), BF), pltpu.VMEM((1024, 768), F32)],
    )
    returned = exchange(result)
    parts_sum = lax.psum_scatter(after_all(parts, back), "seq", scatter_dimension=0, tiled=True)

    wide = [pltpu.VMEM((768, 256), F32)] * 4
    after_grad, query_grad, context_grad, proj_part, terms_two, away = kernel_call(
        backward_kernel,
        [
            shape(flat, F32), shape(flat), shape((1536, 1536)), shape((3, 768, 256)), shape((2, 768), F32),
            shape((HALF_ROWS, 256)),
        ],
        [
            place, doc_lengths, ffn_norm_gain, attn_norm_gain, attn_norm_bias, target, turn_mask, log_total, tally,
            back, after, out_grad.reshape(flat), proj_weight, attended.reshape(flat), query, context, turned,
            qkv_weight,
        ],
        "backward", 12 * 10**9,
        in_specs=[SM] * 2 + [VM] * 7 + [HB] * 9,
        out_specs=[HB] * 4 + [VM, HB],
        scratch=[
            pltpu.VMEM((1024, 768), BF), pltpu.VMEM(flat, F32), pltpu.VMEM(flat, BF), pltpu.VMEM((768, 768), BF),
            pltpu.VMEM(flat, BF), pltpu.VMEM(rows3, BF), pltpu.VMEM((4, 384, 1536), BF),
            pltpu.VMEM((784, 1536), BF), pltpu.VMEM((768, 2304), BF), pltpu.VMEM(flat, F32), pltpu.VMEM(rows3, BF),
            pltpu.VMEM(flat, BF), pltpu.VMEM((1536, 1536), BF), pltpu.VMEM((3, 768, 256), BF),
            pltpu.VMEM((HALF_ROWS, 256), BF), *wide,
            pltpu.SemaphoreType.DMA((9,)), pltpu.SemaphoreType.DMA((4,)), pltpu.SemaphoreType.DMA((7,)),
        ],
    )
    got = lax.ppermute(after_all(away, returned), "seq", SWAP)
    keep = kernel_call(
        keep_kernel,
        [shape((HALF_ROWS, 256))],
        [
            place, attn_norm_gain, attn_norm_bias, terms_two, tally, query_grad, context_grad, proj_part, turned,
            qkv_weight,
        ],
        "keep", 4 * 10**9,
        in_specs=[SM] + [VM] * 4 + [HB] * 5,
        out_specs=[HB],
        scratch=[
            pltpu.VMEM(flat, BF), pltpu.VMEM((1536, 1536), BF), pltpu.VMEM((3, 768, 256), BF),
            pltpu.VMEM((784, 1536), BF), pltpu.VMEM((768, 2304), BF), pltpu.VMEM((HALF_ROWS, 256), BF), *wide,
            pltpu.SemaphoreType.DMA((5,)), pltpu.SemaphoreType.DMA((7,)),
        ],
    )[0]

    bits, turn, part, streams = sum_start(keep, got)

    input_own, input_two, input_one = kernel_call(
        input_part_kernel,
        [shape(flat, F32), shape(rows3), shape(rows3)],
        [after_all(query_grad, streams[0]), context_grad, qkv_weight],
        "input_part", 42 * 10**8,
        in_specs=[HB] * 3,
        scratch=[
            pltpu.VMEM(flat, BF), pltpu.VMEM((1536, 1536), BF), pltpu.VMEM((768, 2304), BF),
            pltpu.SemaphoreType.DMA((4,)),
        ],
    )
    from_one = lax.ppermute(input_one, "seq", SWAP)
    passed = jnp.where(odd == 1, input_two + from_one, input_two)
    from_two = lax.ppermute(passed, "seq", BACK_TWO)
    even = (1 - odd).astype(F32).reshape(1, 1)
    input_grad = kernel_call(
        input_grad_kernel,
        [shape(flat, F32)],
        [
            even, block_input.reshape(flat), attn_norm_gain, input_own, from_one.reshape(flat),
            from_two.reshape(flat), after_grad,
        ],
        "input_grad", 10**7,
        in_specs=[SM] + [VM] * 6,
    )[0]

    block_output = kernel_call(
        output_kernel, [shape(flat)], [after, target, returned], "output", 8 * 10**8
    )[0]
    up_sum, down_sum = kernel_call(
        expert_sum_kernel,
        [shape((1, 768, 384), F32), shape((1, 384, 768), F32)],
        [parts_sum], "expert_sum", 10**6,
    )
    mine = sum_finish(bits, turn, part, streams, ([passed], [block_output, up_sum], [input_grad]))
    other = lax.ppermute(mine, "seq", SWAP)
    sums = [shape((768, 2304), F32), shape((768, 768), F32)]
    away_spec = [pl.BlockSpec(memory_space=pl.ANY)] * 2
    landing = [pltpu.VMEM((2, 768, 768), F32), pltpu.SemaphoreType.DMA((2,))]
    qkv_half, proj_half = kernel_call(
        finish_mine_kernel, sums, [place, mine], "finish_mine", 10**6,
        in_specs=[SM, VM], out_specs=away_spec, scratch=landing,
    )
    line = shape((768,), F32)
    qkv_sum, proj_sum, *rest = kernel_call(
        finish_other_kernel,
        sums + [line] * 4 + [shape((16,), I32), shape((1, 1, 16), I32)],
        [place, other, mine[GEMM_ROWS:], qkv_half, proj_half],
        "finish_other", 10**6,
        in_specs=[SM, VM, VM] + away_spec, out_specs=away_spec + [VM] * 6, scratch=landing,
        aliases={3: 0, 4: 1},
    )
    return (
        block_output.reshape(rows3),
        input_grad.reshape(rows3),
        rest[0],
        rest[1],
        qkv_sum,
        proj_sum,
        rest[2],
        rest[3],
        up_sum,
        down_sum,
        rest[4],
        rest[5],
    )


def solution(mesh):
    placed = (
        P("batch", "seq", None),
        P("batch", "seq"),
        P(),
        P("batch", None),
        P("batch", "seq"),
        P(),
        P(),
        P(),
        P(),
        P(),
        P(),
        P("batch", None, None),
        P("batch", None, None),
        P("batch", "seq", None),
    )
    return jax.shard_map(
        local,
        mesh=mesh,
        in_specs=placed,
        out_specs=(
            P("batch", "seq", None),
            P("batch", "seq", None),
            P(),
            P(),
            P(),
            P(),
            P(),
            P(),
            P("batch", None, "seq"),
            P("batch", "seq", None),
            P(),
            P("batch", "seq", None),
        ),
        check_vma=False,
    )
```

```python
import jax
import jax.numpy as jnp
from jax import lax
from jax.experimental import pallas as pl
from jax.experimental.pallas import tpu as pltpu
from jax.sharding import PartitionSpec as P

BF = jnp.bfloat16
F32 = jnp.float32
I32 = jnp.int32
EPS = 1e-05
MASKED = -1e30
HEADS = 12
HEAD_SIZE = 64
PAIRS = 6
CAP = 64
SWAP = [(i, i ^ 1) for i in range(8)]
UP_ONE = [(i, i + 1) for i in range(0, 8, 2)]
DOWN_ONE = [(i + 1, i) for i in range(0, 8, 2)]
AHEAD_TWO = [(i, i + 2) for i in range(6)]
BACK_TWO = [(i + 2, i) for i in range(6)]
HALF_ROWS = 5120
VMEM_BYTES = 63 * 1024 * 1024
GEMM_ROWS = 4608
VM = pl.BlockSpec(memory_space=pltpu.VMEM)
HB = pl.BlockSpec(memory_space=pl.ANY)
SM = pl.BlockSpec(memory_space=pltpu.SMEM)


def shape(dims, kind=BF):
    return jax.ShapeDtypeStruct(dims, kind)


def kernel_call(body, outs, args, name, flops, grid=None, in_specs=None, out_specs=None, scratch=(), aliases=None):
    moved = sum(a.size * a.dtype.itemsize for a in args) + sum(
        o.size * o.dtype.itemsize for o in outs
    )
    extra = {} if grid is None else {"grid": grid}
    return pl.pallas_call(
        body,
        out_shape=outs,
        in_specs=in_specs or [VM] * len(args),
        out_specs=out_specs or [VM] * len(outs),
        scratch_shapes=list(scratch),
        compiler_params=pltpu.CompilerParams(vmem_limit_bytes=VMEM_BYTES),
        cost_estimate=pl.CostEstimate(flops=flops, bytes_accessed=moved, transcendentals=0),
        name=name,
        input_output_aliases=aliases or {},
        **extra,
    )(*args)


def nn(a, b):
    return jnp.dot(a, b, preferred_element_type=F32)


def nt(a, b):
    return lax.dot_general(a, b, (((1,), (1,)), ((), ())), preferred_element_type=F32)


def tn(a, b):
    return lax.dot_general(a, b, (((0,), (0,)), ((), ())), preferred_element_type=F32)


def iota(dims, axis):
    return lax.broadcasted_iota(I32, dims, axis)


def row(ref):
    return ref[...].reshape(1, 768)


def column(line):
    return jnp.broadcast_to(line, (128, line.shape[1])).T[:, 0:1]


def flat_line(ref):
    return jnp.concatenate([ref[i : i + 1, :] for i in range(4)], axis=1).astype(F32)


def norm_parts(values):
    centred = values - jnp.mean(values, axis=-1, keepdims=True)
    inverse = lax.rsqrt(jnp.mean(centred * centred, axis=-1, keepdims=True) + EPS)
    return centred * inverse, inverse


def norm_back(grad, gain, unit, inverse):
    t = grad * gain
    return inverse * (
        t - jnp.mean(t, axis=-1, keepdims=True) - unit * jnp.mean(t * unit, axis=-1, keepdims=True)
    )


def route_kernel(place, tok, table, turn, grad, target_out, tally, sent):
    ids = jnp.concatenate([tok[i : i + 1, :] for i in range(4)], axis=1)
    live = flat_line(turn)
    high, low = ids >> 7, ids & 127
    picked = tn(table[...].astype(F32).astype(BF), (iota((64, 512), 0) == high).astype(F32).astype(BF))
    chosen = jnp.sum(jnp.where(iota((128, 512), 0) == low, picked, 0.0), axis=0, keepdims=True)
    member = (iota((16, 512), 0) == chosen.astype(I32)).astype(F32)
    earlier = (iota((512, 512), 0) < iota((512, 512), 1)).astype(F32).astype(BF)
    before = nn(member.astype(BF), earlier)
    slot = jnp.sum(before * member, axis=0, keepdims=True)
    target = (chosen * CAP + slot).astype(I32)
    target_out[...] = jnp.broadcast_to(target, (8, 512))
    counts = jnp.sum(member, axis=1, keepdims=True)
    tally[...] = jnp.where(iota((16, 128), 1) == place[0] * 16 + place[1], counts, 0.0)
    for i in range(4):
        placing = jnp.where(iota((256, 512), 0) + 256 * i == target, live, 0.0).astype(BF)
        sent[256 * i : 256 * (i + 1), :] = nn(placing, grad[...]).astype(BF)


def own_kernel(x, gain, bias, weight, unit_out, query, keyval):
    unit, _ = norm_parts(x[...].astype(F32))
    unit_out[...] = unit.astype(BF)
    rows = (unit * row(gain) + row(bias)).astype(BF)
    query[...] = nn(rows, weight[:, :768]).astype(BF)
    keyval[...] = nn(rows, weight[:, 768:]).astype(BF)


def head_masks(scale):
    lane = iota((1, 128), 1)
    first = jnp.where(lane < 64, scale, 0.0).astype(BF)
    second = jnp.where(lane >= 64, scale, 0.0).astype(BF)
    return first, second


def stack_heads(pair, masks):
    return jnp.concatenate([pair * masks[0], pair * masks[1]], axis=0)


def window_bias(place, lengths, r):
    lane = iota((1, 128), 1) + place[0] * 128
    end, start = jnp.int32(0), jnp.zeros((1, 128), I32)
    for j in range(8):
        end = end + lengths[r, j]
        start = jnp.where(end <= lane, end, start)
    start = start - (place[0] - 2) * 128
    key = iota((384, 128), 0)
    allowed = (key >= start) & (key <= iota((384, 128), 1) + 256)
    half = jnp.where(allowed, 0.0, MASKED)
    return jnp.concatenate([half, half], axis=1)


def join_heads(both):
    one = jnp.where(iota((128, 128), 0) < 64, both[:, :128], both[:, 128:])
    return one.T


def copies(sources, targets, sems):
    out = [
        pltpu.make_async_copy(a, b, sems.at[i]) for i, (a, b) in enumerate(zip(sources, targets))
    ]
    for copy in out:
        copy.start()
    return out


def lanes_of(p, offset=0):
    return slice(offset + 128 * p, offset + 128 * (p + 1))


def forward_kernel(
    place, lengths, gain, bias, gain_two, bias_two, target,
    behind_two, early, late, weight, keyval, query, x, proj,
    unit_halo, context_out, attended, log_out, after_out, sent,
    b2, e1, l1, w, q, xv, wp, units, rows_in, context, att, aft, snd, in_sems, out_sems,
):
    loads = copies(
        [behind_two, early, late, weight, keyval, query, x, proj],
        [b2, e1, l1, w, context.at[:, 256:384, :], q, xv, wp],
        in_sems,
    )
    scales = head_masks(HEAD_SIZE ** (-0.5))
    for copy in loads[:3]:
        copy.wait()

    def norm_row(r, carry):
        halo = jnp.concatenate([b2[r], e1[r] + l1[r]], axis=0).astype(F32)
        unit, _ = norm_parts(halo)
        units[r] = unit.astype(BF)
        rows_in[r] = (unit * row(gain) + row(bias)).astype(BF)
        return carry

    lax.fori_loop(0, 4, norm_row, 0)
    unit_copy = pltpu.make_async_copy(units, unit_halo, out_sems.at[0])
    unit_copy.start()
    loads[3].wait()
    for j in range(3):
        cols = slice(512 * j, 512 * (j + 1))
        fresh = nn(rows_in[...].reshape(1024, 768), w[:, 768 + 512 * j : 768 + 512 * (j + 1)])
        context[:, 0:256, cols] = fresh.astype(BF).reshape(4, 256, 512)
    for copy in loads[4:6]:
        copy.wait()
    context_copy = pltpu.make_async_copy(context, context_out, out_sems.at[1])
    context_copy.start()

    def one_row(r, carry):
        mask = window_bias(place, lengths, r)
        pairs = range(PAIRS)
        stacked = [stack_heads(q[r, :, lanes_of(p)], scales) for p in pairs]
        scores = [nt(context[r, :, lanes_of(p)], stacked[p]) + mask for p in pairs]
        tops = [jnp.max(a, axis=0, keepdims=True) for a in scores]
        weights = [jnp.exp(a - t) for a, t in zip(scores, tops)]
        totals = [jnp.sum(a, axis=0, keepdims=True) for a in weights]
        shares = [(a * (1.0 / t)).astype(BF) for a, t in zip(weights, totals)]
        mixed = [tn(context[r, :, lanes_of(p, 768)], shares[p]) for p in pairs]
        for p in pairs:
            log_out[r, p : p + 1, :] = tops[p] + jnp.log(totals[p])
            att[r, :, lanes_of(p)] = join_heads(mixed[p]).astype(BF)
        return carry

    lax.fori_loop(0, 4, one_row, 0)
    att_copy = pltpu.make_async_copy(att, attended, out_sems.at[2])
    att_copy.start()
    loads[6].wait()
    loads[7].wait()
    after = xv[...].reshape(512, 768).astype(F32) + nn(att[...].reshape(512, 768), wp[...])
    aft[...] = after
    after_copy = pltpu.make_async_copy(aft, after_out, out_sems.at[3])
    after_copy.start()
    unit, _ = norm_parts(after)
    rows = (unit * row(gain_two) + row(bias_two)).astype(BF)
    sends = []
    for i in range(2):
        part = slice(512 * i, 512 * (i + 1))
        placing = (iota((512, 512), 0) + 512 * i == target[0:1, :]).astype(F32).astype(BF)
        snd[part, :] = nn(placing, rows).astype(BF)
        sends.append(pltpu.make_async_copy(snd.at[part], sent.at[part], out_sems.at[4 + i]))
        sends[-1].start()
    for copy in [unit_copy, context_copy, att_copy, after_copy] + sends:
        copy.wait()


def active_grad_kernel(grad, down, out):
    out[0] = nt(grad[...], down[...]).astype(BF)


def gelu_both(v):
    c = 0.7978845608028654
    square = v * v
    p = c + (c * 0.044715) * square
    gate = 0.5 + 0.5 * jnp.tanh(v * p)
    value = v * gate
    return value, gate + value * (1.0 - gate) * (6.0 * p - 4.0 * c)


def expert_kernel(x, up, raw, active, hidden_grad, back, total):
    step = pl.program_id(0)

    @pl.when(step == 0)
    def _():
        total[...] = jnp.zeros_like(total)

    parts = [slice(256 * r, 256 * (r + 1)) for r in range(4)]
    hidden = [nn(x[rows, :], up[...]) for rows in parts]
    lows = []
    for rows, v in zip(parts, hidden):
        value, slope = gelu_both(v)
        active[0, rows, :] = value.astype(BF)
        low = (raw[0, rows, :].astype(F32) * slope).astype(BF)
        hidden_grad[0, rows, :] = low
        lows.append(low)
    for rows, low in zip(parts, lows):
        total[rows, :] += nt(low, up[...])

    @pl.when(step == pl.num_programs(0) - 1)
    def _():
        back[...] = total[...].astype(BF)


def turn_kernel(unit, unit_halo, out):
    out[0:768, 0:512] = unit[...].T
    out[0:768, 512:1536] = unit_halo[...].T
    out[768:784, :] = jnp.ones((16, 1536), BF)


def weight_kernel(x, grad, active, hidden_grad, down, out, parts, x_t, grad_t, total):
    step = pl.program_id(0)

    @pl.when(step == 0)
    def _():
        total[...] = jnp.zeros_like(total)
        x_t[...] = x[...].T
        grad_t[...] = grad[...].T

    total[...] += nn(active[0], down[...])
    one = nn(x_t[...], hidden_grad[0]).astype(BF)
    two = nn(grad_t[...], active[0]).astype(BF)
    for j in range(2):
        parts[j, :768, :] = one[:, 384 * j : 384 * (j + 1)]
        parts[j, 768:, :] = two[:, 384 * j : 384 * (j + 1)]

    @pl.when(step == pl.num_programs(0) - 1)
    def _():
        out[...] = total[...].astype(BF)


def output_kernel(after, target, returned, out):
    placing = (iota((512, 1024), 1).astype(F32) == column(target[0:1, :].astype(F32))).astype(F32).astype(BF)
    out[...] = (after[...] + nn(placing, returned[...])).astype(BF)


def fill_halves(
    turned, query_grad, context_grad, weight, gain, bias, proj_part, terms_two, tally,
    out, gain_wide, bias_wide, gain_sum, bias_sum,
):
    gain_wide[...] = jnp.broadcast_to(row(gain), (256, 768)).T
    bias_wide[...] = jnp.broadcast_to(row(bias), (256, 768)).T

    def finish(block, both):
        body, sums = both[0:768], both[768:769]
        half, step = block // 6, block % 6
        out[half, 768 * step : 768 * (step + 1), :] = (
            gain_wide[...] * body + bias_wide[...] * sums
        ).astype(BF)
        wide = weight[:, 256 * block : 256 * (block + 1)].astype(F32)
        if block == 0:
            gain_sum[...] = wide * body
            bias_sum[...] = wide * sums
        else:
            gain_sum[...] += wide * body
            bias_sum[...] += wide * sums

    for j in range(3):
        finish(j, nn(turned[:, 0:512], query_grad[:, 256 * j : 256 * (j + 1)]))
        out[1, 768 * (3 + j) : 768 * (4 + j), :] = proj_part[j]
    for j in range(6):
        finish(3 + j, nn(turned[...], context_grad[:, 256 * j : 256 * (j + 1)]))

    columns = jnp.concatenate(
        [
            jnp.broadcast_to(jnp.sum(gain_sum[...], axis=1, keepdims=True), (768, 128)),
            jnp.broadcast_to(jnp.sum(bias_sum[...], axis=1, keepdims=True), (768, 128)),
        ],
        axis=1,
    ).T
    out[:, GEMM_ROWS:, :] = jnp.zeros((2, HALF_ROWS - GEMM_ROWS, 256), BF)
    for t in range(3):
        lanes = slice(256 * t, 256 * (t + 1))
        block = jnp.concatenate(
            [columns[0:1, lanes], columns[128:129, lanes], terms_two[:, lanes], jnp.zeros((12, 256), F32)],
            axis=0,
        )
        out[0, GEMM_ROWS + 16 * t : GEMM_ROWS + 16 * t + 16, :] = block.astype(BF)
    out[0, GEMM_ROWS + 48 : GEMM_ROWS + 64, 0:128] = tally[...].astype(BF)


def backward_kernel(
    place, lengths, gain_two, gain, bias, target, turn, log_total, tally,
    back, after, grad, proj, attended, query, context, turned, weight,
    after_grad, query_grad, own_grad, input_two, input_one, keep, away,
    bk, af, gr, wp, att, q, ctx, tu, w, ag, do, dq, cg, pp, ip, out,
    gain_wide, bias_wide, gain_sum, bias_sum, terms, in_sems, out_sems,
):
    loads = copies(
        [back, after, grad, proj, attended, query, context, turned, weight],
        [bk, af, gr, wp, att, q, ctx, tu, w],
        in_sems,
    )
    scales = head_masks(HEAD_SIZE ** (-0.5))
    ones = head_masks(1.0)
    placing = (iota((512, 1024), 1).astype(F32) == column(target[0:1, :].astype(F32))).astype(F32).astype(BF)
    live = column(flat_line(turn))
    loads[0].wait()
    normed_grad = nn(placing, bk[...])
    loads[1].wait()
    unit, inverse = norm_parts(af[...])
    terms[0:1, :] = jnp.sum(normed_grad * unit, axis=0, keepdims=True)
    terms[1:2, :] = jnp.sum(normed_grad, axis=0, keepdims=True)
    loads[2].wait()
    total = gr[...].astype(F32) * live + norm_back(normed_grad, row(gain_two), unit, inverse)
    ag[...] = total
    stores = [pltpu.make_async_copy(ag, after_grad, out_sems.at[0])]
    stores[0].start()
    low = total.astype(BF)
    loads[3].wait()
    do[...] = nt(low, wp[...]).astype(BF).reshape(4, 128, 768)
    loads[4].wait()
    mixed = nn(att[...].T, low).astype(BF)
    for j in range(3):
        pp[j] = mixed[:, 256 * j : 256 * (j + 1)]
    loads[5].wait()
    loads[6].wait()

    def one_row(r, carry):
        mask = window_bias(place, lengths, r)
        pairs = range(PAIRS)
        stacked = [stack_heads(q[r, :, lanes_of(p)], scales) for p in pairs]
        grads = [stack_heads(do[r, :, lanes_of(p)], ones) for p in pairs]
        scores = [nt(ctx[r, :, lanes_of(p)], stacked[p]) for p in pairs]
        share_grads = [nt(ctx[r, :, lanes_of(p, 768)], grads[p]) for p in pairs]
        shares = [jnp.exp(scores[p] + mask - log_total[r, p : p + 1, :]) for p in pairs]
        sums = [jnp.sum(a * b, axis=0, keepdims=True) for a, b in zip(shares, share_grads)]
        score_grads = [(a * (b - c)).astype(BF) for a, b, c in zip(shares, share_grads, sums)]
        key_grads = [nn(score_grads[p], stacked[p]).astype(BF) for p in pairs]
        value_grads = [nn(shares[p].astype(BF), grads[p]).astype(BF) for p in pairs]
        turned_grads = [tn(ctx[r, :, lanes_of(p)], score_grads[p]) for p in pairs]
        halo = pl.ds(pl.multiple_of(512 + r * 256, 256), 256)
        own = pl.ds(pl.multiple_of(r * 128, 128), 128)
        for p in pairs:
            cg[halo, lanes_of(p)] = key_grads[p][:256]
            cg[own, lanes_of(p)] = key_grads[p][256:]
            cg[halo, lanes_of(p, 768)] = value_grads[p][:256]
            cg[own, lanes_of(p, 768)] = value_grads[p][256:]
            dq[own, lanes_of(p)] = (join_heads(turned_grads[p]) * HEAD_SIZE ** (-0.5)).astype(BF)
        return carry

    lax.fori_loop(0, 4, one_row, 0)
    loads[7].wait()
    loads[8].wait()

    def store(source, target):
        stores.append(pltpu.make_async_copy(source, target, out_sems.at[len(stores)]))
        stores[-1].start()

    store(dq, query_grad)
    store(cg.at[0:512], own_grad)
    ip[...] = nt(cg[512:1536, :], w[:, 768:]).astype(BF).reshape(4, 256, 768)
    store(ip.at[:, 0:128], input_two)
    store(ip.at[:, 128:256], input_one)
    fill_halves(
        tu, dq, cg, w, gain, bias, pp, terms, tally, out, gain_wide, bias_wide, gain_sum, bias_sum
    )
    core = place[0] % 2

    @pl.when(core == 0)
    def _():
        pltpu.make_async_copy(out.at[0], keep, out_sems.at[5]).start()
        pltpu.make_async_copy(out.at[1], away, out_sems.at[6]).start()

    @pl.when(core == 1)
    def _():
        pltpu.make_async_copy(out.at[1], keep, out_sems.at[5]).start()
        pltpu.make_async_copy(out.at[0], away, out_sems.at[6]).start()

    for copy in stores:
        copy.wait()
    pltpu.make_async_copy(out.at[0], keep, out_sems.at[5]).wait()
    pltpu.make_async_copy(out.at[1], away, out_sems.at[6]).wait()


def place_half(half, data, qkv, proj, stage, sems):
    for j in range(6):
        lanes = slice(256 * (j % 3), 256 * (j % 3 + 1))
        stage[j // 3, :, lanes] = data[768 * j : 768 * (j + 1), :].astype(F32)

    @pl.when(half == 0)
    def _():
        one = pltpu.make_async_copy(stage.at[0], qkv.at[:, 0:768], sems.at[0])
        two = pltpu.make_async_copy(stage.at[1], qkv.at[:, 768:1536], sems.at[1])
        one.start()
        two.start()
        one.wait()
        two.wait()

    @pl.when(half == 1)
    def _():
        one = pltpu.make_async_copy(stage.at[0], qkv.at[:, 1536:2304], sems.at[0])
        two = pltpu.make_async_copy(stage.at[1], proj, sems.at[1])
        one.start()
        two.start()
        one.wait()
        two.wait()


def finish_mine_kernel(place, mine, qkv, proj, stage, sems):
    place_half(place[0] % 2, mine, qkv, proj, stage, sems)


def finish_other_kernel(
    place, other, tail, qkv_in, proj_in, qkv, proj, gain_one, bias_one, gain_two, bias_two, counts, received, stage, sems
):
    both = tail[...].astype(F32) + other[GEMM_ROWS:, :].astype(F32)
    for i, out in enumerate([gain_one, bias_one, gain_two, bias_two]):
        line = jnp.concatenate([both[16 * t + i : 16 * t + i + 1, :] for t in range(3)], axis=1)
        out[...] = line.reshape(768)
    every = both[48:64, 0:128]
    counts[...] = nt(jnp.ones((8, 128), BF), every.astype(BF))[0:1, :].astype(I32).reshape(16)
    chosen = (iota((16, 128), 0) == place[1]) & ((iota((16, 128), 1) >> 4) == place[0])
    mine = jnp.where(chosen, every, 0.0).astype(BF)
    fold = ((iota((128, 16), 0) & 15) == iota((128, 16), 1)).astype(F32).astype(BF)
    received[0] = jnp.sum(nn(mine, fold), axis=0, keepdims=True).astype(I32)
    place_half(1 - place[0] % 2, other, qkv, proj, stage, sems)


def expert_sum_kernel(parts, up, down):
    up[0] = parts[0, :768, :].astype(F32)
    down[0] = parts[0, 768:, :].astype(F32).T


def input_grad_kernel(
    even, gain, query_grad, own_grad, weight, x, from_one, from_two, after_grad, out,
    dq, og, w, xv, one, two, ag, in_sems,
):
    loads = copies(
        [weight, query_grad, own_grad, x, from_one, from_two, after_grad], [w, dq, og, xv, one, two, ag], in_sems
    )
    for copy in loads[:3]:
        copy.wait()
    total = nt(dq[...], w[:, :768]) + nt(og[...], w[:, 768:])
    for copy in loads[3:]:
        copy.wait()
    unit, inverse = norm_parts(xv[...].astype(F32))
    total = total + two[...].astype(F32) + even[0] * one[...].astype(F32)
    out[...] = ag[...] + norm_back(total, row(gain), unit, inverse)


PAIR_ONE = [b ^ 1 for b in range(4)]
PAIR_TWO = [b ^ 3 for b in range(4)]
PAIRS_OF = [PAIR_ONE, PAIR_TWO]
BOTH = ("batch", "seq")


def by_core(even_move, odd_move):
    pairs = []
    for b in range(16):
        for s in range(8):
            x, y = (even_move, odd_move)[s % 2](b & 3, b >> 2)
            pairs.append((b * 8 + s, (y * 4 + x) * 8 + s))
    return pairs


def first_pairs(pair):
    return by_core(lambda x, y: (pair[x], y), lambda x, y: (x, pair[y]))


def second_step(d):
    return by_core(lambda x, y: (x, (y + d) & 3), lambda x, y: ((x + d) & 3, y))


def along_z(d):
    return [(s, (s + 2 * d) & 7) for s in range(8)]


def pick(array, index):
    return lax.dynamic_index_in_dim(array, index, 0, keepdims=False)


def part_of(array, index):
    return lax.dynamic_index_in_dim(array, index % 4, 1, keepdims=False)


def sum_start(keep, got):
    seq, place = lax.axis_index("seq"), lax.axis_index("batch")
    core, x, y = seq % 2, place % 4, place // 4
    one, two = jnp.where(core == 0, x, y), jnp.where(core == 0, y, x)
    bits = [(one & 1) ^ (one >> 1), one >> 1]
    size = HALF_ROWS // 4

    def part(stream, bit):
        at = (stream * 2 + bit) * size
        return rows_at(keep, at, size).astype(F32) + rows_at(got, at, size).astype(F32)

    moved = [
        lax.ppermute(part(i, 1 - bits[i]).astype(BF), BOTH, first_pairs(PAIRS_OF[i])) for i in range(2)
    ]
    return bits, two, part, moved


def rows_at(array, at, size):
    return lax.dynamic_slice(array, (at, 0), (size, array.shape[1]))


def pair_gather(chunks, bits, pairs):
    moved = [lax.ppermute(data, BOTH, first_pairs(pair)) for pair, data in zip(pairs, chunks)]
    return [
        jnp.where(bit == 0, jnp.stack([a, b]), jnp.stack([b, a])).reshape(-1, a.shape[1])
        for bit, a, b in zip(bits, chunks, moved)
    ]


def sum_finish(bits, place, part, moved, beside):
    size = HALF_ROWS // 8
    sums = [part(i, bits[i]) + moved[i].astype(F32) for i in range(2)]
    sent = [rows_at(sums[i], (1 - bits[1 - i]) * size, size).astype(BF) for i in range(2)]
    stay = [rows_at(sums[i], bits[1 - i] * size, size) for i in range(2)]
    moved = [lax.ppermute(sent[i], BOTH, first_pairs(PAIRS_OF[1 - i])) for i in range(2)]
    chunks = [(a + b.astype(F32)).astype(BF) for a, b in zip(stay, moved)]
    size, lanes = chunks[0].shape
    grouped = jnp.stack(chunks).reshape(2, 4, size // 4, lanes)
    total = part_of(grouped, place).astype(F32)
    for d in (2, 1, 3):
        total = total + lax.ppermute(part_of(grouped, place + d), BOTH, second_step(d)).astype(F32)
    whole = after_all(total.astype(BF), *beside[0])
    total = whole.astype(F32)
    for d in (2, 1, 3):
        total = total + lax.ppermute(whole, "seq", along_z(d)).astype(F32)
    piece = after_all(total.astype(BF), *beside[1])
    parts = [piece] + [lax.ppermute(piece, BOTH, second_step(d)) for d in (1, 2, 3)]
    stack = jnp.stack(parts, axis=1)
    ordered = jnp.stack([part_of(stack, place - p + 4) for p in range(4)], axis=1).reshape(2, size, lanes)
    chunks = pair_gather([ordered[0], ordered[1]], bits[::-1], PAIRS_OF[::-1])
    chunks[0] = after_all(chunks[0], *beside[2])
    chunks = pair_gather(chunks, bits, PAIRS_OF)
    return jnp.concatenate(chunks, axis=0)


def after_all(value, *others):
    return lax.optimization_barrier((value, *others))[0]


def exchange(array):
    return lax.all_to_all(
        array.reshape(16, CAP, 768), "batch", split_axis=0, concat_axis=0, tiled=True
    ).reshape(1024, 768)


def local(
    block_input, token_ids, hash_table, doc_lengths, turn_mask, attn_norm_gain, attn_norm_bias,
    qkv_weight, proj_weight, ffn_norm_gain, ffn_norm_bias, expert_up, expert_down, out_grad,
):
    seq = lax.axis_index("seq")
    owner = lax.axis_index("batch")
    odd = seq % 2
    flat = (512, 768)
    rows3 = (4, 128, 768)
    place = jnp.stack([seq, owner]).astype(I32)
    up, down = expert_up[0], expert_down[0]

    behind_two = lax.ppermute(block_input, "seq", AHEAD_TWO)
    early = lax.ppermute(block_input, "seq", UP_ONE)

    table = jnp.pad(hash_table, (0, 8192 - 8008)).reshape(64, 128)
    target, tally, grad_sent = kernel_call(
        route_kernel,
        [shape((8, 512), I32), shape((16, 128), F32), shape((1024, 768))],
        [place, token_ids, table, turn_mask, out_grad.reshape(flat)],
        "route", 10**9,
        in_specs=[SM] + [VM] * 4,
    )
    grad_rows = exchange(grad_sent)

    unit, query, keyval = kernel_call(
        own_kernel,
        [shape(flat), shape(flat), shape((512, 1536))],
        [block_input.reshape(flat), attn_norm_gain, attn_norm_bias, qkv_weight],
        "own", 18 * 10**8,
    )
    late = lax.ppermute(after_all(behind_two, query, grad_sent), "seq", DOWN_ONE)
    query, keyval = query.reshape(rows3), keyval.reshape(4, 128, 1536)

    unit_halo, context, attended, log_total, after, rows_sent = kernel_call(
        forward_kernel,
        [
            shape((4, 256, 768)), shape((4, 384, 1536)), shape(rows3), shape((4, 8, 256), F32),
            shape(flat, F32), shape((1024, 768)),
        ],
        [
            place, doc_lengths, attn_norm_gain, attn_norm_bias, ffn_norm_gain, ffn_norm_bias, target,
            behind_two, early, late, qkv_weight, keyval, query, block_input, proj_weight,
        ],
        "forward", 10**9,
        in_specs=[SM] * 2 + [VM] * 5 + [HB] * 8,
        out_specs=[HB] * 3 + [VM] + [HB] * 2,
        scratch=[
            pltpu.VMEM(rows3, BF), pltpu.VMEM(rows3, BF), pltpu.VMEM(rows3, BF), pltpu.VMEM((768, 2304), BF),
            pltpu.VMEM(rows3, BF), pltpu.VMEM(rows3, BF), pltpu.VMEM((768, 768), BF),
            pltpu.VMEM((4, 256, 768), BF), pltpu.VMEM((4, 256, 768), BF), pltpu.VMEM((4, 384, 1536), BF),
            pltpu.VMEM(rows3, BF), pltpu.VMEM(flat, F32), pltpu.VMEM((1024, 768), BF),
            pltpu.SemaphoreType.DMA((8,)), pltpu.SemaphoreType.DMA((6,)),
        ],
    )
    rows = exchange(rows_sent)

    turned = kernel_call(
        turn_kernel, [shape((784, 1536))], [unit, unit_halo.reshape(1024, 768)], "turn", 10**6
    )[0]
    tile = pl.BlockSpec((1, 1024, 768), lambda i: (i, 0, 0))
    tiled = shape((4, 1024, 768))
    whole = pl.BlockSpec((1024, 768), lambda i: (0, 0))
    raw = kernel_call(
        active_grad_kernel,
        [tiled],
        [after_all(grad_rows, turned), down],
        "active_grad", 48 * 10**8,
        grid=(4,),
        in_specs=[whole, pl.BlockSpec((768, 768), lambda i: (i, 0))],
        out_specs=[tile],
    )[0]

    active, hidden_grad, back_sent = kernel_call(
        expert_kernel,
        [tiled, tiled, shape((1024, 768))],
        [rows, up, raw],
        "expert", 97 * 10**8,
        grid=(4,),
        in_specs=[whole, pl.BlockSpec((768, 768), lambda i: (0, i)), tile],
        out_specs=[tile, tile, whole],
        scratch=[pltpu.VMEM((1024, 768), F32)],
    )
    back = exchange(back_sent)

    result, parts = kernel_call(
        weight_kernel,
        [shape((1024, 768)), shape((8, 1536, 384))],
        [rows, grad_rows, active, hidden_grad, down],
        "weights", 145 * 10**8,
        grid=(4,),
        in_specs=[
            whole,
            whole,
            tile,
            tile,
            pl.BlockSpec((768, 768), lambda i: (i, 0)),
        ],
        out_specs=[
            pl.BlockSpec((1024, 768), lambda i: (0, 0)),
            pl.BlockSpec((2, 1536, 384), lambda i: (i, 0, 0)),
        ],
        scratch=[pltpu.VMEM((768, 1024), BF), pltpu.VMEM((768, 1024), BF), pltpu.VMEM((1024, 768), F32)],
    )
    returned = exchange(result)
    parts_sum = lax.psum_scatter(after_all(parts, back), "seq", scatter_dimension=0, tiled=True)

    after_grad, query_grad, own_grad, input_two, input_one, keep, away = kernel_call(
        backward_kernel,
        [
            shape(flat, F32), shape(flat), shape((512, 1536)), shape(rows3), shape(rows3),
            shape((HALF_ROWS, 256)), shape((HALF_ROWS, 256)),
        ],
        [
            place, doc_lengths, ffn_norm_gain, attn_norm_gain, attn_norm_bias, target, turn_mask, log_total, tally,
            back, after, out_grad.reshape(flat), proj_weight, attended.reshape(flat), query, context, turned,
            qkv_weight,
        ],
        "backward", 16 * 10**9,
        in_specs=[SM] * 2 + [VM] * 7 + [HB] * 9,
        out_specs=[HB] * 7,
        scratch=[
            pltpu.VMEM((1024, 768), BF), pltpu.VMEM(flat, F32), pltpu.VMEM(flat, BF), pltpu.VMEM((768, 768), BF),
            pltpu.VMEM(flat, BF), pltpu.VMEM(rows3, BF), pltpu.VMEM((4, 384, 1536), BF),
            pltpu.VMEM((784, 1536), BF), pltpu.VMEM((768, 2304), BF), pltpu.VMEM(flat, F32), pltpu.VMEM(rows3, BF),
            pltpu.VMEM(flat, BF), pltpu.VMEM((1536, 1536), BF), pltpu.VMEM((3, 768, 256), BF),
            pltpu.VMEM((4, 256, 768), BF), pltpu.VMEM((2, HALF_ROWS, 256), BF),
            pltpu.VMEM((768, 256), F32), pltpu.VMEM((768, 256), F32), pltpu.VMEM((768, 256), F32),
            pltpu.VMEM((768, 256), F32), pltpu.VMEM((2, 768), F32),
            pltpu.SemaphoreType.DMA((9,)), pltpu.SemaphoreType.DMA((7,)),
        ],
    )
    got = lax.ppermute(after_all(away, returned), "seq", SWAP)
    bits, turn, part, streams = sum_start(keep, got)

    from_one = lax.ppermute(input_one, "seq", SWAP)
    passed = jnp.where(odd == 1, input_two + from_one, input_two)
    from_two = lax.ppermute(passed, "seq", BACK_TWO)
    even = (1 - odd).astype(F32).reshape(1)
    input_grad = kernel_call(
        input_grad_kernel,
        [shape(flat, F32)],
        [
            even, attn_norm_gain, query_grad, own_grad, qkv_weight, block_input.reshape(flat),
            from_one.reshape(flat), from_two.reshape(flat), after_grad,
        ],
        "input_grad", 3 * 10**9,
        in_specs=[SM, VM] + [HB] * 7,
        scratch=[
            pltpu.VMEM(flat, BF), pltpu.VMEM((512, 1536), BF), pltpu.VMEM((768, 2304), BF), pltpu.VMEM(flat, BF),
            pltpu.VMEM(flat, BF), pltpu.VMEM(flat, BF), pltpu.VMEM(flat, F32), pltpu.SemaphoreType.DMA((7,)),
        ],
    )[0]
    block_output = kernel_call(
        output_kernel, [shape(flat)], [after, target, returned], "output", 8 * 10**8
    )[0]
    up_sum, down_sum = kernel_call(
        expert_sum_kernel,
        [shape((1, 768, 384), F32), shape((1, 384, 768), F32)],
        [parts_sum], "expert_sum", 10**6,
    )
    mine = sum_finish(bits, turn, part, streams, ([from_two], [block_output, up_sum], [input_grad]))
    other = lax.ppermute(mine, "seq", SWAP)
    sums = [shape((768, 2304), F32), shape((768, 768), F32)]
    away_spec = [pl.BlockSpec(memory_space=pl.ANY)] * 2
    landing = [pltpu.VMEM((2, 768, 768), F32), pltpu.SemaphoreType.DMA((2,))]
    qkv_half, proj_half = kernel_call(
        finish_mine_kernel, sums, [place, mine], "finish_mine", 10**6,
        in_specs=[SM, VM], out_specs=away_spec, scratch=landing,
    )
    line = shape((768,), F32)
    qkv_sum, proj_sum, *rest = kernel_call(
        finish_other_kernel,
        sums + [line] * 4 + [shape((16,), I32), shape((1, 1, 16), I32)],
        [place, other, mine[GEMM_ROWS:], qkv_half, proj_half],
        "finish_other", 10**6,
        in_specs=[SM, VM, VM] + away_spec, out_specs=away_spec + [VM] * 6, scratch=landing,
        aliases={3: 0, 4: 1},
    )
    return (
        block_output.reshape(rows3),
        input_grad.reshape(rows3),
        rest[0],
        rest[1],
        qkv_sum,
        proj_sum,
        rest[2],
        rest[3],
        up_sum,
        down_sum,
        rest[4],
        rest[5],
    )


def solution(mesh):
    placed = (
        P("batch", "seq", None),
        P("batch", "seq"),
        P(),
        P("batch", None),
        P("batch", "seq"),
        P(),
        P(),
        P(),
        P(),
        P(),
        P(),
        P("batch", None, None),
        P("batch", None, None),
        P("batch", "seq", None),
    )
    return jax.shard_map(
        local,
        mesh=mesh,
        in_specs=placed,
        out_specs=(
            P("batch", "seq", None),
            P("batch", "seq", None),
            P(),
            P(),
            P(),
            P(),
            P(),
            P(),
            P("batch", None, "seq"),
            P("batch", "seq", None),
            P(),
            P("batch", "seq", None),
        ),
        check_vma=False,
    )
```

```python
import jax
import jax.numpy as jnp
from jax import lax
from jax.experimental import pallas as pl
from jax.experimental.pallas import tpu as pltpu
from jax.sharding import PartitionSpec as P

BF = jnp.bfloat16
F32 = jnp.float32
I32 = jnp.int32
EPS = 1e-05
MASKED = -1e30
HEADS = 12
HEAD_SIZE = 64
PAIRS = 6
CAP = 64
SWAP = [(i, i ^ 1) for i in range(8)]
UP_ONE = [(i, i + 1) for i in range(0, 8, 2)]
DOWN_ONE = [(i + 1, i) for i in range(0, 8, 2)]
AHEAD_TWO = [(i, i + 2) for i in range(6)]
BACK_TWO = [(i + 2, i) for i in range(6)]
HALF_ROWS = 4864
PIECE = HALF_ROWS // 4
VMEM_BYTES = 63 * 1024 * 1024
GEMM_ROWS = 4608
VM = pl.BlockSpec(memory_space=pltpu.VMEM)
HB = pl.BlockSpec(memory_space=pl.ANY)
SM = pl.BlockSpec(memory_space=pltpu.SMEM)


def shape(dims, kind=BF):
    return jax.ShapeDtypeStruct(dims, kind)


def kernel_call(body, outs, args, name, flops, grid=None, in_specs=None, out_specs=None, scratch=(), aliases=None):
    moved = sum(a.size * a.dtype.itemsize for a in args) + sum(
        o.size * o.dtype.itemsize for o in outs
    )
    extra = {} if grid is None else {"grid": grid}
    return pl.pallas_call(
        body,
        out_shape=outs,
        in_specs=in_specs or [VM] * len(args),
        out_specs=out_specs or [VM] * len(outs),
        scratch_shapes=list(scratch),
        compiler_params=pltpu.CompilerParams(vmem_limit_bytes=VMEM_BYTES),
        cost_estimate=pl.CostEstimate(flops=flops, bytes_accessed=moved, transcendentals=0),
        name=name,
        input_output_aliases=aliases or {},
        **extra,
    )(*args)


def nn(a, b):
    return jnp.dot(a, b, preferred_element_type=F32)


def nt(a, b):
    return lax.dot_general(a, b, (((1,), (1,)), ((), ())), preferred_element_type=F32)


def tn(a, b):
    return lax.dot_general(a, b, (((0,), (0,)), ((), ())), preferred_element_type=F32)


def iota(dims, axis):
    return lax.broadcasted_iota(I32, dims, axis)


def row(ref):
    return ref[...].reshape(1, 768)


def column(line):
    return jnp.broadcast_to(line, (128, line.shape[1])).T[:, 0:1]


def flat_line(ref):
    return jnp.concatenate([ref[i : i + 1, :] for i in range(4)], axis=1).astype(F32)


def norm_parts(values):
    centred = values - jnp.mean(values, axis=-1, keepdims=True)
    inverse = lax.rsqrt(jnp.mean(centred * centred, axis=-1, keepdims=True) + EPS)
    return centred * inverse, inverse


def norm_back(grad, gain, unit, inverse):
    t = grad * gain
    return inverse * (
        t - jnp.mean(t, axis=-1, keepdims=True) - unit * jnp.mean(t * unit, axis=-1, keepdims=True)
    )


def route_kernel(place, tok, table, turn, grad, target_out, tally, sent):
    ids = jnp.concatenate([tok[i : i + 1, :] for i in range(4)], axis=1)
    live = flat_line(turn)
    high, low = ids >> 7, ids & 127
    picked = tn(table[...].astype(F32).astype(BF), (iota((64, 512), 0) == high).astype(F32).astype(BF))
    chosen = jnp.sum(jnp.where(iota((128, 512), 0) == low, picked, 0.0), axis=0, keepdims=True)
    member = (iota((16, 512), 0) == chosen.astype(I32)).astype(F32)
    earlier = (iota((512, 512), 0) < iota((512, 512), 1)).astype(F32).astype(BF)
    before = nn(member.astype(BF), earlier)
    slot = jnp.sum(before * member, axis=0, keepdims=True)
    target = (chosen * CAP + slot).astype(I32)
    target_out[...] = jnp.broadcast_to(target, (8, 512))
    counts = jnp.sum(member, axis=1, keepdims=True)
    tally[...] = jnp.where(iota((16, 128), 1) == place[0] * 16 + place[1], counts, 0.0)
    for i in range(4):
        placing = jnp.where(iota((256, 512), 0) + 256 * i == target, live, 0.0).astype(BF)
        sent[256 * i : 256 * (i + 1), :] = nn(placing, grad[...]).astype(BF)


def own_kernel(x, gain, bias, weight, unit_out, query, keyval):
    unit, _ = norm_parts(x[...].astype(F32))
    unit_out[...] = unit.astype(BF)
    rows = (unit * row(gain) + row(bias)).astype(BF)
    query[...] = nn(rows, weight[:, :768]).astype(BF)
    keyval[...] = nn(rows, weight[:, 768:]).astype(BF)


def head_masks(scale):
    lane = iota((1, 128), 1)
    first = jnp.where(lane < 64, scale, 0.0).astype(BF)
    second = jnp.where(lane >= 64, scale, 0.0).astype(BF)
    return first, second


def stack_heads(pair, masks):
    return jnp.concatenate([pair * masks[0], pair * masks[1]], axis=0)


def window_bias(place, lengths, r):
    lane = iota((1, 128), 1) + place[0] * 128
    end, start = jnp.int32(0), jnp.zeros((1, 128), I32)
    for j in range(8):
        end = end + lengths[r, j]
        start = jnp.where(end <= lane, end, start)
    start = start - (place[0] - 2) * 128
    key = iota((384, 128), 0)
    allowed = (key >= start) & (key <= iota((384, 128), 1) + 256)
    half = jnp.where(allowed, 0.0, MASKED)
    return jnp.concatenate([half, half], axis=1)


def join_heads(both):
    one = jnp.where(iota((128, 128), 0) < 64, both[:, :128], both[:, 128:])
    return one.T


def copies(sources, targets, sems):
    out = [
        pltpu.make_async_copy(a, b, sems.at[i]) for i, (a, b) in enumerate(zip(sources, targets))
    ]
    for copy in out:
        copy.start()
    return out


def lanes_of(p, offset=0):
    return slice(offset + 128 * p, offset + 128 * (p + 1))


def forward_kernel(
    place, lengths, gain, bias, gain_two, bias_two, target,
    behind_two, early, late, weight, keyval, query, x, proj,
    unit_halo, context_out, attended, log_out, after_out, sent,
    b2, e1, l1, w, q, xv, wp, units, rows_in, context, att, aft, snd, in_sems, out_sems,
):
    loads = copies(
        [behind_two, early, late, weight, keyval, query, x, proj],
        [b2, e1, l1, w, context.at[:, 256:384, :], q, xv, wp],
        in_sems,
    )
    scales = head_masks(HEAD_SIZE ** (-0.5))
    for copy in loads[:3]:
        copy.wait()

    def norm_row(r, carry):
        halo = jnp.concatenate([b2[r], e1[r] + l1[r]], axis=0).astype(F32)
        unit, _ = norm_parts(halo)
        units[r] = unit.astype(BF)
        rows_in[r] = (unit * row(gain) + row(bias)).astype(BF)
        return carry

    lax.fori_loop(0, 4, norm_row, 0)
    unit_copy = pltpu.make_async_copy(units, unit_halo, out_sems.at[0])
    unit_copy.start()
    loads[3].wait()
    for j in range(3):
        cols = slice(512 * j, 512 * (j + 1))
        fresh = nn(rows_in[...].reshape(1024, 768), w[:, 768 + 512 * j : 768 + 512 * (j + 1)])
        context[:, 0:256, cols] = fresh.astype(BF).reshape(4, 256, 512)
    for copy in loads[4:6]:
        copy.wait()
    context_copy = pltpu.make_async_copy(context, context_out, out_sems.at[1])
    context_copy.start()

    def one_row(r, carry):
        mask = window_bias(place, lengths, r)
        pairs = range(PAIRS)
        stacked = [stack_heads(q[r, :, lanes_of(p)], scales) for p in pairs]
        scores = [nt(context[r, :, lanes_of(p)], stacked[p]) + mask for p in pairs]
        tops = [jnp.max(a, axis=0, keepdims=True) for a in scores]
        weights = [jnp.exp(a - t) for a, t in zip(scores, tops)]
        totals = [jnp.sum(a, axis=0, keepdims=True) for a in weights]
        shares = [(a * (1.0 / t)).astype(BF) for a, t in zip(weights, totals)]
        mixed = [tn(context[r, :, lanes_of(p, 768)], shares[p]) for p in pairs]
        for p in pairs:
            log_out[r, p : p + 1, :] = tops[p] + jnp.log(totals[p])
            att[r, :, lanes_of(p)] = join_heads(mixed[p]).astype(BF)
        return carry

    lax.fori_loop(0, 4, one_row, 0)
    att_copy = pltpu.make_async_copy(att, attended, out_sems.at[2])
    att_copy.start()
    loads[6].wait()
    loads[7].wait()
    after = xv[...].reshape(512, 768).astype(F32) + nn(att[...].reshape(512, 768), wp[...])
    aft[...] = after
    after_copy = pltpu.make_async_copy(aft, after_out, out_sems.at[3])
    after_copy.start()
    unit, _ = norm_parts(after)
    rows = (unit * row(gain_two) + row(bias_two)).astype(BF)
    sends = []
    for i in range(2):
        part = slice(512 * i, 512 * (i + 1))
        placing = (iota((512, 512), 0) + 512 * i == target[0:1, :]).astype(F32).astype(BF)
        snd[part, :] = nn(placing, rows).astype(BF)
        sends.append(pltpu.make_async_copy(snd.at[part], sent.at[part], out_sems.at[4 + i]))
        sends[-1].start()
    for copy in [unit_copy, context_copy, att_copy, after_copy] + sends:
        copy.wait()


def active_grad_kernel(grad, down, out):
    out[0] = nt(grad[...], down[...]).astype(BF)


def gelu_both(v):
    c = 0.7978845608028654
    square = v * v
    p = c + (c * 0.044715) * square
    gate = 0.5 + 0.5 * jnp.tanh(v * p)
    value = v * gate
    return value, gate + value * (1.0 - gate) * (6.0 * p - 4.0 * c)


def expert_kernel(x, up, raw, active, hidden_grad, back, total):
    step = pl.program_id(0)

    @pl.when(step == 0)
    def _():
        total[...] = jnp.zeros_like(total)

    parts = [slice(256 * r, 256 * (r + 1)) for r in range(4)]
    hidden = [nn(x[rows, :], up[...]) for rows in parts]
    lows = []
    for rows, v in zip(parts, hidden):
        value, slope = gelu_both(v)
        active[0, rows, :] = value.astype(BF)
        low = (raw[0, rows, :].astype(F32) * slope).astype(BF)
        hidden_grad[0, rows, :] = low
        lows.append(low)
    for rows, low in zip(parts, lows):
        total[rows, :] += nt(low, up[...])

    @pl.when(step == pl.num_programs(0) - 1)
    def _():
        back[...] = total[...].astype(BF)


def turn_kernel(unit, unit_halo, out):
    out[0:768, 0:512] = unit[...].T
    out[0:768, 512:1536] = unit_halo[...].T
    out[768:784, :] = jnp.ones((16, 1536), BF)


def weight_kernel(x, grad, active, hidden_grad, down, out, parts, x_t, grad_t, total):
    step = pl.program_id(0)

    @pl.when(step == 0)
    def _():
        total[...] = jnp.zeros_like(total)
        x_t[...] = x[...].T
        grad_t[...] = grad[...].T

    total[...] += nn(active[0], down[...])
    one = nn(x_t[...], hidden_grad[0]).astype(BF)
    two = nn(grad_t[...], active[0]).astype(BF)
    for j in range(2):
        parts[j, :768, :] = one[:, 384 * j : 384 * (j + 1)]
        parts[j, 768:, :] = two[:, 384 * j : 384 * (j + 1)]

    @pl.when(step == pl.num_programs(0) - 1)
    def _():
        out[...] = total[...].astype(BF)


def output_kernel(after, target, returned, out):
    placing = (iota((512, 1024), 1).astype(F32) == column(target[0:1, :].astype(F32))).astype(F32).astype(BF)
    out[...] = (after[...] + nn(placing, returned[...])).astype(BF)


def fill_halves(
    turned, query_grad, context_grad, weight, gain, bias, proj_part, terms_two, tally,
    out, gain_wide, bias_wide, gain_sum, bias_sum,
):
    gain_wide[...] = jnp.broadcast_to(row(gain), (256, 768)).T
    bias_wide[...] = jnp.broadcast_to(row(bias), (256, 768)).T

    def finish(block, both):
        body, sums = both[0:768], both[768:769]
        half, step = block // 6, block % 6
        out[half, 768 * step : 768 * (step + 1), :] = (
            gain_wide[...] * body + bias_wide[...] * sums
        ).astype(BF)
        wide = weight[:, 256 * block : 256 * (block + 1)].astype(F32)
        if block == 0:
            gain_sum[...] = wide * body
            bias_sum[...] = wide * sums
        else:
            gain_sum[...] += wide * body
            bias_sum[...] += wide * sums

    for j in range(3):
        finish(j, nn(turned[:, 0:512], query_grad[:, 256 * j : 256 * (j + 1)]))
        out[1, 768 * (3 + j) : 768 * (4 + j), :] = proj_part[j]
    for j in range(6):
        finish(3 + j, nn(turned[...], context_grad[:, 256 * j : 256 * (j + 1)]))

    columns = jnp.concatenate(
        [
            jnp.broadcast_to(jnp.sum(gain_sum[...], axis=1, keepdims=True), (768, 128)),
            jnp.broadcast_to(jnp.sum(bias_sum[...], axis=1, keepdims=True), (768, 128)),
        ],
        axis=1,
    ).T
    out[:, GEMM_ROWS:, :] = jnp.zeros((2, HALF_ROWS - GEMM_ROWS, 256), BF)
    for t in range(3):
        lanes = slice(256 * t, 256 * (t + 1))
        block = jnp.concatenate(
            [columns[0:1, lanes], columns[128:129, lanes], terms_two[:, lanes], jnp.zeros((12, 256), F32)],
            axis=0,
        )
        out[0, GEMM_ROWS + 16 * t : GEMM_ROWS + 16 * t + 16, :] = block.astype(BF)
    out[0, GEMM_ROWS + 48 : GEMM_ROWS + 64, 0:128] = tally[...].astype(BF)


def backward_kernel(
    place, lengths, gain_two, gain, bias, target, turn, log_total, tally,
    back, after, grad, proj, attended, query, context, turned, weight,
    after_grad, query_grad, own_grad, input_two, input_one, keep, away,
    bk, af, gr, wp, att, q, ctx, tu, w, ag, do, dq, cg, pp, ip, out,
    gain_wide, bias_wide, gain_sum, bias_sum, terms, in_sems, out_sems,
):
    loads = copies(
        [back, after, grad, proj, attended, query, context, turned, weight],
        [bk, af, gr, wp, att, q, ctx, tu, w],
        in_sems,
    )
    scales = head_masks(HEAD_SIZE ** (-0.5))
    ones = head_masks(1.0)
    placing = (iota((512, 1024), 1).astype(F32) == column(target[0:1, :].astype(F32))).astype(F32).astype(BF)
    live = column(flat_line(turn))
    loads[0].wait()
    normed_grad = nn(placing, bk[...])
    loads[1].wait()
    unit, inverse = norm_parts(af[...])
    terms[0:1, :] = jnp.sum(normed_grad * unit, axis=0, keepdims=True)
    terms[1:2, :] = jnp.sum(normed_grad, axis=0, keepdims=True)
    loads[2].wait()
    total = gr[...].astype(F32) * live + norm_back(normed_grad, row(gain_two), unit, inverse)
    ag[...] = total
    stores = [pltpu.make_async_copy(ag, after_grad, out_sems.at[0])]
    stores[0].start()
    low = total.astype(BF)
    loads[3].wait()
    do[...] = nt(low, wp[...]).astype(BF).reshape(4, 128, 768)
    loads[4].wait()
    mixed = nn(att[...].T, low).astype(BF)
    for j in range(3):
        pp[j] = mixed[:, 256 * j : 256 * (j + 1)]
    loads[5].wait()
    loads[6].wait()

    def one_row(r, carry):
        mask = window_bias(place, lengths, r)
        pairs = range(PAIRS)
        stacked = [stack_heads(q[r, :, lanes_of(p)], scales) for p in pairs]
        grads = [stack_heads(do[r, :, lanes_of(p)], ones) for p in pairs]
        scores = [nt(ctx[r, :, lanes_of(p)], stacked[p]) for p in pairs]
        share_grads = [nt(ctx[r, :, lanes_of(p, 768)], grads[p]) for p in pairs]
        shares = [jnp.exp(scores[p] + mask - log_total[r, p : p + 1, :]) for p in pairs]
        sums = [jnp.sum(a * b, axis=0, keepdims=True) for a, b in zip(shares, share_grads)]
        score_grads = [(a * (b - c)).astype(BF) for a, b, c in zip(shares, share_grads, sums)]
        key_grads = [nn(score_grads[p], stacked[p]).astype(BF) for p in pairs]
        value_grads = [nn(shares[p].astype(BF), grads[p]).astype(BF) for p in pairs]
        turned_grads = [tn(ctx[r, :, lanes_of(p)], score_grads[p]) for p in pairs]
        halo = pl.ds(pl.multiple_of(512 + r * 256, 256), 256)
        own = pl.ds(pl.multiple_of(r * 128, 128), 128)
        for p in pairs:
            cg[halo, lanes_of(p)] = key_grads[p][:256]
            cg[own, lanes_of(p)] = key_grads[p][256:]
            cg[halo, lanes_of(p, 768)] = value_grads[p][:256]
            cg[own, lanes_of(p, 768)] = value_grads[p][256:]
            dq[own, lanes_of(p)] = (join_heads(turned_grads[p]) * HEAD_SIZE ** (-0.5)).astype(BF)
        return carry

    lax.fori_loop(0, 4, one_row, 0)
    loads[7].wait()
    loads[8].wait()

    def store(source, target):
        stores.append(pltpu.make_async_copy(source, target, out_sems.at[len(stores)]))
        stores[-1].start()

    store(dq, query_grad)
    store(cg.at[0:512], own_grad)
    ip[...] = nt(cg[512:1536, :], w[:, 768:]).astype(BF).reshape(4, 256, 768)
    store(ip.at[:, 0:128], input_two)
    store(ip.at[:, 128:256], input_one)
    fill_halves(
        tu, dq, cg, w, gain, bias, pp, terms, tally, out, gain_wide, bias_wide, gain_sum, bias_sum
    )
    core = place[0] % 2

    @pl.when(core == 0)
    def _():
        pltpu.make_async_copy(out.at[0], keep, out_sems.at[5]).start()
        pltpu.make_async_copy(out.at[1], away, out_sems.at[6]).start()

    @pl.when(core == 1)
    def _():
        pltpu.make_async_copy(out.at[1], keep, out_sems.at[5]).start()
        pltpu.make_async_copy(out.at[0], away, out_sems.at[6]).start()

    for copy in stores:
        copy.wait()
    pltpu.make_async_copy(out.at[0], keep, out_sems.at[5]).wait()
    pltpu.make_async_copy(out.at[1], away, out_sems.at[6]).wait()


def place_half(half, bits, pieces, qkv, proj, whole, stage, in_sems, sems):
    loads = []
    for i in range(2):
        for j in range(2):
            first = pl.multiple_of((2 * i + (bits[i] + j) % 2) * PIECE, PIECE)
            target = whole.at[pl.ds(first, PIECE)]
            loads.append(pltpu.make_async_copy(pieces[2 * i + j], target, in_sems.at[2 * i + j]))
            loads[-1].start()
    for copy in loads:
        copy.wait()
    for j in range(6):
        lanes = slice(256 * (j % 3), 256 * (j % 3 + 1))
        stage[j // 3, :, lanes] = whole[768 * j : 768 * (j + 1), :].astype(F32)

    def send(targets):
        moves = [pltpu.make_async_copy(stage.at[i], target, sems.at[i]) for i, target in enumerate(targets)]
        for copy in moves:
            copy.start()
        for copy in moves:
            copy.wait()

    @pl.when(half == 0)
    def _():
        send([qkv.at[:, 0:768], qkv.at[:, 768:1536]])

    @pl.when(half == 1)
    def _():
        send([qkv.at[:, 1536:2304], proj])


def finish_mine_kernel(place, a, b, c, d, qkv, proj, tail, whole, stage, in_sems, sems):
    place_half(place[0], (place[2], place[3]), (a, b, c, d), qkv, proj, whole, stage, in_sems, sems)
    tail[...] = whole[GEMM_ROWS : GEMM_ROWS + 64, :]


def finish_other_kernel(
    place, tail, a, b, c, d, qkv_in, proj_in, qkv, proj, gain_one, bias_one, gain_two, bias_two, counts, received,
    whole, stage, in_sems, sems,
):
    place_half(1 - place[0], (place[4], place[5]), (a, b, c, d), qkv, proj, whole, stage, in_sems, sems)
    both = tail[...].astype(F32) + whole[GEMM_ROWS : GEMM_ROWS + 64, :].astype(F32)
    for i, out in enumerate([gain_one, bias_one, gain_two, bias_two]):
        line = jnp.concatenate([both[16 * t + i : 16 * t + i + 1, :] for t in range(3)], axis=1)
        out[...] = line.reshape(768)
    every = both[48:64, 0:128]
    counts[...] = nt(jnp.ones((8, 128), BF), every.astype(BF))[0:1, :].astype(I32).reshape(16)
    chosen = (iota((16, 128), 0) == place[1]) & ((iota((16, 128), 1) >> 4) == place[6])
    mine = jnp.where(chosen, every, 0.0).astype(BF)
    fold = ((iota((128, 16), 0) & 15) == iota((128, 16), 1)).astype(F32).astype(BF)
    received[0] = jnp.sum(nn(mine, fold), axis=0, keepdims=True).astype(I32)


def expert_sum_kernel(parts, up, down):
    up[0] = parts[0, :768, :].astype(F32)
    down[0] = parts[0, 768:, :].astype(F32).T


def input_grad_kernel(
    even, gain, query_grad, own_grad, weight, x, from_one, from_two, after_grad, out,
    dq, og, w, xv, one, two, ag, in_sems,
):
    loads = copies(
        [weight, query_grad, own_grad, x, from_one, from_two, after_grad], [w, dq, og, xv, one, two, ag], in_sems
    )
    for copy in loads[:3]:
        copy.wait()
    total = nt(dq[...], w[:, :768]) + nt(og[...], w[:, 768:])
    for copy in loads[3:]:
        copy.wait()
    unit, inverse = norm_parts(xv[...].astype(F32))
    total = total + two[...].astype(F32) + even[0] * one[...].astype(F32)
    out[...] = ag[...] + norm_back(total, row(gain), unit, inverse)


PAIR_ONE = [b ^ 1 for b in range(4)]
PAIR_TWO = [b ^ 3 for b in range(4)]
PAIRS_OF = [PAIR_ONE, PAIR_TWO]
BOTH = ("batch", "seq")


def by_core(even_move, odd_move):
    pairs = []
    for b in range(16):
        for s in range(8):
            x, y = (even_move, odd_move)[s % 2](b & 3, b >> 2)
            pairs.append((b * 8 + s, (y * 4 + x) * 8 + s))
    return pairs


def first_pairs(pair):
    return by_core(lambda x, y: (pair[x], y), lambda x, y: (x, pair[y]))


def second_step(d):
    return by_core(lambda x, y: (x, (y + d) & 3), lambda x, y: ((x + d) & 3, y))


def along_z(d):
    return [(s, (s + 2 * d) & 7) for s in range(8)]


def pick(array, index):
    return lax.dynamic_index_in_dim(array, index, 0, keepdims=False)


def part_of(array, index):
    return lax.dynamic_index_in_dim(array, index % 4, 1, keepdims=False)


def bits_of(place):
    return [(place & 1) ^ (place >> 1), place >> 1]


def sum_start(keep, got):
    seq, place = lax.axis_index("seq"), lax.axis_index("batch")
    core, x, y = seq % 2, place % 4, place // 4
    one, two = jnp.where(core == 0, x, y), jnp.where(core == 0, y, x)
    bits = bits_of(one)

    def part(stream, bit):
        at = (stream * 2 + bit) * PIECE
        return rows_at(keep, at, PIECE).astype(F32) + rows_at(got, at, PIECE).astype(F32)

    moved = [
        lax.ppermute(part(i, 1 - bits[i]).astype(BF), BOTH, first_pairs(PAIRS_OF[i])) for i in range(2)
    ]
    return bits, two, part, moved


def rows_at(array, at, size):
    return lax.dynamic_slice(array, (at, 0), (size, array.shape[1]))


def pair_gather(chunks, bits, pairs):
    moved = [lax.ppermute(data, BOTH, first_pairs(pair)) for pair, data in zip(pairs, chunks)]
    return [
        jnp.where(bit == 0, jnp.stack([a, b]), jnp.stack([b, a])).reshape(-1, a.shape[1])
        for bit, a, b in zip(bits, chunks, moved)
    ]


def sum_finish(bits, place, part, moved, beside):
    size = PIECE // 2
    moved = [after_all(moved[0], *beside[0]), moved[1]]
    sums = [part(i, bits[i]) + moved[i].astype(F32) for i in range(2)]
    sent = [rows_at(sums[i], (1 - bits[1 - i]) * size, size).astype(BF) for i in range(2)]
    stay = [rows_at(sums[i], bits[1 - i] * size, size) for i in range(2)]
    moved = [lax.ppermute(sent[i], BOTH, first_pairs(PAIRS_OF[1 - i])) for i in range(2)]
    chunks = [(a + b.astype(F32)).astype(BF) for a, b in zip(stay, moved)]
    chunks[0] = after_all(chunks[0], *beside[1])
    size, lanes = chunks[0].shape
    grouped = jnp.stack(chunks).reshape(2, 4, size // 4, lanes)
    total = part_of(grouped, place).astype(F32)
    for d in (2, 1, 3):
        total = total + lax.ppermute(part_of(grouped, place + d), BOTH, second_step(d)).astype(F32)
    whole = total.astype(BF)
    total = whole.astype(F32)
    for d in (2, 1, 3):
        total = total + lax.ppermute(whole, "seq", along_z(d)).astype(F32)
    piece = total.astype(BF)
    parts = [piece] + [lax.ppermute(piece, BOTH, second_step(d)) for d in (1, 2, 3)]
    stack = jnp.stack(parts, axis=1)
    ordered = jnp.stack([part_of(stack, place - p + 4) for p in range(4)], axis=1).reshape(2, size, lanes)
    chunks = pair_gather([ordered[0], ordered[1]], bits[::-1], PAIRS_OF[::-1])
    moved = [lax.ppermute(data, BOTH, first_pairs(pair)) for pair, data in zip(PAIRS_OF, chunks)]
    mine = [chunks[0], moved[0], chunks[1], moved[1]]
    late = [after_all(a, *beside[2]) for a in moved]
    swapped = [lax.ppermute(a, "seq", SWAP) for a in (chunks[0], late[0], chunks[1], late[1])]
    return mine, swapped


def after_all(value, *others):
    return lax.optimization_barrier((value, *others))[0]


def exchange(array):
    return lax.all_to_all(
        array.reshape(16, CAP, 768), "batch", split_axis=0, concat_axis=0, tiled=True
    ).reshape(1024, 768)


def local(
    block_input, token_ids, hash_table, doc_lengths, turn_mask, attn_norm_gain, attn_norm_bias,
    qkv_weight, proj_weight, ffn_norm_gain, ffn_norm_bias, expert_up, expert_down, out_grad,
):
    seq = lax.axis_index("seq")
    owner = lax.axis_index("batch")
    odd = seq % 2
    flat = (512, 768)
    rows3 = (4, 128, 768)
    place = jnp.stack([seq, owner]).astype(I32)
    up, down = expert_up[0], expert_down[0]

    behind_two = lax.ppermute(block_input, "seq", AHEAD_TWO)
    early = lax.ppermute(block_input, "seq", UP_ONE)

    table = jnp.pad(hash_table, (0, 8192 - 8008)).reshape(64, 128)
    target, tally, grad_sent = kernel_call(
        route_kernel,
        [shape((8, 512), I32), shape((16, 128), F32), shape((1024, 768))],
        [place, token_ids, table, turn_mask, out_grad.reshape(flat)],
        "route", 10**9,
        in_specs=[SM] + [VM] * 4,
    )
    grad_rows = exchange(grad_sent)

    unit, query, keyval = kernel_call(
        own_kernel,
        [shape(flat), shape(flat), shape((512, 1536))],
        [block_input.reshape(flat), attn_norm_gain, attn_norm_bias, qkv_weight],
        "own", 18 * 10**8,
    )
    late = lax.ppermute(after_all(behind_two, query, grad_sent), "seq", DOWN_ONE)
    query, keyval = query.reshape(rows3), keyval.reshape(4, 128, 1536)

    unit_halo, context, attended, log_total, after, rows_sent = kernel_call(
        forward_kernel,
        [
            shape((4, 256, 768)), shape((4, 384, 1536)), shape(rows3), shape((4, 8, 256), F32),
            shape(flat, F32), shape((1024, 768)),
        ],
        [
            place, doc_lengths, attn_norm_gain, attn_norm_bias, ffn_norm_gain, ffn_norm_bias, target,
            behind_two, early, late, qkv_weight, keyval, query, block_input, proj_weight,
        ],
        "forward", 10**9,
        in_specs=[SM] * 2 + [VM] * 5 + [HB] * 8,
        out_specs=[HB] * 3 + [VM] + [HB] * 2,
        scratch=[
            pltpu.VMEM(rows3, BF), pltpu.VMEM(rows3, BF), pltpu.VMEM(rows3, BF), pltpu.VMEM((768, 2304), BF),
            pltpu.VMEM(rows3, BF), pltpu.VMEM(rows3, BF), pltpu.VMEM((768, 768), BF),
            pltpu.VMEM((4, 256, 768), BF), pltpu.VMEM((4, 256, 768), BF), pltpu.VMEM((4, 384, 1536), BF),
            pltpu.VMEM(rows3, BF), pltpu.VMEM(flat, F32), pltpu.VMEM((1024, 768), BF),
            pltpu.SemaphoreType.DMA((8,)), pltpu.SemaphoreType.DMA((6,)),
        ],
    )
    rows = exchange(rows_sent)

    turned = kernel_call(
        turn_kernel, [shape((784, 1536))], [unit, unit_halo.reshape(1024, 768)], "turn", 10**6
    )[0]
    tile = pl.BlockSpec((1, 1024, 768), lambda i: (i, 0, 0))
    tiled = shape((4, 1024, 768))
    whole = pl.BlockSpec((1024, 768), lambda i: (0, 0))
    raw = kernel_call(
        active_grad_kernel,
        [tiled],
        [after_all(grad_rows, turned), down],
        "active_grad", 48 * 10**8,
        grid=(4,),
        in_specs=[whole, pl.BlockSpec((768, 768), lambda i: (i, 0))],
        out_specs=[tile],
    )[0]

    active, hidden_grad, back_sent = kernel_call(
        expert_kernel,
        [tiled, tiled, shape((1024, 768))],
        [rows, up, raw],
        "expert", 97 * 10**8,
        grid=(4,),
        in_specs=[whole, pl.BlockSpec((768, 768), lambda i: (0, i)), tile],
        out_specs=[tile, tile, whole],
        scratch=[pltpu.VMEM((1024, 768), F32)],
    )
    back = exchange(back_sent)

    result, parts = kernel_call(
        weight_kernel,
        [shape((1024, 768)), shape((8, 1536, 384))],
        [rows, grad_rows, active, hidden_grad, down],
        "weights", 145 * 10**8,
        grid=(4,),
        in_specs=[
            whole,
            whole,
            tile,
            tile,
            pl.BlockSpec((768, 768), lambda i: (i, 0)),
        ],
        out_specs=[
            pl.BlockSpec((1024, 768), lambda i: (0, 0)),
            pl.BlockSpec((2, 1536, 384), lambda i: (i, 0, 0)),
        ],
        scratch=[pltpu.VMEM((768, 1024), BF), pltpu.VMEM((768, 1024), BF), pltpu.VMEM((1024, 768), F32)],
    )
    returned = exchange(result)
    parts_sum = lax.psum_scatter(after_all(parts, back), "seq", scatter_dimension=0, tiled=True)

    after_grad, query_grad, own_grad, input_two, input_one, keep, away = kernel_call(
        backward_kernel,
        [
            shape(flat, F32), shape(flat), shape((512, 1536)), shape(rows3), shape(rows3),
            shape((HALF_ROWS, 256)), shape((HALF_ROWS, 256)),
        ],
        [
            place, doc_lengths, ffn_norm_gain, attn_norm_gain, attn_norm_bias, target, turn_mask, log_total, tally,
            back, after, out_grad.reshape(flat), proj_weight, attended.reshape(flat), query, context, turned,
            qkv_weight,
        ],
        "backward", 16 * 10**9,
        in_specs=[SM] * 2 + [VM] * 7 + [HB] * 9,
        out_specs=[HB] * 7,
        scratch=[
            pltpu.VMEM((1024, 768), BF), pltpu.VMEM(flat, F32), pltpu.VMEM(flat, BF), pltpu.VMEM((768, 768), BF),
            pltpu.VMEM(flat, BF), pltpu.VMEM(rows3, BF), pltpu.VMEM((4, 384, 1536), BF),
            pltpu.VMEM((784, 1536), BF), pltpu.VMEM((768, 2304), BF), pltpu.VMEM(flat, F32), pltpu.VMEM(rows3, BF),
            pltpu.VMEM(flat, BF), pltpu.VMEM((1536, 1536), BF), pltpu.VMEM((3, 768, 256), BF),
            pltpu.VMEM((4, 256, 768), BF), pltpu.VMEM((2, HALF_ROWS, 256), BF),
            pltpu.VMEM((768, 256), F32), pltpu.VMEM((768, 256), F32), pltpu.VMEM((768, 256), F32),
            pltpu.VMEM((768, 256), F32), pltpu.VMEM((2, 768), F32),
            pltpu.SemaphoreType.DMA((9,)), pltpu.SemaphoreType.DMA((7,)),
        ],
    )
    got = lax.ppermute(after_all(away, returned), "seq", SWAP)
    from_one = lax.ppermute(input_one, "seq", SWAP)
    bits, turn, part, streams = sum_start(keep, after_all(got, from_one))

    passed = jnp.where(odd == 1, input_two + from_one, input_two)
    from_two = lax.ppermute(passed, "seq", BACK_TWO)
    even = (1 - odd).astype(F32).reshape(1)
    input_grad = kernel_call(
        input_grad_kernel,
        [shape(flat, F32)],
        [
            even, attn_norm_gain, query_grad, own_grad, qkv_weight, block_input.reshape(flat),
            from_one.reshape(flat), from_two.reshape(flat), after_grad,
        ],
        "input_grad", 3 * 10**9,
        in_specs=[SM, VM] + [HB] * 7,
        scratch=[
            pltpu.VMEM(flat, BF), pltpu.VMEM((512, 1536), BF), pltpu.VMEM((768, 2304), BF), pltpu.VMEM(flat, BF),
            pltpu.VMEM(flat, BF), pltpu.VMEM(flat, BF), pltpu.VMEM(flat, F32), pltpu.SemaphoreType.DMA((7,)),
        ],
    )[0]
    block_output = kernel_call(
        output_kernel, [shape(flat)], [after, target, returned], "output", 8 * 10**8
    )[0]
    up_sum, down_sum = kernel_call(
        expert_sum_kernel,
        [shape((1, 768, 384), F32), shape((1, 384, 768), F32)],
        [parts_sum], "expert_sum", 10**6,
    )
    mine, swapped = sum_finish(
        bits, turn, part, streams, ([block_output, passed], [from_two, up_sum], [input_grad])
    )
    spots = jnp.stack([odd, owner, *bits, *bits_of(turn), seq]).astype(I32)
    sums = [shape((768, 2304), F32), shape((768, 768), F32)]
    landing = [
        pltpu.VMEM((HALF_ROWS, 256), BF), pltpu.VMEM((2, 768, 768), F32),
        pltpu.SemaphoreType.DMA((4,)), pltpu.SemaphoreType.DMA((2,)),
    ]
    qkv_half, proj_half, tail = kernel_call(
        finish_mine_kernel, sums + [shape((64, 256))], [spots, *mine], "finish_mine", 10**6,
        in_specs=[SM] + [HB] * 4, out_specs=[HB, HB, VM], scratch=landing,
    )
    line = shape((768,), F32)
    qkv_sum, proj_sum, *rest = kernel_call(
        finish_other_kernel,
        sums + [line] * 4 + [shape((16,), I32), shape((1, 1, 16), I32)],
        [spots, tail, *swapped, qkv_half, proj_half],
        "finish_other", 10**6,
        in_specs=[SM, VM] + [HB] * 6, out_specs=[HB] * 2 + [VM] * 6, scratch=landing,
        aliases={6: 0, 7: 1},
    )
    return (
        block_output.reshape(rows3),
        input_grad.reshape(rows3),
        rest[0],
        rest[1],
        qkv_sum,
        proj_sum,
        rest[2],
        rest[3],
        up_sum,
        down_sum,
        rest[4],
        rest[5],
    )


def solution(mesh):
    placed = (
        P("batch", "seq", None),
        P("batch", "seq"),
        P(),
        P("batch", None),
        P("batch", "seq"),
        P(),
        P(),
        P(),
        P(),
        P(),
        P(),
        P("batch", None, None),
        P("batch", None, None),
        P("batch", "seq", None),
    )
    return jax.shard_map(
        local,
        mesh=mesh,
        in_specs=placed,
        out_specs=(
            P("batch", "seq", None),
            P("batch", "seq", None),
            P(),
            P(),
            P(),
            P(),
            P(),
            P(),
            P("batch", None, "seq"),
            P("batch", "seq", None),
            P(),
            P("batch", "seq", None),
        ),
        check_vma=False,
    )
```

```python
import jax
import jax.numpy as jnp
from jax import lax
from jax.experimental import pallas as pl
from jax.experimental.pallas import tpu as pltpu
from jax.sharding import PartitionSpec as P

BF = jnp.bfloat16
F32 = jnp.float32
I32 = jnp.int32
EPS = 1e-05
MASKED = -1e30
HEADS = 12
HEAD_SIZE = 64
PAIRS = 6
CAP = 64
SWAP = [(i, i ^ 1) for i in range(8)]
UP_ONE = [(i, i + 1) for i in range(0, 8, 2)]
DOWN_ONE = [(i + 1, i) for i in range(0, 8, 2)]
AHEAD_TWO = [(i, i + 2) for i in range(6)]
BACK_TWO = [(i + 2, i) for i in range(6)]
HALF_ROWS = 4864
PIECE = HALF_ROWS // 4
VMEM_BYTES = 63 * 1024 * 1024
GEMM_ROWS = 4608
VM = pl.BlockSpec(memory_space=pltpu.VMEM)
HB = pl.BlockSpec(memory_space=pl.ANY)
SM = pl.BlockSpec(memory_space=pltpu.SMEM)


def shape(dims, kind=BF):
    return jax.ShapeDtypeStruct(dims, kind)


def kernel_call(body, outs, args, name, flops, grid=None, in_specs=None, out_specs=None, scratch=(), aliases=None):
    moved = sum(a.size * a.dtype.itemsize for a in args) + sum(
        o.size * o.dtype.itemsize for o in outs
    )
    extra = {} if grid is None else {"grid": grid}
    return pl.pallas_call(
        body,
        out_shape=outs,
        in_specs=in_specs or [VM] * len(args),
        out_specs=out_specs or [VM] * len(outs),
        scratch_shapes=list(scratch),
        compiler_params=pltpu.CompilerParams(vmem_limit_bytes=VMEM_BYTES),
        cost_estimate=pl.CostEstimate(flops=flops, bytes_accessed=moved, transcendentals=0),
        name=name,
        input_output_aliases=aliases or {},
        **extra,
    )(*args)


def nn(a, b):
    return jnp.dot(a, b, preferred_element_type=F32)


def nt(a, b):
    return lax.dot_general(a, b, (((1,), (1,)), ((), ())), preferred_element_type=F32)


def tn(a, b):
    return lax.dot_general(a, b, (((0,), (0,)), ((), ())), preferred_element_type=F32)


def iota(dims, axis):
    return lax.broadcasted_iota(I32, dims, axis)


def row(ref):
    return ref[...].reshape(1, 768)


def column(line):
    return jnp.broadcast_to(line, (128, line.shape[1])).T[:, 0:1]


def flat_line(ref):
    return jnp.concatenate([ref[i : i + 1, :] for i in range(4)], axis=1).astype(F32)


def norm_parts(values):
    centred = values - jnp.mean(values, axis=-1, keepdims=True)
    inverse = lax.rsqrt(jnp.mean(centred * centred, axis=-1, keepdims=True) + EPS)
    return centred * inverse, inverse


def norm_back(grad, gain, unit, inverse):
    t = grad * gain
    return inverse * (
        t - jnp.mean(t, axis=-1, keepdims=True) - unit * jnp.mean(t * unit, axis=-1, keepdims=True)
    )


def entry_kernel(
    place, tok, table, turn, gain, bias, x, grad, weight, target_out, tally, sent, unit_out, query, keyval,
    xv, gv, w, sv, uv, rv, kv, in_sems, out_sems,
):
    loads = copies([x, grad, weight], [xv, gv, w], in_sems)
    ids = jnp.concatenate([tok[i : i + 1, :] for i in range(4)], axis=1)
    live = flat_line(turn)
    high, low = ids >> 7, ids & 127
    picked = tn(table[...].astype(F32).astype(BF), (iota((64, 512), 0) == high).astype(F32).astype(BF))
    chosen = jnp.sum(jnp.where(iota((128, 512), 0) == low, picked, 0.0), axis=0, keepdims=True)
    member = (iota((16, 512), 0) == chosen.astype(I32)).astype(F32)
    earlier = (iota((512, 512), 0) < iota((512, 512), 1)).astype(F32).astype(BF)
    before = nn(member.astype(BF), earlier)
    slot = jnp.sum(before * member, axis=0, keepdims=True)
    target = (chosen * CAP + slot).astype(I32)
    target_out[...] = jnp.broadcast_to(target, (8, 512))
    counts = jnp.sum(member, axis=1, keepdims=True)
    tally[...] = jnp.where(iota((16, 128), 1) == place[0] * 16 + place[1], counts, 0.0)
    stores = []

    def store(source, goal):
        stores.append(pltpu.make_async_copy(source, goal, out_sems.at[len(stores)]))
        stores[-1].start()

    loads[0].wait()
    unit, _ = norm_parts(xv[...].astype(F32))
    uv[...] = unit.astype(BF)
    store(uv, unit_out)
    rows = (unit * row(gain) + row(bias)).astype(BF)
    loads[1].wait()
    for i in range(2):
        placing = jnp.where(iota((512, 512), 0) + 512 * i == target, live, 0.0).astype(BF)
        sv[512 * i : 512 * (i + 1), :] = nn(placing, gv[...]).astype(BF)
    store(sv, sent)
    loads[2].wait()
    rv[...] = rows

    def block(j, carry):
        kv[j] = nn(rv[...], w[:, cols_at(j, 768)]).astype(BF)
        return carry

    lax.fori_loop(0, 3, block, 0)
    store(kv.at[0], query)
    store(kv.at[1], keyval.at[:, 0:768])
    store(kv.at[2], keyval.at[:, 768:1536])
    for copy in stores:
        copy.wait()


def head_masks(scale):
    lane = iota((1, 128), 1)
    first = jnp.where(lane < 64, scale, 0.0).astype(BF)
    second = jnp.where(lane >= 64, scale, 0.0).astype(BF)
    return first, second


def stack_heads(pair, masks):
    return jnp.concatenate([pair * masks[0], pair * masks[1]], axis=0)


def window_bias(place, lengths, r):
    lane = iota((1, 128), 1) + place[0] * 128
    end, start = jnp.int32(0), jnp.zeros((1, 128), I32)
    for j in range(8):
        end = end + lengths[r, j]
        start = jnp.where(end <= lane, end, start)
    start = start - (place[0] - 2) * 128
    key = iota((384, 128), 0)
    allowed = (key >= start) & (key <= iota((384, 128), 1) + 256)
    half = jnp.where(allowed, 0.0, MASKED)
    return jnp.concatenate([half, half], axis=1)


def join_heads(both):
    one = jnp.where(iota((128, 128), 0) < 64, both[:, :128], both[:, 128:])
    return one.T


def copies(sources, targets, sems):
    out = [
        pltpu.make_async_copy(a, b, sems.at[i]) for i, (a, b) in enumerate(zip(sources, targets))
    ]
    for copy in out:
        copy.start()
    return out


def lanes_of(p, offset=0):
    return slice(offset + 128 * p, offset + 128 * (p + 1))


def forward_kernel(
    place, lengths, gain, bias, gain_two, bias_two, target,
    behind_two, early, late, weight, keyval, query, x, proj,
    unit_halo, context_out, attended, log_out, after_out, sent,
    b2, e1, l1, w, q, xv, wp, units, rows_in, context, att, aft, snd, in_sems, out_sems,
):
    loads = copies(
        [behind_two, early, late, weight, keyval, query, x, proj],
        [b2, e1, l1, w, context.at[:, 256:384, :], q, xv, wp],
        in_sems,
    )
    scales = head_masks(HEAD_SIZE ** (-0.5))
    for copy in loads[:3]:
        copy.wait()

    def norm_row(r, carry):
        halo = jnp.concatenate([b2[r], e1[r] + l1[r]], axis=0).astype(F32)
        unit, _ = norm_parts(halo)
        units[r] = unit.astype(BF)
        rows_in[r] = (unit * row(gain) + row(bias)).astype(BF)
        return carry

    lax.fori_loop(0, 4, norm_row, 0)
    unit_copy = pltpu.make_async_copy(units, unit_halo, out_sems.at[0])
    unit_copy.start()
    loads[3].wait()

    def keyval_block(j, carry):
        source = pl.ds(pl.multiple_of(768 + 512 * j, 256), 512)
        fresh = nn(rows_in[...].reshape(1024, 768), w[:, source])
        context[:, 0:256, cols_at(j, 512)] = fresh.astype(BF).reshape(4, 256, 512)
        return carry

    lax.fori_loop(0, 3, keyval_block, 0)
    for copy in loads[4:6]:
        copy.wait()
    context_copy = pltpu.make_async_copy(context, context_out, out_sems.at[1])
    context_copy.start()

    def one_row(r, carry):
        mask = window_bias(place, lengths, r)
        pairs = range(PAIRS)
        stacked = [stack_heads(q[r, :, lanes_of(p)], scales) for p in pairs]
        scores = [nt(context[r, :, lanes_of(p)], stacked[p]) + mask for p in pairs]
        tops = [jnp.max(a, axis=0, keepdims=True) for a in scores]
        weights = [jnp.exp(a - t) for a, t in zip(scores, tops)]
        totals = [jnp.sum(a, axis=0, keepdims=True) for a in weights]
        shares = [(a * (1.0 / t)).astype(BF) for a, t in zip(weights, totals)]
        mixed = [tn(context[r, :, lanes_of(p, 768)], shares[p]) for p in pairs]
        for p in pairs:
            log_out[r, p : p + 1, :] = tops[p] + jnp.log(totals[p])
            att[r, :, lanes_of(p)] = join_heads(mixed[p]).astype(BF)
        return carry

    lax.fori_loop(0, 4, one_row, 0)
    att_copy = pltpu.make_async_copy(att, attended, out_sems.at[2])
    att_copy.start()
    loads[6].wait()
    loads[7].wait()
    after = xv[...].reshape(512, 768).astype(F32) + nn(att[...].reshape(512, 768), wp[...])
    aft[...] = after
    after_copy = pltpu.make_async_copy(aft, after_out, out_sems.at[3])
    after_copy.start()
    unit, _ = norm_parts(after)
    rows = (unit * row(gain_two) + row(bias_two)).astype(BF)
    sends = []
    for i in range(2):
        part = slice(512 * i, 512 * (i + 1))
        placing = (iota((512, 512), 0) + 512 * i == target[0:1, :]).astype(F32).astype(BF)
        snd[part, :] = nn(placing, rows).astype(BF)
        sends.append(pltpu.make_async_copy(snd.at[part], sent.at[part], out_sems.at[4 + i]))
        sends[-1].start()
    for copy in [unit_copy, context_copy, att_copy, after_copy] + sends:
        copy.wait()


def active_grad_kernel(grad, down, out):
    out[0] = nt(grad[...], down[...]).astype(BF)


def gelu_both(v):
    c = 0.7978845608028654
    square = v * v
    p = c + (c * 0.044715) * square
    gate = 0.5 + 0.5 * jnp.tanh(v * p)
    value = v * gate
    return value, gate + value * (1.0 - gate) * (6.0 * p - 4.0 * c)


def expert_kernel(x, up, raw, active, hidden_grad, back, total):
    step = pl.program_id(0)

    @pl.when(step == 0)
    def _():
        total[...] = jnp.zeros_like(total)

    parts = [slice(256 * r, 256 * (r + 1)) for r in range(4)]
    hidden = [nn(x[rows, :], up[...]) for rows in parts]
    lows = []
    for rows, v in zip(parts, hidden):
        value, slope = gelu_both(v)
        active[0, rows, :] = value.astype(BF)
        low = (raw[0, rows, :].astype(F32) * slope).astype(BF)
        hidden_grad[0, rows, :] = low
        lows.append(low)
    for rows, low in zip(parts, lows):
        total[rows, :] += nt(low, up[...])

    @pl.when(step == pl.num_programs(0) - 1)
    def _():
        back[...] = total[...].astype(BF)


def turn_kernel(unit, unit_halo, out):
    out[0:768, 0:512] = unit[...].T
    out[0:768, 512:1536] = unit_halo[...].T
    out[768:784, :] = jnp.ones((16, 1536), BF)


def weight_kernel(place, x, grad, active, hidden_grad, down, out, mine, away, x_t, grad_t, total):
    step = pl.program_id(0)

    @pl.when(step == 0)
    def _():
        total[...] = jnp.zeros_like(total)
        x_t[...] = x[...].T
        grad_t[...] = grad[...].T

    total[...] += nn(active[0], down[...])
    one = nn(x_t[...], hidden_grad[0])
    two = nn(grad_t[...], active[0])
    even = place[0] % 2 == 0
    for i, both in enumerate([one, two]):
        mine[0, i] = jnp.where(even, both[:, :384], both[:, 384:]).astype(BF)
        away[0, i] = jnp.where(even, both[:, 384:], both[:, :384]).astype(BF)

    @pl.when(step == pl.num_programs(0) - 1)
    def _():
        out[...] = total[...].astype(BF)


def output_kernel(after, target, returned, out):
    placing = (iota((512, 1024), 1).astype(F32) == column(target[0:1, :].astype(F32))).astype(F32).astype(BF)
    out[...] = (after[...] + nn(placing, returned[...])).astype(BF)


def cols_at(j, size=256):
    return pl.ds(pl.multiple_of(size * j, size), size)


def fill_halves(
    turned, query_grad, context_grad, weight, gain, bias, proj_part, terms_two, tally,
    out, gain_wide, bias_wide, gain_sum, bias_sum,
):
    gain_wide[...] = jnp.broadcast_to(row(gain), (256, 768)).T
    bias_wide[...] = jnp.broadcast_to(row(bias), (256, 768)).T

    def finish(block, both):
        body, sums = both[0:768], both[768:769]
        half, step = block // 6, block % 6
        out[half, 768 * step : 768 * (step + 1), :] = (
            gain_wide[...] * body + bias_wide[...] * sums
        ).astype(BF)
        wide = weight[:, 256 * block : 256 * (block + 1)].astype(F32)
        if block == 0:
            gain_sum[...] = wide * body
            bias_sum[...] = wide * sums
        else:
            gain_sum[...] += wide * body
            bias_sum[...] += wide * sums

    for j in range(3):
        finish(j, nn(turned[:, 0:512], query_grad[:, 256 * j : 256 * (j + 1)]))
        out[1, 768 * (3 + j) : 768 * (4 + j), :] = proj_part[j]
    for j in range(6):
        finish(3 + j, nn(turned[...], context_grad[:, 256 * j : 256 * (j + 1)]))

    columns = jnp.concatenate(
        [
            jnp.broadcast_to(jnp.sum(gain_sum[...], axis=1, keepdims=True), (768, 128)),
            jnp.broadcast_to(jnp.sum(bias_sum[...], axis=1, keepdims=True), (768, 128)),
        ],
        axis=1,
    ).T
    out[:, GEMM_ROWS:, :] = jnp.zeros((2, HALF_ROWS - GEMM_ROWS, 256), BF)
    for t in range(3):
        lanes = slice(256 * t, 256 * (t + 1))
        block = jnp.concatenate(
            [columns[0:1, lanes], columns[128:129, lanes], terms_two[:, lanes], jnp.zeros((12, 256), F32)],
            axis=0,
        )
        out[0, GEMM_ROWS + 16 * t : GEMM_ROWS + 16 * t + 16, :] = block.astype(BF)
    out[0, GEMM_ROWS + 48 : GEMM_ROWS + 64, 0:128] = tally[...].astype(BF)


def backward_kernel(
    place, lengths, gain_two, gain, bias, target, turn, log_total, tally,
    back, after, grad, proj, attended, query, context, turned, weight,
    after_grad, query_grad, own_grad, input_two, input_one, keep, away,
    bk, af, gr, wp, att, q, ctx, tu, w, ag, do, dq, cg, pp, ip, out,
    gain_wide, bias_wide, gain_sum, bias_sum, terms, in_sems, out_sems,
):
    loads = copies(
        [back, after, grad, proj, attended, query, context, turned, weight],
        [bk, af, gr, wp, att, q, ctx, tu, w],
        in_sems,
    )
    scales = head_masks(HEAD_SIZE ** (-0.5))
    ones = head_masks(1.0)
    placing = (iota((512, 1024), 1).astype(F32) == column(target[0:1, :].astype(F32))).astype(F32).astype(BF)
    live = column(flat_line(turn))
    loads[0].wait()
    normed_grad = nn(placing, bk[...])
    loads[1].wait()
    unit, inverse = norm_parts(af[...])
    terms[0:1, :] = jnp.sum(normed_grad * unit, axis=0, keepdims=True)
    terms[1:2, :] = jnp.sum(normed_grad, axis=0, keepdims=True)
    loads[2].wait()
    total = gr[...].astype(F32) * live + norm_back(normed_grad, row(gain_two), unit, inverse)
    ag[...] = total
    stores = [pltpu.make_async_copy(ag, after_grad, out_sems.at[0])]
    stores[0].start()
    low = total.astype(BF)
    loads[3].wait()
    do[...] = nt(low, wp[...]).astype(BF).reshape(4, 128, 768)
    loads[4].wait()
    mixed = nn(att[...].T, low).astype(BF)
    for j in range(3):
        pp[j] = mixed[:, 256 * j : 256 * (j + 1)]
    loads[5].wait()
    loads[6].wait()

    def one_row(r, carry):
        mask = window_bias(place, lengths, r)
        pairs = range(PAIRS)
        stacked = [stack_heads(q[r, :, lanes_of(p)], scales) for p in pairs]
        grads = [stack_heads(do[r, :, lanes_of(p)], ones) for p in pairs]
        scores = [nt(ctx[r, :, lanes_of(p)], stacked[p]) for p in pairs]
        share_grads = [nt(ctx[r, :, lanes_of(p, 768)], grads[p]) for p in pairs]
        shares = [jnp.exp(scores[p] + mask - log_total[r, p : p + 1, :]) for p in pairs]
        sums = [jnp.sum(a * b, axis=0, keepdims=True) for a, b in zip(shares, share_grads)]
        score_grads = [(a * (b - c)).astype(BF) for a, b, c in zip(shares, share_grads, sums)]
        key_grads = [nn(score_grads[p], stacked[p]).astype(BF) for p in pairs]
        value_grads = [nn(shares[p].astype(BF), grads[p]).astype(BF) for p in pairs]
        turned_grads = [tn(ctx[r, :, lanes_of(p)], score_grads[p]) for p in pairs]
        halo = pl.ds(pl.multiple_of(512 + r * 256, 256), 256)
        own = pl.ds(pl.multiple_of(r * 128, 128), 128)
        for p in pairs:
            cg[halo, lanes_of(p)] = key_grads[p][:256]
            cg[own, lanes_of(p)] = key_grads[p][256:]
            cg[halo, lanes_of(p, 768)] = value_grads[p][:256]
            cg[own, lanes_of(p, 768)] = value_grads[p][256:]
            dq[own, lanes_of(p)] = (join_heads(turned_grads[p]) * HEAD_SIZE ** (-0.5)).astype(BF)
        return carry

    lax.fori_loop(0, 4, one_row, 0)
    loads[7].wait()
    loads[8].wait()

    def store(source, target):
        stores.append(pltpu.make_async_copy(source, target, out_sems.at[len(stores)]))
        stores[-1].start()

    store(dq, query_grad)
    store(cg.at[0:512], own_grad)
    ip[...] = nt(cg[512:1536, :], w[:, 768:]).astype(BF).reshape(4, 256, 768)
    store(ip.at[:, 0:128], input_two)
    store(ip.at[:, 128:256], input_one)
    fill_halves(
        tu, dq, cg, w, gain, bias, pp, terms, tally, out, gain_wide, bias_wide, gain_sum, bias_sum
    )
    core = place[0] % 2

    @pl.when(core == 0)
    def _():
        pltpu.make_async_copy(out.at[0], keep, out_sems.at[5]).start()
        pltpu.make_async_copy(out.at[1], away, out_sems.at[6]).start()

    @pl.when(core == 1)
    def _():
        pltpu.make_async_copy(out.at[1], keep, out_sems.at[5]).start()
        pltpu.make_async_copy(out.at[0], away, out_sems.at[6]).start()

    for copy in stores:
        copy.wait()
    pltpu.make_async_copy(out.at[0], keep, out_sems.at[5]).wait()
    pltpu.make_async_copy(out.at[1], away, out_sems.at[6]).wait()


def place_half(half, bits, pieces, qkv, proj, whole, stage, in_sems, sems):
    loads = []
    for i in range(2):
        for j in range(2):
            first = pl.multiple_of((2 * i + (bits[i] + j) % 2) * PIECE, PIECE)
            target = whole.at[pl.ds(first, PIECE)]
            loads.append(pltpu.make_async_copy(pieces[2 * i + j], target, in_sems.at[2 * i + j]))
            loads[-1].start()
    for copy in loads:
        copy.wait()
    for j in range(6):
        stage[j] = whole[768 * j : 768 * (j + 1), :].astype(F32)
        lanes = slice(256 * (j % 3), 256 * (j % 3 + 1))

        @pl.when(half == 0)
        def _():
            pltpu.make_async_copy(stage.at[j], qkv.at[:, 256 * j : 256 * (j + 1)], sems.at[j]).start()

        @pl.when(half == 1)
        def _():
            target = qkv.at[:, 1536 + 256 * j : 1792 + 256 * j] if j < 3 else proj.at[:, lanes]
            pltpu.make_async_copy(stage.at[j], target, sems.at[j]).start()

    for j in range(6):
        pltpu.make_async_copy(stage.at[j], proj.at[:, 0:256], sems.at[j]).wait()


def finish_mine_kernel(place, a, b, c, d, qkv, proj, tail, whole, stage, in_sems, sems):
    place_half(place[0], (place[2], place[3]), (a, b, c, d), qkv, proj, whole, stage, in_sems, sems)
    tail[...] = whole[GEMM_ROWS : GEMM_ROWS + 64, :]


def finish_other_kernel(
    place, tail, a, b, c, d, qkv_in, proj_in, qkv, proj, gain_one, bias_one, gain_two, bias_two, counts, received,
    whole, stage, in_sems, sems,
):
    place_half(1 - place[0], (place[4], place[5]), (a, b, c, d), qkv, proj, whole, stage, in_sems, sems)
    both = tail[...].astype(F32) + whole[GEMM_ROWS : GEMM_ROWS + 64, :].astype(F32)
    for i, out in enumerate([gain_one, bias_one, gain_two, bias_two]):
        line = jnp.concatenate([both[16 * t + i : 16 * t + i + 1, :] for t in range(3)], axis=1)
        out[...] = line.reshape(768)
    every = both[48:64, 0:128]
    counts[...] = nt(jnp.ones((8, 128), BF), every.astype(BF))[0:1, :].astype(I32).reshape(16)
    chosen = (iota((16, 128), 0) == place[1]) & ((iota((16, 128), 1) >> 4) == place[6])
    mine = jnp.where(chosen, every, 0.0).astype(BF)
    fold = ((iota((128, 16), 0) & 15) == iota((128, 16), 1)).astype(F32).astype(BF)
    received[0] = jnp.sum(nn(mine, fold), axis=0, keepdims=True).astype(I32)


def chunk_of(a, b):
    return 2 * b + (a + b) % 2


def add_chunks(plan, buffer, in_sems):
    loads = []
    for n, picks in enumerate(plan):
        for m, pick_ref in enumerate(picks):
            loads.append(pltpu.make_async_copy(pick_ref, buffer.at[n, m], in_sems.at[n, m]))
            loads[-1].start()
    return loads


def summed(buffer, n, count):
    total = buffer[n, 0].astype(F32)
    for m in range(1, count):
        total = total + buffer[n, m].astype(F32)
    return total


def expert_first_kernel(spots, own, got, one, two, buffer, made, in_sems, out_sems):
    a, b = spots[7], spots[8]
    wanted = [(chunk_of(1 - a, k), 0) for k in range(2)] + [(chunk_of(k, 1 - b), 1) for k in range(2)]
    plan = [[own.at[c, t], got.at[c, t]] for c, t in wanted]
    loads = add_chunks(plan, buffer, in_sems)
    stores = []
    for n in range(4):
        loads[2 * n].wait()
        loads[2 * n + 1].wait()
        made[n] = summed(buffer, n, 2).astype(BF)
        stores.append(pltpu.make_async_copy(made.at[n], (one, two)[n // 2].at[n % 2], out_sems.at[n]))
        stores[-1].start()
    for copy in stores:
        copy.wait()


def expert_second_kernel(spots, own, got, first, second, one, two, buffer, made, in_sems, out_sems):
    a, b = spots[7], spots[8]
    c, d = chunk_of(a, 1 - b), chunk_of(1 - a, b)
    plan = [
        [own.at[c, 0], got.at[c, 0], first.at[1 - b]],
        [own.at[d, 1], got.at[d, 1], second.at[1 - a]],
    ]
    loads = add_chunks(plan, buffer, in_sems)
    stores = []
    for n in range(2):
        for copy in loads[3 * n : 3 * n + 3]:
            copy.wait()
        made[n] = summed(buffer, n, 3).astype(BF)
        stores.append(pltpu.make_async_copy(made.at[n], (one, two)[n], out_sems.at[n]))
        stores[-1].start()
    for copy in stores:
        copy.wait()


def expert_last_kernel(spots, own, got, first, second, third, fourth, up, down, buffer, in_sems):
    a, b = spots[7], spots[8]
    c = chunk_of(a, b)
    plan = [
        [own.at[c, 0], got.at[c, 0], first.at[b], third],
        [own.at[c, 1], got.at[c, 1], second.at[a], fourth],
    ]
    loads = add_chunks(plan, buffer, in_sems)
    for copy in loads[:4]:
        copy.wait()
    up[0] = summed(buffer, 0, 4)
    for copy in loads[4:]:
        copy.wait()
    down[0] = summed(buffer, 1, 4).T


def input_grad_kernel(
    even, gain, query_grad, own_grad, weight, x, from_one, two_a, two_b, after_grad, out,
    dq, og, w, xv, one, two, ag, sums, in_sems,
):
    loads = copies(
        [weight, query_grad, own_grad, x, from_one, two_a, two_b, after_grad],
        [w, dq, og, xv, one, two.at[0:256], two.at[256:512], ag],
        in_sems,
    )
    for copy in loads[:3]:
        copy.wait()

    def part(r, carry):
        rows = pl.ds(pl.multiple_of(256 * r, 256), 256)
        sums[rows, :] = nt(dq[rows, :], w[:, :768]) + nt(og[rows, :], w[:, 768:])
        return carry

    lax.fori_loop(0, 2, part, 0)
    for copy in loads[3:]:
        copy.wait()
    unit, inverse = norm_parts(xv[...].astype(F32))
    total = sums[...] + two[...].astype(F32) + even[0] * one[...].astype(F32)
    out[...] = ag[...] + norm_back(total, row(gain), unit, inverse)


PAIR_ONE = [b ^ 1 for b in range(4)]
PAIR_TWO = [b ^ 3 for b in range(4)]
PAIRS_OF = [PAIR_ONE, PAIR_TWO]
BOTH = ("batch", "seq")


def by_core(even_move, odd_move):
    pairs = []
    for b in range(16):
        for s in range(8):
            x, y = (even_move, odd_move)[s % 2](b & 3, b >> 2)
            pairs.append((b * 8 + s, (y * 4 + x) * 8 + s))
    return pairs


def first_pairs(pair):
    return by_core(lambda x, y: (pair[x], y), lambda x, y: (x, pair[y]))


def second_step(d):
    return by_core(lambda x, y: (x, (y + d) & 3), lambda x, y: ((x + d) & 3, y))


def along_z(d):
    return [(s, (s + 2 * d) & 7) for s in range(8)]


def pick(array, index):
    return lax.dynamic_index_in_dim(array, index, 0, keepdims=False)


def part_of(array, index):
    return lax.dynamic_index_in_dim(array, index % 4, 1, keepdims=False)


def bits_of(place):
    return [(place & 1) ^ (place >> 1), place >> 1]


def z_pairs(pair):
    return [(s, pair[s // 2] * 2 + s % 2) for s in range(8)]


def sum_start(bits, keep, got):
    def part(stream, bit):
        at = (stream * 2 + bit) * PIECE
        return rows_at(keep, at, PIECE).astype(F32) + rows_at(got, at, PIECE).astype(F32)

    return part, [part(i, 1 - bits[i]).astype(BF) for i in range(2)]


def pair_moves(data, pairs):
    return [lax.ppermute(a, BOTH, first_pairs(pair)) for a, pair in zip(data, pairs)]


def rows_at(array, at, size):
    return lax.dynamic_slice(array, (at, 0), (size, array.shape[1]))


def sum_middle(bits, part, moved):
    size = PIECE // 2
    sums = [part(i, bits[i]) + moved[i].astype(F32) for i in range(2)]
    sent = [rows_at(sums[i], (1 - bits[1 - i]) * size, size).astype(BF) for i in range(2)]
    return [rows_at(sums[i], bits[1 - i] * size, size) for i in range(2)], sent


def group(chunks):
    size, lanes = chunks[0].shape
    return jnp.stack(chunks).reshape(2, 4, size // 4, lanes)


def sum_across(place, grouped):
    total = part_of(grouped, place).astype(F32)
    for d in (2, 1, 3):
        total = total + lax.ppermute(part_of(grouped, place + d), BOTH, second_step(d)).astype(F32)
    return total.astype(BF)


def sum_along(whole):
    total = whole.astype(F32)
    for d in (2, 1, 3):
        total = total + lax.ppermute(whole, "seq", along_z(d)).astype(F32)
    return total.astype(BF)


def gather_across(place, piece):
    size, lanes = PIECE // 2, piece.shape[-1]
    parts = [piece] + [lax.ppermute(piece, BOTH, second_step(d)) for d in (1, 2, 3)]
    stack = jnp.stack(parts, axis=1)
    ordered = jnp.stack([part_of(stack, place - p + 4) for p in range(4)], axis=1).reshape(2, size, lanes)
    return [ordered[0], ordered[1]]


def gather_pairs(bits, ordered):
    moved = pair_moves(ordered, PAIRS_OF[::-1])
    return [
        jnp.where(bit == 0, jnp.stack([a, b]), jnp.stack([b, a])).reshape(PIECE, a.shape[1])
        for bit, a, b in zip(bits[::-1], ordered, moved)
    ]


def hold(*values):
    return lax.optimization_barrier(values)


def exchange(array):
    return lax.all_to_all(
        array.reshape(16, CAP, 768), "batch", split_axis=0, concat_axis=0, tiled=True
    ).reshape(1024, 768)


def local(
    block_input, token_ids, hash_table, doc_lengths, turn_mask, attn_norm_gain, attn_norm_bias,
    qkv_weight, proj_weight, ffn_norm_gain, ffn_norm_bias, expert_up, expert_down, out_grad,
):
    seq = lax.axis_index("seq")
    owner = lax.axis_index("batch")
    odd = seq % 2
    flat = (512, 768)
    rows3 = (4, 128, 768)
    place = jnp.stack([seq, owner]).astype(I32)
    up, down = expert_up[0], expert_down[0]

    behind_two = lax.ppermute(block_input, "seq", AHEAD_TWO)
    early = lax.ppermute(block_input, "seq", UP_ONE)

    table = jnp.pad(hash_table, (0, 8192 - 8008)).reshape(64, 128)
    target, tally, grad_sent, unit, query, keyval = kernel_call(
        entry_kernel,
        [
            shape((8, 512), I32), shape((16, 128), F32), shape((1024, 768)), shape(flat), shape(flat),
            shape((512, 1536)),
        ],
        [
            place, token_ids, table, turn_mask, attn_norm_gain, attn_norm_bias, block_input.reshape(flat),
            out_grad.reshape(flat), qkv_weight,
        ],
        "entry", 3 * 10**9,
        in_specs=[SM] + [VM] * 5 + [HB] * 3,
        out_specs=[VM] * 2 + [HB] * 4,
        scratch=[
            pltpu.VMEM(flat, BF), pltpu.VMEM(flat, BF), pltpu.VMEM((768, 2304), BF), pltpu.VMEM((1024, 768), BF),
            pltpu.VMEM(flat, BF), pltpu.VMEM(flat, BF), pltpu.VMEM((3, 512, 768), BF),
            pltpu.SemaphoreType.DMA((3,)), pltpu.SemaphoreType.DMA((5,)),
        ],
    )
    grad_rows = exchange(grad_sent)

    behind_two, query = hold(behind_two, query)
    late = lax.ppermute(behind_two, "seq", DOWN_ONE)
    query, keyval = query.reshape(rows3), keyval.reshape(4, 128, 1536)

    unit_halo, context, attended, log_total, after, rows_sent = kernel_call(
        forward_kernel,
        [
            shape((4, 256, 768)), shape((4, 384, 1536)), shape(rows3), shape((4, 8, 256), F32),
            shape(flat, F32), shape((1024, 768)),
        ],
        [
            place, doc_lengths, attn_norm_gain, attn_norm_bias, ffn_norm_gain, ffn_norm_bias, target,
            behind_two, early, late, qkv_weight, keyval, query, block_input, proj_weight,
        ],
        "forward", 10**9,
        in_specs=[SM] * 2 + [VM] * 5 + [HB] * 8,
        out_specs=[HB] * 3 + [VM] + [HB] * 2,
        scratch=[
            pltpu.VMEM(rows3, BF), pltpu.VMEM(rows3, BF), pltpu.VMEM(rows3, BF), pltpu.VMEM((768, 2304), BF),
            pltpu.VMEM(rows3, BF), pltpu.VMEM(rows3, BF), pltpu.VMEM((768, 768), BF),
            pltpu.VMEM((4, 256, 768), BF), pltpu.VMEM((4, 256, 768), BF), pltpu.VMEM((4, 384, 1536), BF),
            pltpu.VMEM(rows3, BF), pltpu.VMEM(flat, F32), pltpu.VMEM((1024, 768), BF),
            pltpu.SemaphoreType.DMA((8,)), pltpu.SemaphoreType.DMA((6,)),
        ],
    )
    rows = exchange(rows_sent)

    turned = kernel_call(
        turn_kernel, [shape((784, 1536))], [unit, unit_halo.reshape(1024, 768)], "turn", 10**6
    )[0]
    grad_rows, turned = hold(grad_rows, turned)
    tile = pl.BlockSpec((1, 1024, 768), lambda i: (i, 0, 0))
    tiled = shape((4, 1024, 768))
    whole = pl.BlockSpec((1024, 768), lambda i: (0, 0))
    raw = kernel_call(
        active_grad_kernel,
        [tiled],
        [grad_rows, down],
        "active_grad", 48 * 10**8,
        grid=(4,),
        in_specs=[whole, pl.BlockSpec((768, 768), lambda i: (i, 0))],
        out_specs=[tile],
    )[0]

    active, hidden_grad, back_sent = kernel_call(
        expert_kernel,
        [tiled, tiled, shape((1024, 768))],
        [rows, up, raw],
        "expert", 97 * 10**8,
        grid=(4,),
        in_specs=[whole, pl.BlockSpec((768, 768), lambda i: (0, i)), tile],
        out_specs=[tile, tile, whole],
        scratch=[pltpu.VMEM((1024, 768), F32)],
    )
    back = exchange(back_sent)

    result, parts, parts_away = kernel_call(
        weight_kernel,
        [shape((1024, 768)), shape((4, 2, 768, 384)), shape((4, 2, 768, 384))],
        [place, rows, grad_rows, active, hidden_grad, down],
        "weights", 145 * 10**8,
        grid=(4,),
        in_specs=[
            SM,
            whole,
            whole,
            tile,
            tile,
            pl.BlockSpec((768, 768), lambda i: (i, 0)),
        ],
        out_specs=[
            pl.BlockSpec((1024, 768), lambda i: (0, 0)),
            pl.BlockSpec((1, 2, 768, 384), lambda i: (i, 0, 0, 0)),
            pl.BlockSpec((1, 2, 768, 384), lambda i: (i, 0, 0, 0)),
        ],
        scratch=[pltpu.VMEM((768, 1024), BF), pltpu.VMEM((768, 1024), BF), pltpu.VMEM((1024, 768), F32)],
    )
    returned = exchange(result)
    parts_away, back = hold(parts_away, back)
    parts_got = lax.ppermute(parts_away, "seq", SWAP)
    depth = seq // 2
    turn = jnp.where(odd == 0, owner // 4, owner % 4)
    bits = bits_of(jnp.where(odd == 0, owner % 4, owner // 4))
    spots = jnp.stack([odd, owner, *bits, *bits_of(turn), seq, *bits_of(depth)]).astype(I32)
    block = shape((768, 384))
    first_sent = kernel_call(
        expert_first_kernel, [shape((2, 768, 384))] * 2, [spots, parts, parts_got], "expert_first", 10**6,
        in_specs=[SM] + [HB] * 2, out_specs=[HB] * 2,
        scratch=[
            pltpu.VMEM((4, 2, 768, 384), BF), pltpu.VMEM((4, 768, 384), BF),
            pltpu.SemaphoreType.DMA((4, 2)), pltpu.SemaphoreType.DMA((4,)),
        ],
    )
    back, *first_sent = hold(back, *first_sent)
    routes = [z_pairs(pair) for pair in PAIRS_OF]
    first_got = [lax.ppermute(a, "seq", route) for a, route in zip(first_sent, routes)]

    after_grad, query_grad, own_grad, input_two, input_one, keep, away = kernel_call(
        backward_kernel,
        [
            shape(flat, F32), shape(flat), shape((512, 1536)), shape(rows3), shape(rows3),
            shape((HALF_ROWS, 256)), shape((HALF_ROWS, 256)),
        ],
        [
            place, doc_lengths, ffn_norm_gain, attn_norm_gain, attn_norm_bias, target, turn_mask, log_total, tally,
            back, after, out_grad.reshape(flat), proj_weight, attended.reshape(flat), query, context, turned,
            qkv_weight,
        ],
        "backward", 16 * 10**9,
        in_specs=[SM] * 2 + [VM] * 7 + [HB] * 9,
        out_specs=[HB] * 7,
        scratch=[
            pltpu.VMEM((1024, 768), BF), pltpu.VMEM(flat, F32), pltpu.VMEM(flat, BF), pltpu.VMEM((768, 768), BF),
            pltpu.VMEM(flat, BF), pltpu.VMEM(rows3, BF), pltpu.VMEM((4, 384, 1536), BF),
            pltpu.VMEM((784, 1536), BF), pltpu.VMEM((768, 2304), BF), pltpu.VMEM(flat, F32), pltpu.VMEM(rows3, BF),
            pltpu.VMEM(flat, BF), pltpu.VMEM((1536, 1536), BF), pltpu.VMEM((3, 768, 256), BF),
            pltpu.VMEM((4, 256, 768), BF), pltpu.VMEM((2, HALF_ROWS, 256), BF),
            pltpu.VMEM((768, 256), F32), pltpu.VMEM((768, 256), F32), pltpu.VMEM((768, 256), F32),
            pltpu.VMEM((768, 256), F32), pltpu.VMEM((2, 768), F32),
            pltpu.SemaphoreType.DMA((9,)), pltpu.SemaphoreType.DMA((7,)),
        ],
    )
    away, returned, *first_got = hold(away, returned, *first_got)
    got = lax.ppermute(away, "seq", SWAP)
    from_one = lax.ppermute(input_one, "seq", SWAP)
    second_sent = kernel_call(
        expert_second_kernel, [block] * 2, [spots, parts, parts_got, *first_got], "expert_second", 10**6,
        in_specs=[SM] + [HB] * 4, out_specs=[HB] * 2,
        scratch=[
            pltpu.VMEM((2, 3, 768, 384), BF), pltpu.VMEM((2, 768, 384), BF),
            pltpu.SemaphoreType.DMA((2, 3)), pltpu.SemaphoreType.DMA((2,)),
        ],
    )
    got, from_one, *second_sent = hold(got, from_one, *second_sent)
    part, sent = sum_start(bits, keep, got)
    passed = jnp.where(odd == 1, input_two + from_one, input_two)
    sent[0], sent[1], returned, passed, *second_sent = hold(sent[0], sent[1], returned, passed, *second_sent)

    moved = pair_moves(sent, PAIRS_OF)
    second_got = [lax.ppermute(second_sent[i], "seq", routes[1 - i]) for i in range(2)]
    block_output = kernel_call(
        output_kernel, [shape(flat)], [after, target, returned], "output", 8 * 10**8
    )[0]
    moved[0], moved[1], block_output, passed, *second_got = hold(
        moved[0], moved[1], block_output, passed, *second_got
    )

    chunks, sent = sum_middle(bits, part, moved)
    sent[0], sent[1], passed = hold(sent[0], sent[1], passed)
    moved = pair_moves(sent, PAIRS_OF[::-1])
    two_a = lax.ppermute(passed[0:2], "seq", BACK_TWO)
    chunks = [(a + b.astype(F32)).astype(BF) for a, b in zip(chunks, moved)]
    grouped = group(chunks)
    grouped, passed, two_a = hold(grouped, passed, two_a)

    two_b = lax.ppermute(passed[2:4], "seq", BACK_TWO)
    whole = sum_across(turn, grouped)
    whole, two_b = hold(whole, two_b)
    piece = sum_along(whole)
    ordered = gather_across(turn, piece)
    chunks = gather_pairs(bits, ordered)
    up_sum, down_sum = kernel_call(
        expert_last_kernel,
        [shape((1, 768, 384), F32), shape((1, 384, 768), F32)],
        [spots, parts, parts_got, *first_got, *second_got],
        "expert_last", 10**6,
        in_specs=[SM] + [HB] * 6,
        scratch=[pltpu.VMEM((2, 4, 768, 384), BF), pltpu.SemaphoreType.DMA((2, 4))],
    )
    even = (1 - odd).astype(F32).reshape(1)
    input_grad = kernel_call(
        input_grad_kernel,
        [shape(flat, F32)],
        [
            even, attn_norm_gain, query_grad, own_grad, qkv_weight, block_input.reshape(flat),
            from_one.reshape(flat), two_a.reshape(256, 768), two_b.reshape(256, 768), after_grad,
        ],
        "input_grad", 3 * 10**9,
        in_specs=[SM, VM] + [HB] * 8,
        scratch=[
            pltpu.VMEM(flat, BF), pltpu.VMEM((512, 1536), BF), pltpu.VMEM((768, 2304), BF), pltpu.VMEM(flat, BF),
            pltpu.VMEM(flat, BF), pltpu.VMEM(flat, BF), pltpu.VMEM(flat, F32), pltpu.VMEM(flat, F32),
            pltpu.SemaphoreType.DMA((8,)),
        ],
    )[0]
    moved = pair_moves(chunks, PAIRS_OF)
    moved[0], moved[1], input_grad, up_sum = hold(moved[0], moved[1], input_grad, up_sum)
    mine = [chunks[0], moved[0], chunks[1], moved[1]]
    swapped = [lax.ppermute(a, "seq", SWAP) for a in mine]
    sums = [shape((768, 2304), F32), shape((768, 768), F32)]
    landing = [
        pltpu.VMEM((HALF_ROWS, 256), BF), pltpu.VMEM((6, 768, 256), F32),
        pltpu.SemaphoreType.DMA((4,)), pltpu.SemaphoreType.DMA((6,)),
    ]
    qkv_half, proj_half, tail = kernel_call(
        finish_mine_kernel, sums + [shape((64, 256))], [spots, *mine], "finish_mine", 10**6,
        in_specs=[SM] + [HB] * 4, out_specs=[HB, HB, VM], scratch=landing,
    )
    line = shape((768,), F32)
    qkv_sum, proj_sum, *rest = kernel_call(
        finish_other_kernel,
        sums + [line] * 4 + [shape((16,), I32), shape((1, 1, 16), I32)],
        [spots, tail, *swapped, qkv_half, proj_half],
        "finish_other", 10**6,
        in_specs=[SM, VM] + [HB] * 6, out_specs=[HB] * 2 + [VM] * 6, scratch=landing,
        aliases={6: 0, 7: 1},
    )
    return (
        block_output.reshape(rows3),
        input_grad.reshape(rows3),
        rest[0],
        rest[1],
        qkv_sum,
        proj_sum,
        rest[2],
        rest[3],
        up_sum,
        down_sum,
        rest[4],
        rest[5],
    )


def solution(mesh):
    placed = (
        P("batch", "seq", None),
        P("batch", "seq"),
        P(),
        P("batch", None),
        P("batch", "seq"),
        P(),
        P(),
        P(),
        P(),
        P(),
        P(),
        P("batch", None, None),
        P("batch", None, None),
        P("batch", "seq", None),
    )
    return jax.shard_map(
        local,
        mesh=mesh,
        in_specs=placed,
        out_specs=(
            P("batch", "seq", None),
            P("batch", "seq", None),
            P(),
            P(),
            P(),
            P(),
            P(),
            P(),
            P("batch", None, "seq"),
            P("batch", "seq", None),
            P(),
            P("batch", "seq", None),
        ),
        check_vma=False,
    )
```

```python
import jax
import jax.numpy as jnp
from jax import lax
from jax.experimental import pallas as pl
from jax.experimental.pallas import tpu as pltpu
from jax.sharding import PartitionSpec as P

BF = jnp.bfloat16
F32 = jnp.float32
I32 = jnp.int32
EPS = 1e-05
MASKED = -1e30
HEADS = 12
HEAD_SIZE = 64
PAIRS = 6
CAP = 64
SWAP = [(i, i ^ 1) for i in range(8)]
UP_ONE = [(i, i + 1) for i in range(0, 8, 2)]
DOWN_ONE = [(i + 1, i) for i in range(0, 8, 2)]
AHEAD_TWO = [(i, i + 2) for i in range(6)]
BACK_TWO = [(i + 2, i) for i in range(6)]
HALF_ROWS = 4864
PIECE = HALF_ROWS // 4
VMEM_BYTES = 63 * 1024 * 1024 + 640 * 1024
GEMM_ROWS = 4608
VM = pl.BlockSpec(memory_space=pltpu.VMEM)
HB = pl.BlockSpec(memory_space=pl.ANY)
SM = pl.BlockSpec(memory_space=pltpu.SMEM)


def shape(dims, kind=BF):
    return jax.ShapeDtypeStruct(dims, kind)


def kernel_call(body, outs, args, name, flops, grid=None, in_specs=None, out_specs=None, scratch=(), aliases=None):
    moved = sum(a.size * a.dtype.itemsize for a in args) + sum(
        o.size * o.dtype.itemsize for o in outs
    )
    extra = {} if grid is None else {"grid": grid}
    return pl.pallas_call(
        body,
        out_shape=outs,
        in_specs=in_specs or [VM] * len(args),
        out_specs=out_specs or [VM] * len(outs),
        scratch_shapes=list(scratch),
        compiler_params=pltpu.CompilerParams(vmem_limit_bytes=VMEM_BYTES),
        cost_estimate=pl.CostEstimate(flops=flops, bytes_accessed=moved, transcendentals=0),
        name=name,
        input_output_aliases=aliases or {},
        **extra,
    )(*args)


def nn(a, b):
    return jnp.dot(a, b, preferred_element_type=F32)


def nt(a, b):
    return lax.dot_general(a, b, (((1,), (1,)), ((), ())), preferred_element_type=F32)


def tn(a, b):
    return lax.dot_general(a, b, (((0,), (0,)), ((), ())), preferred_element_type=F32)


def iota(dims, axis):
    return lax.broadcasted_iota(I32, dims, axis)


def row(ref):
    return ref[...].reshape(1, 768)


def column(line):
    return jnp.broadcast_to(line, (128, line.shape[1])).T[:, 0:1]


def flat_line(ref):
    return jnp.concatenate([ref[i : i + 1, :] for i in range(4)], axis=1).astype(F32)


def norm_parts(values):
    centred = values - jnp.mean(values, axis=-1, keepdims=True)
    inverse = lax.rsqrt(jnp.mean(centred * centred, axis=-1, keepdims=True) + EPS)
    return centred * inverse, inverse


def norm_back(grad, gain, unit, inverse):
    t = grad * gain
    return inverse * (
        t - jnp.mean(t, axis=-1, keepdims=True) - unit * jnp.mean(t * unit, axis=-1, keepdims=True)
    )


def entry_kernel(
    place, tok, table, turn, gain, bias, x, grad, weight, target_out, tally, sent, unit_out, query, keyval,
    xv, gv, w, sv, uv, rv, kv, in_sems, out_sems,
):
    loads = copies([x, grad, weight], [xv, gv, w], in_sems)
    ids = jnp.concatenate([tok[i : i + 1, :] for i in range(4)], axis=1)
    live = flat_line(turn)
    high, low = ids >> 7, ids & 127
    picked = tn(table[...].astype(F32).astype(BF), (iota((64, 512), 0) == high).astype(F32).astype(BF))
    chosen = jnp.sum(jnp.where(iota((128, 512), 0) == low, picked, 0.0), axis=0, keepdims=True)
    member = (iota((16, 512), 0) == chosen.astype(I32)).astype(F32)
    earlier = (iota((512, 512), 0) < iota((512, 512), 1)).astype(F32).astype(BF)
    before = nn(member.astype(BF), earlier)
    slot = jnp.sum(before * member, axis=0, keepdims=True)
    target = (chosen * CAP + slot).astype(I32)
    target_out[...] = jnp.broadcast_to(target, (8, 512))
    counts = jnp.sum(member, axis=1, keepdims=True)
    tally[...] = jnp.where(iota((16, 128), 1) == place[0] * 16 + place[1], counts, 0.0)
    stores = []

    def store(source, goal):
        stores.append(pltpu.make_async_copy(source, goal, out_sems.at[len(stores)]))
        stores[-1].start()

    loads[0].wait()
    unit, _ = norm_parts(xv[...].astype(F32))
    uv[...] = unit.astype(BF)
    store(uv, unit_out)
    rows = (unit * row(gain) + row(bias)).astype(BF)
    loads[1].wait()
    for i in range(2):
        placing = jnp.where(iota((512, 512), 0) + 512 * i == target, live, 0.0).astype(BF)
        sv[512 * i : 512 * (i + 1), :] = nn(placing, gv[...]).astype(BF)
    store(sv, sent)
    loads[2].wait()
    rv[...] = rows

    def block(j, carry):
        kv[j] = nn(rv[...], w[:, cols_at(j, 768)]).astype(BF)
        return carry

    lax.fori_loop(0, 3, block, 0)
    store(kv.at[0], query)
    store(kv.at[1], keyval.at[:, 0:768])
    store(kv.at[2], keyval.at[:, 768:1536])
    for copy in stores:
        copy.wait()


def head_masks(scale):
    lane = iota((1, 128), 1)
    first = jnp.where(lane < 64, scale, 0.0).astype(BF)
    second = jnp.where(lane >= 64, scale, 0.0).astype(BF)
    return first, second


def stack_heads(pair, masks):
    return jnp.concatenate([pair * masks[0], pair * masks[1]], axis=0)


def window_bias(place, lengths, r):
    lane = iota((1, 128), 1) + place[0] * 128
    end, start = jnp.int32(0), jnp.zeros((1, 128), I32)
    for j in range(8):
        end = end + lengths[r, j]
        start = jnp.where(end <= lane, end, start)
    start = start - (place[0] - 2) * 128
    key = iota((384, 128), 0)
    allowed = (key >= start) & (key <= iota((384, 128), 1) + 256)
    half = jnp.where(allowed, 0.0, MASKED)
    return jnp.concatenate([half, half], axis=1)


def join_heads(both):
    one = jnp.where(iota((128, 128), 0) < 64, both[:, :128], both[:, 128:])
    return one.T


def copies(sources, targets, sems):
    out = [
        pltpu.make_async_copy(a, b, sems.at[i]) for i, (a, b) in enumerate(zip(sources, targets))
    ]
    for copy in out:
        copy.start()
    return out


def lanes_of(p, offset=0):
    return slice(offset + 128 * p, offset + 128 * (p + 1))


def forward_kernel(
    place, lengths, gain, bias, gain_two, bias_two, target,
    behind_two, early, late, weight, keyval, query, x, proj,
    unit_halo, context_out, attended, log_out, after_out, sent,
    b2, e1, l1, w, q, xv, wp, units, rows_in, context, att, aft, snd, in_sems, out_sems,
):
    loads = copies(
        [behind_two, early, late, weight, keyval, query, x, proj],
        [b2, e1, l1, w, context.at[:, 256:384, :], q, xv, wp],
        in_sems,
    )
    scales = head_masks(HEAD_SIZE ** (-0.5))
    for copy in loads[:3]:
        copy.wait()

    def norm_row(r, carry):
        halo = jnp.concatenate([b2[r], e1[r] + l1[r]], axis=0).astype(F32)
        unit, _ = norm_parts(halo)
        units[r] = unit.astype(BF)
        rows_in[r] = (unit * row(gain) + row(bias)).astype(BF)
        return carry

    lax.fori_loop(0, 4, norm_row, 0)
    unit_copy = pltpu.make_async_copy(units, unit_halo, out_sems.at[0])
    unit_copy.start()
    loads[3].wait()

    def keyval_block(j, carry):
        source = pl.ds(pl.multiple_of(768 + 512 * j, 256), 512)
        fresh = nn(rows_in[...].reshape(1024, 768), w[:, source])
        context[:, 0:256, cols_at(j, 512)] = fresh.astype(BF).reshape(4, 256, 512)
        return carry

    lax.fori_loop(0, 3, keyval_block, 0)
    for copy in loads[4:6]:
        copy.wait()
    context_copy = pltpu.make_async_copy(context, context_out, out_sems.at[1])
    context_copy.start()

    def one_row(r, carry):
        mask = window_bias(place, lengths, r)
        pairs = range(PAIRS)
        stacked = [stack_heads(q[r, :, lanes_of(p)], scales) for p in pairs]
        scores = [nt(context[r, :, lanes_of(p)], stacked[p]) + mask for p in pairs]
        tops = [jnp.max(a, axis=0, keepdims=True) for a in scores]
        weights = [jnp.exp(a - t) for a, t in zip(scores, tops)]
        totals = [jnp.sum(a, axis=0, keepdims=True) for a in weights]
        shares = [(a * (1.0 / t)).astype(BF) for a, t in zip(weights, totals)]
        mixed = [tn(context[r, :, lanes_of(p, 768)], shares[p]) for p in pairs]
        for p in pairs:
            log_out[r, p : p + 1, :] = tops[p] + jnp.log(totals[p])
            att[r, :, lanes_of(p)] = join_heads(mixed[p]).astype(BF)
        return carry

    lax.fori_loop(0, 4, one_row, 0)
    att_copy = pltpu.make_async_copy(att, attended, out_sems.at[2])
    att_copy.start()
    loads[6].wait()
    loads[7].wait()
    after = xv[...].reshape(512, 768).astype(F32) + nn(att[...].reshape(512, 768), wp[...])
    aft[...] = after
    after_copy = pltpu.make_async_copy(aft, after_out, out_sems.at[3])
    after_copy.start()
    unit, _ = norm_parts(after)
    rows = (unit * row(gain_two) + row(bias_two)).astype(BF)
    sends = []
    for i in range(2):
        part = slice(512 * i, 512 * (i + 1))
        placing = (iota((512, 512), 0) + 512 * i == target[0:1, :]).astype(F32).astype(BF)
        snd[part, :] = nn(placing, rows).astype(BF)
        sends.append(pltpu.make_async_copy(snd.at[part], sent.at[part], out_sems.at[4 + i]))
        sends[-1].start()
    for copy in [unit_copy, context_copy, att_copy, after_copy] + sends:
        copy.wait()


def active_grad_kernel(grad, down, out):
    out[0] = nt(grad[...], down[...]).astype(BF)


def gelu_both(v):
    c = 0.7978845608028654
    square = v * v
    p = c + (c * 0.044715) * square
    gate = 0.5 + 0.5 * jnp.tanh(v * p)
    value = v * gate
    return value, gate + value * (1.0 - gate) * (6.0 * p - 4.0 * c)


def expert_kernel(x, up, raw, active, hidden_grad, back, total):
    step = pl.program_id(0)

    @pl.when(step == 0)
    def _():
        total[...] = jnp.zeros_like(total)

    parts = [slice(256 * r, 256 * (r + 1)) for r in range(4)]
    hidden = [nn(x[rows, :], up[...]) for rows in parts]
    lows = []
    for rows, v in zip(parts, hidden):
        value, slope = gelu_both(v)
        active[0, rows, :] = value.astype(BF)
        low = (raw[0, rows, :].astype(F32) * slope).astype(BF)
        hidden_grad[0, rows, :] = low
        lows.append(low)
    for rows, low in zip(parts, lows):
        total[rows, :] += nt(low, up[...])

    @pl.when(step == pl.num_programs(0) - 1)
    def _():
        back[...] = total[...].astype(BF)


def turn_kernel(unit, unit_halo, grad, out, grad_t):
    out[0:768, 0:512] = unit[...].T
    out[0:768, 512:1536] = unit_halo[...].T
    out[768:784, :] = jnp.ones((16, 1536), BF)
    grad_t[...] = grad[...].T


def weight_kernel(x, grad_t, active, hidden_grad, down, out, parts, x_t, total):
    step = pl.program_id(0)

    @pl.when(step == 0)
    def _():
        total[...] = jnp.zeros_like(total)
        x_t[...] = x[...].T

    total[...] += nn(active[0], down[...])
    one = nn(x_t[...], hidden_grad[0]).astype(BF)
    two = nn(grad_t[...], active[0]).astype(BF)
    for j in range(2):
        parts[j, 0] = one[:, 384 * j : 384 * (j + 1)]
        parts[j, 1] = two[:, 384 * j : 384 * (j + 1)]

    @pl.when(step == pl.num_programs(0) - 1)
    def _():
        out[...] = total[...].astype(BF)


def output_kernel(after, target, returned, out):
    placing = (iota((512, 1024), 1).astype(F32) == column(target[0:1, :].astype(F32))).astype(F32).astype(BF)
    out[...] = (after[...] + nn(placing, returned[...])).astype(BF)


def cols_at(j, size=256):
    return pl.ds(pl.multiple_of(size * j, size), size)


def fill_halves(
    turned, query_grad, context_grad, weight, gain, bias, proj_part, terms_two, tally,
    out, gain_wide, bias_wide, gain_sum, bias_sum,
):
    gain_wide[...] = jnp.broadcast_to(row(gain), (256, 768)).T
    bias_wide[...] = jnp.broadcast_to(row(bias), (256, 768)).T

    def finish(block, both):
        body, sums = both[0:768], both[768:769]
        half, step = block // 6, block % 6
        out[half, 768 * step : 768 * (step + 1), :] = (
            gain_wide[...] * body + bias_wide[...] * sums
        ).astype(BF)
        wide = weight[:, 256 * block : 256 * (block + 1)].astype(F32)
        if block == 0:
            gain_sum[...] = wide * body
            bias_sum[...] = wide * sums
        else:
            gain_sum[...] += wide * body
            bias_sum[...] += wide * sums

    for j in range(3):
        finish(j, nn(turned[:, 0:512], query_grad[:, 256 * j : 256 * (j + 1)]))
        out[1, 768 * (3 + j) : 768 * (4 + j), :] = proj_part[j]
    for j in range(6):
        finish(3 + j, nn(turned[...], context_grad[:, 256 * j : 256 * (j + 1)]))

    columns = jnp.concatenate(
        [
            jnp.broadcast_to(jnp.sum(gain_sum[...], axis=1, keepdims=True), (768, 128)),
            jnp.broadcast_to(jnp.sum(bias_sum[...], axis=1, keepdims=True), (768, 128)),
        ],
        axis=1,
    ).T
    out[:, GEMM_ROWS:, :] = jnp.zeros((2, HALF_ROWS - GEMM_ROWS, 256), BF)
    for t in range(3):
        lanes = slice(256 * t, 256 * (t + 1))
        block = jnp.concatenate(
            [columns[0:1, lanes], columns[128:129, lanes], terms_two[:, lanes], jnp.zeros((12, 256), F32)],
            axis=0,
        )
        out[0, GEMM_ROWS + 16 * t : GEMM_ROWS + 16 * t + 16, :] = block.astype(BF)
    out[0, GEMM_ROWS + 48 : GEMM_ROWS + 64, 0:128] = tally[...].astype(BF)


def backward_kernel(
    place, lengths, gain_two, gain, bias, target, turn, log_total, tally,
    back, after, grad, proj, attended, query, context, turned, weight,
    after_grad, query_grad, own_grad, input_two, input_one, keep, away,
    bk, af, gr, wp, att, q, ctx, tu, w, ag, do, dq, cg, pp, ip, out,
    gain_wide, bias_wide, gain_sum, bias_sum, terms, in_sems, out_sems,
):
    loads = copies(
        [back, after, grad, proj, attended, query, context, turned, weight],
        [bk, af, gr, wp, att, q, ctx, tu, w],
        in_sems,
    )
    scales = head_masks(HEAD_SIZE ** (-0.5))
    ones = head_masks(1.0)
    placing = (iota((512, 1024), 1).astype(F32) == column(target[0:1, :].astype(F32))).astype(F32).astype(BF)
    live = column(flat_line(turn))
    loads[0].wait()
    normed_grad = nn(placing, bk[...])
    loads[1].wait()
    unit, inverse = norm_parts(af[...])
    terms[0:1, :] = jnp.sum(normed_grad * unit, axis=0, keepdims=True)
    terms[1:2, :] = jnp.sum(normed_grad, axis=0, keepdims=True)
    loads[2].wait()
    total = gr[...].astype(F32) * live + norm_back(normed_grad, row(gain_two), unit, inverse)
    ag[...] = total
    stores = [pltpu.make_async_copy(ag, after_grad, out_sems.at[0])]
    stores[0].start()
    low = total.astype(BF)
    loads[3].wait()
    do[...] = nt(low, wp[...]).astype(BF).reshape(4, 128, 768)
    loads[4].wait()
    mixed = nn(att[...].T, low).astype(BF)
    for j in range(3):
        pp[j] = mixed[:, 256 * j : 256 * (j + 1)]
    loads[5].wait()
    loads[6].wait()

    def one_row(r, carry):
        mask = window_bias(place, lengths, r)
        pairs = range(PAIRS)
        stacked = [stack_heads(q[r, :, lanes_of(p)], scales) for p in pairs]
        grads = [stack_heads(do[r, :, lanes_of(p)], ones) for p in pairs]
        scores = [nt(ctx[r, :, lanes_of(p)], stacked[p]) for p in pairs]
        share_grads = [nt(ctx[r, :, lanes_of(p, 768)], grads[p]) for p in pairs]
        shares = [jnp.exp(scores[p] + mask - log_total[r, p : p + 1, :]) for p in pairs]
        sums = [jnp.sum(a * b, axis=0, keepdims=True) for a, b in zip(shares, share_grads)]
        score_grads = [(a * (b - c)).astype(BF) for a, b, c in zip(shares, share_grads, sums)]
        key_grads = [nn(score_grads[p], stacked[p]).astype(BF) for p in pairs]
        value_grads = [nn(shares[p].astype(BF), grads[p]).astype(BF) for p in pairs]
        turned_grads = [tn(ctx[r, :, lanes_of(p)], score_grads[p]) for p in pairs]
        halo = pl.ds(pl.multiple_of(512 + r * 256, 256), 256)
        own = pl.ds(pl.multiple_of(r * 128, 128), 128)
        for p in pairs:
            cg[halo, lanes_of(p)] = key_grads[p][:256]
            cg[own, lanes_of(p)] = key_grads[p][256:]
            cg[halo, lanes_of(p, 768)] = value_grads[p][:256]
            cg[own, lanes_of(p, 768)] = value_grads[p][256:]
            dq[own, lanes_of(p)] = (join_heads(turned_grads[p]) * HEAD_SIZE ** (-0.5)).astype(BF)
        return carry

    lax.fori_loop(0, 4, one_row, 0)
    loads[7].wait()
    loads[8].wait()

    def store(source, target):
        stores.append(pltpu.make_async_copy(source, target, out_sems.at[len(stores)]))
        stores[-1].start()

    store(dq, query_grad)
    store(cg.at[0:512], own_grad)
    ip[...] = nt(cg[512:1536, :], w[:, 768:]).astype(BF).reshape(4, 256, 768)
    store(ip.at[:, 0:128], input_two)
    store(ip.at[:, 128:256], input_one)
    fill_halves(
        tu, dq, cg, w, gain, bias, pp, terms, tally, out, gain_wide, bias_wide, gain_sum, bias_sum
    )
    core = place[0] % 2

    @pl.when(core == 0)
    def _():
        pltpu.make_async_copy(out.at[0], keep, out_sems.at[5]).start()
        pltpu.make_async_copy(out.at[1], away, out_sems.at[6]).start()

    @pl.when(core == 1)
    def _():
        pltpu.make_async_copy(out.at[1], keep, out_sems.at[5]).start()
        pltpu.make_async_copy(out.at[0], away, out_sems.at[6]).start()

    for copy in stores:
        copy.wait()
    pltpu.make_async_copy(out.at[0], keep, out_sems.at[5]).wait()
    pltpu.make_async_copy(out.at[1], away, out_sems.at[6]).wait()


def place_half(half, bits, pieces, qkv, proj, whole, stage, in_sems, sems):
    loads = []
    for i in range(2):
        for j in range(2):
            first = pl.multiple_of((2 * i + (bits[i] + j) % 2) * PIECE, PIECE)
            target = whole.at[pl.ds(first, PIECE)]
            loads.append(pltpu.make_async_copy(pieces[2 * i + j], target, in_sems.at[2 * i + j]))
            loads[-1].start()
    for copy in loads:
        copy.wait()
    for j in range(6):
        stage[j] = whole[768 * j : 768 * (j + 1), :].astype(F32)
        lanes = slice(256 * (j % 3), 256 * (j % 3 + 1))

        @pl.when(half == 0)
        def _():
            pltpu.make_async_copy(stage.at[j], qkv.at[:, 256 * j : 256 * (j + 1)], sems.at[j]).start()

        @pl.when(half == 1)
        def _():
            target = qkv.at[:, 1536 + 256 * j : 1792 + 256 * j] if j < 3 else proj.at[:, lanes]
            pltpu.make_async_copy(stage.at[j], target, sems.at[j]).start()

    for j in range(6):
        pltpu.make_async_copy(stage.at[j], proj.at[:, 0:256], sems.at[j]).wait()


def finish_mine_kernel(place, a, b, c, d, qkv, proj, tail, whole, stage, in_sems, sems):
    place_half(place[0], (place[2], place[3]), (a, b, c, d), qkv, proj, whole, stage, in_sems, sems)
    tail[...] = whole[GEMM_ROWS : GEMM_ROWS + 64, :]


def finish_other_kernel(
    place, tail, a, b, c, d, qkv_in, proj_in, qkv, proj, gain_one, bias_one, gain_two, bias_two, counts, received,
    whole, stage, in_sems, sems,
):
    place_half(1 - place[0], (place[4], place[5]), (a, b, c, d), qkv, proj, whole, stage, in_sems, sems)
    both = tail[...].astype(F32) + whole[GEMM_ROWS : GEMM_ROWS + 64, :].astype(F32)
    for i, out in enumerate([gain_one, bias_one, gain_two, bias_two]):
        line = jnp.concatenate([both[16 * t + i : 16 * t + i + 1, :] for t in range(3)], axis=1)
        out[...] = line.reshape(768)
    every = both[48:64, 0:128]
    counts[...] = nt(jnp.ones((8, 128), BF), every.astype(BF))[0:1, :].astype(I32).reshape(16)
    chosen = (iota((16, 128), 0) == place[1]) & ((iota((16, 128), 1) >> 4) == place[6])
    mine = jnp.where(chosen, every, 0.0).astype(BF)
    fold = ((iota((128, 16), 0) & 15) == iota((128, 16), 1)).astype(F32).astype(BF)
    received[0] = jnp.sum(nn(mine, fold), axis=0, keepdims=True).astype(I32)


def expert_sum_kernel(parts, up, down):
    up[0] = parts[0, 0].astype(F32)
    down[0] = parts[0, 1].astype(F32).T


def input_grad_kernel(
    even, gain, query_grad, own_grad, weight, x, from_one, two_a, two_b, after_grad, out,
    dq, og, w, xv, one, two, ag, sums, in_sems,
):
    loads = copies(
        [weight, query_grad, own_grad, x, from_one, two_a, two_b, after_grad],
        [w, dq, og, xv, one, two.at[0:256], two.at[256:512], ag],
        in_sems,
    )
    for copy in loads[:3]:
        copy.wait()

    def part(r, carry):
        rows = pl.ds(pl.multiple_of(256 * r, 256), 256)
        sums[rows, :] = nt(dq[rows, :], w[:, :768]) + nt(og[rows, :], w[:, 768:])
        return carry

    lax.fori_loop(0, 2, part, 0)
    for copy in loads[3:]:
        copy.wait()
    unit, inverse = norm_parts(xv[...].astype(F32))
    total = sums[...] + two[...].astype(F32) + even[0] * one[...].astype(F32)
    out[...] = ag[...] + norm_back(total, row(gain), unit, inverse)


PAIR_ONE = [b ^ 1 for b in range(4)]
PAIR_TWO = [b ^ 3 for b in range(4)]
PAIRS_OF = [PAIR_ONE, PAIR_TWO]
BOTH = ("batch", "seq")


def by_core(even_move, odd_move):
    pairs = []
    for b in range(16):
        for s in range(8):
            x, y = (even_move, odd_move)[s % 2](b & 3, b >> 2)
            pairs.append((b * 8 + s, (y * 4 + x) * 8 + s))
    return pairs


def first_pairs(pair):
    return by_core(lambda x, y: (pair[x], y), lambda x, y: (x, pair[y]))


def second_step(d):
    return by_core(lambda x, y: (x, (y + d) & 3), lambda x, y: ((x + d) & 3, y))


def along_z(d):
    return [(s, (s + 2 * d) & 7) for s in range(8)]


def pick(array, index):
    return lax.dynamic_index_in_dim(array, index, 0, keepdims=False)


def part_of(array, index):
    return lax.dynamic_index_in_dim(array, index % 4, 1, keepdims=False)


def bits_of(place):
    return [(place & 1) ^ (place >> 1), place >> 1]


def sum_start(bits, keep, got):
    def part(stream, bit):
        at = (stream * 2 + bit) * PIECE
        return rows_at(keep, at, PIECE).astype(F32) + rows_at(got, at, PIECE).astype(F32)

    return part, [part(i, 1 - bits[i]).astype(BF) for i in range(2)]


def pair_moves(data, pairs):
    return [lax.ppermute(a, BOTH, first_pairs(pair)) for a, pair in zip(data, pairs)]


def rows_at(array, at, size):
    return lax.dynamic_slice(array, (at, 0), (size, array.shape[1]))


def sum_middle(bits, part, moved):
    size = PIECE // 2
    sums = [part(i, bits[i]) + moved[i].astype(F32) for i in range(2)]
    sent = [rows_at(sums[i], (1 - bits[1 - i]) * size, size).astype(BF) for i in range(2)]
    return [rows_at(sums[i], bits[1 - i] * size, size) for i in range(2)], sent


def group(chunks):
    size, lanes = chunks[0].shape
    return jnp.stack(chunks).reshape(2, 4, size // 4, lanes)


def sum_across(place, grouped):
    total = part_of(grouped, place).astype(F32)
    for d in (2, 1, 3):
        total = total + lax.ppermute(part_of(grouped, place + d), BOTH, second_step(d)).astype(F32)
    return total.astype(BF)


def sum_along(whole):
    total = whole.astype(F32)
    for d in (2, 1, 3):
        total = total + lax.ppermute(whole, "seq", along_z(d)).astype(F32)
    return total.astype(BF)


def gather_across(place, piece):
    size, lanes = PIECE // 2, piece.shape[-1]
    parts = [piece] + [lax.ppermute(piece, BOTH, second_step(d)) for d in (1, 2, 3)]
    stack = jnp.stack(parts, axis=1)
    ordered = jnp.stack([part_of(stack, place - p + 4) for p in range(4)], axis=1).reshape(2, size, lanes)
    return [ordered[0], ordered[1]]


def gather_pairs(bits, ordered):
    moved = pair_moves(ordered, PAIRS_OF[::-1])
    return [
        jnp.where(bit == 0, jnp.stack([a, b]), jnp.stack([b, a])).reshape(PIECE, a.shape[1])
        for bit, a, b in zip(bits[::-1], ordered, moved)
    ]


def hold(*values):
    return lax.optimization_barrier(values)


def exchange(array):
    return lax.all_to_all(
        array.reshape(16, CAP, 768), "batch", split_axis=0, concat_axis=0, tiled=True
    ).reshape(1024, 768)


def local(
    block_input, token_ids, hash_table, doc_lengths, turn_mask, attn_norm_gain, attn_norm_bias,
    qkv_weight, proj_weight, ffn_norm_gain, ffn_norm_bias, expert_up, expert_down, out_grad,
):
    seq = lax.axis_index("seq")
    owner = lax.axis_index("batch")
    odd = seq % 2
    flat = (512, 768)
    rows3 = (4, 128, 768)
    place = jnp.stack([seq, owner]).astype(I32)
    up, down = expert_up[0], expert_down[0]

    behind_two = lax.ppermute(block_input, "seq", AHEAD_TWO)
    early = lax.ppermute(block_input, "seq", UP_ONE)

    table = jnp.pad(hash_table, (0, 8192 - 8008)).reshape(64, 128)
    target, tally, grad_sent, unit, query, keyval = kernel_call(
        entry_kernel,
        [
            shape((8, 512), I32), shape((16, 128), F32), shape((1024, 768)), shape(flat), shape(flat),
            shape((512, 1536)),
        ],
        [
            place, token_ids, table, turn_mask, attn_norm_gain, attn_norm_bias, block_input.reshape(flat),
            out_grad.reshape(flat), qkv_weight,
        ],
        "entry", 3 * 10**9,
        in_specs=[SM] + [VM] * 5 + [HB] * 3,
        out_specs=[VM] * 2 + [HB] * 4,
        scratch=[
            pltpu.VMEM(flat, BF), pltpu.VMEM(flat, BF), pltpu.VMEM((768, 2304), BF), pltpu.VMEM((1024, 768), BF),
            pltpu.VMEM(flat, BF), pltpu.VMEM(flat, BF), pltpu.VMEM((3, 512, 768), BF),
            pltpu.SemaphoreType.DMA((3,)), pltpu.SemaphoreType.DMA((5,)),
        ],
    )
    grad_rows = exchange(grad_sent)

    behind_two, query = hold(behind_two, query)
    late = lax.ppermute(behind_two, "seq", DOWN_ONE)
    query, keyval = query.reshape(rows3), keyval.reshape(4, 128, 1536)

    unit_halo, context, attended, log_total, after, rows_sent = kernel_call(
        forward_kernel,
        [
            shape((4, 256, 768)), shape((4, 384, 1536)), shape(rows3), shape((4, 8, 256), F32),
            shape(flat, F32), shape((1024, 768)),
        ],
        [
            place, doc_lengths, attn_norm_gain, attn_norm_bias, ffn_norm_gain, ffn_norm_bias, target,
            behind_two, early, late, qkv_weight, keyval, query, block_input, proj_weight,
        ],
        "forward", 10**9,
        in_specs=[SM] * 2 + [VM] * 5 + [HB] * 8,
        out_specs=[HB] * 3 + [VM] + [HB] * 2,
        scratch=[
            pltpu.VMEM(rows3, BF), pltpu.VMEM(rows3, BF), pltpu.VMEM(rows3, BF), pltpu.VMEM((768, 2304), BF),
            pltpu.VMEM(rows3, BF), pltpu.VMEM(rows3, BF), pltpu.VMEM((768, 768), BF),
            pltpu.VMEM((4, 256, 768), BF), pltpu.VMEM((4, 256, 768), BF), pltpu.VMEM((4, 384, 1536), BF),
            pltpu.VMEM(rows3, BF), pltpu.VMEM(flat, F32), pltpu.VMEM((1024, 768), BF),
            pltpu.SemaphoreType.DMA((8,)), pltpu.SemaphoreType.DMA((6,)),
        ],
    )
    rows = exchange(rows_sent)

    turned, grad_t = kernel_call(
        turn_kernel,
        [shape((784, 1536)), shape((768, 1024))],
        [unit, unit_halo.reshape(1024, 768), grad_rows],
        "turn", 10**6,
    )
    grad_rows, turned, grad_t = hold(grad_rows, turned, grad_t)
    tile = pl.BlockSpec((1, 1024, 768), lambda i: (i, 0, 0))
    tiled = shape((4, 1024, 768))
    whole = pl.BlockSpec((1024, 768), lambda i: (0, 0))
    raw = kernel_call(
        active_grad_kernel,
        [tiled],
        [grad_rows, down],
        "active_grad", 48 * 10**8,
        grid=(4,),
        in_specs=[whole, pl.BlockSpec((768, 768), lambda i: (i, 0))],
        out_specs=[tile],
    )[0]

    active, hidden_grad, back_sent = kernel_call(
        expert_kernel,
        [tiled, tiled, shape((1024, 768))],
        [rows, up, raw],
        "expert", 97 * 10**8,
        grid=(4,),
        in_specs=[whole, pl.BlockSpec((768, 768), lambda i: (0, i)), tile],
        out_specs=[tile, tile, whole],
        scratch=[pltpu.VMEM((1024, 768), F32)],
    )
    back = exchange(back_sent)

    result, parts = kernel_call(
        weight_kernel,
        [shape((1024, 768)), shape((8, 2, 768, 384))],
        [rows, grad_t, active, hidden_grad, down],
        "weights", 145 * 10**8,
        grid=(4,),
        in_specs=[
            whole,
            pl.BlockSpec((768, 1024), lambda i: (0, 0)),
            tile,
            tile,
            pl.BlockSpec((768, 768), lambda i: (i, 0)),
        ],
        out_specs=[whole, pl.BlockSpec((2, 2, 768, 384), lambda i: (i, 0, 0, 0))],
        scratch=[pltpu.VMEM((768, 1024), BF), pltpu.VMEM((1024, 768), F32)],
    )
    returned = exchange(result)
    parts, back = hold(parts, back)
    parts_sum = lax.psum_scatter(parts, "seq", scatter_dimension=0, tiled=True)
    turn = jnp.where(odd == 0, owner // 4, owner % 4)
    bits = bits_of(jnp.where(odd == 0, owner % 4, owner // 4))
    spots = jnp.stack([odd, owner, *bits, *bits_of(turn), seq]).astype(I32)
    after_grad, query_grad, own_grad, input_two, input_one, keep, away = kernel_call(
        backward_kernel,
        [
            shape(flat, F32), shape(flat), shape((512, 1536)), shape(rows3), shape(rows3),
            shape((HALF_ROWS, 256)), shape((HALF_ROWS, 256)),
        ],
        [
            place, doc_lengths, ffn_norm_gain, attn_norm_gain, attn_norm_bias, target, turn_mask, log_total, tally,
            back, after, out_grad.reshape(flat), proj_weight, attended.reshape(flat), query, context, turned,
            qkv_weight,
        ],
        "backward", 16 * 10**9,
        in_specs=[SM] * 2 + [VM] * 7 + [HB] * 9,
        out_specs=[HB] * 7,
        scratch=[
            pltpu.VMEM((1024, 768), BF), pltpu.VMEM(flat, F32), pltpu.VMEM(flat, BF), pltpu.VMEM((768, 768), BF),
            pltpu.VMEM(flat, BF), pltpu.VMEM(rows3, BF), pltpu.VMEM((4, 384, 1536), BF),
            pltpu.VMEM((784, 1536), BF), pltpu.VMEM((768, 2304), BF), pltpu.VMEM(flat, F32), pltpu.VMEM(rows3, BF),
            pltpu.VMEM(flat, BF), pltpu.VMEM((1536, 1536), BF), pltpu.VMEM((3, 768, 256), BF),
            pltpu.VMEM((4, 256, 768), BF), pltpu.VMEM((2, HALF_ROWS, 256), BF),
            pltpu.VMEM((768, 256), F32), pltpu.VMEM((768, 256), F32), pltpu.VMEM((768, 256), F32),
            pltpu.VMEM((768, 256), F32), pltpu.VMEM((2, 768), F32),
            pltpu.SemaphoreType.DMA((9,)), pltpu.SemaphoreType.DMA((7,)),
        ],
    )
    away, returned = hold(away, returned)
    got = lax.ppermute(away, "seq", SWAP)
    from_one = lax.ppermute(input_one, "seq", SWAP)
    got, from_one = hold(got, from_one)
    part, sent = sum_start(bits, keep, got)
    passed = jnp.where(odd == 1, input_two + from_one, input_two)
    sent[0], sent[1], returned, passed = hold(sent[0], sent[1], returned, passed)

    moved = pair_moves(sent, PAIRS_OF)
    block_output = kernel_call(
        output_kernel, [shape(flat)], [after, target, returned], "output", 8 * 10**8
    )[0]
    moved[0], moved[1], block_output, passed = hold(moved[0], moved[1], block_output, passed)

    chunks, sent = sum_middle(bits, part, moved)
    sent[0], sent[1], passed = hold(sent[0], sent[1], passed)
    moved = pair_moves(sent, PAIRS_OF[::-1])
    two_a = lax.ppermute(passed[0:2], "seq", BACK_TWO)
    chunks = [(a + b.astype(F32)).astype(BF) for a, b in zip(chunks, moved)]
    grouped = group(chunks)
    grouped, passed, two_a = hold(grouped, passed, two_a)
    two_b = lax.ppermute(passed[2:4], "seq", BACK_TWO)
    whole = sum_across(turn, grouped)
    whole, two_b = hold(whole, two_b)
    piece = sum_along(whole)
    ordered = gather_across(turn, piece)
    ordered[0], ordered[1], parts_sum = hold(ordered[0], ordered[1], parts_sum)
    up_sum, down_sum = kernel_call(
        expert_sum_kernel,
        [shape((1, 768, 384), F32), shape((1, 384, 768), F32)],
        [parts_sum], "expert_sum", 10**6,
    )
    chunks = gather_pairs(bits, ordered)
    chunks[0], chunks[1], up_sum = hold(chunks[0], chunks[1], up_sum)
    even = (1 - odd).astype(F32).reshape(1)
    input_grad = kernel_call(
        input_grad_kernel,
        [shape(flat, F32)],
        [
            even, attn_norm_gain, query_grad, own_grad, qkv_weight, block_input.reshape(flat),
            from_one.reshape(flat), two_a.reshape(256, 768), two_b.reshape(256, 768), after_grad,
        ],
        "input_grad", 3 * 10**9,
        in_specs=[SM, VM] + [HB] * 8,
        scratch=[
            pltpu.VMEM(flat, BF), pltpu.VMEM((512, 1536), BF), pltpu.VMEM((768, 2304), BF), pltpu.VMEM(flat, BF),
            pltpu.VMEM(flat, BF), pltpu.VMEM(flat, BF), pltpu.VMEM(flat, F32), pltpu.VMEM(flat, F32),
            pltpu.SemaphoreType.DMA((8,)),
        ],
    )[0]
    moved = pair_moves(chunks, PAIRS_OF)
    moved[0], moved[1], input_grad = hold(moved[0], moved[1], input_grad)
    mine = [chunks[0], moved[0], chunks[1], moved[1]]
    swapped = [lax.ppermute(a, "seq", SWAP) for a in mine]
    sums = [shape((768, 2304), F32), shape((768, 768), F32)]
    landing = [
        pltpu.VMEM((HALF_ROWS, 256), BF), pltpu.VMEM((6, 768, 256), F32),
        pltpu.SemaphoreType.DMA((4,)), pltpu.SemaphoreType.DMA((6,)),
    ]
    qkv_half, proj_half, tail = kernel_call(
        finish_mine_kernel, sums + [shape((64, 256))], [spots, *mine], "finish_mine", 10**6,
        in_specs=[SM] + [HB] * 4, out_specs=[HB, HB, VM], scratch=landing,
    )
    line = shape((768,), F32)
    qkv_sum, proj_sum, *rest = kernel_call(
        finish_other_kernel,
        sums + [line] * 4 + [shape((16,), I32), shape((1, 1, 16), I32)],
        [spots, tail, *swapped, qkv_half, proj_half],
        "finish_other", 10**6,
        in_specs=[SM, VM] + [HB] * 6, out_specs=[HB] * 2 + [VM] * 6, scratch=landing,
        aliases={6: 0, 7: 1},
    )
    return (
        block_output.reshape(rows3),
        input_grad.reshape(rows3),
        rest[0],
        rest[1],
        qkv_sum,
        proj_sum,
        rest[2],
        rest[3],
        up_sum,
        down_sum,
        rest[4],
        rest[5],
    )


def solution(mesh):
    placed = (
        P("batch", "seq", None),
        P("batch", "seq"),
        P(),
        P("batch", None),
        P("batch", "seq"),
        P(),
        P(),
        P(),
        P(),
        P(),
        P(),
        P("batch", None, None),
        P("batch", None, None),
        P("batch", "seq", None),
    )
    return jax.shard_map(
        local,
        mesh=mesh,
        in_specs=placed,
        out_specs=(
            P("batch", "seq", None),
            P("batch", "seq", None),
            P(),
            P(),
            P(),
            P(),
            P(),
            P(),
            P("batch", None, "seq"),
            P("batch", "seq", None),
            P(),
            P("batch", "seq", None),
        ),
        check_vma=False,
    )
```

```python
import jax
import jax.numpy as jnp
from jax import lax
from jax.experimental import pallas as pl
from jax.experimental.pallas import tpu as pltpu
from jax.sharding import PartitionSpec as P

BF = jnp.bfloat16
F32 = jnp.float32
I32 = jnp.int32
EPS = 1e-05
MASKED = -1e30
HEADS = 12
HEAD_SIZE = 64
PAIRS = 6
CAP = 64
SWAP = [(i, i ^ 1) for i in range(8)]
UP_ONE = [(i, i + 1) for i in range(0, 8, 2)]
DOWN_ONE = [(i + 1, i) for i in range(0, 8, 2)]
AHEAD_TWO = [(i, i + 2) for i in range(6)]
BACK_TWO = [(i + 2, i) for i in range(6)]
HALF_ROWS = 4864
PIECE = HALF_ROWS // 4
VMEM_BYTES = 63 * 1024 * 1024 + 640 * 1024
GEMM_ROWS = 4608
VM = pl.BlockSpec(memory_space=pltpu.VMEM)
HB = pl.BlockSpec(memory_space=pl.ANY)
SM = pl.BlockSpec(memory_space=pltpu.SMEM)


def shape(dims, kind=BF):
    return jax.ShapeDtypeStruct(dims, kind)


def kernel_call(body, outs, args, name, flops, grid=None, in_specs=None, out_specs=None, scratch=(), aliases=None):
    moved = sum(a.size * a.dtype.itemsize for a in args) + sum(
        o.size * o.dtype.itemsize for o in outs
    )
    extra = {} if grid is None else {"grid": grid}
    return pl.pallas_call(
        body,
        out_shape=outs,
        in_specs=in_specs or [VM] * len(args),
        out_specs=out_specs or [VM] * len(outs),
        scratch_shapes=list(scratch),
        compiler_params=pltpu.CompilerParams(vmem_limit_bytes=VMEM_BYTES),
        cost_estimate=pl.CostEstimate(flops=flops, bytes_accessed=moved, transcendentals=0),
        name=name,
        input_output_aliases=aliases or {},
        **extra,
    )(*args)


def nn(a, b):
    return jnp.dot(a, b, preferred_element_type=F32)


def nt(a, b):
    return lax.dot_general(a, b, (((1,), (1,)), ((), ())), preferred_element_type=F32)


def tn(a, b):
    return lax.dot_general(a, b, (((0,), (0,)), ((), ())), preferred_element_type=F32)


def iota(dims, axis):
    return lax.broadcasted_iota(I32, dims, axis)


def row(ref):
    return ref[...].reshape(1, 768)


def column(line):
    return jnp.broadcast_to(line, (128, line.shape[1])).T[:, 0:1]


def flat_line(ref):
    return jnp.concatenate([ref[i : i + 1, :] for i in range(4)], axis=1).astype(F32)


def norm_parts(values):
    centred = values - jnp.mean(values, axis=-1, keepdims=True)
    inverse = lax.rsqrt(jnp.mean(centred * centred, axis=-1, keepdims=True) + EPS)
    return centred * inverse, inverse


def norm_back(grad, gain, unit, inverse):
    t = grad * gain
    return inverse * (
        t - jnp.mean(t, axis=-1, keepdims=True) - unit * jnp.mean(t * unit, axis=-1, keepdims=True)
    )


def entry_kernel(
    place, tok, table, turn, gain, bias, x, grad, weight, target_out, tally, sent, unit_out, query, keyval,
    xv, gv, w, sv, uv, rv, kv, in_sems, out_sems,
):
    loads = copies([x, grad, weight], [xv, gv, w], in_sems)
    ids = jnp.concatenate([tok[i : i + 1, :] for i in range(4)], axis=1)
    live = flat_line(turn)
    high, low = ids >> 7, ids & 127
    picked = tn(table[...].astype(F32).astype(BF), (iota((64, 512), 0) == high).astype(F32).astype(BF))
    chosen = jnp.sum(jnp.where(iota((128, 512), 0) == low, picked, 0.0), axis=0, keepdims=True)
    member = (iota((16, 512), 0) == chosen.astype(I32)).astype(F32)
    earlier = (iota((512, 512), 0) < iota((512, 512), 1)).astype(F32).astype(BF)
    before = nn(member.astype(BF), earlier)
    slot = jnp.sum(before * member, axis=0, keepdims=True)
    target = (chosen * CAP + slot).astype(I32)
    target_out[...] = jnp.broadcast_to(target, (8, 512))
    counts = jnp.sum(member, axis=1, keepdims=True)
    tally[...] = jnp.where(iota((16, 128), 1) == place[0] * 16 + place[1], counts, 0.0)
    stores = []

    def store(source, goal):
        stores.append(pltpu.make_async_copy(source, goal, out_sems.at[len(stores)]))
        stores[-1].start()

    loads[0].wait()
    unit, _ = norm_parts(xv[...].astype(F32))
    uv[...] = unit.astype(BF)
    store(uv, unit_out)
    rows = (unit * row(gain) + row(bias)).astype(BF)
    loads[1].wait()
    for i in range(2):
        placing = jnp.where(iota((512, 512), 0) + 512 * i == target, live, 0.0).astype(BF)
        sv[512 * i : 512 * (i + 1), :] = nn(placing, gv[...]).astype(BF)
    store(sv, sent)
    loads[2].wait()
    rv[...] = rows

    def block(j, carry):
        kv[j] = nn(rv[...], w[:, cols_at(j, 768)]).astype(BF)
        return carry

    lax.fori_loop(0, 3, block, 0)
    store(kv.at[0], query)
    store(kv.at[1], keyval.at[:, 0:768])
    store(kv.at[2], keyval.at[:, 768:1536])
    for copy in stores:
        copy.wait()


def head_masks(scale):
    lane = iota((1, 128), 1)
    first = jnp.where(lane < 64, scale, 0.0).astype(BF)
    second = jnp.where(lane >= 64, scale, 0.0).astype(BF)
    return first, second


def stack_heads(pair, masks):
    return jnp.concatenate([pair * masks[0], pair * masks[1]], axis=0)


def window_bias(place, lengths, r):
    lane = iota((1, 128), 1) + place[0] * 128
    end, start = jnp.int32(0), jnp.zeros((1, 128), I32)
    for j in range(8):
        end = end + lengths[r, j]
        start = jnp.where(end <= lane, end, start)
    start = start - (place[0] - 2) * 128
    key = iota((384, 128), 0)
    allowed = (key >= start) & (key <= iota((384, 128), 1) + 256)
    half = jnp.where(allowed, 0.0, MASKED)
    return jnp.concatenate([half, half], axis=1)


def join_heads(both):
    one = jnp.where(iota((128, 128), 0) < 64, both[:, :128], both[:, 128:])
    return one.T


def copies(sources, targets, sems):
    out = [
        pltpu.make_async_copy(a, b, sems.at[i]) for i, (a, b) in enumerate(zip(sources, targets))
    ]
    for copy in out:
        copy.start()
    return out


def lanes_of(p, offset=0):
    return slice(offset + 128 * p, offset + 128 * (p + 1))


def forward_kernel(
    place, lengths, gain, bias, gain_two, bias_two, target,
    behind_two, early, late, weight, keyval, query, x, proj,
    unit_halo, context_out, attended, log_out, after_out, sent,
    b2, e1, l1, w, q, xv, wp, units, rows_in, context, att, aft, snd, in_sems, out_sems,
):
    loads = copies(
        [behind_two, early, late, weight, keyval, query, x, proj],
        [b2, e1, l1, w, context.at[:, 256:384, :], q, xv, wp],
        in_sems,
    )
    scales = head_masks(HEAD_SIZE ** (-0.5))
    for copy in loads[:3]:
        copy.wait()

    def norm_row(r, carry):
        halo = jnp.concatenate([b2[r], e1[r] + l1[r]], axis=0).astype(F32)
        unit, _ = norm_parts(halo)
        units[r] = unit.astype(BF)
        rows_in[r] = (unit * row(gain) + row(bias)).astype(BF)
        return carry

    lax.fori_loop(0, 4, norm_row, 0)
    unit_copy = pltpu.make_async_copy(units, unit_halo, out_sems.at[0])
    unit_copy.start()
    loads[3].wait()

    def keyval_block(j, carry):
        source = pl.ds(pl.multiple_of(768 + 512 * j, 256), 512)
        fresh = nn(rows_in[...].reshape(1024, 768), w[:, source])
        context[:, 0:256, cols_at(j, 512)] = fresh.astype(BF).reshape(4, 256, 512)
        return carry

    lax.fori_loop(0, 3, keyval_block, 0)
    for copy in loads[4:6]:
        copy.wait()
    context_copy = pltpu.make_async_copy(context, context_out, out_sems.at[1])
    context_copy.start()

    def one_row(r, carry):
        mask = window_bias(place, lengths, r)
        pairs = range(PAIRS)
        stacked = [stack_heads(q[r, :, lanes_of(p)], scales) for p in pairs]
        scores = [nt(context[r, :, lanes_of(p)], stacked[p]) + mask for p in pairs]
        tops = [jnp.max(a, axis=0, keepdims=True) for a in scores]
        weights = [jnp.exp(a - t) for a, t in zip(scores, tops)]
        totals = [jnp.sum(a, axis=0, keepdims=True) for a in weights]
        shares = [(a * (1.0 / t)).astype(BF) for a, t in zip(weights, totals)]
        mixed = [tn(context[r, :, lanes_of(p, 768)], shares[p]) for p in pairs]
        for p in pairs:
            log_out[r, p : p + 1, :] = tops[p] + jnp.log(totals[p])
            att[r, :, lanes_of(p)] = join_heads(mixed[p]).astype(BF)
        return carry

    lax.fori_loop(0, 4, one_row, 0)
    att_copy = pltpu.make_async_copy(att, attended, out_sems.at[2])
    att_copy.start()
    loads[6].wait()
    loads[7].wait()
    after = xv[...].reshape(512, 768).astype(F32) + nn(att[...].reshape(512, 768), wp[...])
    aft[...] = after
    after_copy = pltpu.make_async_copy(aft, after_out, out_sems.at[3])
    after_copy.start()
    unit, _ = norm_parts(after)
    rows = (unit * row(gain_two) + row(bias_two)).astype(BF)
    sends = []
    for i in range(2):
        part = slice(512 * i, 512 * (i + 1))
        placing = (iota((512, 512), 0) + 512 * i == target[0:1, :]).astype(F32).astype(BF)
        snd[part, :] = nn(placing, rows).astype(BF)
        sends.append(pltpu.make_async_copy(snd.at[part], sent.at[part], out_sems.at[4 + i]))
        sends[-1].start()
    for copy in [unit_copy, context_copy, att_copy, after_copy] + sends:
        copy.wait()


def active_grad_kernel(grad, down, out):
    out[0] = nt(grad[...], down[...]).astype(BF)


def gelu_both(v):
    c = 0.7978845608028654
    square = v * v
    p = c + (c * 0.044715) * square
    gate = 0.5 + 0.5 * jnp.tanh(v * p)
    value = v * gate
    return value, gate + value * (1.0 - gate) * (6.0 * p - 4.0 * c)


def expert_kernel(x, up, raw, active, hidden_grad, back, total):
    step = pl.program_id(0)

    @pl.when(step == 0)
    def _():
        total[...] = jnp.zeros_like(total)

    parts = [slice(256 * r, 256 * (r + 1)) for r in range(4)]
    hidden = [nn(x[rows, :], up[...]) for rows in parts]
    lows = []
    for rows, v in zip(parts, hidden):
        value, slope = gelu_both(v)
        active[0, rows, :] = value.astype(BF)
        low = (raw[0, rows, :].astype(F32) * slope).astype(BF)
        hidden_grad[0, rows, :] = low
        lows.append(low)
    for rows, low in zip(parts, lows):
        total[rows, :] += nt(low, up[...])

    @pl.when(step == pl.num_programs(0) - 1)
    def _():
        back[...] = total[...].astype(BF)


def turn_kernel(unit, unit_halo, grad, out, grad_t):
    out[0:768, 0:512] = unit[...].T
    out[0:768, 512:1536] = unit_halo[...].T
    out[768:784, :] = jnp.ones((16, 1536), BF)
    grad_t[...] = grad[...].T


def weight_kernel(place, x, grad_t, active, hidden_grad, down, out, mine, away, x_t, total):
    step = pl.program_id(0)

    @pl.when(step == 0)
    def _():
        total[...] = jnp.zeros_like(total)
        x_t[...] = x[...].T

    total[...] += nn(active[0], down[...])
    one = nn(x_t[...], hidden_grad[0])
    two = nn(grad_t[...], active[0])
    even = place[0] % 2 == 0
    for i, both in enumerate([one, two]):
        mine[0, i] = jnp.where(even, both[:, :384], both[:, 384:]).astype(BF)
        away[0, i] = jnp.where(even, both[:, 384:], both[:, :384]).astype(BF)

    @pl.when(step == pl.num_programs(0) - 1)
    def _():
        out[...] = total[...].astype(BF)


def output_kernel(after, target, returned, out):
    placing = (iota((512, 1024), 1).astype(F32) == column(target[0:1, :].astype(F32))).astype(F32).astype(BF)
    out[...] = (after[...] + nn(placing, returned[...])).astype(BF)


def cols_at(j, size=256):
    return pl.ds(pl.multiple_of(size * j, size), size)


def fill_halves(
    turned, query_grad, context_grad, weight, gain, bias, proj_part, terms_two, tally,
    out, gain_wide, bias_wide, gain_sum, bias_sum,
):
    gain_wide[...] = jnp.broadcast_to(row(gain), (256, 768)).T
    bias_wide[...] = jnp.broadcast_to(row(bias), (256, 768)).T

    def finish(block, both):
        body, sums = both[0:768], both[768:769]
        half, step = block // 6, block % 6
        out[half, 768 * step : 768 * (step + 1), :] = (
            gain_wide[...] * body + bias_wide[...] * sums
        ).astype(BF)
        wide = weight[:, 256 * block : 256 * (block + 1)].astype(F32)
        if block == 0:
            gain_sum[...] = wide * body
            bias_sum[...] = wide * sums
        else:
            gain_sum[...] += wide * body
            bias_sum[...] += wide * sums

    for j in range(3):
        finish(j, nn(turned[:, 0:512], query_grad[:, 256 * j : 256 * (j + 1)]))
        out[1, 768 * (3 + j) : 768 * (4 + j), :] = proj_part[j]
    for j in range(6):
        finish(3 + j, nn(turned[...], context_grad[:, 256 * j : 256 * (j + 1)]))

    columns = jnp.concatenate(
        [
            jnp.broadcast_to(jnp.sum(gain_sum[...], axis=1, keepdims=True), (768, 128)),
            jnp.broadcast_to(jnp.sum(bias_sum[...], axis=1, keepdims=True), (768, 128)),
        ],
        axis=1,
    ).T
    out[:, GEMM_ROWS:, :] = jnp.zeros((2, HALF_ROWS - GEMM_ROWS, 256), BF)
    for t in range(3):
        lanes = slice(256 * t, 256 * (t + 1))
        block = jnp.concatenate(
            [columns[0:1, lanes], columns[128:129, lanes], terms_two[:, lanes], jnp.zeros((12, 256), F32)],
            axis=0,
        )
        out[0, GEMM_ROWS + 16 * t : GEMM_ROWS + 16 * t + 16, :] = block.astype(BF)
    out[0, GEMM_ROWS + 48 : GEMM_ROWS + 64, 0:128] = tally[...].astype(BF)


def backward_kernel(
    place, lengths, gain_two, gain, bias, target, turn, log_total, tally,
    back, after, grad, proj, attended, query, context, turned, weight,
    after_grad, query_grad, own_grad, input_two, input_one, keep, away,
    bk, af, gr, wp, att, q, ctx, tu, w, ag, do, dq, cg, pp, ip, out,
    gain_wide, bias_wide, gain_sum, bias_sum, terms, in_sems, out_sems,
):
    loads = copies(
        [back, after, grad, proj, attended, query, context, turned, weight],
        [bk, af, gr, wp, att, q, ctx, tu, w],
        in_sems,
    )
    scales = head_masks(HEAD_SIZE ** (-0.5))
    ones = head_masks(1.0)
    placing = (iota((512, 1024), 1).astype(F32) == column(target[0:1, :].astype(F32))).astype(F32).astype(BF)
    live = column(flat_line(turn))
    loads[0].wait()
    normed_grad = nn(placing, bk[...])
    loads[1].wait()
    unit, inverse = norm_parts(af[...])
    terms[0:1, :] = jnp.sum(normed_grad * unit, axis=0, keepdims=True)
    terms[1:2, :] = jnp.sum(normed_grad, axis=0, keepdims=True)
    loads[2].wait()
    total = gr[...].astype(F32) * live + norm_back(normed_grad, row(gain_two), unit, inverse)
    ag[...] = total
    stores = [pltpu.make_async_copy(ag, after_grad, out_sems.at[0])]
    stores[0].start()
    low = total.astype(BF)
    loads[3].wait()
    do[...] = nt(low, wp[...]).astype(BF).reshape(4, 128, 768)
    loads[4].wait()
    mixed = nn(att[...].T, low).astype(BF)
    for j in range(3):
        pp[j] = mixed[:, 256 * j : 256 * (j + 1)]
    loads[5].wait()
    loads[6].wait()

    def one_row(r, carry):
        mask = window_bias(place, lengths, r)
        pairs = range(PAIRS)
        stacked = [stack_heads(q[r, :, lanes_of(p)], scales) for p in pairs]
        grads = [stack_heads(do[r, :, lanes_of(p)], ones) for p in pairs]
        scores = [nt(ctx[r, :, lanes_of(p)], stacked[p]) for p in pairs]
        share_grads = [nt(ctx[r, :, lanes_of(p, 768)], grads[p]) for p in pairs]
        shares = [jnp.exp(scores[p] + mask - log_total[r, p : p + 1, :]) for p in pairs]
        sums = [jnp.sum(a * b, axis=0, keepdims=True) for a, b in zip(shares, share_grads)]
        score_grads = [(a * (b - c)).astype(BF) for a, b, c in zip(shares, share_grads, sums)]
        key_grads = [nn(score_grads[p], stacked[p]).astype(BF) for p in pairs]
        value_grads = [nn(shares[p].astype(BF), grads[p]).astype(BF) for p in pairs]
        turned_grads = [tn(ctx[r, :, lanes_of(p)], score_grads[p]) for p in pairs]
        halo = pl.ds(pl.multiple_of(512 + r * 256, 256), 256)
        own = pl.ds(pl.multiple_of(r * 128, 128), 128)
        for p in pairs:
            cg[halo, lanes_of(p)] = key_grads[p][:256]
            cg[own, lanes_of(p)] = key_grads[p][256:]
            cg[halo, lanes_of(p, 768)] = value_grads[p][:256]
            cg[own, lanes_of(p, 768)] = value_grads[p][256:]
            dq[own, lanes_of(p)] = (join_heads(turned_grads[p]) * HEAD_SIZE ** (-0.5)).astype(BF)
        return carry

    lax.fori_loop(0, 4, one_row, 0)
    loads[7].wait()
    loads[8].wait()

    def store(source, target):
        stores.append(pltpu.make_async_copy(source, target, out_sems.at[len(stores)]))
        stores[-1].start()

    store(dq, query_grad)
    store(cg.at[0:512], own_grad)
    ip[...] = nt(cg[512:1536, :], w[:, 768:]).astype(BF).reshape(4, 256, 768)
    store(ip.at[:, 0:128], input_two)
    store(ip.at[:, 128:256], input_one)
    fill_halves(
        tu, dq, cg, w, gain, bias, pp, terms, tally, out, gain_wide, bias_wide, gain_sum, bias_sum
    )
    core = place[0] % 2

    @pl.when(core == 0)
    def _():
        pltpu.make_async_copy(out.at[0], keep, out_sems.at[5]).start()
        pltpu.make_async_copy(out.at[1], away, out_sems.at[6]).start()

    @pl.when(core == 1)
    def _():
        pltpu.make_async_copy(out.at[1], keep, out_sems.at[5]).start()
        pltpu.make_async_copy(out.at[0], away, out_sems.at[6]).start()

    for copy in stores:
        copy.wait()
    pltpu.make_async_copy(out.at[0], keep, out_sems.at[5]).wait()
    pltpu.make_async_copy(out.at[1], away, out_sems.at[6]).wait()


def place_half(half, bits, pieces, qkv, proj, whole, stage, in_sems, sems):
    loads = []
    for i in range(2):
        for j in range(2):
            first = pl.multiple_of((2 * i + (bits[i] + j) % 2) * PIECE, PIECE)
            target = whole.at[pl.ds(first, PIECE)]
            loads.append(pltpu.make_async_copy(pieces[2 * i + j], target, in_sems.at[2 * i + j]))
            loads[-1].start()
    for copy in loads:
        copy.wait()
    for j in range(6):
        stage[j] = whole[768 * j : 768 * (j + 1), :].astype(F32)
        lanes = slice(256 * (j % 3), 256 * (j % 3 + 1))

        @pl.when(half == 0)
        def _():
            pltpu.make_async_copy(stage.at[j], qkv.at[:, 256 * j : 256 * (j + 1)], sems.at[j]).start()

        @pl.when(half == 1)
        def _():
            target = qkv.at[:, 1536 + 256 * j : 1792 + 256 * j] if j < 3 else proj.at[:, lanes]
            pltpu.make_async_copy(stage.at[j], target, sems.at[j]).start()

    for j in range(6):
        pltpu.make_async_copy(stage.at[j], proj.at[:, 0:256], sems.at[j]).wait()


def finish_mine_kernel(place, a, b, c, d, qkv, proj, tail, whole, stage, in_sems, sems):
    place_half(place[0], (place[2], place[3]), (a, b, c, d), qkv, proj, whole, stage, in_sems, sems)
    tail[...] = whole[GEMM_ROWS : GEMM_ROWS + 64, :]


def finish_other_kernel(
    place, tail, a, b, c, d, qkv_in, proj_in, qkv, proj, gain_one, bias_one, gain_two, bias_two, counts, received,
    whole, stage, in_sems, sems,
):
    place_half(1 - place[0], (place[4], place[5]), (a, b, c, d), qkv, proj, whole, stage, in_sems, sems)
    both = tail[...].astype(F32) + whole[GEMM_ROWS : GEMM_ROWS + 64, :].astype(F32)
    for i, out in enumerate([gain_one, bias_one, gain_two, bias_two]):
        line = jnp.concatenate([both[16 * t + i : 16 * t + i + 1, :] for t in range(3)], axis=1)
        out[...] = line.reshape(768)
    every = both[48:64, 0:128]
    counts[...] = nt(jnp.ones((8, 128), BF), every.astype(BF))[0:1, :].astype(I32).reshape(16)
    chosen = (iota((16, 128), 0) == place[1]) & ((iota((16, 128), 1) >> 4) == place[6])
    mine = jnp.where(chosen, every, 0.0).astype(BF)
    fold = ((iota((128, 16), 0) & 15) == iota((128, 16), 1)).astype(F32).astype(BF)
    received[0] = jnp.sum(nn(mine, fold), axis=0, keepdims=True).astype(I32)


def chunk_of(a, b):
    return 2 * b + (a + b) % 2


def add_chunks(plan, buffer, in_sems):
    loads = []
    for n, picks in enumerate(plan):
        for m, pick_ref in enumerate(picks):
            loads.append(pltpu.make_async_copy(pick_ref, buffer.at[n, m], in_sems.at[n, m]))
            loads[-1].start()
    return loads


def summed(buffer, n, count):
    total = buffer[n, 0].astype(F32)
    for m in range(1, count):
        total = total + buffer[n, m].astype(F32)
    return total


def expert_first_kernel(spots, own, got, one, two, buffer, made, in_sems, out_sems):
    a, b = spots[7], spots[8]
    wanted = [(chunk_of(1 - a, k), 0) for k in range(2)] + [(chunk_of(k, 1 - b), 1) for k in range(2)]
    plan = [[own.at[c, t], got.at[c, t]] for c, t in wanted]
    loads = add_chunks(plan, buffer, in_sems)
    stores = []
    for n in range(4):
        loads[2 * n].wait()
        loads[2 * n + 1].wait()
        made[n] = summed(buffer, n, 2).astype(BF)
        stores.append(pltpu.make_async_copy(made.at[n], (one, two)[n // 2].at[n % 2], out_sems.at[n]))
        stores[-1].start()
    for copy in stores:
        copy.wait()


def expert_second_kernel(
    spots, own, got, first, second, one, two, three, four, buffer, made, in_sems, out_sems
):
    a, b = spots[7], spots[8]
    c, d = chunk_of(a, 1 - b), chunk_of(1 - a, b)
    plan = [
        [own.at[c, 0], got.at[c, 0], first.at[1 - b]],
        [own.at[d, 1], got.at[d, 1], second.at[1 - a]],
    ]
    loads = add_chunks(plan, buffer, in_sems)
    stores = []
    for n in range(2):
        for copy in loads[3 * n : 3 * n + 3]:
            copy.wait()
        made[n] = summed(buffer, n, 3).astype(BF)
        for m in range(2):
            target = ((one, two), (three, four))[m][n]
            stores.append(pltpu.make_async_copy(made.at[n, 384 * m : 384 * (m + 1)], target, out_sems.at[n, m]))
            stores[-1].start()
    for copy in stores:
        copy.wait()


def expert_last_kernel(
    spots, own, got, first, second, third, fourth, fifth, sixth, up, down, buffer, in_sems, late_sems
):
    a, b = spots[7], spots[8]
    c = chunk_of(a, b)
    plan = [
        [own.at[c, 0], got.at[c, 0], first.at[b]],
        [own.at[c, 1], got.at[c, 1], second.at[a]],
    ]
    loads = add_chunks(plan, buffer, in_sems)
    for n in range(2):
        for m in range(2):
            source = ((third, fourth), (fifth, sixth))[m][n]
            target = buffer.at[n, 3, 384 * m : 384 * (m + 1)]
            loads.append(pltpu.make_async_copy(source, target, late_sems.at[n, m]))
            loads[-1].start()
    for copy in loads:
        copy.wait()
    up[0] = summed(buffer, 0, 4)
    down[0] = summed(buffer, 1, 4).T


def input_own_kernel(query_grad, own_grad, weight, out, dq, og, w, in_sems):
    for copy in copies([weight, query_grad, own_grad], [w, dq, og], in_sems):
        copy.wait()
    out[...] = nt(dq[...], w[:, :768]) + nt(og[...], w[:, 768:])


def input_grad_kernel(
    even, gain, own, x, from_one, two_a, two_b, after_grad, out, ov, xv, one, two, ag, in_sems,
):
    loads = copies(
        [x, own, from_one, two_a, two_b, after_grad],
        [xv, ov, one, two.at[0:256], two.at[256:512], ag],
        in_sems,
    )
    loads[0].wait()
    unit, inverse = norm_parts(xv[...].astype(F32))
    for copy in loads[1:]:
        copy.wait()
    total = ov[...] + two[...].astype(F32) + even[0] * one[...].astype(F32)
    out[...] = ag[...] + norm_back(total, row(gain), unit, inverse)


PAIR_ONE = [b ^ 1 for b in range(4)]
PAIR_TWO = [b ^ 3 for b in range(4)]
PAIRS_OF = [PAIR_ONE, PAIR_TWO]
BOTH = ("batch", "seq")


def by_core(even_move, odd_move):
    pairs = []
    for b in range(16):
        for s in range(8):
            x, y = (even_move, odd_move)[s % 2](b & 3, b >> 2)
            pairs.append((b * 8 + s, (y * 4 + x) * 8 + s))
    return pairs


def first_pairs(pair):
    return by_core(lambda x, y: (pair[x], y), lambda x, y: (x, pair[y]))


def second_step(d):
    return by_core(lambda x, y: (x, (y + d) & 3), lambda x, y: ((x + d) & 3, y))


def along_z(d):
    return [(s, (s + 2 * d) & 7) for s in range(8)]


def pick(array, index):
    return lax.dynamic_index_in_dim(array, index, 0, keepdims=False)


def part_of(array, index):
    return lax.dynamic_index_in_dim(array, index % 4, 1, keepdims=False)


def bits_of(place):
    return [(place & 1) ^ (place >> 1), place >> 1]


def z_pairs(pair):
    return [(s, pair[s // 2] * 2 + s % 2) for s in range(8)]


def sum_start(bits, keep, got):
    def part(stream, bit):
        at = (stream * 2 + bit) * PIECE
        return rows_at(keep, at, PIECE).astype(F32) + rows_at(got, at, PIECE).astype(F32)

    return part, [part(i, 1 - bits[i]).astype(BF) for i in range(2)]


def pair_moves(data, pairs):
    return [lax.ppermute(a, BOTH, first_pairs(pair)) for a, pair in zip(data, pairs)]


def rows_at(array, at, size):
    return lax.dynamic_slice(array, (at, 0), (size, array.shape[1]))


def sum_middle(bits, part, moved):
    size = PIECE // 2
    sums = [part(i, bits[i]) + moved[i].astype(F32) for i in range(2)]
    sent = [rows_at(sums[i], (1 - bits[1 - i]) * size, size).astype(BF) for i in range(2)]
    return [rows_at(sums[i], bits[1 - i] * size, size) for i in range(2)], sent


def group(chunks):
    size, lanes = chunks[0].shape
    return jnp.stack(chunks).reshape(2, 4, size // 4, lanes)


def sum_across(place, grouped):
    total = part_of(grouped, place).astype(F32)
    for d in (2, 1, 3):
        total = total + lax.ppermute(part_of(grouped, place + d), BOTH, second_step(d)).astype(F32)
    return total.astype(BF)


def sum_along(whole):
    total = whole.astype(F32)
    for d in (2, 1, 3):
        total = total + lax.ppermute(whole, "seq", along_z(d)).astype(F32)
    return total.astype(BF)


def gather_across(place, piece):
    size, lanes = PIECE // 2, piece.shape[-1]
    parts = [piece] + [lax.ppermute(piece, BOTH, second_step(d)) for d in (1, 2, 3)]
    stack = jnp.stack(parts, axis=1)
    ordered = jnp.stack([part_of(stack, place - p + 4) for p in range(4)], axis=1).reshape(2, size, lanes)
    return [ordered[0], ordered[1]]


def gather_pairs(bits, ordered):
    moved = pair_moves(ordered, PAIRS_OF[::-1])
    return [
        jnp.where(bit == 0, jnp.stack([a, b]), jnp.stack([b, a])).reshape(PIECE, a.shape[1])
        for bit, a, b in zip(bits[::-1], ordered, moved)
    ]


def hold(*values):
    return lax.optimization_barrier(values)


def exchange(array):
    return lax.all_to_all(
        array.reshape(16, CAP, 768), "batch", split_axis=0, concat_axis=0, tiled=True
    ).reshape(1024, 768)


def local(
    block_input, token_ids, hash_table, doc_lengths, turn_mask, attn_norm_gain, attn_norm_bias,
    qkv_weight, proj_weight, ffn_norm_gain, ffn_norm_bias, expert_up, expert_down, out_grad,
):
    seq = lax.axis_index("seq")
    owner = lax.axis_index("batch")
    odd = seq % 2
    flat = (512, 768)
    rows3 = (4, 128, 768)
    place = jnp.stack([seq, owner]).astype(I32)
    up, down = expert_up[0], expert_down[0]

    behind_two = lax.ppermute(block_input, "seq", AHEAD_TWO)
    early = lax.ppermute(block_input, "seq", UP_ONE)

    table = jnp.pad(hash_table, (0, 8192 - 8008)).reshape(64, 128)
    target, tally, grad_sent, unit, query, keyval = kernel_call(
        entry_kernel,
        [
            shape((8, 512), I32), shape((16, 128), F32), shape((1024, 768)), shape(flat), shape(flat),
            shape((512, 1536)),
        ],
        [
            place, token_ids, table, turn_mask, attn_norm_gain, attn_norm_bias, block_input.reshape(flat),
            out_grad.reshape(flat), qkv_weight,
        ],
        "entry", 3 * 10**9,
        in_specs=[SM] + [VM] * 5 + [HB] * 3,
        out_specs=[VM] * 2 + [HB] * 4,
        scratch=[
            pltpu.VMEM(flat, BF), pltpu.VMEM(flat, BF), pltpu.VMEM((768, 2304), BF), pltpu.VMEM((1024, 768), BF),
            pltpu.VMEM(flat, BF), pltpu.VMEM(flat, BF), pltpu.VMEM((3, 512, 768), BF),
            pltpu.SemaphoreType.DMA((3,)), pltpu.SemaphoreType.DMA((5,)),
        ],
    )
    grad_rows = exchange(grad_sent)

    behind_two, query = hold(behind_two, query)
    late = lax.ppermute(behind_two, "seq", DOWN_ONE)
    query, keyval = query.reshape(rows3), keyval.reshape(4, 128, 1536)

    unit_halo, context, attended, log_total, after, rows_sent = kernel_call(
        forward_kernel,
        [
            shape((4, 256, 768)), shape((4, 384, 1536)), shape(rows3), shape((4, 8, 256), F32),
            shape(flat, F32), shape((1024, 768)),
        ],
        [
            place, doc_lengths, attn_norm_gain, attn_norm_bias, ffn_norm_gain, ffn_norm_bias, target,
            behind_two, early, late, qkv_weight, keyval, query, block_input, proj_weight,
        ],
        "forward", 10**9,
        in_specs=[SM] * 2 + [VM] * 5 + [HB] * 8,
        out_specs=[HB] * 3 + [VM] + [HB] * 2,
        scratch=[
            pltpu.VMEM(rows3, BF), pltpu.VMEM(rows3, BF), pltpu.VMEM(rows3, BF), pltpu.VMEM((768, 2304), BF),
            pltpu.VMEM(rows3, BF), pltpu.VMEM(rows3, BF), pltpu.VMEM((768, 768), BF),
            pltpu.VMEM((4, 256, 768), BF), pltpu.VMEM((4, 256, 768), BF), pltpu.VMEM((4, 384, 1536), BF),
            pltpu.VMEM(rows3, BF), pltpu.VMEM(flat, F32), pltpu.VMEM((1024, 768), BF),
            pltpu.SemaphoreType.DMA((8,)), pltpu.SemaphoreType.DMA((6,)),
        ],
    )
    rows = exchange(rows_sent)

    turned, grad_t = kernel_call(
        turn_kernel,
        [shape((784, 1536)), shape((768, 1024))],
        [unit, unit_halo.reshape(1024, 768), grad_rows],
        "turn", 10**6,
    )
    grad_rows, turned, grad_t = hold(grad_rows, turned, grad_t)
    tile = pl.BlockSpec((1, 1024, 768), lambda i: (i, 0, 0))
    tiled = shape((4, 1024, 768))
    whole = pl.BlockSpec((1024, 768), lambda i: (0, 0))
    raw = kernel_call(
        active_grad_kernel,
        [tiled],
        [grad_rows, down],
        "active_grad", 48 * 10**8,
        grid=(4,),
        in_specs=[whole, pl.BlockSpec((768, 768), lambda i: (i, 0))],
        out_specs=[tile],
    )[0]

    active, hidden_grad, back_sent = kernel_call(
        expert_kernel,
        [tiled, tiled, shape((1024, 768))],
        [rows, up, raw],
        "expert", 97 * 10**8,
        grid=(4,),
        in_specs=[whole, pl.BlockSpec((768, 768), lambda i: (0, i)), tile],
        out_specs=[tile, tile, whole],
        scratch=[pltpu.VMEM((1024, 768), F32)],
    )
    back = exchange(back_sent)

    result, parts, parts_away = kernel_call(
        weight_kernel,
        [shape((1024, 768)), shape((4, 2, 768, 384)), shape((4, 2, 768, 384))],
        [place, rows, grad_t, active, hidden_grad, down],
        "weights", 145 * 10**8,
        grid=(4,),
        in_specs=[
            SM,
            whole,
            pl.BlockSpec((768, 1024), lambda i: (0, 0)),
            tile,
            tile,
            pl.BlockSpec((768, 768), lambda i: (i, 0)),
        ],
        out_specs=[
            pl.BlockSpec((1024, 768), lambda i: (0, 0)),
            pl.BlockSpec((1, 2, 768, 384), lambda i: (i, 0, 0, 0)),
            pl.BlockSpec((1, 2, 768, 384), lambda i: (i, 0, 0, 0)),
        ],
        scratch=[pltpu.VMEM((768, 1024), BF), pltpu.VMEM((1024, 768), F32)],
    )
    returned = exchange(result)
    parts_away, back = hold(parts_away, back)
    parts_got = lax.ppermute(parts_away, "seq", SWAP)
    depth = seq // 2
    turn = jnp.where(odd == 0, owner // 4, owner % 4)
    bits = bits_of(jnp.where(odd == 0, owner % 4, owner // 4))
    spots = jnp.stack([odd, owner, *bits, *bits_of(turn), seq, *bits_of(depth)]).astype(I32)
    block = shape((768, 384))
    first_sent = kernel_call(
        expert_first_kernel, [shape((2, 768, 384))] * 2, [spots, parts, parts_got], "expert_first", 10**6,
        in_specs=[SM] + [HB] * 2, out_specs=[HB] * 2,
        scratch=[
            pltpu.VMEM((4, 2, 768, 384), BF), pltpu.VMEM((4, 768, 384), BF),
            pltpu.SemaphoreType.DMA((4, 2)), pltpu.SemaphoreType.DMA((4,)),
        ],
    )
    back, *first_sent = hold(back, *first_sent)
    routes = [z_pairs(pair) for pair in PAIRS_OF]
    first_got = [lax.ppermute(a, "seq", route) for a, route in zip(first_sent, routes)]

    after_grad, query_grad, own_grad, input_two, input_one, keep, away = kernel_call(
        backward_kernel,
        [
            shape(flat, F32), shape(flat), shape((512, 1536)), shape(rows3), shape(rows3),
            shape((HALF_ROWS, 256)), shape((HALF_ROWS, 256)),
        ],
        [
            place, doc_lengths, ffn_norm_gain, attn_norm_gain, attn_norm_bias, target, turn_mask, log_total, tally,
            back, after, out_grad.reshape(flat), proj_weight, attended.reshape(flat), query, context, turned,
            qkv_weight,
        ],
        "backward", 16 * 10**9,
        in_specs=[SM] * 2 + [VM] * 7 + [HB] * 9,
        out_specs=[HB] * 7,
        scratch=[
            pltpu.VMEM((1024, 768), BF), pltpu.VMEM(flat, F32), pltpu.VMEM(flat, BF), pltpu.VMEM((768, 768), BF),
            pltpu.VMEM(flat, BF), pltpu.VMEM(rows3, BF), pltpu.VMEM((4, 384, 1536), BF),
            pltpu.VMEM((784, 1536), BF), pltpu.VMEM((768, 2304), BF), pltpu.VMEM(flat, F32), pltpu.VMEM(rows3, BF),
            pltpu.VMEM(flat, BF), pltpu.VMEM((1536, 1536), BF), pltpu.VMEM((3, 768, 256), BF),
            pltpu.VMEM((4, 256, 768), BF), pltpu.VMEM((2, HALF_ROWS, 256), BF),
            pltpu.VMEM((768, 256), F32), pltpu.VMEM((768, 256), F32), pltpu.VMEM((768, 256), F32),
            pltpu.VMEM((768, 256), F32), pltpu.VMEM((2, 768), F32),
            pltpu.SemaphoreType.DMA((9,)), pltpu.SemaphoreType.DMA((7,)),
        ],
    )
    away, returned, *first_got = hold(away, returned, *first_got)
    got = lax.ppermute(away, "seq", SWAP)
    from_one = lax.ppermute(input_one, "seq", SWAP)
    second_sent = kernel_call(
        expert_second_kernel, [shape((384, 384))] * 4, [spots, parts, parts_got, *first_got], "expert_second", 10**6,
        in_specs=[SM] + [HB] * 4, out_specs=[HB] * 4,
        scratch=[
            pltpu.VMEM((2, 3, 768, 384), BF), pltpu.VMEM((2, 768, 384), BF),
            pltpu.SemaphoreType.DMA((2, 3)), pltpu.SemaphoreType.DMA((2, 2)),
        ],
    )
    own_part = kernel_call(
        input_own_kernel, [shape(flat, F32)], [query_grad, own_grad, qkv_weight], "input_own", 2 * 10**9,
        in_specs=[HB] * 3,
        scratch=[
            pltpu.VMEM(flat, BF), pltpu.VMEM((512, 1536), BF), pltpu.VMEM((768, 2304), BF),
            pltpu.SemaphoreType.DMA((3,)),
        ],
    )[0]
    got, from_one, own_part, *second_sent = hold(got, from_one, own_part, *second_sent)
    part, sent = sum_start(bits, keep, got)
    passed = jnp.where(odd == 1, input_two + from_one, input_two)
    sent[0], sent[1], returned, passed = hold(sent[0], sent[1], returned, passed)

    moved = pair_moves(sent, PAIRS_OF)
    two_a = lax.ppermute(passed[0:2], "seq", BACK_TWO)
    block_output = kernel_call(
        output_kernel, [shape(flat)], [after, target, returned], "output", 8 * 10**8
    )[0]
    moved[0], moved[1], block_output, passed, two_a = hold(moved[0], moved[1], block_output, passed, two_a)

    chunks, sent = sum_middle(bits, part, moved)
    sent[0], sent[1], passed = hold(sent[0], sent[1], passed)
    moved = pair_moves(sent, PAIRS_OF[::-1])
    two_b = lax.ppermute(passed[2:4], "seq", BACK_TWO)
    chunks = [(a + b.astype(F32)).astype(BF) for a, b in zip(chunks, moved)]
    grouped = group(chunks)
    grouped, two_b = hold(grouped, two_b)

    whole = sum_across(turn, grouped)
    piece = sum_along(whole)
    piece, *second_sent = hold(piece, *second_sent)
    early_got = [lax.ppermute(second_sent[i], "seq", routes[1 - i]) for i in range(2)]
    ordered = gather_across(turn, piece)
    ordered[0], ordered[1], second_sent[2], second_sent[3], *early_got = hold(
        ordered[0], ordered[1], second_sent[2], second_sent[3], *early_got
    )
    late_got = [lax.ppermute(second_sent[2 + i], "seq", routes[1 - i]) for i in range(2)]
    chunks = gather_pairs(bits, ordered)
    chunks[0], chunks[1], *late_got = hold(chunks[0], chunks[1], *late_got)
    second_got = [*early_got, *late_got]
    up_sum, down_sum = kernel_call(
        expert_last_kernel,
        [shape((1, 768, 384), F32), shape((1, 384, 768), F32)],
        [spots, parts, parts_got, *first_got, *second_got],
        "expert_last", 10**6,
        in_specs=[SM] + [HB] * 8,
        scratch=[
            pltpu.VMEM((2, 4, 768, 384), BF), pltpu.SemaphoreType.DMA((2, 3)), pltpu.SemaphoreType.DMA((2, 2)),
        ],
    )
    even = (1 - odd).astype(F32).reshape(1)
    input_grad = kernel_call(
        input_grad_kernel,
        [shape(flat, F32)],
        [
            even, attn_norm_gain, own_part, block_input.reshape(flat), from_one.reshape(flat),
            two_a.reshape(256, 768), two_b.reshape(256, 768), after_grad,
        ],
        "input_grad", 10**7,
        in_specs=[SM, VM] + [HB] * 6,
        scratch=[
            pltpu.VMEM(flat, F32), pltpu.VMEM(flat, BF), pltpu.VMEM(flat, BF), pltpu.VMEM(flat, BF),
            pltpu.VMEM(flat, F32), pltpu.SemaphoreType.DMA((6,)),
        ],
    )[0]
    moved = pair_moves(chunks, PAIRS_OF)
    moved[0], moved[1], input_grad, up_sum = hold(moved[0], moved[1], input_grad, up_sum)
    mine = [chunks[0], moved[0], chunks[1], moved[1]]
    swapped = [lax.ppermute(a, "seq", SWAP) for a in mine]
    sums = [shape((768, 2304), F32), shape((768, 768), F32)]
    landing = [
        pltpu.VMEM((HALF_ROWS, 256), BF), pltpu.VMEM((6, 768, 256), F32),
        pltpu.SemaphoreType.DMA((4,)), pltpu.SemaphoreType.DMA((6,)),
    ]
    qkv_half, proj_half, tail = kernel_call(
        finish_mine_kernel, sums + [shape((64, 256))], [spots, *mine], "finish_mine", 10**6,
        in_specs=[SM] + [HB] * 4, out_specs=[HB, HB, VM], scratch=landing,
    )
    line = shape((768,), F32)
    qkv_sum, proj_sum, *rest = kernel_call(
        finish_other_kernel,
        sums + [line] * 4 + [shape((16,), I32), shape((1, 1, 16), I32)],
        [spots, tail, *swapped, qkv_half, proj_half],
        "finish_other", 10**6,
        in_specs=[SM, VM] + [HB] * 6, out_specs=[HB] * 2 + [VM] * 6, scratch=landing,
        aliases={6: 0, 7: 1},
    )
    return (
        block_output.reshape(rows3),
        input_grad.reshape(rows3),
        rest[0],
        rest[1],
        qkv_sum,
        proj_sum,
        rest[2],
        rest[3],
        up_sum,
        down_sum,
        rest[4],
        rest[5],
    )


def solution(mesh):
    placed = (
        P("batch", "seq", None),
        P("batch", "seq"),
        P(),
        P("batch", None),
        P("batch", "seq"),
        P(),
        P(),
        P(),
        P(),
        P(),
        P(),
        P("batch", None, None),
        P("batch", None, None),
        P("batch", "seq", None),
    )
    return jax.shard_map(
        local,
        mesh=mesh,
        in_specs=placed,
        out_specs=(
            P("batch", "seq", None),
            P("batch", "seq", None),
            P(),
            P(),
            P(),
            P(),
            P(),
            P(),
            P("batch", None, "seq"),
            P("batch", "seq", None),
            P(),
            P("batch", "seq", None),
        ),
        check_vma=False,
    )
```

```python
import jax
import jax.numpy as jnp
from jax import lax
from jax.experimental import pallas as pl
from jax.experimental.pallas import tpu as pltpu
from jax.sharding import PartitionSpec as P

BF = jnp.bfloat16
F32 = jnp.float32
I32 = jnp.int32
EPS = 1e-05
MASKED = -1e30
HEADS = 12
HEAD_SIZE = 64
PAIRS = 6
CAP = 64
SWAP = [(i, i ^ 1) for i in range(8)]
UP_ONE = [(i, i + 1) for i in range(0, 8, 2)]
DOWN_ONE = [(i + 1, i) for i in range(0, 8, 2)]
AHEAD_TWO = [(i, i + 2) for i in range(6)]
BACK_TWO = [(i + 2, i) for i in range(6)]
HALF_ROWS = 4864
PIECE = HALF_ROWS // 4
VMEM_BYTES = 63 * 1024 * 1024 + 640 * 1024
GEMM_ROWS = 4608
VM = pl.BlockSpec(memory_space=pltpu.VMEM)
HB = pl.BlockSpec(memory_space=pl.ANY)
SM = pl.BlockSpec(memory_space=pltpu.SMEM)


def shape(dims, kind=BF):
    return jax.ShapeDtypeStruct(dims, kind)


def kernel_call(body, outs, args, name, flops, grid=None, in_specs=None, out_specs=None, scratch=(), aliases=None):
    moved = sum(a.size * a.dtype.itemsize for a in args) + sum(
        o.size * o.dtype.itemsize for o in outs
    )
    extra = {} if grid is None else {"grid": grid}
    return pl.pallas_call(
        body,
        out_shape=outs,
        in_specs=in_specs or [VM] * len(args),
        out_specs=out_specs or [VM] * len(outs),
        scratch_shapes=list(scratch),
        compiler_params=pltpu.CompilerParams(vmem_limit_bytes=VMEM_BYTES),
        cost_estimate=pl.CostEstimate(flops=flops, bytes_accessed=moved, transcendentals=0),
        name=name,
        input_output_aliases=aliases or {},
        **extra,
    )(*args)


def nn(a, b):
    return jnp.dot(a, b, preferred_element_type=F32)


def nt(a, b):
    return lax.dot_general(a, b, (((1,), (1,)), ((), ())), preferred_element_type=F32)


def tn(a, b):
    return lax.dot_general(a, b, (((0,), (0,)), ((), ())), preferred_element_type=F32)


def iota(dims, axis):
    return lax.broadcasted_iota(I32, dims, axis)


def row(ref):
    return ref[...].reshape(1, 768)


def column(line):
    return jnp.broadcast_to(line, (128, line.shape[1])).T[:, 0:1]


def flat_line(ref):
    return jnp.concatenate([ref[i : i + 1, :] for i in range(4)], axis=1).astype(F32)


def norm_parts(values):
    centred = values - jnp.mean(values, axis=-1, keepdims=True)
    inverse = lax.rsqrt(jnp.mean(centred * centred, axis=-1, keepdims=True) + EPS)
    return centred * inverse, inverse


def norm_back(grad, gain, unit, inverse):
    t = grad * gain
    return inverse * (
        t - jnp.mean(t, axis=-1, keepdims=True) - unit * jnp.mean(t * unit, axis=-1, keepdims=True)
    )


def entry_kernel(
    place, tok, table, turn, gain, bias, x, grad, weight, target_out, tally, sent, unit_out, query, keyval,
    xv, gv, w, sv, uv, rv, kv, in_sems, out_sems,
):
    loads = copies([x, grad, weight], [xv, gv, w], in_sems)
    ids = jnp.concatenate([tok[i : i + 1, :] for i in range(4)], axis=1)
    live = flat_line(turn)
    high, low = ids >> 7, ids & 127
    picked = tn(table[...].astype(F32).astype(BF), (iota((64, 512), 0) == high).astype(F32).astype(BF))
    chosen = jnp.sum(jnp.where(iota((128, 512), 0) == low, picked, 0.0), axis=0, keepdims=True)
    member = (iota((16, 512), 0) == chosen.astype(I32)).astype(F32)
    earlier = (iota((512, 512), 0) < iota((512, 512), 1)).astype(F32).astype(BF)
    before = nn(member.astype(BF), earlier)
    slot = jnp.sum(before * member, axis=0, keepdims=True)
    target = (chosen * CAP + slot).astype(I32)
    target_out[...] = jnp.broadcast_to(target, (8, 512))
    counts = jnp.sum(member, axis=1, keepdims=True)
    tally[...] = jnp.where(iota((16, 128), 1) == place[0] * 16 + place[1], counts, 0.0)
    stores = []

    def store(source, goal):
        stores.append(pltpu.make_async_copy(source, goal, out_sems.at[len(stores)]))
        stores[-1].start()

    loads[0].wait()
    unit, _ = norm_parts(xv[...].astype(F32))
    uv[...] = unit.astype(BF)
    store(uv, unit_out)
    rows = (unit * row(gain) + row(bias)).astype(BF)
    loads[1].wait()
    for i in range(2):
        placing = jnp.where(iota((512, 512), 0) + 512 * i == target, live, 0.0).astype(BF)
        sv[512 * i : 512 * (i + 1), :] = nn(placing, gv[...]).astype(BF)
    store(sv, sent)
    loads[2].wait()
    rv[...] = rows

    def block(j, carry):
        kv[j] = nn(rv[...], w[:, cols_at(j, 768)]).astype(BF)
        return carry

    lax.fori_loop(0, 3, block, 0)
    store(kv.at[0], query)
    store(kv.at[1], keyval.at[:, 0:768])
    store(kv.at[2], keyval.at[:, 768:1536])
    for copy in stores:
        copy.wait()


def head_masks(scale):
    lane = iota((1, 128), 1)
    first = jnp.where(lane < 64, scale, 0.0).astype(BF)
    second = jnp.where(lane >= 64, scale, 0.0).astype(BF)
    return first, second


def stack_heads(pair, masks):
    return jnp.concatenate([pair * masks[0], pair * masks[1]], axis=0)


def window_bias(place, lengths, r):
    lane = iota((1, 128), 1) + place[0] * 128
    end, start = jnp.int32(0), jnp.zeros((1, 128), I32)
    for j in range(8):
        end = end + lengths[r, j]
        start = jnp.where(end <= lane, end, start)
    start = start - (place[0] - 2) * 128
    key = iota((384, 128), 0)
    allowed = (key >= start) & (key <= iota((384, 128), 1) + 256)
    half = jnp.where(allowed, 0.0, MASKED)
    return jnp.concatenate([half, half], axis=1)


def join_heads(both):
    one = jnp.where(iota((128, 128), 0) < 64, both[:, :128], both[:, 128:])
    return one.T


def copies(sources, targets, sems):
    out = [
        pltpu.make_async_copy(a, b, sems.at[i]) for i, (a, b) in enumerate(zip(sources, targets))
    ]
    for copy in out:
        copy.start()
    return out


def lanes_of(p, offset=0):
    return slice(offset + 128 * p, offset + 128 * (p + 1))


def forward_kernel(
    place, lengths, gain, bias, gain_two, bias_two, target,
    behind_two, early, late, weight, keyval, query, x, proj,
    unit_halo, context_out, attended, log_out, after_out, sent,
    b2, e1, l1, w, q, xv, wp, units, rows_in, context, att, aft, snd, in_sems, out_sems,
):
    loads = copies(
        [behind_two, early, late, weight, keyval, query, x, proj],
        [b2, e1, l1, w, context.at[:, 256:384, :], q, xv, wp],
        in_sems,
    )
    scales = head_masks(HEAD_SIZE ** (-0.5))
    for copy in loads[:3]:
        copy.wait()

    def norm_row(r, carry):
        halo = jnp.concatenate([b2[r], e1[r] + l1[r]], axis=0).astype(F32)
        unit, _ = norm_parts(halo)
        units[r] = unit.astype(BF)
        rows_in[r] = (unit * row(gain) + row(bias)).astype(BF)
        return carry

    lax.fori_loop(0, 4, norm_row, 0)
    unit_copy = pltpu.make_async_copy(units, unit_halo, out_sems.at[0])
    unit_copy.start()
    loads[3].wait()

    def keyval_block(j, carry):
        source = pl.ds(pl.multiple_of(768 + 512 * j, 256), 512)
        fresh = nn(rows_in[...].reshape(1024, 768), w[:, source])
        context[:, 0:256, cols_at(j, 512)] = fresh.astype(BF).reshape(4, 256, 512)
        return carry

    lax.fori_loop(0, 3, keyval_block, 0)
    for copy in loads[4:6]:
        copy.wait()
    context_copy = pltpu.make_async_copy(context, context_out, out_sems.at[1])
    context_copy.start()

    def one_row(r, carry):
        mask = window_bias(place, lengths, r)
        pairs = range(PAIRS)
        stacked = [stack_heads(q[r, :, lanes_of(p)], scales) for p in pairs]
        scores = [nt(context[r, :, lanes_of(p)], stacked[p]) + mask for p in pairs]
        tops = [jnp.max(a, axis=0, keepdims=True) for a in scores]
        weights = [jnp.exp(a - t) for a, t in zip(scores, tops)]
        totals = [jnp.sum(a, axis=0, keepdims=True) for a in weights]
        shares = [(a * (1.0 / t)).astype(BF) for a, t in zip(weights, totals)]
        mixed = [tn(context[r, :, lanes_of(p, 768)], shares[p]) for p in pairs]
        for p in pairs:
            log_out[r, p : p + 1, :] = tops[p] + jnp.log(totals[p])
            att[r, :, lanes_of(p)] = join_heads(mixed[p]).astype(BF)
        return carry

    lax.fori_loop(0, 4, one_row, 0)
    att_copy = pltpu.make_async_copy(att, attended, out_sems.at[2])
    att_copy.start()
    loads[6].wait()
    loads[7].wait()
    after = xv[...].reshape(512, 768).astype(F32) + nn(att[...].reshape(512, 768), wp[...])
    aft[...] = after
    after_copy = pltpu.make_async_copy(aft, after_out, out_sems.at[3])
    after_copy.start()
    unit, _ = norm_parts(after)
    rows = (unit * row(gain_two) + row(bias_two)).astype(BF)
    sends = []
    for i in range(2):
        part = slice(512 * i, 512 * (i + 1))
        placing = (iota((512, 512), 0) + 512 * i == target[0:1, :]).astype(F32).astype(BF)
        snd[part, :] = nn(placing, rows).astype(BF)
        sends.append(pltpu.make_async_copy(snd.at[part], sent.at[part], out_sems.at[4 + i]))
        sends[-1].start()
    for copy in [unit_copy, context_copy, att_copy, after_copy] + sends:
        copy.wait()


def active_grad_kernel(grad, down, out):
    out[0] = nt(grad[...], down[...]).astype(BF)


def gelu_both(v):
    c = 0.7978845608028654
    square = v * v
    p = c + (c * 0.044715) * square
    gate = 0.5 + 0.5 * jnp.tanh(v * p)
    value = v * gate
    return value, gate + value * (1.0 - gate) * (6.0 * p - 4.0 * c)


def expert_kernel(x, up, raw, active, hidden_grad, back, total):
    step = pl.program_id(0)

    @pl.when(step == 0)
    def _():
        total[...] = jnp.zeros_like(total)

    parts = [slice(256 * r, 256 * (r + 1)) for r in range(4)]
    hidden = [nn(x[rows, :], up[...]) for rows in parts]
    lows = []
    for rows, v in zip(parts, hidden):
        value, slope = gelu_both(v)
        active[0, rows, :] = value.astype(BF)
        low = (raw[0, rows, :].astype(F32) * slope).astype(BF)
        hidden_grad[0, rows, :] = low
        lows.append(low)
    for rows, low in zip(parts, lows):
        total[rows, :] += nt(low, up[...])

    @pl.when(step == pl.num_programs(0) - 1)
    def _():
        back[...] = total[...].astype(BF)


def turn_kernel(unit, unit_halo, grad, out, grad_t):
    out[0:768, 0:512] = unit[...].T
    out[0:768, 512:1536] = unit_halo[...].T
    out[768:784, :] = jnp.ones((16, 1536), BF)
    grad_t[...] = grad[...].T


def weight_kernel(place, x, grad_t, active, hidden_grad, down, out, mine, away, x_t, total):
    step = pl.program_id(0)

    @pl.when(step == 0)
    def _():
        total[...] = jnp.zeros_like(total)
        x_t[...] = x[...].T

    total[...] += nn(active[0], down[...])
    one = nn(x_t[...], hidden_grad[0])
    two = nn(grad_t[...], active[0])
    even = place[0] % 2 == 0
    for i, both in enumerate([one, two]):
        mine[0, i] = jnp.where(even, both[:, :384], both[:, 384:]).astype(BF)
        away[0, i] = jnp.where(even, both[:, 384:], both[:, :384]).astype(BF)

    @pl.when(step == pl.num_programs(0) - 1)
    def _():
        out[...] = total[...].astype(BF)


def output_kernel(after, target, returned, out):
    placing = (iota((512, 1024), 1).astype(F32) == column(target[0:1, :].astype(F32))).astype(F32).astype(BF)
    out[...] = (after[...] + nn(placing, returned[...])).astype(BF)


def cols_at(j, size=256):
    return pl.ds(pl.multiple_of(size * j, size), size)


def fill_halves(
    turned, query_grad, context_grad, weight, gain, bias, proj_part, terms_two, tally,
    out, gain_wide, bias_wide, gain_sum, bias_sum,
):
    gain_wide[...] = jnp.broadcast_to(row(gain), (256, 768)).T
    bias_wide[...] = jnp.broadcast_to(row(bias), (256, 768)).T

    def finish(block, both):
        body, sums = both[0:768], both[768:769]
        half, step = block // 6, block % 6
        out[half, 768 * step : 768 * (step + 1), :] = (
            gain_wide[...] * body + bias_wide[...] * sums
        ).astype(BF)
        wide = weight[:, 256 * block : 256 * (block + 1)].astype(F32)
        if block == 0:
            gain_sum[...] = wide * body
            bias_sum[...] = wide * sums
        else:
            gain_sum[...] += wide * body
            bias_sum[...] += wide * sums

    for j in range(3):
        finish(j, nn(turned[:, 0:512], query_grad[:, 256 * j : 256 * (j + 1)]))
        out[1, 768 * (3 + j) : 768 * (4 + j), :] = proj_part[j]
    for j in range(6):
        finish(3 + j, nn(turned[...], context_grad[:, 256 * j : 256 * (j + 1)]))

    columns = jnp.concatenate(
        [
            jnp.broadcast_to(jnp.sum(gain_sum[...], axis=1, keepdims=True), (768, 128)),
            jnp.broadcast_to(jnp.sum(bias_sum[...], axis=1, keepdims=True), (768, 128)),
        ],
        axis=1,
    ).T
    out[:, GEMM_ROWS:, :] = jnp.zeros((2, HALF_ROWS - GEMM_ROWS, 256), BF)
    for t in range(3):
        lanes = slice(256 * t, 256 * (t + 1))
        block = jnp.concatenate(
            [columns[0:1, lanes], columns[128:129, lanes], terms_two[:, lanes], jnp.zeros((12, 256), F32)],
            axis=0,
        )
        out[0, GEMM_ROWS + 16 * t : GEMM_ROWS + 16 * t + 16, :] = block.astype(BF)
    out[0, GEMM_ROWS + 48 : GEMM_ROWS + 64, 0:128] = tally[...].astype(BF)


def backward_kernel(
    place, lengths, gain_two, gain, bias, target, turn, log_total, tally,
    back, after, grad, proj, attended, query, context, turned, weight,
    after_grad, query_grad, own_grad, input_two, input_one, keep, away,
    bk, af, gr, wp, att, q, ctx, tu, w, ag, do, dq, cg, pp, ip, out,
    gain_wide, bias_wide, gain_sum, bias_sum, terms, in_sems, out_sems,
):
    loads = copies(
        [back, after, grad, proj, attended, query, context, turned, weight],
        [bk, af, gr, wp, att, q, ctx, tu, w],
        in_sems,
    )
    scales = head_masks(HEAD_SIZE ** (-0.5))
    ones = head_masks(1.0)
    placing = (iota((512, 1024), 1).astype(F32) == column(target[0:1, :].astype(F32))).astype(F32).astype(BF)
    live = column(flat_line(turn))
    loads[0].wait()
    normed_grad = nn(placing, bk[...])
    loads[1].wait()
    unit, inverse = norm_parts(af[...])
    terms[0:1, :] = jnp.sum(normed_grad * unit, axis=0, keepdims=True)
    terms[1:2, :] = jnp.sum(normed_grad, axis=0, keepdims=True)
    loads[2].wait()
    total = gr[...].astype(F32) * live + norm_back(normed_grad, row(gain_two), unit, inverse)
    ag[...] = total
    stores = [pltpu.make_async_copy(ag, after_grad, out_sems.at[0])]
    stores[0].start()
    low = total.astype(BF)
    loads[3].wait()
    do[...] = nt(low, wp[...]).astype(BF).reshape(4, 128, 768)
    loads[4].wait()
    mixed = nn(att[...].T, low).astype(BF)
    for j in range(3):
        pp[j] = mixed[:, 256 * j : 256 * (j + 1)]
    loads[5].wait()
    loads[6].wait()

    def one_row(r, carry):
        mask = window_bias(place, lengths, r)
        pairs = range(PAIRS)
        stacked = [stack_heads(q[r, :, lanes_of(p)], scales) for p in pairs]
        grads = [stack_heads(do[r, :, lanes_of(p)], ones) for p in pairs]
        scores = [nt(ctx[r, :, lanes_of(p)], stacked[p]) for p in pairs]
        share_grads = [nt(ctx[r, :, lanes_of(p, 768)], grads[p]) for p in pairs]
        shares = [jnp.exp(scores[p] + mask - log_total[r, p : p + 1, :]) for p in pairs]
        sums = [jnp.sum(a * b, axis=0, keepdims=True) for a, b in zip(shares, share_grads)]
        score_grads = [(a * (b - c)).astype(BF) for a, b, c in zip(shares, share_grads, sums)]
        key_grads = [nn(score_grads[p], stacked[p]).astype(BF) for p in pairs]
        value_grads = [nn(shares[p].astype(BF), grads[p]).astype(BF) for p in pairs]
        turned_grads = [tn(ctx[r, :, lanes_of(p)], score_grads[p]) for p in pairs]
        halo = pl.ds(pl.multiple_of(512 + r * 256, 256), 256)
        own = pl.ds(pl.multiple_of(r * 128, 128), 128)
        for p in pairs:
            cg[halo, lanes_of(p)] = key_grads[p][:256]
            cg[own, lanes_of(p)] = key_grads[p][256:]
            cg[halo, lanes_of(p, 768)] = value_grads[p][:256]
            cg[own, lanes_of(p, 768)] = value_grads[p][256:]
            dq[own, lanes_of(p)] = (join_heads(turned_grads[p]) * HEAD_SIZE ** (-0.5)).astype(BF)
        return carry

    lax.fori_loop(0, 4, one_row, 0)
    loads[7].wait()
    loads[8].wait()

    def store(source, target):
        stores.append(pltpu.make_async_copy(source, target, out_sems.at[len(stores)]))
        stores[-1].start()

    store(dq, query_grad)
    store(cg.at[0:512], own_grad)
    ip[...] = nt(cg[512:1536, :], w[:, 768:]).astype(BF).reshape(4, 256, 768)
    store(ip.at[:, 0:128], input_two)
    store(ip.at[:, 128:256], input_one)
    fill_halves(
        tu, dq, cg, w, gain, bias, pp, terms, tally, out, gain_wide, bias_wide, gain_sum, bias_sum
    )
    core = place[0] % 2

    @pl.when(core == 0)
    def _():
        pltpu.make_async_copy(out.at[0], keep, out_sems.at[5]).start()
        pltpu.make_async_copy(out.at[1], away, out_sems.at[6]).start()

    @pl.when(core == 1)
    def _():
        pltpu.make_async_copy(out.at[1], keep, out_sems.at[5]).start()
        pltpu.make_async_copy(out.at[0], away, out_sems.at[6]).start()

    for copy in stores:
        copy.wait()
    pltpu.make_async_copy(out.at[0], keep, out_sems.at[5]).wait()
    pltpu.make_async_copy(out.at[1], away, out_sems.at[6]).wait()


def place_half(half, bits, pieces, qkv, proj, whole, stage, in_sems, sems):
    loads = []
    for i in range(2):
        for j in range(2):
            first = pl.multiple_of((2 * i + (bits[i] + j) % 2) * PIECE, PIECE)
            target = whole.at[pl.ds(first, PIECE)]
            loads.append(pltpu.make_async_copy(pieces[2 * i + j], target, in_sems.at[2 * i + j]))
            loads[-1].start()
    for copy in loads:
        copy.wait()
    for j in range(6):
        stage[j] = whole[768 * j : 768 * (j + 1), :].astype(F32)
        lanes = slice(256 * (j % 3), 256 * (j % 3 + 1))

        @pl.when(half == 0)
        def _():
            pltpu.make_async_copy(stage.at[j], qkv.at[:, 256 * j : 256 * (j + 1)], sems.at[j]).start()

        @pl.when(half == 1)
        def _():
            target = qkv.at[:, 1536 + 256 * j : 1792 + 256 * j] if j < 3 else proj.at[:, lanes]
            pltpu.make_async_copy(stage.at[j], target, sems.at[j]).start()

    for j in range(6):
        pltpu.make_async_copy(stage.at[j], proj.at[:, 0:256], sems.at[j]).wait()


def finish_mine_kernel(place, a, b, c, d, qkv, proj, tail, whole, stage, in_sems, sems):
    place_half(place[0], (place[2], place[3]), (a, b, c, d), qkv, proj, whole, stage, in_sems, sems)
    tail[...] = whole[GEMM_ROWS : GEMM_ROWS + 64, :]


def finish_other_kernel(
    place, tail, a, b, c, d, qkv_in, proj_in, qkv, proj, gain_one, bias_one, gain_two, bias_two, counts, received,
    whole, stage, in_sems, sems,
):
    place_half(1 - place[0], (place[4], place[5]), (a, b, c, d), qkv, proj, whole, stage, in_sems, sems)
    both = tail[...].astype(F32) + whole[GEMM_ROWS : GEMM_ROWS + 64, :].astype(F32)
    for i, out in enumerate([gain_one, bias_one, gain_two, bias_two]):
        line = jnp.concatenate([both[16 * t + i : 16 * t + i + 1, :] for t in range(3)], axis=1)
        out[...] = line.reshape(768)
    every = both[48:64, 0:128]
    counts[...] = nt(jnp.ones((8, 128), BF), every.astype(BF))[0:1, :].astype(I32).reshape(16)
    chosen = (iota((16, 128), 0) == place[1]) & ((iota((16, 128), 1) >> 4) == place[6])
    mine = jnp.where(chosen, every, 0.0).astype(BF)
    fold = ((iota((128, 16), 0) & 15) == iota((128, 16), 1)).astype(F32).astype(BF)
    received[0] = jnp.sum(nn(mine, fold), axis=0, keepdims=True).astype(I32)


def chunk_of(a, b):
    return 2 * b + (a + b) % 2


def add_chunks(plan, buffer, in_sems):
    loads = []
    for n, picks in enumerate(plan):
        for m, pick_ref in enumerate(picks):
            loads.append(pltpu.make_async_copy(pick_ref, buffer.at[n, m], in_sems.at[n, m]))
            loads[-1].start()
    return loads


def summed(buffer, n, count):
    total = buffer[n, 0].astype(F32)
    for m in range(1, count):
        total = total + buffer[n, m].astype(F32)
    return total


def expert_first_kernel(spots, own, got, one, two, buffer, made, in_sems, out_sems):
    a, b = spots[7], spots[8]
    wanted = [(chunk_of(1 - a, k), 0) for k in range(2)] + [(chunk_of(k, 1 - b), 1) for k in range(2)]
    plan = [[own.at[c, t], got.at[c, t]] for c, t in wanted]
    loads = add_chunks(plan, buffer, in_sems)
    stores = []
    for n in range(4):
        loads[2 * n].wait()
        loads[2 * n + 1].wait()
        made[n] = summed(buffer, n, 2).astype(BF)
        stores.append(pltpu.make_async_copy(made.at[n], (one, two)[n // 2].at[n % 2], out_sems.at[n]))
        stores[-1].start()
    for copy in stores:
        copy.wait()


def expert_second_kernel(spots, own, got, first, second, one, two, buffer, made, in_sems, out_sems):
    a, b = spots[7], spots[8]
    c, d = chunk_of(a, 1 - b), chunk_of(1 - a, b)
    plan = [
        [own.at[c, 0], got.at[c, 0], first.at[1 - b]],
        [own.at[d, 1], got.at[d, 1], second.at[1 - a]],
    ]
    loads = add_chunks(plan, buffer, in_sems)
    stores = []
    for n in range(2):
        for copy in loads[3 * n : 3 * n + 3]:
            copy.wait()
        made[n] = summed(buffer, n, 3).astype(BF)
        stores.append(pltpu.make_async_copy(made.at[n], (one, two)[n], out_sems.at[n]))
        stores[-1].start()
    for copy in stores:
        copy.wait()


def expert_last_kernel(spots, own, got, first, second, third, fourth, up, down, buffer, in_sems):
    a, b = spots[7], spots[8]
    c = chunk_of(a, b)
    plan = [
        [own.at[c, 0], got.at[c, 0], first.at[b], third],
        [own.at[c, 1], got.at[c, 1], second.at[a], fourth],
    ]
    loads = add_chunks(plan, buffer, in_sems)
    for copy in loads[:4]:
        copy.wait()
    up[0] = summed(buffer, 0, 4)
    for copy in loads[4:]:
        copy.wait()
    down[0] = summed(buffer, 1, 4).T


def input_own_kernel(query_grad, own_grad, weight, out, dq, og, w, in_sems):
    for copy in copies([weight, query_grad, own_grad], [w, dq, og], in_sems):
        copy.wait()
    out[...] = nt(dq[...], w[:, :768]) + nt(og[...], w[:, 768:])


def input_grad_kernel(
    even, gain, own, x, from_one, two_a, two_b, after_grad, out, ov, xv, one, two, ag, in_sems,
):
    loads = copies(
        [x, own, from_one, two_a, two_b, after_grad],
        [xv, ov, one, two.at[0:256], two.at[256:512], ag],
        in_sems,
    )
    loads[0].wait()
    unit, inverse = norm_parts(xv[...].astype(F32))
    for copy in loads[1:]:
        copy.wait()
    total = ov[...] + two[...].astype(F32) + even[0] * one[...].astype(F32)
    out[...] = ag[...] + norm_back(total, row(gain), unit, inverse)


PAIR_ONE = [b ^ 1 for b in range(4)]
PAIR_TWO = [b ^ 3 for b in range(4)]
PAIRS_OF = [PAIR_ONE, PAIR_TWO]
BOTH = ("batch", "seq")


def by_core(even_move, odd_move):
    pairs = []
    for b in range(16):
        for s in range(8):
            x, y = (even_move, odd_move)[s % 2](b & 3, b >> 2)
            pairs.append((b * 8 + s, (y * 4 + x) * 8 + s))
    return pairs


def first_pairs(pair):
    return by_core(lambda x, y: (pair[x], y), lambda x, y: (x, pair[y]))


def second_step(d):
    return by_core(lambda x, y: (x, (y + d) & 3), lambda x, y: ((x + d) & 3, y))


def along_z(d):
    return [(s, (s + 2 * d) & 7) for s in range(8)]


def pick(array, index):
    return lax.dynamic_index_in_dim(array, index, 0, keepdims=False)


def part_of(array, index):
    return lax.dynamic_index_in_dim(array, index % 4, 1, keepdims=False)


def bits_of(place):
    return [(place & 1) ^ (place >> 1), place >> 1]


def z_pairs(pair):
    return [(s, pair[s // 2] * 2 + s % 2) for s in range(8)]


def sum_start(bits, keep, got):
    def part(stream, bit):
        at = (stream * 2 + bit) * PIECE
        return rows_at(keep, at, PIECE).astype(F32) + rows_at(got, at, PIECE).astype(F32)

    return part, [part(i, 1 - bits[i]).astype(BF) for i in range(2)]


def pair_moves(data, pairs):
    return [lax.ppermute(a, BOTH, first_pairs(pair)) for a, pair in zip(data, pairs)]


def rows_at(array, at, size):
    return lax.dynamic_slice(array, (at, 0), (size, array.shape[1]))


def sum_middle(bits, part, moved):
    size = PIECE // 2
    sums = [part(i, bits[i]) + moved[i].astype(F32) for i in range(2)]
    sent = [rows_at(sums[i], (1 - bits[1 - i]) * size, size).astype(BF) for i in range(2)]
    return [rows_at(sums[i], bits[1 - i] * size, size) for i in range(2)], sent


def group(chunks):
    size, lanes = chunks[0].shape
    return jnp.stack(chunks).reshape(2, 4, size // 4, lanes)


def sum_across(place, grouped):
    total = part_of(grouped, place).astype(F32)
    for d in (2, 1, 3):
        total = total + lax.ppermute(part_of(grouped, place + d), BOTH, second_step(d)).astype(F32)
    return total.astype(BF)


def sum_along(whole):
    total = whole.astype(F32)
    for d in (2, 1, 3):
        total = total + lax.ppermute(whole, "seq", along_z(d)).astype(F32)
    return total.astype(BF)


def gather_across(place, piece):
    size, lanes = PIECE // 2, piece.shape[-1]
    parts = [piece] + [lax.ppermute(piece, BOTH, second_step(d)) for d in (1, 2, 3)]
    stack = jnp.stack(parts, axis=1)
    ordered = jnp.stack([part_of(stack, place - p + 4) for p in range(4)], axis=1).reshape(2, size, lanes)
    return [ordered[0], ordered[1]]


def gather_pairs(bits, ordered):
    moved = pair_moves(ordered, PAIRS_OF[::-1])
    return [
        jnp.where(bit == 0, jnp.stack([a, b]), jnp.stack([b, a])).reshape(PIECE, a.shape[1])
        for bit, a, b in zip(bits[::-1], ordered, moved)
    ]


def hold(*values):
    return lax.optimization_barrier(values)


def exchange(array):
    return lax.all_to_all(
        array.reshape(16, CAP, 768), "batch", split_axis=0, concat_axis=0, tiled=True
    ).reshape(1024, 768)


def local(
    block_input, token_ids, hash_table, doc_lengths, turn_mask, attn_norm_gain, attn_norm_bias,
    qkv_weight, proj_weight, ffn_norm_gain, ffn_norm_bias, expert_up, expert_down, out_grad,
):
    seq = lax.axis_index("seq")
    owner = lax.axis_index("batch")
    odd = seq % 2
    flat = (512, 768)
    rows3 = (4, 128, 768)
    place = jnp.stack([seq, owner]).astype(I32)
    up, down = expert_up[0], expert_down[0]

    behind_two = lax.ppermute(block_input, "seq", AHEAD_TWO)
    early = lax.ppermute(block_input, "seq", UP_ONE)

    table = jnp.pad(hash_table, (0, 8192 - 8008)).reshape(64, 128)
    target, tally, grad_sent, unit, query, keyval = kernel_call(
        entry_kernel,
        [
            shape((8, 512), I32), shape((16, 128), F32), shape((1024, 768)), shape(flat), shape(flat),
            shape((512, 1536)),
        ],
        [
            place, token_ids, table, turn_mask, attn_norm_gain, attn_norm_bias, block_input.reshape(flat),
            out_grad.reshape(flat), qkv_weight,
        ],
        "entry", 3 * 10**9,
        in_specs=[SM] + [VM] * 5 + [HB] * 3,
        out_specs=[VM] * 2 + [HB] * 4,
        scratch=[
            pltpu.VMEM(flat, BF), pltpu.VMEM(flat, BF), pltpu.VMEM((768, 2304), BF), pltpu.VMEM((1024, 768), BF),
            pltpu.VMEM(flat, BF), pltpu.VMEM(flat, BF), pltpu.VMEM((3, 512, 768), BF),
            pltpu.SemaphoreType.DMA((3,)), pltpu.SemaphoreType.DMA((5,)),
        ],
    )
    grad_rows = exchange(grad_sent)

    behind_two, query = hold(behind_two, query)
    late = lax.ppermute(behind_two, "seq", DOWN_ONE)
    query, keyval = query.reshape(rows3), keyval.reshape(4, 128, 1536)

    unit_halo, context, attended, log_total, after, rows_sent = kernel_call(
        forward_kernel,
        [
            shape((4, 256, 768)), shape((4, 384, 1536)), shape(rows3), shape((4, 8, 256), F32),
            shape(flat, F32), shape((1024, 768)),
        ],
        [
            place, doc_lengths, attn_norm_gain, attn_norm_bias, ffn_norm_gain, ffn_norm_bias, target,
            behind_two, early, late, qkv_weight, keyval, query, block_input, proj_weight,
        ],
        "forward", 10**9,
        in_specs=[SM] * 2 + [VM] * 5 + [HB] * 8,
        out_specs=[HB] * 3 + [VM] + [HB] * 2,
        scratch=[
            pltpu.VMEM(rows3, BF), pltpu.VMEM(rows3, BF), pltpu.VMEM(rows3, BF), pltpu.VMEM((768, 2304), BF),
            pltpu.VMEM(rows3, BF), pltpu.VMEM(rows3, BF), pltpu.VMEM((768, 768), BF),
            pltpu.VMEM((4, 256, 768), BF), pltpu.VMEM((4, 256, 768), BF), pltpu.VMEM((4, 384, 1536), BF),
            pltpu.VMEM(rows3, BF), pltpu.VMEM(flat, F32), pltpu.VMEM((1024, 768), BF),
            pltpu.SemaphoreType.DMA((8,)), pltpu.SemaphoreType.DMA((6,)),
        ],
    )
    rows = exchange(rows_sent)

    turned, grad_t = kernel_call(
        turn_kernel,
        [shape((784, 1536)), shape((768, 1024))],
        [unit, unit_halo.reshape(1024, 768), grad_rows],
        "turn", 10**6,
    )
    grad_rows, turned, grad_t = hold(grad_rows, turned, grad_t)
    tile = pl.BlockSpec((1, 1024, 768), lambda i: (i, 0, 0))
    tiled = shape((4, 1024, 768))
    whole = pl.BlockSpec((1024, 768), lambda i: (0, 0))
    raw = kernel_call(
        active_grad_kernel,
        [tiled],
        [grad_rows, down],
        "active_grad", 48 * 10**8,
        grid=(4,),
        in_specs=[whole, pl.BlockSpec((768, 768), lambda i: (i, 0))],
        out_specs=[tile],
    )[0]

    active, hidden_grad, back_sent = kernel_call(
        expert_kernel,
        [tiled, tiled, shape((1024, 768))],
        [rows, up, raw],
        "expert", 97 * 10**8,
        grid=(4,),
        in_specs=[whole, pl.BlockSpec((768, 768), lambda i: (0, i)), tile],
        out_specs=[tile, tile, whole],
        scratch=[pltpu.VMEM((1024, 768), F32)],
    )
    back = exchange(back_sent)

    result, parts, parts_away = kernel_call(
        weight_kernel,
        [shape((1024, 768)), shape((4, 2, 768, 384)), shape((4, 2, 768, 384))],
        [place, rows, grad_t, active, hidden_grad, down],
        "weights", 145 * 10**8,
        grid=(4,),
        in_specs=[
            SM,
            whole,
            pl.BlockSpec((768, 1024), lambda i: (0, 0)),
            tile,
            tile,
            pl.BlockSpec((768, 768), lambda i: (i, 0)),
        ],
        out_specs=[
            pl.BlockSpec((1024, 768), lambda i: (0, 0)),
            pl.BlockSpec((1, 2, 768, 384), lambda i: (i, 0, 0, 0)),
            pl.BlockSpec((1, 2, 768, 384), lambda i: (i, 0, 0, 0)),
        ],
        scratch=[pltpu.VMEM((768, 1024), BF), pltpu.VMEM((1024, 768), F32)],
    )
    returned = exchange(result)
    parts_away, back = hold(parts_away, back)
    parts_got = lax.ppermute(parts_away, "seq", SWAP)
    depth = seq // 2
    turn = jnp.where(odd == 0, owner // 4, owner % 4)
    bits = bits_of(jnp.where(odd == 0, owner % 4, owner // 4))
    spots = jnp.stack([odd, owner, *bits, *bits_of(turn), seq, *bits_of(depth)]).astype(I32)
    block = shape((768, 384))
    first_sent = kernel_call(
        expert_first_kernel, [shape((2, 768, 384))] * 2, [spots, parts, parts_got], "expert_first", 10**6,
        in_specs=[SM] + [HB] * 2, out_specs=[HB] * 2,
        scratch=[
            pltpu.VMEM((4, 2, 768, 384), BF), pltpu.VMEM((4, 768, 384), BF),
            pltpu.SemaphoreType.DMA((4, 2)), pltpu.SemaphoreType.DMA((4,)),
        ],
    )
    back, *first_sent = hold(back, *first_sent)
    routes = [z_pairs(pair) for pair in PAIRS_OF]
    first_got = [lax.ppermute(a, "seq", route) for a, route in zip(first_sent, routes)]

    after_grad, query_grad, own_grad, input_two, input_one, keep, away = kernel_call(
        backward_kernel,
        [
            shape(flat, F32), shape(flat), shape((512, 1536)), shape(rows3), shape(rows3),
            shape((HALF_ROWS, 256)), shape((HALF_ROWS, 256)),
        ],
        [
            place, doc_lengths, ffn_norm_gain, attn_norm_gain, attn_norm_bias, target, turn_mask, log_total, tally,
            back, after, out_grad.reshape(flat), proj_weight, attended.reshape(flat), query, context, turned,
            qkv_weight,
        ],
        "backward", 16 * 10**9,
        in_specs=[SM] * 2 + [VM] * 7 + [HB] * 9,
        out_specs=[HB] * 7,
        scratch=[
            pltpu.VMEM((1024, 768), BF), pltpu.VMEM(flat, F32), pltpu.VMEM(flat, BF), pltpu.VMEM((768, 768), BF),
            pltpu.VMEM(flat, BF), pltpu.VMEM(rows3, BF), pltpu.VMEM((4, 384, 1536), BF),
            pltpu.VMEM((784, 1536), BF), pltpu.VMEM((768, 2304), BF), pltpu.VMEM(flat, F32), pltpu.VMEM(rows3, BF),
            pltpu.VMEM(flat, BF), pltpu.VMEM((1536, 1536), BF), pltpu.VMEM((3, 768, 256), BF),
            pltpu.VMEM((4, 256, 768), BF), pltpu.VMEM((2, HALF_ROWS, 256), BF),
            pltpu.VMEM((768, 256), F32), pltpu.VMEM((768, 256), F32), pltpu.VMEM((768, 256), F32),
            pltpu.VMEM((768, 256), F32), pltpu.VMEM((2, 768), F32),
            pltpu.SemaphoreType.DMA((9,)), pltpu.SemaphoreType.DMA((7,)),
        ],
    )
    away, returned, *first_got = hold(away, returned, *first_got)
    got = lax.ppermute(away, "seq", SWAP)
    from_one = lax.ppermute(input_one, "seq", SWAP)
    second_sent = kernel_call(
        expert_second_kernel, [block] * 2, [spots, parts, parts_got, *first_got], "expert_second", 10**6,
        in_specs=[SM] + [HB] * 4, out_specs=[HB] * 2,
        scratch=[
            pltpu.VMEM((2, 3, 768, 384), BF), pltpu.VMEM((2, 768, 384), BF),
            pltpu.SemaphoreType.DMA((2, 3)), pltpu.SemaphoreType.DMA((2,)),
        ],
    )
    block_output = kernel_call(
        output_kernel, [shape(flat)], [after, target, returned], "output", 8 * 10**8
    )[0]
    got, from_one, block_output, *second_sent = hold(got, from_one, block_output, *second_sent)
    part, sent = sum_start(bits, keep, got)
    sent[0], sent[1], query_grad, *second_sent = hold(sent[0], sent[1], query_grad, *second_sent)

    moved = pair_moves(sent, PAIRS_OF)
    second_got = [lax.ppermute(second_sent[i], "seq", routes[1 - i]) for i in range(2)]
    own_part = kernel_call(
        input_own_kernel, [shape(flat, F32)], [query_grad, own_grad, qkv_weight], "input_own", 2 * 10**9,
        in_specs=[HB] * 3,
        scratch=[
            pltpu.VMEM(flat, BF), pltpu.VMEM((512, 1536), BF), pltpu.VMEM((768, 2304), BF),
            pltpu.SemaphoreType.DMA((3,)),
        ],
    )[0]
    moved[0], moved[1], own_part, *second_got = hold(moved[0], moved[1], own_part, *second_got)

    chunks, sent = sum_middle(bits, part, moved)
    sent[0], sent[1], *second_got = hold(sent[0], sent[1], *second_got)
    moved = pair_moves(sent, PAIRS_OF[::-1])
    up_sum, down_sum = kernel_call(
        expert_last_kernel,
        [shape((1, 768, 384), F32), shape((1, 384, 768), F32)],
        [spots, parts, parts_got, *first_got, *second_got],
        "expert_last", 10**6,
        in_specs=[SM] + [HB] * 6,
        scratch=[pltpu.VMEM((2, 4, 768, 384), BF), pltpu.SemaphoreType.DMA((2, 4))],
    )
    moved[0], moved[1], up_sum = hold(moved[0], moved[1], up_sum)
    chunks = [(a + b.astype(F32)).astype(BF) for a, b in zip(chunks, moved)]
    grouped = group(chunks)
    grouped, from_one = hold(grouped, from_one)
    passed = jnp.where(odd == 1, input_two + from_one, input_two)
    whole = sum_across(turn, grouped)
    whole, passed = hold(whole, passed)
    piece = sum_along(whole)
    piece, passed = hold(piece, passed)
    two_a = lax.ppermute(passed[0:2], "seq", BACK_TWO)
    ordered = gather_across(turn, piece)
    ordered[0], ordered[1], passed, two_a = hold(ordered[0], ordered[1], passed, two_a)
    two_b = lax.ppermute(passed[2:4], "seq", BACK_TWO)
    chunks = gather_pairs(bits, ordered)
    chunks[0], chunks[1], two_b = hold(chunks[0], chunks[1], two_b)
    even = (1 - odd).astype(F32).reshape(1)
    input_grad = kernel_call(
        input_grad_kernel,
        [shape(flat, F32)],
        [
            even, attn_norm_gain, own_part, block_input.reshape(flat), from_one.reshape(flat),
            two_a.reshape(256, 768), two_b.reshape(256, 768), after_grad,
        ],
        "input_grad", 10**7,
        in_specs=[SM, VM] + [HB] * 6,
        scratch=[
            pltpu.VMEM(flat, F32), pltpu.VMEM(flat, BF), pltpu.VMEM(flat, BF), pltpu.VMEM(flat, BF),
            pltpu.VMEM(flat, F32), pltpu.SemaphoreType.DMA((6,)),
        ],
    )[0]
    moved = pair_moves(chunks, PAIRS_OF)
    moved[0], moved[1], input_grad = hold(moved[0], moved[1], input_grad)
    mine = [chunks[0], moved[0], chunks[1], moved[1]]
    swapped = [lax.ppermute(a, "seq", SWAP) for a in mine]
    sums = [shape((768, 2304), F32), shape((768, 768), F32)]
    landing = [
        pltpu.VMEM((HALF_ROWS, 256), BF), pltpu.VMEM((6, 768, 256), F32),
        pltpu.SemaphoreType.DMA((4,)), pltpu.SemaphoreType.DMA((6,)),
    ]
    qkv_half, proj_half, tail = kernel_call(
        finish_mine_kernel, sums + [shape((64, 256))], [spots, *mine], "finish_mine", 10**6,
        in_specs=[SM] + [HB] * 4, out_specs=[HB, HB, VM], scratch=landing,
    )
    line = shape((768,), F32)
    qkv_sum, proj_sum, *rest = kernel_call(
        finish_other_kernel,
        sums + [line] * 4 + [shape((16,), I32), shape((1, 1, 16), I32)],
        [spots, tail, *swapped, qkv_half, proj_half],
        "finish_other", 10**6,
        in_specs=[SM, VM] + [HB] * 6, out_specs=[HB] * 2 + [VM] * 6, scratch=landing,
        aliases={6: 0, 7: 1},
    )
    return (
        block_output.reshape(rows3),
        input_grad.reshape(rows3),
        rest[0],
        rest[1],
        qkv_sum,
        proj_sum,
        rest[2],
        rest[3],
        up_sum,
        down_sum,
        rest[4],
        rest[5],
    )


def solution(mesh):
    placed = (
        P("batch", "seq", None),
        P("batch", "seq"),
        P(),
        P("batch", None),
        P("batch", "seq"),
        P(),
        P(),
        P(),
        P(),
        P(),
        P(),
        P("batch", None, None),
        P("batch", None, None),
        P("batch", "seq", None),
    )
    return jax.shard_map(
        local,
        mesh=mesh,
        in_specs=placed,
        out_specs=(
            P("batch", "seq", None),
            P("batch", "seq", None),
            P(),
            P(),
            P(),
            P(),
            P(),
            P(),
            P("batch", None, "seq"),
            P("batch", "seq", None),
            P(),
            P("batch", "seq", None),
        ),
        check_vma=False,
    )
```

```python
import jax
import jax.numpy as jnp
from jax import lax
from jax.experimental import pallas as pl
from jax.experimental.pallas import tpu as pltpu
from jax.sharding import PartitionSpec as P

BF = jnp.bfloat16
F32 = jnp.float32
I32 = jnp.int32
EPS = 1e-05
MASKED = -1e30
HEADS = 12
HEAD_SIZE = 64
PAIRS = 6
CAP = 64
SWAP = [(i, i ^ 1) for i in range(8)]
UP_ONE = [(i, i + 1) for i in range(0, 8, 2)]
DOWN_ONE = [(i + 1, i) for i in range(0, 8, 2)]
AHEAD_TWO = [(i, i + 2) for i in range(6)]
BACK_TWO = [(i + 2, i) for i in range(6)]
HALF_ROWS = 4864
PIECE = HALF_ROWS // 4
RIDE = PIECE // 4
VMEM_BYTES = 63 * 1024 * 1024 + 640 * 1024
GEMM_ROWS = 4608
VM = pl.BlockSpec(memory_space=pltpu.VMEM)
HB = pl.BlockSpec(memory_space=pl.ANY)
SM = pl.BlockSpec(memory_space=pltpu.SMEM)


def shape(dims, kind=BF):
    return jax.ShapeDtypeStruct(dims, kind)


def kernel_call(body, outs, args, name, flops, grid=None, in_specs=None, out_specs=None, scratch=(), aliases=None):
    moved = sum(a.size * a.dtype.itemsize for a in args) + sum(
        o.size * o.dtype.itemsize for o in outs
    )
    extra = {} if grid is None else {"grid": grid}
    return pl.pallas_call(
        body,
        out_shape=outs,
        in_specs=in_specs or [VM] * len(args),
        out_specs=out_specs or [VM] * len(outs),
        scratch_shapes=list(scratch),
        compiler_params=pltpu.CompilerParams(vmem_limit_bytes=VMEM_BYTES),
        cost_estimate=pl.CostEstimate(flops=flops, bytes_accessed=moved, transcendentals=0),
        name=name,
        input_output_aliases=aliases or {},
        **extra,
    )(*args)


def nn(a, b):
    return jnp.dot(a, b, preferred_element_type=F32)


def nt(a, b):
    return lax.dot_general(a, b, (((1,), (1,)), ((), ())), preferred_element_type=F32)


def tn(a, b):
    return lax.dot_general(a, b, (((0,), (0,)), ((), ())), preferred_element_type=F32)


def iota(dims, axis):
    return lax.broadcasted_iota(I32, dims, axis)


def row(ref):
    return ref[...].reshape(1, 768)


def column(line):
    return jnp.broadcast_to(line, (128, line.shape[1])).T[:, 0:1]


def flat_line(ref):
    return jnp.concatenate([ref[i : i + 1, :] for i in range(4)], axis=1).astype(F32)


def norm_parts(values):
    centred = values - jnp.mean(values, axis=-1, keepdims=True)
    inverse = lax.rsqrt(jnp.mean(centred * centred, axis=-1, keepdims=True) + EPS)
    return centred * inverse, inverse


def norm_back(grad, gain, unit, inverse):
    t = grad * gain
    return inverse * (
        t - jnp.mean(t, axis=-1, keepdims=True) - unit * jnp.mean(t * unit, axis=-1, keepdims=True)
    )


def entry_kernel(
    place, tok, table, turn, gain, bias, x, grad, weight, target_out, tally, sent, unit_out, query, keyval,
    xv, gv, w, sv, uv, rv, kv, in_sems, out_sems,
):
    loads = copies([x, grad, weight], [xv, gv, w], in_sems)
    ids = jnp.concatenate([tok[i : i + 1, :] for i in range(4)], axis=1)
    live = flat_line(turn)
    high, low = ids >> 7, ids & 127
    picked = tn(table[...].astype(F32).astype(BF), (iota((64, 512), 0) == high).astype(F32).astype(BF))
    chosen = jnp.sum(jnp.where(iota((128, 512), 0) == low, picked, 0.0), axis=0, keepdims=True)
    member = (iota((16, 512), 0) == chosen.astype(I32)).astype(F32)
    earlier = (iota((512, 512), 0) < iota((512, 512), 1)).astype(F32).astype(BF)
    before = nn(member.astype(BF), earlier)
    slot = jnp.sum(before * member, axis=0, keepdims=True)
    target = (chosen * CAP + slot).astype(I32)
    target_out[...] = jnp.broadcast_to(target, (8, 512))
    counts = jnp.sum(member, axis=1, keepdims=True)
    tally[...] = jnp.where(iota((16, 128), 1) == place[0] * 16 + place[1], counts, 0.0)
    stores = []

    def store(source, goal):
        stores.append(pltpu.make_async_copy(source, goal, out_sems.at[len(stores)]))
        stores[-1].start()

    loads[0].wait()
    unit, _ = norm_parts(xv[...].astype(F32))
    uv[...] = unit.astype(BF)
    store(uv, unit_out)
    rows = (unit * row(gain) + row(bias)).astype(BF)
    loads[1].wait()
    for i in range(2):
        placing = jnp.where(iota((512, 512), 0) + 512 * i == target, live, 0.0).astype(BF)
        sv[512 * i : 512 * (i + 1), :] = nn(placing, gv[...]).astype(BF)
    store(sv, sent)
    loads[2].wait()
    rv[...] = rows

    def block(j, carry):
        kv[j] = nn(rv[...], w[:, cols_at(j, 768)]).astype(BF)
        return carry

    lax.fori_loop(0, 3, block, 0)
    store(kv.at[0], query)
    store(kv.at[1], keyval.at[:, 0:768])
    store(kv.at[2], keyval.at[:, 768:1536])
    for copy in stores:
        copy.wait()


def head_masks(scale):
    lane = iota((1, 128), 1)
    first = jnp.where(lane < 64, scale, 0.0).astype(BF)
    second = jnp.where(lane >= 64, scale, 0.0).astype(BF)
    return first, second


def stack_heads(pair, masks):
    return jnp.concatenate([pair * masks[0], pair * masks[1]], axis=0)


def window_bias(place, lengths, r):
    lane = iota((1, 128), 1) + place[0] * 128
    end, start = jnp.int32(0), jnp.zeros((1, 128), I32)
    for j in range(8):
        end = end + lengths[r, j]
        start = jnp.where(end <= lane, end, start)
    start = start - (place[0] - 2) * 128
    key = iota((384, 128), 0)
    allowed = (key >= start) & (key <= iota((384, 128), 1) + 256)
    half = jnp.where(allowed, 0.0, MASKED)
    return jnp.concatenate([half, half], axis=1)


def join_heads(both):
    one = jnp.where(iota((128, 128), 0) < 64, both[:, :128], both[:, 128:])
    return one.T


def copies(sources, targets, sems):
    out = [
        pltpu.make_async_copy(a, b, sems.at[i]) for i, (a, b) in enumerate(zip(sources, targets))
    ]
    for copy in out:
        copy.start()
    return out


def lanes_of(p, offset=0):
    return slice(offset + 128 * p, offset + 128 * (p + 1))


def forward_kernel(
    place, lengths, gain, bias, gain_two, bias_two, target,
    behind_two, early, late, weight, keyval, query, x, proj,
    unit_halo, context_out, attended, log_out, after_out, sent,
    b2, e1, l1, w, q, xv, wp, units, rows_in, context, att, aft, snd, in_sems, out_sems,
):
    loads = copies(
        [behind_two, early, late, weight, keyval, query, x, proj],
        [b2, e1, l1, w, context.at[:, 256:384, :], q, xv, wp],
        in_sems,
    )
    scales = head_masks(HEAD_SIZE ** (-0.5))
    for copy in loads[:3]:
        copy.wait()

    def norm_row(r, carry):
        halo = jnp.concatenate([b2[r], e1[r] + l1[r]], axis=0).astype(F32)
        unit, _ = norm_parts(halo)
        units[r] = unit.astype(BF)
        rows_in[r] = (unit * row(gain) + row(bias)).astype(BF)
        return carry

    lax.fori_loop(0, 4, norm_row, 0)
    unit_copy = pltpu.make_async_copy(units, unit_halo, out_sems.at[0])
    unit_copy.start()
    loads[3].wait()

    def keyval_block(j, carry):
        source = pl.ds(pl.multiple_of(768 + 512 * j, 256), 512)
        fresh = nn(rows_in[...].reshape(1024, 768), w[:, source])
        context[:, 0:256, cols_at(j, 512)] = fresh.astype(BF).reshape(4, 256, 512)
        return carry

    lax.fori_loop(0, 3, keyval_block, 0)
    for copy in loads[4:6]:
        copy.wait()
    context_copy = pltpu.make_async_copy(context, context_out, out_sems.at[1])
    context_copy.start()

    def one_row(r, carry):
        mask = window_bias(place, lengths, r)
        pairs = range(PAIRS)
        stacked = [stack_heads(q[r, :, lanes_of(p)], scales) for p in pairs]
        scores = [nt(context[r, :, lanes_of(p)], stacked[p]) + mask for p in pairs]
        tops = [jnp.max(a, axis=0, keepdims=True) for a in scores]
        weights = [jnp.exp(a - t) for a, t in zip(scores, tops)]
        totals = [jnp.sum(a, axis=0, keepdims=True) for a in weights]
        shares = [(a * (1.0 / t)).astype(BF) for a, t in zip(weights, totals)]
        mixed = [tn(context[r, :, lanes_of(p, 768)], shares[p]) for p in pairs]
        for p in pairs:
            log_out[r, p : p + 1, :] = tops[p] + jnp.log(totals[p])
            att[r, :, lanes_of(p)] = join_heads(mixed[p]).astype(BF)
        return carry

    lax.fori_loop(0, 4, one_row, 0)
    att_copy = pltpu.make_async_copy(att, attended, out_sems.at[2])
    att_copy.start()
    loads[6].wait()
    loads[7].wait()
    after = xv[...].reshape(512, 768).astype(F32) + nn(att[...].reshape(512, 768), wp[...])
    aft[...] = after
    after_copy = pltpu.make_async_copy(aft, after_out, out_sems.at[3])
    after_copy.start()
    unit, _ = norm_parts(after)
    rows = (unit * row(gain_two) + row(bias_two)).astype(BF)
    sends = []
    for i in range(2):
        part = slice(512 * i, 512 * (i + 1))
        placing = (iota((512, 512), 0) + 512 * i == target[0:1, :]).astype(F32).astype(BF)
        snd[part, :] = nn(placing, rows).astype(BF)
        sends.append(pltpu.make_async_copy(snd.at[part], sent.at[part], out_sems.at[4 + i]))
        sends[-1].start()
    for copy in [unit_copy, context_copy, att_copy, after_copy] + sends:
        copy.wait()


def active_grad_kernel(grad, down, out):
    out[0] = nt(grad[...], down[...]).astype(BF)


def gelu_both(v):
    c = 0.7978845608028654
    square = v * v
    p = c + (c * 0.044715) * square
    gate = 0.5 + 0.5 * jnp.tanh(v * p)
    value = v * gate
    return value, gate + value * (1.0 - gate) * (6.0 * p - 4.0 * c)


def expert_kernel(x, up, raw, active, hidden_grad, back, total):
    step = pl.program_id(0)

    @pl.when(step == 0)
    def _():
        total[...] = jnp.zeros_like(total)

    parts = [slice(256 * r, 256 * (r + 1)) for r in range(4)]
    hidden = [nn(x[rows, :], up[...]) for rows in parts]
    lows = []
    for rows, v in zip(parts, hidden):
        value, slope = gelu_both(v)
        active[0, rows, :] = value.astype(BF)
        low = (raw[0, rows, :].astype(F32) * slope).astype(BF)
        hidden_grad[0, rows, :] = low
        lows.append(low)
    for rows, low in zip(parts, lows):
        total[rows, :] += nt(low, up[...])

    @pl.when(step == pl.num_programs(0) - 1)
    def _():
        back[...] = total[...].astype(BF)


def turn_kernel(unit, unit_halo, grad, out, grad_t):
    out[0:768, 0:512] = unit[...].T
    out[0:768, 512:1536] = unit_halo[...].T
    out[768:784, :] = jnp.ones((16, 1536), BF)
    grad_t[...] = grad[...].T


def weight_kernel(place, x, grad_t, active, hidden_grad, down, out, mine, away, x_t, total):
    step = pl.program_id(0)

    @pl.when(step == 0)
    def _():
        total[...] = jnp.zeros_like(total)
        x_t[...] = x[...].T

    total[...] += nn(active[0], down[...])
    one = nn(x_t[...], hidden_grad[0])
    two = nn(grad_t[...], active[0])
    even = place[0] % 2 == 0
    for i, both in enumerate([one, two]):
        mine[0, i] = jnp.where(even, both[:, :384], both[:, 384:]).astype(BF)
        away[0, i] = jnp.where(even, both[:, 384:], both[:, :384]).astype(BF)

    @pl.when(step == pl.num_programs(0) - 1)
    def _():
        out[...] = total[...].astype(BF)


def output_kernel(after, target, returned, out):
    placing = (iota((512, 1024), 1).astype(F32) == column(target[0:1, :].astype(F32))).astype(F32).astype(BF)
    out[...] = (after[...] + nn(placing, returned[...])).astype(BF)


def cols_at(j, size=256):
    return pl.ds(pl.multiple_of(size * j, size), size)


def fill_halves(
    turned, query_grad, context_grad, weight, gain, bias, proj_part, terms_two, tally,
    out, gain_wide, bias_wide, gain_sum, bias_sum, send,
):
    gain_wide[...] = jnp.broadcast_to(row(gain), (256, 768)).T
    bias_wide[...] = jnp.broadcast_to(row(bias), (256, 768)).T

    def finish(block, both):
        body, sums = both[0:768], both[768:769]
        half, step = block // 6, block % 6
        out[half, 768 * step : 768 * (step + 1), :] = (
            gain_wide[...] * body + bias_wide[...] * sums
        ).astype(BF)
        send(half, step)
        wide = weight[:, 256 * block : 256 * (block + 1)].astype(F32)
        if block == 0:
            gain_sum[...] = wide * body
            bias_sum[...] = wide * sums
        else:
            gain_sum[...] += wide * body
            bias_sum[...] += wide * sums

    for j in range(3):
        finish(j, nn(turned[:, 0:512], query_grad[:, 256 * j : 256 * (j + 1)]))
        out[1, 768 * (3 + j) : 768 * (4 + j), :] = proj_part[j]
        send(1, 3 + j)
    for j in range(6):
        finish(3 + j, nn(turned[...], context_grad[:, 256 * j : 256 * (j + 1)]))

    columns = jnp.concatenate(
        [
            jnp.broadcast_to(jnp.sum(gain_sum[...], axis=1, keepdims=True), (768, 128)),
            jnp.broadcast_to(jnp.sum(bias_sum[...], axis=1, keepdims=True), (768, 128)),
        ],
        axis=1,
    ).T
    out[:, GEMM_ROWS:, :] = jnp.zeros((2, HALF_ROWS - GEMM_ROWS, 256), BF)
    for t in range(3):
        lanes = slice(256 * t, 256 * (t + 1))
        block = jnp.concatenate(
            [columns[0:1, lanes], columns[128:129, lanes], terms_two[:, lanes], jnp.zeros((12, 256), F32)],
            axis=0,
        )
        out[0, GEMM_ROWS + 16 * t : GEMM_ROWS + 16 * t + 16, :] = block.astype(BF)
    out[0, GEMM_ROWS + 48 : GEMM_ROWS + 64, 0:128] = tally[...].astype(BF)
    send(0, 6)
    send(1, 6)


def backward_kernel(
    place, lengths, gain_two, gain, bias, target, turn, log_total, tally,
    back, after, grad, proj, attended, query, context, turned, weight,
    after_grad, query_grad, own_grad, input_two, input_one, keep, away,
    bk, af, gr, wp, att, q, ctx, tu, w, ag, do, dq, cg, pp, ip, out,
    gain_wide, bias_wide, gain_sum, bias_sum, terms, in_sems, out_sems, pay_sems,
):
    loads = copies(
        [back, after, grad, proj, attended, query, context, turned, weight],
        [bk, af, gr, wp, att, q, ctx, tu, w],
        in_sems,
    )
    scales = head_masks(HEAD_SIZE ** (-0.5))
    ones = head_masks(1.0)
    placing = (iota((512, 1024), 1).astype(F32) == column(target[0:1, :].astype(F32))).astype(F32).astype(BF)
    live = column(flat_line(turn))
    loads[0].wait()
    normed_grad = nn(placing, bk[...])
    loads[1].wait()
    unit, inverse = norm_parts(af[...])
    terms[0:1, :] = jnp.sum(normed_grad * unit, axis=0, keepdims=True)
    terms[1:2, :] = jnp.sum(normed_grad, axis=0, keepdims=True)
    loads[2].wait()
    total = gr[...].astype(F32) * live + norm_back(normed_grad, row(gain_two), unit, inverse)
    ag[...] = total
    stores = [pltpu.make_async_copy(ag, after_grad, out_sems.at[0])]
    stores[0].start()
    low = total.astype(BF)
    loads[3].wait()
    do[...] = nt(low, wp[...]).astype(BF).reshape(4, 128, 768)
    loads[4].wait()
    mixed = nn(att[...].T, low).astype(BF)
    for j in range(3):
        pp[j] = mixed[:, 256 * j : 256 * (j + 1)]
    loads[5].wait()
    loads[6].wait()

    def one_row(r, carry):
        mask = window_bias(place, lengths, r)
        pairs = range(PAIRS)
        stacked = [stack_heads(q[r, :, lanes_of(p)], scales) for p in pairs]
        grads = [stack_heads(do[r, :, lanes_of(p)], ones) for p in pairs]
        scores = [nt(ctx[r, :, lanes_of(p)], stacked[p]) for p in pairs]
        share_grads = [nt(ctx[r, :, lanes_of(p, 768)], grads[p]) for p in pairs]
        shares = [jnp.exp(scores[p] + mask - log_total[r, p : p + 1, :]) for p in pairs]
        sums = [jnp.sum(a * b, axis=0, keepdims=True) for a, b in zip(shares, share_grads)]
        score_grads = [(a * (b - c)).astype(BF) for a, b, c in zip(shares, share_grads, sums)]
        key_grads = [nn(score_grads[p], stacked[p]).astype(BF) for p in pairs]
        value_grads = [nn(shares[p].astype(BF), grads[p]).astype(BF) for p in pairs]
        turned_grads = [tn(ctx[r, :, lanes_of(p)], score_grads[p]) for p in pairs]
        halo = pl.ds(pl.multiple_of(512 + r * 256, 256), 256)
        own = pl.ds(pl.multiple_of(r * 128, 128), 128)
        for p in pairs:
            cg[halo, lanes_of(p)] = key_grads[p][:256]
            cg[own, lanes_of(p)] = key_grads[p][256:]
            cg[halo, lanes_of(p, 768)] = value_grads[p][:256]
            cg[own, lanes_of(p, 768)] = value_grads[p][256:]
            dq[own, lanes_of(p)] = (join_heads(turned_grads[p]) * HEAD_SIZE ** (-0.5)).astype(BF)
        return carry

    lax.fori_loop(0, 4, one_row, 0)
    loads[7].wait()
    loads[8].wait()

    def store(source, target):
        stores.append(pltpu.make_async_copy(source, target, out_sems.at[len(stores)]))
        stores[-1].start()

    store(dq, query_grad)
    store(cg.at[0:512], own_grad)
    ip[...] = nt(cg[512:1536, :], w[:, 768:]).astype(BF).reshape(4, 256, 768)
    store(ip.at[:, 0:128], input_two)
    store(ip.at[:, 128:256], input_one)
    core = place[0] % 2

    def rows_of(step):
        return slice(768 * step, min(768 * (step + 1), HALF_ROWS))

    def send(half, step):
        for c in range(2):

            @pl.when(core == c)
            def _():
                target = keep if half == c else away
                pltpu.make_async_copy(
                    out.at[half, rows_of(step)], target.at[rows_of(step)], pay_sems.at[half, step]
                ).start()

    fill_halves(
        tu, dq, cg, w, gain, bias, pp, terms, tally, out, gain_wide, bias_wide, gain_sum, bias_sum, send
    )
    for copy in stores:
        copy.wait()
    for half in range(2):
        for step in range(7):
            pltpu.make_async_copy(
                out.at[half, rows_of(step)], keep.at[rows_of(step)], pay_sems.at[half, step]
            ).wait()


def place_half(half, bits, pieces, qkv, proj, whole, stage, in_sems, sems):
    loads = []
    for i in range(2):
        for j in range(2):
            first = pl.multiple_of((2 * i + (bits[i] + j) % 2) * PIECE, PIECE)
            target = whole.at[pl.ds(first, PIECE)]
            loads.append(pltpu.make_async_copy(pieces[2 * i + j], target, in_sems.at[2 * i + j]))
            loads[-1].start()
    for copy in loads:
        copy.wait()
    for j in range(6):
        stage[j] = whole[768 * j : 768 * (j + 1), :].astype(F32)
        lanes = slice(256 * (j % 3), 256 * (j % 3 + 1))

        @pl.when(half == 0)
        def _():
            pltpu.make_async_copy(stage.at[j], qkv.at[:, 256 * j : 256 * (j + 1)], sems.at[j]).start()

        @pl.when(half == 1)
        def _():
            target = qkv.at[:, 1536 + 256 * j : 1792 + 256 * j] if j < 3 else proj.at[:, lanes]
            pltpu.make_async_copy(stage.at[j], target, sems.at[j]).start()

    for j in range(6):
        pltpu.make_async_copy(stage.at[j], proj.at[:, 0:256], sems.at[j]).wait()


def finish_mine_kernel(place, a, b, c, d, qkv, proj, tail, whole, stage, in_sems, sems):
    place_half(place[0], (place[2], place[3]), (a, b, c, d), qkv, proj, whole, stage, in_sems, sems)
    tail[...] = whole[GEMM_ROWS : GEMM_ROWS + 64, :]


def finish_other_kernel(
    place, tail, a, b, c, d, qkv_in, proj_in, qkv, proj, gain_one, bias_one, gain_two, bias_two, counts, received,
    whole, stage, in_sems, sems,
):
    place_half(1 - place[0], (place[4], place[5]), (a, b, c, d), qkv, proj, whole, stage, in_sems, sems)
    both = tail[...].astype(F32) + whole[GEMM_ROWS : GEMM_ROWS + 64, :].astype(F32)
    for i, out in enumerate([gain_one, bias_one, gain_two, bias_two]):
        line = jnp.concatenate([both[16 * t + i : 16 * t + i + 1, :] for t in range(3)], axis=1)
        out[...] = line.reshape(768)
    every = both[48:64, 0:128]
    counts[...] = nt(jnp.ones((8, 128), BF), every.astype(BF))[0:1, :].astype(I32).reshape(16)
    chosen = (iota((16, 128), 0) == place[1]) & ((iota((16, 128), 1) >> 4) == place[6])
    mine = jnp.where(chosen, every, 0.0).astype(BF)
    fold = ((iota((128, 16), 0) & 15) == iota((128, 16), 1)).astype(F32).astype(BF)
    received[0] = jnp.sum(nn(mine, fold), axis=0, keepdims=True).astype(I32)


def chunk_of(a, b):
    return 2 * b + (a + b) % 2


def add_chunks(plan, buffer, in_sems):
    loads = []
    for n, picks in enumerate(plan):
        for m, pick_ref in enumerate(picks):
            loads.append(pltpu.make_async_copy(pick_ref, buffer.at[n, m], in_sems.at[n, m]))
            loads[-1].start()
    return loads


def summed(buffer, n, count):
    total = buffer[n, 0].astype(F32)
    for m in range(1, count):
        total = total + buffer[n, m].astype(F32)
    return total


def expert_first_kernel(spots, own, got, one, two, buffer, made, in_sems, out_sems):
    a, b = spots[7], spots[8]
    wanted = [(chunk_of(1 - a, k), 0) for k in range(2)] + [(chunk_of(k, 1 - b), 1) for k in range(2)]
    plan = [[own.at[c, t], got.at[c, t]] for c, t in wanted]
    loads = add_chunks(plan, buffer, in_sems)
    stores = []
    for n in range(4):
        loads[2 * n].wait()
        loads[2 * n + 1].wait()
        made[n] = summed(buffer, n, 2).astype(BF)
        stores.append(pltpu.make_async_copy(made.at[n], (one, two)[n // 2].at[n % 2], out_sems.at[n]))
        stores[-1].start()
    for copy in stores:
        copy.wait()


def expert_second_kernel(spots, own, got, first, second, one, two, buffer, made, in_sems, out_sems):
    a, b = spots[7], spots[8]
    c, d = chunk_of(a, 1 - b), chunk_of(1 - a, b)
    plan = [
        [own.at[c, 0], got.at[c, 0], first.at[1 - b]],
        [own.at[d, 1], got.at[d, 1], second.at[1 - a]],
    ]
    loads = add_chunks(plan, buffer, in_sems)
    stores = []
    for n in range(2):
        for copy in loads[3 * n : 3 * n + 3]:
            copy.wait()
        made[n] = summed(buffer, n, 3).astype(BF)
        stores.append(pltpu.make_async_copy(made.at[n], (one, two)[n], out_sems.at[n]))
        stores[-1].start()
    for copy in stores:
        copy.wait()


def expert_last_kernel(spots, own, got, first, second, third, fourth, up, down, buffer, in_sems):
    a, b = spots[7], spots[8]
    c = chunk_of(a, b)
    plan = [
        [own.at[c, 0], got.at[c, 0], first.at[b], third],
        [own.at[c, 1], got.at[c, 1], second.at[a], fourth],
    ]
    loads = add_chunks(plan, buffer, in_sems)
    for copy in loads[:4]:
        copy.wait()
    up[0] = summed(buffer, 0, 4)
    for copy in loads[4:]:
        copy.wait()
    down[0] = summed(buffer, 1, 4).T


def input_own_kernel(query_grad, own_grad, weight, out, dq, og, w, in_sems):
    for copy in copies([weight, query_grad, own_grad], [w, dq, og], in_sems):
        copy.wait()
    out[...] = nt(dq[...], w[:, :768]) + nt(og[...], w[:, 768:])


def input_grad_kernel(
    flags, gain, own, x, from_one, two_a, ride, after_grad, out, ov, xv, one, two, ag, in_sems,
):
    loads = copies(
        [x, own, from_one, two_a, after_grad] + [ride.at[RIDE + 256 * j : RIDE + 256 * (j + 1)] for j in range(3)],
        [xv, ov, one, two.at[0:256], ag] + [two.at[256:512, 256 * j : 256 * (j + 1)] for j in range(3)],
        in_sems,
    )
    loads[0].wait()
    unit, inverse = norm_parts(xv[...].astype(F32))
    for copy in loads[1:]:
        copy.wait()
    total = ov[...] + flags[1] * two[...].astype(F32) + flags[0] * one[...].astype(F32)
    out[...] = ag[...] + norm_back(total, row(gain), unit, inverse)


PAIR_ONE = [b ^ 1 for b in range(4)]
PAIR_TWO = [b ^ 3 for b in range(4)]
PAIRS_OF = [PAIR_ONE, PAIR_TWO]
BOTH = ("batch", "seq")


def by_core(even_move, odd_move):
    pairs = []
    for b in range(16):
        for s in range(8):
            x, y = (even_move, odd_move)[s % 2](b & 3, b >> 2)
            pairs.append((b * 8 + s, (y * 4 + x) * 8 + s))
    return pairs


def first_pairs(pair):
    return by_core(lambda x, y: (pair[x], y), lambda x, y: (x, pair[y]))


def second_step(d):
    return by_core(lambda x, y: (x, (y + d) & 3), lambda x, y: ((x + d) & 3, y))


def along_z(d):
    return [(s, (s + 2 * d) & 7) for s in range(8)]


def pick(array, index):
    return lax.dynamic_index_in_dim(array, index, 0, keepdims=False)


def part_of(array, index):
    return lax.dynamic_index_in_dim(array, index % 4, 1, keepdims=False)


def bits_of(place):
    return [(place & 1) ^ (place >> 1), place >> 1]


def z_pairs(pair):
    return [(s, pair[s // 2] * 2 + s % 2) for s in range(8)]


def sum_start(bits, keep, got):
    def part(stream, bit):
        at = (stream * 2 + bit) * PIECE
        return rows_at(keep, at, PIECE).astype(F32) + rows_at(got, at, PIECE).astype(F32)

    return part, [part(i, 1 - bits[i]).astype(BF) for i in range(2)]


def pair_moves(data, pairs):
    return [lax.ppermute(a, BOTH, first_pairs(pair)) for a, pair in zip(data, pairs)]


def rows_at(array, at, size):
    return lax.dynamic_slice(array, (at, 0), (size, array.shape[1]))


def sum_middle(bits, part, moved):
    size = PIECE // 2
    sums = [part(i, bits[i]) + moved[i].astype(F32) for i in range(2)]
    sent = [rows_at(sums[i], (1 - bits[1 - i]) * size, size).astype(BF) for i in range(2)]
    return [rows_at(sums[i], bits[1 - i] * size, size) for i in range(2)], sent


def group(chunks):
    size, lanes = chunks[0].shape
    return jnp.stack(chunks).reshape(2, 4, size // 4, lanes)


def sum_across(place, grouped):
    total = part_of(grouped, place).astype(F32)
    for d in (2, 1, 3):
        total = total + lax.ppermute(part_of(grouped, place + d), BOTH, second_step(d)).astype(F32)
    return total.astype(BF)


def sum_along(whole, extra):
    total = whole.astype(F32)
    for d in (2, 1):
        total = total + lax.ppermute(whole, "seq", along_z(d)).astype(F32)
    blocks = [extra[:, 256 * j : 256 * (j + 1)] for j in range(3)]
    ride = lax.ppermute(jnp.concatenate([whole.reshape(RIDE, 256), *blocks]), "seq", along_z(3))
    total = total + ride[:RIDE].reshape(whole.shape).astype(F32)
    return total.astype(BF), ride


def gather_across(place, piece):
    size, lanes = PIECE // 2, piece.shape[-1]
    parts = [piece] + [lax.ppermute(piece, BOTH, second_step(d)) for d in (1, 2, 3)]
    stack = jnp.stack(parts, axis=1)
    ordered = jnp.stack([part_of(stack, place - p + 4) for p in range(4)], axis=1).reshape(2, size, lanes)
    return [ordered[0], ordered[1]]


def gather_pairs(bits, ordered):
    moved = pair_moves(ordered, PAIRS_OF[::-1])
    return [
        jnp.where(bit == 0, jnp.stack([a, b]), jnp.stack([b, a])).reshape(PIECE, a.shape[1])
        for bit, a, b in zip(bits[::-1], ordered, moved)
    ]


def hold(*values):
    return lax.optimization_barrier(values)


def exchange(array):
    return lax.all_to_all(
        array.reshape(16, CAP, 768), "batch", split_axis=0, concat_axis=0, tiled=True
    ).reshape(1024, 768)


def local(
    block_input, token_ids, hash_table, doc_lengths, turn_mask, attn_norm_gain, attn_norm_bias,
    qkv_weight, proj_weight, ffn_norm_gain, ffn_norm_bias, expert_up, expert_down, out_grad,
):
    seq = lax.axis_index("seq")
    owner = lax.axis_index("batch")
    odd = seq % 2
    flat = (512, 768)
    rows3 = (4, 128, 768)
    place = jnp.stack([seq, owner]).astype(I32)
    up, down = expert_up[0], expert_down[0]

    behind_two = lax.ppermute(block_input, "seq", AHEAD_TWO)
    early = lax.ppermute(block_input, "seq", UP_ONE)

    table = jnp.pad(hash_table, (0, 8192 - 8008)).reshape(64, 128)
    target, tally, grad_sent, unit, query, keyval = kernel_call(
        entry_kernel,
        [
            shape((8, 512), I32), shape((16, 128), F32), shape((1024, 768)), shape(flat), shape(flat),
            shape((512, 1536)),
        ],
        [
            place, token_ids, table, turn_mask, attn_norm_gain, attn_norm_bias, block_input.reshape(flat),
            out_grad.reshape(flat), qkv_weight,
        ],
        "entry", 3 * 10**9,
        in_specs=[SM] + [VM] * 5 + [HB] * 3,
        out_specs=[VM] * 2 + [HB] * 4,
        scratch=[
            pltpu.VMEM(flat, BF), pltpu.VMEM(flat, BF), pltpu.VMEM((768, 2304), BF), pltpu.VMEM((1024, 768), BF),
            pltpu.VMEM(flat, BF), pltpu.VMEM(flat, BF), pltpu.VMEM((3, 512, 768), BF),
            pltpu.SemaphoreType.DMA((3,)), pltpu.SemaphoreType.DMA((5,)),
        ],
    )
    grad_rows = exchange(grad_sent)

    behind_two, query = hold(behind_two, query)
    late = lax.ppermute(behind_two, "seq", DOWN_ONE)
    query, keyval = query.reshape(rows3), keyval.reshape(4, 128, 1536)

    unit_halo, context, attended, log_total, after, rows_sent = kernel_call(
        forward_kernel,
        [
            shape((4, 256, 768)), shape((4, 384, 1536)), shape(rows3), shape((4, 8, 256), F32),
            shape(flat, F32), shape((1024, 768)),
        ],
        [
            place, doc_lengths, attn_norm_gain, attn_norm_bias, ffn_norm_gain, ffn_norm_bias, target,
            behind_two, early, late, qkv_weight, keyval, query, block_input, proj_weight,
        ],
        "forward", 10**9,
        in_specs=[SM] * 2 + [VM] * 5 + [HB] * 8,
        out_specs=[HB] * 3 + [VM] + [HB] * 2,
        scratch=[
            pltpu.VMEM(rows3, BF), pltpu.VMEM(rows3, BF), pltpu.VMEM(rows3, BF), pltpu.VMEM((768, 2304), BF),
            pltpu.VMEM(rows3, BF), pltpu.VMEM(rows3, BF), pltpu.VMEM((768, 768), BF),
            pltpu.VMEM((4, 256, 768), BF), pltpu.VMEM((4, 256, 768), BF), pltpu.VMEM((4, 384, 1536), BF),
            pltpu.VMEM(rows3, BF), pltpu.VMEM(flat, F32), pltpu.VMEM((1024, 768), BF),
            pltpu.SemaphoreType.DMA((8,)), pltpu.SemaphoreType.DMA((6,)),
        ],
    )
    rows = exchange(rows_sent)

    turned, grad_t = kernel_call(
        turn_kernel,
        [shape((784, 1536)), shape((768, 1024))],
        [unit, unit_halo.reshape(1024, 768), grad_rows],
        "turn", 10**6,
    )
    grad_rows, turned, grad_t = hold(grad_rows, turned, grad_t)
    tile = pl.BlockSpec((1, 1024, 768), lambda i: (i, 0, 0))
    tiled = shape((4, 1024, 768))
    whole = pl.BlockSpec((1024, 768), lambda i: (0, 0))
    raw = kernel_call(
        active_grad_kernel,
        [tiled],
        [grad_rows, down],
        "active_grad", 48 * 10**8,
        grid=(4,),
        in_specs=[whole, pl.BlockSpec((768, 768), lambda i: (i, 0))],
        out_specs=[tile],
    )[0]

    active, hidden_grad, back_sent = kernel_call(
        expert_kernel,
        [tiled, tiled, shape((1024, 768))],
        [rows, up, raw],
        "expert", 97 * 10**8,
        grid=(4,),
        in_specs=[whole, pl.BlockSpec((768, 768), lambda i: (0, i)), tile],
        out_specs=[tile, tile, whole],
        scratch=[pltpu.VMEM((1024, 768), F32)],
    )
    back = exchange(back_sent)

    result, parts, parts_away = kernel_call(
        weight_kernel,
        [shape((1024, 768)), shape((4, 2, 768, 384)), shape((4, 2, 768, 384))],
        [place, rows, grad_t, active, hidden_grad, down],
        "weights", 145 * 10**8,
        grid=(4,),
        in_specs=[
            SM,
            whole,
            pl.BlockSpec((768, 1024), lambda i: (0, 0)),
            tile,
            tile,
            pl.BlockSpec((768, 768), lambda i: (i, 0)),
        ],
        out_specs=[
            pl.BlockSpec((1024, 768), lambda i: (0, 0)),
            pl.BlockSpec((1, 2, 768, 384), lambda i: (i, 0, 0, 0)),
            pl.BlockSpec((1, 2, 768, 384), lambda i: (i, 0, 0, 0)),
        ],
        scratch=[pltpu.VMEM((768, 1024), BF), pltpu.VMEM((1024, 768), F32)],
    )
    returned = exchange(result)
    parts_away, back = hold(parts_away, back)
    parts_got = lax.ppermute(parts_away, "seq", SWAP)
    depth = seq // 2
    turn = jnp.where(odd == 0, owner // 4, owner % 4)
    bits = bits_of(jnp.where(odd == 0, owner % 4, owner // 4))
    spots = jnp.stack([odd, owner, *bits, *bits_of(turn), seq, *bits_of(depth)]).astype(I32)
    block = shape((768, 384))
    first_sent = kernel_call(
        expert_first_kernel, [shape((2, 768, 384))] * 2, [spots, parts, parts_got], "expert_first", 10**6,
        in_specs=[SM] + [HB] * 2, out_specs=[HB] * 2,
        scratch=[
            pltpu.VMEM((4, 2, 768, 384), BF), pltpu.VMEM((4, 768, 384), BF),
            pltpu.SemaphoreType.DMA((4, 2)), pltpu.SemaphoreType.DMA((4,)),
        ],
    )
    back, *first_sent = hold(back, *first_sent)
    routes = [z_pairs(pair) for pair in PAIRS_OF]
    first_got = [lax.ppermute(a, "seq", route) for a, route in zip(first_sent, routes)]

    after_grad, query_grad, own_grad, input_two, input_one, keep, away = kernel_call(
        backward_kernel,
        [
            shape(flat, F32), shape(flat), shape((512, 1536)), shape(rows3), shape(rows3),
            shape((HALF_ROWS, 256)), shape((HALF_ROWS, 256)),
        ],
        [
            place, doc_lengths, ffn_norm_gain, attn_norm_gain, attn_norm_bias, target, turn_mask, log_total, tally,
            back, after, out_grad.reshape(flat), proj_weight, attended.reshape(flat), query, context, turned,
            qkv_weight,
        ],
        "backward", 16 * 10**9,
        in_specs=[SM] * 2 + [VM] * 7 + [HB] * 9,
        out_specs=[HB] * 7,
        scratch=[
            pltpu.VMEM((1024, 768), BF), pltpu.VMEM(flat, F32), pltpu.VMEM(flat, BF), pltpu.VMEM((768, 768), BF),
            pltpu.VMEM(flat, BF), pltpu.VMEM(rows3, BF), pltpu.VMEM((4, 384, 1536), BF),
            pltpu.VMEM((784, 1536), BF), pltpu.VMEM((768, 2304), BF), pltpu.VMEM(flat, F32), pltpu.VMEM(rows3, BF),
            pltpu.VMEM(flat, BF), pltpu.VMEM((1536, 1536), BF), pltpu.VMEM((3, 768, 256), BF),
            pltpu.VMEM((4, 256, 768), BF), pltpu.VMEM((2, HALF_ROWS, 256), BF),
            pltpu.VMEM((768, 256), F32), pltpu.VMEM((768, 256), F32), pltpu.VMEM((768, 256), F32),
            pltpu.VMEM((768, 256), F32), pltpu.VMEM((2, 768), F32),
            pltpu.SemaphoreType.DMA((9,)), pltpu.SemaphoreType.DMA((5,)), pltpu.SemaphoreType.DMA((2, 7)),
        ],
    )
    away, returned, *first_got = hold(away, returned, *first_got)
    got = lax.ppermute(away, "seq", SWAP)
    from_one = lax.ppermute(input_one, "seq", SWAP)
    second_sent = kernel_call(
        expert_second_kernel, [block] * 2, [spots, parts, parts_got, *first_got], "expert_second", 10**6,
        in_specs=[SM] + [HB] * 4, out_specs=[HB] * 2,
        scratch=[
            pltpu.VMEM((2, 3, 768, 384), BF), pltpu.VMEM((2, 768, 384), BF),
            pltpu.SemaphoreType.DMA((2, 3)), pltpu.SemaphoreType.DMA((2,)),
        ],
    )
    passed = jnp.where(odd == 1, input_two + from_one, input_two)
    two_a = lax.ppermute(passed[0:2], "seq", BACK_TWO)
    got, *second_sent = hold(got, *second_sent)
    part, sent = sum_start(bits, keep, got)
    sent[0], sent[1], two_a, query_grad, *second_sent = hold(sent[0], sent[1], two_a, query_grad, *second_sent)

    moved = pair_moves(sent, PAIRS_OF)
    second_got = [lax.ppermute(second_sent[i], "seq", routes[1 - i]) for i in range(2)]
    own_part = kernel_call(
        input_own_kernel, [shape(flat, F32)], [query_grad, own_grad, qkv_weight], "input_own", 2 * 10**9,
        in_specs=[HB] * 3,
        scratch=[
            pltpu.VMEM(flat, BF), pltpu.VMEM((512, 1536), BF), pltpu.VMEM((768, 2304), BF),
            pltpu.SemaphoreType.DMA((3,)),
        ],
    )[0]
    moved[0], moved[1], own_part = hold(moved[0], moved[1], own_part)

    chunks, sent = sum_middle(bits, part, moved)
    sent[0], sent[1], *second_got = hold(sent[0], sent[1], *second_got)
    moved = pair_moves(sent, PAIRS_OF[::-1])
    up_sum, down_sum = kernel_call(
        expert_last_kernel,
        [shape((1, 768, 384), F32), shape((1, 384, 768), F32)],
        [spots, parts, parts_got, *first_got, *second_got],
        "expert_last", 10**6,
        in_specs=[SM] + [HB] * 6,
        scratch=[pltpu.VMEM((2, 4, 768, 384), BF), pltpu.SemaphoreType.DMA((2, 4))],
    )
    moved[0], moved[1], up_sum = hold(moved[0], moved[1], up_sum)
    chunks = [(a + b.astype(F32)).astype(BF) for a, b in zip(chunks, moved)]
    whole = sum_across(turn, group(chunks))
    whole, passed, returned = hold(whole, passed, returned)
    block_output = kernel_call(
        output_kernel, [shape(flat)], [after, target, returned], "output", 8 * 10**8
    )[0]
    piece, ride = sum_along(whole, passed[2:4].reshape(256, 768))
    piece, block_output = hold(piece, block_output)
    ordered = gather_across(turn, piece)
    chunks = gather_pairs(bits, ordered)
    flags = jnp.stack([1 - odd, (seq < 6).astype(I32)]).astype(F32)
    input_grad = kernel_call(
        input_grad_kernel,
        [shape(flat, F32)],
        [
            flags, attn_norm_gain, own_part, block_input.reshape(flat), from_one.reshape(flat),
            two_a.reshape(256, 768), ride, after_grad,
        ],
        "input_grad", 10**7,
        in_specs=[SM, VM] + [HB] * 6,
        scratch=[
            pltpu.VMEM(flat, F32), pltpu.VMEM(flat, BF), pltpu.VMEM(flat, BF), pltpu.VMEM(flat, BF),
            pltpu.VMEM(flat, F32), pltpu.SemaphoreType.DMA((8,)),
        ],
    )[0]
    moved = pair_moves(chunks, PAIRS_OF)
    moved[0], moved[1], input_grad = hold(moved[0], moved[1], input_grad)
    mine = [chunks[0], moved[0], chunks[1], moved[1]]
    swapped = [lax.ppermute(a, "seq", SWAP) for a in mine]
    sums = [shape((768, 2304), F32), shape((768, 768), F32)]
    landing = [
        pltpu.VMEM((HALF_ROWS, 256), BF), pltpu.VMEM((6, 768, 256), F32),
        pltpu.SemaphoreType.DMA((4,)), pltpu.SemaphoreType.DMA((6,)),
    ]
    qkv_half, proj_half, tail = kernel_call(
        finish_mine_kernel, sums + [shape((64, 256))], [spots, *mine], "finish_mine", 10**6,
        in_specs=[SM] + [HB] * 4, out_specs=[HB, HB, VM], scratch=landing,
    )
    line = shape((768,), F32)
    qkv_sum, proj_sum, *rest = kernel_call(
        finish_other_kernel,
        sums + [line] * 4 + [shape((16,), I32), shape((1, 1, 16), I32)],
        [spots, tail, *swapped, qkv_half, proj_half],
        "finish_other", 10**6,
        in_specs=[SM, VM] + [HB] * 6, out_specs=[HB] * 2 + [VM] * 6, scratch=landing,
        aliases={6: 0, 7: 1},
    )
    return (
        block_output.reshape(rows3),
        input_grad.reshape(rows3),
        rest[0],
        rest[1],
        qkv_sum,
        proj_sum,
        rest[2],
        rest[3],
        up_sum,
        down_sum,
        rest[4],
        rest[5],
    )


def solution(mesh):
    placed = (
        P("batch", "seq", None),
        P("batch", "seq"),
        P(),
        P("batch", None),
        P("batch", "seq"),
        P(),
        P(),
        P(),
        P(),
        P(),
        P(),
        P("batch", None, None),
        P("batch", None, None),
        P("batch", "seq", None),
    )
    return jax.shard_map(
        local,
        mesh=mesh,
        in_specs=placed,
        out_specs=(
            P("batch", "seq", None),
            P("batch", "seq", None),
            P(),
            P(),
            P(),
            P(),
            P(),
            P(),
            P("batch", None, "seq"),
            P("batch", "seq", None),
            P(),
            P("batch", "seq", None),
        ),
        check_vma=False,
    )
```

```python
import jax
import jax.numpy as jnp
from jax import lax
from jax.experimental import pallas as pl
from jax.experimental.pallas import tpu as pltpu
from jax.sharding import PartitionSpec as P

BF = jnp.bfloat16
F32 = jnp.float32
I32 = jnp.int32
EPS = 1e-05
MASKED = -1e30
HEADS = 12
HEAD_SIZE = 64
PAIRS = 6
CAP = 64
SWAP = [(i, i ^ 1) for i in range(8)]
UP_ONE = [(i, i + 1) for i in range(0, 8, 2)]
DOWN_ONE = [(i + 1, i) for i in range(0, 8, 2)]
AHEAD_TWO = [(i, i + 2) for i in range(6)]
BACK_TWO = [(i + 2, i) for i in range(6)]
HALF_ROWS = 4864
PIECE = HALF_ROWS // 4
VMEM_BYTES = 63 * 1024 * 1024 + 640 * 1024
GEMM_ROWS = 4608
VM = pl.BlockSpec(memory_space=pltpu.VMEM)
HB = pl.BlockSpec(memory_space=pl.ANY)
SM = pl.BlockSpec(memory_space=pltpu.SMEM)


def shape(dims, kind=BF):
    return jax.ShapeDtypeStruct(dims, kind)


def kernel_call(body, outs, args, name, flops, grid=None, in_specs=None, out_specs=None, scratch=(), aliases=None):
    moved = sum(a.size * a.dtype.itemsize for a in args) + sum(
        o.size * o.dtype.itemsize for o in outs
    )
    extra = {} if grid is None else {"grid": grid}
    return pl.pallas_call(
        body,
        out_shape=outs,
        in_specs=in_specs or [VM] * len(args),
        out_specs=out_specs or [VM] * len(outs),
        scratch_shapes=list(scratch),
        compiler_params=pltpu.CompilerParams(vmem_limit_bytes=VMEM_BYTES),
        cost_estimate=pl.CostEstimate(flops=flops, bytes_accessed=moved, transcendentals=0),
        name=name,
        input_output_aliases=aliases or {},
        **extra,
    )(*args)


def nn(a, b):
    return jnp.dot(a, b, preferred_element_type=F32)


def nt(a, b):
    return lax.dot_general(a, b, (((1,), (1,)), ((), ())), preferred_element_type=F32)


def tn(a, b):
    return lax.dot_general(a, b, (((0,), (0,)), ((), ())), preferred_element_type=F32)


def iota(dims, axis):
    return lax.broadcasted_iota(I32, dims, axis)


def row(ref):
    return ref[...].reshape(1, 768)


def column(line):
    return jnp.broadcast_to(line, (128, line.shape[1])).T[:, 0:1]


def flat_line(ref):
    return jnp.concatenate([ref[i : i + 1, :] for i in range(4)], axis=1).astype(F32)


def norm_parts(values):
    centred = values - jnp.mean(values, axis=-1, keepdims=True)
    inverse = lax.rsqrt(jnp.mean(centred * centred, axis=-1, keepdims=True) + EPS)
    return centred * inverse, inverse


def norm_back(grad, gain, unit, inverse):
    t = grad * gain
    return inverse * (
        t - jnp.mean(t, axis=-1, keepdims=True) - unit * jnp.mean(t * unit, axis=-1, keepdims=True)
    )


def entry_kernel(
    place, tok, table, turn, gain, bias, x, grad, weight, target_out, tally, sent, unit_out, query, keyval,
    xv, gv, w, sv, uv, rv, kv, in_sems, out_sems,
):
    loads = copies([x, grad, weight], [xv, gv, w], in_sems)
    ids = jnp.concatenate([tok[i : i + 1, :] for i in range(4)], axis=1)
    live = flat_line(turn)
    high, low = ids >> 7, ids & 127
    picked = tn(table[...].astype(F32).astype(BF), (iota((64, 512), 0) == high).astype(F32).astype(BF))
    chosen = jnp.sum(jnp.where(iota((128, 512), 0) == low, picked, 0.0), axis=0, keepdims=True)
    member = (iota((16, 512), 0) == chosen.astype(I32)).astype(F32)
    earlier = (iota((512, 512), 0) < iota((512, 512), 1)).astype(F32).astype(BF)
    before = nn(member.astype(BF), earlier)
    slot = jnp.sum(before * member, axis=0, keepdims=True)
    target = (chosen * CAP + slot).astype(I32)
    target_out[...] = jnp.broadcast_to(target, (8, 512))
    counts = jnp.sum(member, axis=1, keepdims=True)
    tally[...] = jnp.where(iota((16, 128), 1) == place[0] * 16 + place[1], counts, 0.0)
    stores = []

    def store(source, goal):
        stores.append(pltpu.make_async_copy(source, goal, out_sems.at[len(stores)]))
        stores[-1].start()

    loads[0].wait()
    unit, _ = norm_parts(xv[...].astype(F32))
    uv[...] = unit.astype(BF)
    store(uv, unit_out)
    rows = (unit * row(gain) + row(bias)).astype(BF)
    loads[1].wait()
    for i in range(2):
        placing = jnp.where(iota((512, 512), 0) + 512 * i == target, live, 0.0).astype(BF)
        sv[512 * i : 512 * (i + 1), :] = nn(placing, gv[...]).astype(BF)
    store(sv, sent)
    loads[2].wait()
    rv[...] = rows

    def block(j, carry):
        kv[j] = nn(rv[...], w[:, cols_at(j, 768)]).astype(BF)
        return carry

    lax.fori_loop(0, 3, block, 0)
    store(kv.at[0], query)
    store(kv.at[1], keyval.at[:, 0:768])
    store(kv.at[2], keyval.at[:, 768:1536])
    for copy in stores:
        copy.wait()


def head_masks(scale):
    lane = iota((1, 128), 1)
    first = jnp.where(lane < 64, scale, 0.0).astype(BF)
    second = jnp.where(lane >= 64, scale, 0.0).astype(BF)
    return first, second


def stack_heads(pair, masks):
    return jnp.concatenate([pair * masks[0], pair * masks[1]], axis=0)


def window_bias(place, lengths, r):
    lane = iota((1, 128), 1) + place[0] * 128
    end, start = jnp.int32(0), jnp.zeros((1, 128), I32)
    for j in range(8):
        end = end + lengths[r, j]
        start = jnp.where(end <= lane, end, start)
    start = start - (place[0] - 2) * 128
    key = iota((384, 128), 0)
    allowed = (key >= start) & (key <= iota((384, 128), 1) + 256)
    half = jnp.where(allowed, 0.0, MASKED)
    return jnp.concatenate([half, half], axis=1)


def join_heads(both):
    one = jnp.where(iota((128, 128), 0) < 64, both[:, :128], both[:, 128:])
    return one.T


def copies(sources, targets, sems):
    out = [
        pltpu.make_async_copy(a, b, sems.at[i]) for i, (a, b) in enumerate(zip(sources, targets))
    ]
    for copy in out:
        copy.start()
    return out


def lanes_of(p, offset=0):
    return slice(offset + 128 * p, offset + 128 * (p + 1))


def forward_kernel(
    place, lengths, gain, bias, gain_two, bias_two, target,
    behind_two, early, late, weight, keyval, query, x, proj,
    unit_halo, context_out, attended, log_out, after_out, sent,
    b2, e1, l1, w, q, xv, wp, units, rows_in, context, att, aft, snd, in_sems, out_sems,
):
    loads = copies(
        [behind_two, early, late, weight, keyval, query, x, proj],
        [b2, e1, l1, w, context.at[:, 256:384, :], q, xv, wp],
        in_sems,
    )
    scales = head_masks(HEAD_SIZE ** (-0.5))
    for copy in loads[:3]:
        copy.wait()

    def norm_row(r, carry):
        halo = jnp.concatenate([b2[r], e1[r] + l1[r]], axis=0).astype(F32)
        unit, _ = norm_parts(halo)
        units[r] = unit.astype(BF)
        rows_in[r] = (unit * row(gain) + row(bias)).astype(BF)
        return carry

    lax.fori_loop(0, 4, norm_row, 0)
    unit_copy = pltpu.make_async_copy(units, unit_halo, out_sems.at[0])
    unit_copy.start()
    loads[3].wait()

    def keyval_block(j, carry):
        source = pl.ds(pl.multiple_of(768 + 512 * j, 256), 512)
        fresh = nn(rows_in[...].reshape(1024, 768), w[:, source])
        context[:, 0:256, cols_at(j, 512)] = fresh.astype(BF).reshape(4, 256, 512)
        return carry

    lax.fori_loop(0, 3, keyval_block, 0)
    for copy in loads[4:6]:
        copy.wait()
    context_copy = pltpu.make_async_copy(context, context_out, out_sems.at[1])
    context_copy.start()

    def one_row(r, carry):
        mask = window_bias(place, lengths, r)
        pairs = range(PAIRS)
        stacked = [stack_heads(q[r, :, lanes_of(p)], scales) for p in pairs]
        scores = [nt(context[r, :, lanes_of(p)], stacked[p]) + mask for p in pairs]
        tops = [jnp.max(a, axis=0, keepdims=True) for a in scores]
        weights = [jnp.exp(a - t) for a, t in zip(scores, tops)]
        totals = [jnp.sum(a, axis=0, keepdims=True) for a in weights]
        shares = [(a * (1.0 / t)).astype(BF) for a, t in zip(weights, totals)]
        mixed = [tn(context[r, :, lanes_of(p, 768)], shares[p]) for p in pairs]
        for p in pairs:
            log_out[r, p : p + 1, :] = tops[p] + jnp.log(totals[p])
            att[r, :, lanes_of(p)] = join_heads(mixed[p]).astype(BF)
        return carry

    lax.fori_loop(0, 4, one_row, 0)
    att_copy = pltpu.make_async_copy(att, attended, out_sems.at[2])
    att_copy.start()
    loads[6].wait()
    loads[7].wait()
    after = xv[...].reshape(512, 768).astype(F32) + nn(att[...].reshape(512, 768), wp[...])
    aft[...] = after
    after_copy = pltpu.make_async_copy(aft, after_out, out_sems.at[3])
    after_copy.start()
    unit, _ = norm_parts(after)
    rows = (unit * row(gain_two) + row(bias_two)).astype(BF)
    sends = []
    for i in range(2):
        part = slice(512 * i, 512 * (i + 1))
        placing = (iota((512, 512), 0) + 512 * i == target[0:1, :]).astype(F32).astype(BF)
        snd[part, :] = nn(placing, rows).astype(BF)
        sends.append(pltpu.make_async_copy(snd.at[part], sent.at[part], out_sems.at[4 + i]))
        sends[-1].start()
    for copy in [unit_copy, context_copy, att_copy, after_copy] + sends:
        copy.wait()


def active_grad_kernel(grad, down, out):
    out[0] = nt(grad[...], down[...]).astype(BF)


def gelu_both(v):
    c = 0.7978845608028654
    square = v * v
    p = c + (c * 0.044715) * square
    gate = 0.5 + 0.5 * jnp.tanh(v * p)
    value = v * gate
    return value, gate + value * (1.0 - gate) * (6.0 * p - 4.0 * c)


def expert_kernel(x, up, raw, active, hidden_grad, back, total):
    step = pl.program_id(0)

    @pl.when(step == 0)
    def _():
        total[...] = jnp.zeros_like(total)

    parts = [slice(256 * r, 256 * (r + 1)) for r in range(4)]
    hidden = [nn(x[rows, :], up[...]) for rows in parts]
    lows = []
    for rows, v in zip(parts, hidden):
        value, slope = gelu_both(v)
        active[0, rows, :] = value.astype(BF)
        low = (raw[0, rows, :].astype(F32) * slope).astype(BF)
        hidden_grad[0, rows, :] = low
        lows.append(low)
    for rows, low in zip(parts, lows):
        total[rows, :] += nt(low, up[...])

    @pl.when(step == pl.num_programs(0) - 1)
    def _():
        back[...] = total[...].astype(BF)


def turn_kernel(unit, unit_halo, grad, out, grad_t):
    out[0:768, 0:512] = unit[...].T
    out[0:768, 512:1536] = unit_halo[...].T
    out[768:784, :] = jnp.ones((16, 1536), BF)
    grad_t[...] = grad[...].T


def weight_kernel(place, x, grad_t, active, hidden_grad, down, out, mine, away, x_t, total):
    step = pl.program_id(0)

    @pl.when(step == 0)
    def _():
        total[...] = jnp.zeros_like(total)
        x_t[...] = x[...].T

    total[...] += nn(active[0], down[...])
    one = nn(x_t[...], hidden_grad[0])
    two = nn(grad_t[...], active[0])
    even = place[0] % 2 == 0
    for i, both in enumerate([one, two]):
        mine[0, i] = jnp.where(even, both[:, :384], both[:, 384:]).astype(BF)
        away[0, i] = jnp.where(even, both[:, 384:], both[:, :384]).astype(BF)

    @pl.when(step == pl.num_programs(0) - 1)
    def _():
        out[...] = total[...].astype(BF)


def output_kernel(after, target, returned, out):
    placing = (iota((512, 1024), 1).astype(F32) == column(target[0:1, :].astype(F32))).astype(F32).astype(BF)
    out[...] = (after[...] + nn(placing, returned[...])).astype(BF)


def cols_at(j, size=256):
    return pl.ds(pl.multiple_of(size * j, size), size)


def fill_halves(
    turned, query_grad, context_grad, weight, gain, bias, proj_part, terms_two, tally,
    out, gain_wide, bias_wide, gain_sum, bias_sum,
):
    gain_wide[...] = jnp.broadcast_to(row(gain), (256, 768)).T
    bias_wide[...] = jnp.broadcast_to(row(bias), (256, 768)).T

    def finish(block, both):
        body, sums = both[0:768], both[768:769]
        half, step = block // 6, block % 6
        out[half, 768 * step : 768 * (step + 1), :] = (
            gain_wide[...] * body + bias_wide[...] * sums
        ).astype(BF)
        wide = weight[:, 256 * block : 256 * (block + 1)].astype(F32)
        if block == 0:
            gain_sum[...] = wide * body
            bias_sum[...] = wide * sums
        else:
            gain_sum[...] += wide * body
            bias_sum[...] += wide * sums

    for j in range(3):
        finish(j, nn(turned[:, 0:512], query_grad[:, 256 * j : 256 * (j + 1)]))
        out[1, 768 * (3 + j) : 768 * (4 + j), :] = proj_part[j]
    for j in range(6):
        finish(3 + j, nn(turned[...], context_grad[:, 256 * j : 256 * (j + 1)]))

    columns = jnp.concatenate(
        [
            jnp.broadcast_to(jnp.sum(gain_sum[...], axis=1, keepdims=True), (768, 128)),
            jnp.broadcast_to(jnp.sum(bias_sum[...], axis=1, keepdims=True), (768, 128)),
        ],
        axis=1,
    ).T
    out[:, GEMM_ROWS:, :] = jnp.zeros((2, HALF_ROWS - GEMM_ROWS, 256), BF)
    for t in range(3):
        lanes = slice(256 * t, 256 * (t + 1))
        block = jnp.concatenate(
            [columns[0:1, lanes], columns[128:129, lanes], terms_two[:, lanes], jnp.zeros((12, 256), F32)],
            axis=0,
        )
        out[0, GEMM_ROWS + 16 * t : GEMM_ROWS + 16 * t + 16, :] = block.astype(BF)
    out[0, GEMM_ROWS + 48 : GEMM_ROWS + 64, 0:128] = tally[...].astype(BF)


def backward_kernel(
    place, lengths, gain_two, gain, bias, target, turn, log_total, tally,
    back, after, grad, proj, attended, query, context, turned, weight,
    after_grad, query_grad, own_grad, input_two, input_one, keep, away,
    bk, af, gr, wp, att, q, ctx, tu, w, ag, do, dq, cg, pp, ip, out,
    gain_wide, bias_wide, gain_sum, bias_sum, terms, in_sems, out_sems,
):
    loads = copies(
        [back, after, grad, proj, attended, query, context, turned, weight],
        [bk, af, gr, wp, att, q, ctx, tu, w],
        in_sems,
    )
    scales = head_masks(HEAD_SIZE ** (-0.5))
    ones = head_masks(1.0)
    placing = (iota((512, 1024), 1).astype(F32) == column(target[0:1, :].astype(F32))).astype(F32).astype(BF)
    live = column(flat_line(turn))
    loads[0].wait()
    normed_grad = nn(placing, bk[...])
    loads[1].wait()
    unit, inverse = norm_parts(af[...])
    terms[0:1, :] = jnp.sum(normed_grad * unit, axis=0, keepdims=True)
    terms[1:2, :] = jnp.sum(normed_grad, axis=0, keepdims=True)
    loads[2].wait()
    total = gr[...].astype(F32) * live + norm_back(normed_grad, row(gain_two), unit, inverse)
    ag[...] = total
    stores = [pltpu.make_async_copy(ag, after_grad, out_sems.at[0])]
    stores[0].start()
    low = total.astype(BF)
    loads[3].wait()
    do[...] = nt(low, wp[...]).astype(BF).reshape(4, 128, 768)
    loads[4].wait()
    mixed = nn(att[...].T, low).astype(BF)
    for j in range(3):
        pp[j] = mixed[:, 256 * j : 256 * (j + 1)]
    loads[5].wait()
    loads[6].wait()

    def one_row(r, carry):
        mask = window_bias(place, lengths, r)
        pairs = range(PAIRS)
        stacked = [stack_heads(q[r, :, lanes_of(p)], scales) for p in pairs]
        grads = [stack_heads(do[r, :, lanes_of(p)], ones) for p in pairs]
        scores = [nt(ctx[r, :, lanes_of(p)], stacked[p]) for p in pairs]
        share_grads = [nt(ctx[r, :, lanes_of(p, 768)], grads[p]) for p in pairs]
        shares = [jnp.exp(scores[p] + mask - log_total[r, p : p + 1, :]) for p in pairs]
        sums = [jnp.sum(a * b, axis=0, keepdims=True) for a, b in zip(shares, share_grads)]
        score_grads = [(a * (b - c)).astype(BF) for a, b, c in zip(shares, share_grads, sums)]
        key_grads = [nn(score_grads[p], stacked[p]).astype(BF) for p in pairs]
        value_grads = [nn(shares[p].astype(BF), grads[p]).astype(BF) for p in pairs]
        turned_grads = [tn(ctx[r, :, lanes_of(p)], score_grads[p]) for p in pairs]
        halo = pl.ds(pl.multiple_of(512 + r * 256, 256), 256)
        own = pl.ds(pl.multiple_of(r * 128, 128), 128)
        for p in pairs:
            cg[halo, lanes_of(p)] = key_grads[p][:256]
            cg[own, lanes_of(p)] = key_grads[p][256:]
            cg[halo, lanes_of(p, 768)] = value_grads[p][:256]
            cg[own, lanes_of(p, 768)] = value_grads[p][256:]
            dq[own, lanes_of(p)] = (join_heads(turned_grads[p]) * HEAD_SIZE ** (-0.5)).astype(BF)
        return carry

    lax.fori_loop(0, 4, one_row, 0)
    loads[7].wait()
    loads[8].wait()

    def store(source, target):
        stores.append(pltpu.make_async_copy(source, target, out_sems.at[len(stores)]))
        stores[-1].start()

    store(dq, query_grad)
    store(cg.at[0:512], own_grad)
    ip[...] = nt(cg[512:1536, :], w[:, 768:]).astype(BF).reshape(4, 256, 768)
    store(ip.at[:, 0:128], input_two)
    store(ip.at[:, 128:256], input_one)
    fill_halves(
        tu, dq, cg, w, gain, bias, pp, terms, tally, out, gain_wide, bias_wide, gain_sum, bias_sum
    )
    core = place[0] % 2

    @pl.when(core == 0)
    def _():
        pltpu.make_async_copy(out.at[0], keep, out_sems.at[5]).start()
        pltpu.make_async_copy(out.at[1], away, out_sems.at[6]).start()

    @pl.when(core == 1)
    def _():
        pltpu.make_async_copy(out.at[1], keep, out_sems.at[5]).start()
        pltpu.make_async_copy(out.at[0], away, out_sems.at[6]).start()

    for copy in stores:
        copy.wait()
    pltpu.make_async_copy(out.at[0], keep, out_sems.at[5]).wait()
    pltpu.make_async_copy(out.at[1], away, out_sems.at[6]).wait()


def place_half(half, bits, pieces, qkv, proj, whole, stage, in_sems, sems):
    loads = []
    for i in range(2):
        for j in range(2):
            first = pl.multiple_of((2 * i + (bits[i] + j) % 2) * PIECE, PIECE)
            target = whole.at[pl.ds(first, PIECE)]
            loads.append(pltpu.make_async_copy(pieces[2 * i + j], target, in_sems.at[2 * i + j]))
            loads[-1].start()
    for copy in loads:
        copy.wait()
    for j in range(6):
        stage[j] = whole[768 * j : 768 * (j + 1), :].astype(F32)
        lanes = slice(256 * (j % 3), 256 * (j % 3 + 1))

        @pl.when(half == 0)
        def _():
            pltpu.make_async_copy(stage.at[j], qkv.at[:, 256 * j : 256 * (j + 1)], sems.at[j]).start()

        @pl.when(half == 1)
        def _():
            target = qkv.at[:, 1536 + 256 * j : 1792 + 256 * j] if j < 3 else proj.at[:, lanes]
            pltpu.make_async_copy(stage.at[j], target, sems.at[j]).start()

    for j in range(6):
        pltpu.make_async_copy(stage.at[j], proj.at[:, 0:256], sems.at[j]).wait()


def finish_mine_kernel(place, a, b, c, d, qkv, proj, tail, whole, stage, in_sems, sems):
    place_half(place[0], (place[2], place[3]), (a, b, c, d), qkv, proj, whole, stage, in_sems, sems)
    tail[...] = whole[GEMM_ROWS : GEMM_ROWS + 64, :]


def finish_other_kernel(
    place, tail, a, b, c, d, qkv_in, proj_in, qkv, proj, gain_one, bias_one, gain_two, bias_two, counts, received,
    whole, stage, in_sems, sems,
):
    place_half(1 - place[0], (place[4], place[5]), (a, b, c, d), qkv, proj, whole, stage, in_sems, sems)
    both = tail[...].astype(F32) + whole[GEMM_ROWS : GEMM_ROWS + 64, :].astype(F32)
    for i, out in enumerate([gain_one, bias_one, gain_two, bias_two]):
        line = jnp.concatenate([both[16 * t + i : 16 * t + i + 1, :] for t in range(3)], axis=1)
        out[...] = line.reshape(768)
    every = both[48:64, 0:128]
    counts[...] = nt(jnp.ones((8, 128), BF), every.astype(BF))[0:1, :].astype(I32).reshape(16)
    chosen = (iota((16, 128), 0) == place[1]) & ((iota((16, 128), 1) >> 4) == place[6])
    mine = jnp.where(chosen, every, 0.0).astype(BF)
    fold = ((iota((128, 16), 0) & 15) == iota((128, 16), 1)).astype(F32).astype(BF)
    received[0] = jnp.sum(nn(mine, fold), axis=0, keepdims=True).astype(I32)


def chunk_of(a, b):
    return 2 * b + (a + b) % 2


def add_chunks(plan, buffer, in_sems):
    loads = []
    for n, picks in enumerate(plan):
        for m, pick_ref in enumerate(picks):
            loads.append(pltpu.make_async_copy(pick_ref, buffer.at[n, m], in_sems.at[n, m]))
            loads[-1].start()
    return loads


def summed(buffer, n, count):
    total = buffer[n, 0].astype(F32)
    for m in range(1, count):
        total = total + buffer[n, m].astype(F32)
    return total


def expert_first_kernel(spots, own, got, one, two, buffer, made, in_sems, out_sems):
    a, b = spots[7], spots[8]
    wanted = [(chunk_of(1 - a, k), 0) for k in range(2)] + [(chunk_of(k, 1 - b), 1) for k in range(2)]
    plan = [[own.at[c, t], got.at[c, t]] for c, t in wanted]
    loads = add_chunks(plan, buffer, in_sems)
    stores = []
    for n in range(4):
        loads[2 * n].wait()
        loads[2 * n + 1].wait()
        made[n] = summed(buffer, n, 2).astype(BF)
        stores.append(pltpu.make_async_copy(made.at[n], (one, two)[n // 2].at[n % 2], out_sems.at[n]))
        stores[-1].start()
    for copy in stores:
        copy.wait()


def expert_second_kernel(spots, own, got, first, second, one, two, buffer, made, in_sems, out_sems):
    a, b = spots[7], spots[8]
    c, d = chunk_of(a, 1 - b), chunk_of(1 - a, b)
    plan = [
        [own.at[c, 0], got.at[c, 0], first.at[1 - b]],
        [own.at[d, 1], got.at[d, 1], second.at[1 - a]],
    ]
    loads = add_chunks(plan, buffer, in_sems)
    stores = []
    for n in range(2):
        for copy in loads[3 * n : 3 * n + 3]:
            copy.wait()
        made[n] = summed(buffer, n, 3).astype(BF)
        stores.append(pltpu.make_async_copy(made.at[n], (one, two)[n], out_sems.at[n]))
        stores[-1].start()
    for copy in stores:
        copy.wait()


def expert_last_kernel(spots, own, got, first, second, third, fourth, up, down, buffer, in_sems):
    a, b = spots[7], spots[8]
    c = chunk_of(a, b)
    plan = [
        [own.at[c, 0], got.at[c, 0], first.at[b], third],
        [own.at[c, 1], got.at[c, 1], second.at[a], fourth],
    ]
    loads = add_chunks(plan, buffer, in_sems)
    for copy in loads[:4]:
        copy.wait()
    up[0] = summed(buffer, 0, 4)
    for copy in loads[4:]:
        copy.wait()
    down[0] = summed(buffer, 1, 4).T


def input_own_kernel(query_grad, own_grad, weight, out, dq, og, w, in_sems):
    for copy in copies([weight, query_grad, own_grad], [w, dq, og], in_sems):
        copy.wait()
    out[...] = nt(dq[...], w[:, :768]) + nt(og[...], w[:, 768:])


def input_grad_kernel(
    even, gain, own, x, from_one, from_two, after_grad, out, ov, xv, one, two, ag, in_sems,
):
    loads = copies(
        [x, own, from_one, from_two, after_grad],
        [xv, ov, one, two, ag],
        in_sems,
    )
    loads[0].wait()
    unit, inverse = norm_parts(xv[...].astype(F32))
    for copy in loads[1:]:
        copy.wait()
    total = ov[...] + two[...].astype(F32) + even[0] * one[...].astype(F32)
    out[...] = ag[...] + norm_back(total, row(gain), unit, inverse)


PAIR_ONE = [b ^ 1 for b in range(4)]
PAIR_TWO = [b ^ 3 for b in range(4)]
PAIRS_OF = [PAIR_ONE, PAIR_TWO]
BOTH = ("batch", "seq")


def by_core(even_move, odd_move):
    pairs = []
    for b in range(16):
        for s in range(8):
            x, y = (even_move, odd_move)[s % 2](b & 3, b >> 2)
            pairs.append((b * 8 + s, (y * 4 + x) * 8 + s))
    return pairs


def first_pairs(pair):
    return by_core(lambda x, y: (pair[x], y), lambda x, y: (x, pair[y]))


def second_step(d):
    return by_core(lambda x, y: (x, (y + d) & 3), lambda x, y: ((x + d) & 3, y))


def along_z(d):
    return [(s, (s + 2 * d) & 7) for s in range(8)]


def pick(array, index):
    return lax.dynamic_index_in_dim(array, index, 0, keepdims=False)


def part_of(array, index):
    return lax.dynamic_index_in_dim(array, index % 4, 1, keepdims=False)


def bits_of(place):
    return [(place & 1) ^ (place >> 1), place >> 1]


def z_pairs(pair):
    return [(s, pair[s // 2] * 2 + s % 2) for s in range(8)]


def sum_start(bits, keep, got):
    def part(stream, bit, first=0, size=PIECE):
        at = (stream * 2 + bit) * PIECE + first
        return rows_at(keep, at, size).astype(F32) + rows_at(got, at, size).astype(F32)

    return part, [part(i, 1 - bits[i]).astype(BF) for i in range(2)]


def pair_moves(data, pairs):
    return [lax.ppermute(a, BOTH, first_pairs(pair)) for a, pair in zip(data, pairs)]


def rows_at(array, at, size):
    return lax.dynamic_slice(array, (at, 0), (size, array.shape[1]))


def sum_middle(bits, part, moved):
    size = PIECE // 2

    def rows_of(i, bit):
        return part(i, bits[i], bit * size, size) + rows_at(moved[i], bit * size, size).astype(F32)

    return [rows_of(i, bits[1 - i]) for i in range(2)], [rows_of(i, 1 - bits[1 - i]).astype(BF) for i in range(2)]


def group(chunks):
    size, lanes = chunks[0].shape
    return jnp.stack(chunks).reshape(2, 4, size // 4, lanes)


def sum_across(place, grouped):
    total = part_of(grouped, place).astype(F32)
    for d in (2, 1, 3):
        total = total + lax.ppermute(part_of(grouped, place + d), BOTH, second_step(d)).astype(F32)
    return total.astype(BF)


def sum_along(whole):
    total = whole.astype(F32)
    for d in (2, 1, 3):
        total = total + lax.ppermute(whole, "seq", along_z(d)).astype(F32)
    return total.astype(BF)


def gather_across(place, piece):
    size, lanes = PIECE // 2, piece.shape[-1]
    parts = [piece] + [lax.ppermute(piece, BOTH, second_step(d)) for d in (1, 2, 3)]
    stack = jnp.stack(parts, axis=1)
    ordered = jnp.stack([part_of(stack, place - p + 4) for p in range(4)], axis=1).reshape(2, size, lanes)
    return [ordered[0], ordered[1]]


def gather_pairs(bits, ordered):
    moved = pair_moves(ordered, PAIRS_OF[::-1])
    return [
        jnp.where(bit == 0, jnp.stack([a, b]), jnp.stack([b, a])).reshape(PIECE, a.shape[1])
        for bit, a, b in zip(bits[::-1], ordered, moved)
    ]


def hold(*values):
    return lax.optimization_barrier(values)


def exchange(array):
    return lax.all_to_all(
        array.reshape(16, CAP, 768), "batch", split_axis=0, concat_axis=0, tiled=True
    ).reshape(1024, 768)


def local(
    block_input, token_ids, hash_table, doc_lengths, turn_mask, attn_norm_gain, attn_norm_bias,
    qkv_weight, proj_weight, ffn_norm_gain, ffn_norm_bias, expert_up, expert_down, out_grad,
):
    seq = lax.axis_index("seq")
    owner = lax.axis_index("batch")
    odd = seq % 2
    flat = (512, 768)
    rows3 = (4, 128, 768)
    place = jnp.stack([seq, owner]).astype(I32)
    up, down = expert_up[0], expert_down[0]

    behind_two = lax.ppermute(block_input, "seq", AHEAD_TWO)
    early = lax.ppermute(block_input, "seq", UP_ONE)

    table = jnp.pad(hash_table, (0, 8192 - 8008)).reshape(64, 128)
    target, tally, grad_sent, unit, query, keyval = kernel_call(
        entry_kernel,
        [
            shape((8, 512), I32), shape((16, 128), F32), shape((1024, 768)), shape(flat), shape(flat),
            shape((512, 1536)),
        ],
        [
            place, token_ids, table, turn_mask, attn_norm_gain, attn_norm_bias, block_input.reshape(flat),
            out_grad.reshape(flat), qkv_weight,
        ],
        "entry", 3 * 10**9,
        in_specs=[SM] + [VM] * 5 + [HB] * 3,
        out_specs=[VM] * 2 + [HB] * 4,
        scratch=[
            pltpu.VMEM(flat, BF), pltpu.VMEM(flat, BF), pltpu.VMEM((768, 2304), BF), pltpu.VMEM((1024, 768), BF),
            pltpu.VMEM(flat, BF), pltpu.VMEM(flat, BF), pltpu.VMEM((3, 512, 768), BF),
            pltpu.SemaphoreType.DMA((3,)), pltpu.SemaphoreType.DMA((5,)),
        ],
    )
    grad_rows = exchange(grad_sent)

    behind_two, query = hold(behind_two, query)
    late = lax.ppermute(behind_two, "seq", DOWN_ONE)
    query, keyval = query.reshape(rows3), keyval.reshape(4, 128, 1536)

    unit_halo, context, attended, log_total, after, rows_sent = kernel_call(
        forward_kernel,
        [
            shape((4, 256, 768)), shape((4, 384, 1536)), shape(rows3), shape((4, 8, 256), F32),
            shape(flat, F32), shape((1024, 768)),
        ],
        [
            place, doc_lengths, attn_norm_gain, attn_norm_bias, ffn_norm_gain, ffn_norm_bias, target,
            behind_two, early, late, qkv_weight, keyval, query, block_input, proj_weight,
        ],
        "forward", 10**9,
        in_specs=[SM] * 2 + [VM] * 5 + [HB] * 8,
        out_specs=[HB] * 3 + [VM] + [HB] * 2,
        scratch=[
            pltpu.VMEM(rows3, BF), pltpu.VMEM(rows3, BF), pltpu.VMEM(rows3, BF), pltpu.VMEM((768, 2304), BF),
            pltpu.VMEM(rows3, BF), pltpu.VMEM(rows3, BF), pltpu.VMEM((768, 768), BF),
            pltpu.VMEM((4, 256, 768), BF), pltpu.VMEM((4, 256, 768), BF), pltpu.VMEM((4, 384, 1536), BF),
            pltpu.VMEM(rows3, BF), pltpu.VMEM(flat, F32), pltpu.VMEM((1024, 768), BF),
            pltpu.SemaphoreType.DMA((8,)), pltpu.SemaphoreType.DMA((6,)),
        ],
    )
    rows = exchange(rows_sent)

    turned, grad_t = kernel_call(
        turn_kernel,
        [shape((784, 1536)), shape((768, 1024))],
        [unit, unit_halo.reshape(1024, 768), grad_rows],
        "turn", 10**6,
    )
    grad_rows, turned, grad_t = hold(grad_rows, turned, grad_t)
    tile = pl.BlockSpec((1, 1024, 768), lambda i: (i, 0, 0))
    tiled = shape((4, 1024, 768))
    whole = pl.BlockSpec((1024, 768), lambda i: (0, 0))
    raw = kernel_call(
        active_grad_kernel,
        [tiled],
        [grad_rows, down],
        "active_grad", 48 * 10**8,
        grid=(4,),
        in_specs=[whole, pl.BlockSpec((768, 768), lambda i: (i, 0))],
        out_specs=[tile],
    )[0]

    active, hidden_grad, back_sent = kernel_call(
        expert_kernel,
        [tiled, tiled, shape((1024, 768))],
        [rows, up, raw],
        "expert", 97 * 10**8,
        grid=(4,),
        in_specs=[whole, pl.BlockSpec((768, 768), lambda i: (0, i)), tile],
        out_specs=[tile, tile, whole],
        scratch=[pltpu.VMEM((1024, 768), F32)],
    )
    back = exchange(back_sent)

    result, parts, parts_away = kernel_call(
        weight_kernel,
        [shape((1024, 768)), shape((4, 2, 768, 384)), shape((4, 2, 768, 384))],
        [place, rows, grad_t, active, hidden_grad, down],
        "weights", 145 * 10**8,
        grid=(4,),
        in_specs=[
            SM,
            whole,
            pl.BlockSpec((768, 1024), lambda i: (0, 0)),
            tile,
            tile,
            pl.BlockSpec((768, 768), lambda i: (i, 0)),
        ],
        out_specs=[
            pl.BlockSpec((1024, 768), lambda i: (0, 0)),
            pl.BlockSpec((1, 2, 768, 384), lambda i: (i, 0, 0, 0)),
            pl.BlockSpec((1, 2, 768, 384), lambda i: (i, 0, 0, 0)),
        ],
        scratch=[pltpu.VMEM((768, 1024), BF), pltpu.VMEM((1024, 768), F32)],
    )
    returned = exchange(result)
    parts_away, back = hold(parts_away, back)
    parts_got = lax.ppermute(parts_away, "seq", SWAP)
    depth = seq // 2
    turn = jnp.where(odd == 0, owner // 4, owner % 4)
    bits = bits_of(jnp.where(odd == 0, owner % 4, owner // 4))
    spots = jnp.stack([odd, owner, *bits, *bits_of(turn), seq, *bits_of(depth)]).astype(I32)
    block = shape((768, 384))
    first_sent = kernel_call(
        expert_first_kernel, [shape((2, 768, 384))] * 2, [spots, parts, parts_got], "expert_first", 10**6,
        in_specs=[SM] + [HB] * 2, out_specs=[HB] * 2,
        scratch=[
            pltpu.VMEM((4, 2, 768, 384), BF), pltpu.VMEM((4, 768, 384), BF),
            pltpu.SemaphoreType.DMA((4, 2)), pltpu.SemaphoreType.DMA((4,)),
        ],
    )
    back, *first_sent = hold(back, *first_sent)
    routes = [z_pairs(pair) for pair in PAIRS_OF]
    first_got = [lax.ppermute(a, "seq", route) for a, route in zip(first_sent, routes)]

    after_grad, query_grad, own_grad, input_two, input_one, keep, away = kernel_call(
        backward_kernel,
        [
            shape(flat, F32), shape(flat), shape((512, 1536)), shape(rows3), shape(rows3),
            shape((HALF_ROWS, 256)), shape((HALF_ROWS, 256)),
        ],
        [
            place, doc_lengths, ffn_norm_gain, attn_norm_gain, attn_norm_bias, target, turn_mask, log_total, tally,
            back, after, out_grad.reshape(flat), proj_weight, attended.reshape(flat), query, context, turned,
            qkv_weight,
        ],
        "backward", 16 * 10**9,
        in_specs=[SM] * 2 + [VM] * 7 + [HB] * 9,
        out_specs=[HB] * 7,
        scratch=[
            pltpu.VMEM((1024, 768), BF), pltpu.VMEM(flat, F32), pltpu.VMEM(flat, BF), pltpu.VMEM((768, 768), BF),
            pltpu.VMEM(flat, BF), pltpu.VMEM(rows3, BF), pltpu.VMEM((4, 384, 1536), BF),
            pltpu.VMEM((784, 1536), BF), pltpu.VMEM((768, 2304), BF), pltpu.VMEM(flat, F32), pltpu.VMEM(rows3, BF),
            pltpu.VMEM(flat, BF), pltpu.VMEM((1536, 1536), BF), pltpu.VMEM((3, 768, 256), BF),
            pltpu.VMEM((4, 256, 768), BF), pltpu.VMEM((2, HALF_ROWS, 256), BF),
            pltpu.VMEM((768, 256), F32), pltpu.VMEM((768, 256), F32), pltpu.VMEM((768, 256), F32),
            pltpu.VMEM((768, 256), F32), pltpu.VMEM((2, 768), F32),
            pltpu.SemaphoreType.DMA((9,)), pltpu.SemaphoreType.DMA((7,)),
        ],
    )
    away, returned, *first_got = hold(away, returned, *first_got)
    got = lax.ppermute(away, "seq", SWAP)
    from_one = lax.ppermute(input_one, "seq", SWAP)
    second_sent = kernel_call(
        expert_second_kernel, [block] * 2, [spots, parts, parts_got, *first_got], "expert_second", 10**6,
        in_specs=[SM] + [HB] * 4, out_specs=[HB] * 2,
        scratch=[
            pltpu.VMEM((2, 3, 768, 384), BF), pltpu.VMEM((2, 768, 384), BF),
            pltpu.SemaphoreType.DMA((2, 3)), pltpu.SemaphoreType.DMA((2,)),
        ],
    )
    block_output = kernel_call(
        output_kernel, [shape(flat)], [after, target, returned], "output", 8 * 10**8
    )[0]
    got, from_one, block_output, *second_sent = hold(got, from_one, block_output, *second_sent)
    part, sent = sum_start(bits, keep, got)
    sent[0], sent[1], query_grad, *second_sent = hold(sent[0], sent[1], query_grad, *second_sent)

    moved = pair_moves(sent, PAIRS_OF)
    second_got = [lax.ppermute(second_sent[i], "seq", routes[1 - i]) for i in range(2)]
    own_part = kernel_call(
        input_own_kernel, [shape(flat, F32)], [query_grad, own_grad, qkv_weight], "input_own", 2 * 10**9,
        in_specs=[HB] * 3,
        scratch=[
            pltpu.VMEM(flat, BF), pltpu.VMEM((512, 1536), BF), pltpu.VMEM((768, 2304), BF),
            pltpu.SemaphoreType.DMA((3,)),
        ],
    )[0]
    moved[0], moved[1], own_part = hold(moved[0], moved[1], own_part)

    chunks, sent = sum_middle(bits, part, moved)
    moved = pair_moves(sent, PAIRS_OF[::-1])
    moved[0], moved[1], *second_got = hold(moved[0], moved[1], *second_got)
    chunks = [(a + b.astype(F32)).astype(BF) for a, b in zip(chunks, moved)]
    grouped = group(chunks)
    grouped, from_one = hold(grouped, from_one)
    passed = jnp.where(odd == 1, input_two + from_one, input_two)
    whole = sum_across(turn, grouped)
    whole, passed, *second_got = hold(whole, passed, *second_got)
    up_sum, down_sum = kernel_call(
        expert_last_kernel,
        [shape((1, 768, 384), F32), shape((1, 384, 768), F32)],
        [spots, parts, parts_got, *first_got, *second_got],
        "expert_last", 10**6,
        in_specs=[SM] + [HB] * 6,
        scratch=[pltpu.VMEM((2, 4, 768, 384), BF), pltpu.SemaphoreType.DMA((2, 4))],
    )
    piece = sum_along(whole)
    piece, passed, up_sum = hold(piece, passed, up_sum)
    from_two = lax.ppermute(passed, "seq", BACK_TWO)
    chunks = gather_pairs(bits, gather_across(turn, piece))
    chunks[0], chunks[1], from_two = hold(chunks[0], chunks[1], from_two)
    even = (1 - odd).astype(F32).reshape(1)
    input_grad = kernel_call(
        input_grad_kernel,
        [shape(flat, F32)],
        [
            even, attn_norm_gain, own_part, block_input.reshape(flat), from_one.reshape(flat),
            from_two.reshape(flat), after_grad,
        ],
        "input_grad", 10**7,
        in_specs=[SM, VM] + [HB] * 5,
        scratch=[
            pltpu.VMEM(flat, F32), pltpu.VMEM(flat, BF), pltpu.VMEM(flat, BF), pltpu.VMEM(flat, BF),
            pltpu.VMEM(flat, F32), pltpu.SemaphoreType.DMA((5,)),
        ],
    )[0]
    moved = pair_moves(chunks, PAIRS_OF)
    moved[0], moved[1], input_grad = hold(moved[0], moved[1], input_grad)
    mine = [chunks[0], moved[0], chunks[1], moved[1]]
    swapped = [lax.ppermute(a, "seq", SWAP) for a in mine]
    sums = [shape((768, 2304), F32), shape((768, 768), F32)]
    landing = [
        pltpu.VMEM((HALF_ROWS, 256), BF), pltpu.VMEM((6, 768, 256), F32),
        pltpu.SemaphoreType.DMA((4,)), pltpu.SemaphoreType.DMA((6,)),
    ]
    qkv_half, proj_half, tail = kernel_call(
        finish_mine_kernel, sums + [shape((64, 256))], [spots, *mine], "finish_mine", 10**6,
        in_specs=[SM] + [HB] * 4, out_specs=[HB, HB, VM], scratch=landing,
    )
    line = shape((768,), F32)
    qkv_sum, proj_sum, *rest = kernel_call(
        finish_other_kernel,
        sums + [line] * 4 + [shape((16,), I32), shape((1, 1, 16), I32)],
        [spots, tail, *swapped, qkv_half, proj_half],
        "finish_other", 10**6,
        in_specs=[SM, VM] + [HB] * 6, out_specs=[HB] * 2 + [VM] * 6, scratch=landing,
        aliases={6: 0, 7: 1},
    )
    return (
        block_output.reshape(rows3),
        input_grad.reshape(rows3),
        rest[0],
        rest[1],
        qkv_sum,
        proj_sum,
        rest[2],
        rest[3],
        up_sum,
        down_sum,
        rest[4],
        rest[5],
    )


def solution(mesh):
    placed = (
        P("batch", "seq", None),
        P("batch", "seq"),
        P(),
        P("batch", None),
        P("batch", "seq"),
        P(),
        P(),
        P(),
        P(),
        P(),
        P(),
        P("batch", None, None),
        P("batch", None, None),
        P("batch", "seq", None),
    )
    return jax.shard_map(
        local,
        mesh=mesh,
        in_specs=placed,
        out_specs=(
            P("batch", "seq", None),
            P("batch", "seq", None),
            P(),
            P(),
            P(),
            P(),
            P(),
            P(),
            P("batch", None, "seq"),
            P("batch", "seq", None),
            P(),
            P("batch", "seq", None),
        ),
        check_vma=False,
    )
```

```python
import jax
import jax.numpy as jnp
from jax import lax
from jax.experimental import pallas as pl
from jax.experimental.pallas import tpu as pltpu
from jax.sharding import PartitionSpec as P

BF = jnp.bfloat16
F32 = jnp.float32
I32 = jnp.int32
EPS = 1e-05
MASKED = -1e30
HEADS = 12
HEAD_SIZE = 64
PAIRS = 6
CAP = 64
SWAP = [(i, i ^ 1) for i in range(8)]
UP_ONE = [(i, i + 1) for i in range(0, 8, 2)]
DOWN_ONE = [(i + 1, i) for i in range(0, 8, 2)]
AHEAD_TWO = [(i, i + 2) for i in range(6)]
BACK_TWO = [(i + 2, i) for i in range(6)]
HALF_ROWS = 4864
PIECE = HALF_ROWS // 4
VMEM_BYTES = 63 * 1024 * 1024 + 640 * 1024
GEMM_ROWS = 4608
VM = pl.BlockSpec(memory_space=pltpu.VMEM)
HB = pl.BlockSpec(memory_space=pl.ANY)
SM = pl.BlockSpec(memory_space=pltpu.SMEM)


def shape(dims, kind=BF):
    return jax.ShapeDtypeStruct(dims, kind)


def kernel_call(body, outs, args, name, flops, grid=None, in_specs=None, out_specs=None, scratch=(), aliases=None):
    moved = sum(a.size * a.dtype.itemsize for a in args) + sum(
        o.size * o.dtype.itemsize for o in outs
    )
    extra = {} if grid is None else {"grid": grid}
    return pl.pallas_call(
        body,
        out_shape=outs,
        in_specs=in_specs or [VM] * len(args),
        out_specs=out_specs or [VM] * len(outs),
        scratch_shapes=list(scratch),
        compiler_params=pltpu.CompilerParams(vmem_limit_bytes=VMEM_BYTES),
        cost_estimate=pl.CostEstimate(flops=flops, bytes_accessed=moved, transcendentals=0),
        name=name,
        input_output_aliases=aliases or {},
        **extra,
    )(*args)


def nn(a, b):
    return jnp.dot(a, b, preferred_element_type=F32)


def nt(a, b):
    return lax.dot_general(a, b, (((1,), (1,)), ((), ())), preferred_element_type=F32)


def tn(a, b):
    return lax.dot_general(a, b, (((0,), (0,)), ((), ())), preferred_element_type=F32)


def iota(dims, axis):
    return lax.broadcasted_iota(I32, dims, axis)


def row(ref):
    return ref[...].reshape(1, 768)


def column(line):
    return jnp.broadcast_to(line, (128, line.shape[1])).T[:, 0:1]


def flat_line(ref):
    return jnp.concatenate([ref[i : i + 1, :] for i in range(4)], axis=1).astype(F32)


def norm_parts(values):
    centred = values - jnp.mean(values, axis=-1, keepdims=True)
    inverse = lax.rsqrt(jnp.mean(centred * centred, axis=-1, keepdims=True) + EPS)
    return centred * inverse, inverse


def norm_back(grad, gain, unit, inverse):
    t = grad * gain
    return inverse * (
        t - jnp.mean(t, axis=-1, keepdims=True) - unit * jnp.mean(t * unit, axis=-1, keepdims=True)
    )


def entry_kernel(
    place, tok, table, turn, gain, bias, x, grad, weight, target_out, tally, sent, unit_out, query, keyval,
    xv, gv, w, sv, uv, rv, kv, in_sems, out_sems,
):
    loads = copies([x, grad, weight], [xv, gv, w], in_sems)
    ids = jnp.concatenate([tok[i : i + 1, :] for i in range(4)], axis=1)
    live = flat_line(turn)
    high, low = ids >> 7, ids & 127
    picked = tn(table[...].astype(F32).astype(BF), (iota((64, 512), 0) == high).astype(F32).astype(BF))
    chosen = jnp.sum(jnp.where(iota((128, 512), 0) == low, picked, 0.0), axis=0, keepdims=True)
    member = (iota((16, 512), 0) == chosen.astype(I32)).astype(F32)
    earlier = (iota((512, 512), 0) < iota((512, 512), 1)).astype(F32).astype(BF)
    before = nn(member.astype(BF), earlier)
    slot = jnp.sum(before * member, axis=0, keepdims=True)
    target = (chosen * CAP + slot).astype(I32)
    target_out[...] = jnp.broadcast_to(target, (8, 512))
    counts = jnp.sum(member, axis=1, keepdims=True)
    tally[...] = jnp.where(iota((16, 128), 1) == place[0] * 16 + place[1], counts, 0.0)
    stores = []

    def store(source, goal):
        stores.append(pltpu.make_async_copy(source, goal, out_sems.at[len(stores)]))
        stores[-1].start()

    loads[0].wait()
    unit, _ = norm_parts(xv[...].astype(F32))
    uv[...] = unit.astype(BF)
    store(uv, unit_out)
    rows = (unit * row(gain) + row(bias)).astype(BF)
    loads[1].wait()
    for i in range(2):
        placing = jnp.where(iota((512, 512), 0) + 512 * i == target, live, 0.0).astype(BF)
        sv[512 * i : 512 * (i + 1), :] = nn(placing, gv[...]).astype(BF)
    store(sv, sent)
    loads[2].wait()
    rv[...] = rows

    def block(j, carry):
        kv[j] = nn(rv[...], w[:, cols_at(j, 768)]).astype(BF)
        return carry

    lax.fori_loop(0, 3, block, 0)
    store(kv.at[0], query)
    store(kv.at[1], keyval.at[:, 0:768])
    store(kv.at[2], keyval.at[:, 768:1536])
    for copy in stores:
        copy.wait()


def head_masks(scale):
    lane = iota((1, 128), 1)
    first = jnp.where(lane < 64, scale, 0.0).astype(BF)
    second = jnp.where(lane >= 64, scale, 0.0).astype(BF)
    return first, second


def stack_heads(pair, masks):
    return jnp.concatenate([pair * masks[0], pair * masks[1]], axis=0)


def window_bias(place, lengths, r):
    lane = iota((1, 128), 1) + place[0] * 128
    end, start = jnp.int32(0), jnp.zeros((1, 128), I32)
    for j in range(8):
        end = end + lengths[r, j]
        start = jnp.where(end <= lane, end, start)
    start = start - (place[0] - 2) * 128
    key = iota((384, 128), 0)
    allowed = (key >= start) & (key <= iota((384, 128), 1) + 256)
    half = jnp.where(allowed, 0.0, MASKED)
    return jnp.concatenate([half, half], axis=1)


def join_heads(both):
    one = jnp.where(iota((128, 128), 0) < 64, both[:, :128], both[:, 128:])
    return one.T


def copies(sources, targets, sems):
    out = [
        pltpu.make_async_copy(a, b, sems.at[i]) for i, (a, b) in enumerate(zip(sources, targets))
    ]
    for copy in out:
        copy.start()
    return out


def lanes_of(p, offset=0):
    return slice(offset + 128 * p, offset + 128 * (p + 1))


def forward_kernel(
    place, lengths, gain, bias, gain_two, bias_two, target,
    behind_two, early, late, weight, keyval, query, x, proj,
    unit_halo, context_out, attended, log_out, after_out, sent,
    b2, e1, l1, w, q, xv, wp, units, rows_in, context, att, aft, snd, in_sems, out_sems,
):
    loads = copies(
        [behind_two, early, late, weight, keyval, query, x, proj],
        [b2, e1, l1, w, context.at[:, 256:384, :], q, xv, wp],
        in_sems,
    )
    scales = head_masks(HEAD_SIZE ** (-0.5))
    for copy in loads[:3]:
        copy.wait()

    def norm_row(r, carry):
        halo = jnp.concatenate([b2[r], e1[r] + l1[r]], axis=0).astype(F32)
        unit, _ = norm_parts(halo)
        units[r] = unit.astype(BF)
        rows_in[r] = (unit * row(gain) + row(bias)).astype(BF)
        return carry

    lax.fori_loop(0, 4, norm_row, 0)
    unit_copy = pltpu.make_async_copy(units, unit_halo, out_sems.at[0])
    unit_copy.start()
    loads[3].wait()

    def keyval_block(j, carry):
        source = pl.ds(pl.multiple_of(768 + 512 * j, 256), 512)
        fresh = nn(rows_in[...].reshape(1024, 768), w[:, source])
        context[:, 0:256, cols_at(j, 512)] = fresh.astype(BF).reshape(4, 256, 512)
        return carry

    lax.fori_loop(0, 3, keyval_block, 0)
    for copy in loads[4:6]:
        copy.wait()
    context_copy = pltpu.make_async_copy(context, context_out, out_sems.at[1])
    context_copy.start()

    def one_row(r, carry):
        mask = window_bias(place, lengths, r)
        pairs = range(PAIRS)
        stacked = [stack_heads(q[r, :, lanes_of(p)], scales) for p in pairs]
        scores = [nt(context[r, :, lanes_of(p)], stacked[p]) + mask for p in pairs]
        tops = [jnp.max(a, axis=0, keepdims=True) for a in scores]
        weights = [jnp.exp(a - t) for a, t in zip(scores, tops)]
        totals = [jnp.sum(a, axis=0, keepdims=True) for a in weights]
        shares = [(a * (1.0 / t)).astype(BF) for a, t in zip(weights, totals)]
        mixed = [tn(context[r, :, lanes_of(p, 768)], shares[p]) for p in pairs]
        for p in pairs:
            log_out[r, p : p + 1, :] = tops[p] + jnp.log(totals[p])
            att[r, :, lanes_of(p)] = join_heads(mixed[p]).astype(BF)
        return carry

    lax.fori_loop(0, 4, one_row, 0)
    att_copy = pltpu.make_async_copy(att, attended, out_sems.at[2])
    att_copy.start()
    loads[6].wait()
    loads[7].wait()
    after = xv[...].reshape(512, 768).astype(F32) + nn(att[...].reshape(512, 768), wp[...])
    aft[...] = after
    after_copy = pltpu.make_async_copy(aft, after_out, out_sems.at[3])
    after_copy.start()
    unit, _ = norm_parts(after)
    rows = (unit * row(gain_two) + row(bias_two)).astype(BF)
    sends = []
    for i in range(2):
        part = slice(512 * i, 512 * (i + 1))
        placing = (iota((512, 512), 0) + 512 * i == target[0:1, :]).astype(F32).astype(BF)
        snd[part, :] = nn(placing, rows).astype(BF)
        sends.append(pltpu.make_async_copy(snd.at[part], sent.at[part], out_sems.at[4 + i]))
        sends[-1].start()
    for copy in [unit_copy, context_copy, att_copy, after_copy] + sends:
        copy.wait()


def active_grad_kernel(grad, down, out):
    out[0] = nt(grad[...], down[...]).astype(BF)


def gelu_both(v):
    c = 0.7978845608028654
    square = v * v
    p = c + (c * 0.044715) * square
    gate = 0.5 + 0.5 * jnp.tanh(v * p)
    value = v * gate
    return value, gate + value * (1.0 - gate) * (6.0 * p - 4.0 * c)


def expert_kernel(x, up, raw, active, hidden_grad, back, total):
    step = pl.program_id(0)

    @pl.when(step == 0)
    def _():
        total[...] = jnp.zeros_like(total)

    parts = [slice(256 * r, 256 * (r + 1)) for r in range(4)]
    hidden = [nn(x[rows, :], up[...]) for rows in parts]
    lows = []
    for rows, v in zip(parts, hidden):
        value, slope = gelu_both(v)
        active[0, rows, :] = value.astype(BF)
        low = (raw[0, rows, :].astype(F32) * slope).astype(BF)
        hidden_grad[0, rows, :] = low
        lows.append(low)
    for rows, low in zip(parts, lows):
        total[rows, :] += nt(low, up[...])

    @pl.when(step == pl.num_programs(0) - 1)
    def _():
        back[...] = total[...].astype(BF)


def turn_kernel(unit, unit_halo, grad, out, grad_t):
    out[0:768, 0:512] = unit[...].T
    out[0:768, 512:1536] = unit_halo[...].T
    out[768:784, :] = jnp.ones((16, 1536), BF)
    grad_t[...] = grad[...].T


def weight_kernel(place, x, grad_t, active, hidden_grad, down, out, mine, away, x_t, total):
    step = pl.program_id(0)

    @pl.when(step == 0)
    def _():
        total[...] = jnp.zeros_like(total)
        x_t[...] = x[...].T

    total[...] += nn(active[0], down[...])
    one = nn(x_t[...], hidden_grad[0])
    two = nn(grad_t[...], active[0])
    even = place[0] % 2 == 0
    for i, both in enumerate([one, two]):
        mine[0, i] = jnp.where(even, both[:, :384], both[:, 384:]).astype(BF)
        away[0, i] = jnp.where(even, both[:, 384:], both[:, :384]).astype(BF)

    @pl.when(step == pl.num_programs(0) - 1)
    def _():
        out[...] = total[...].astype(BF)


def output_kernel(after, target, returned, out):
    placing = (iota((512, 1024), 1).astype(F32) == column(target[0:1, :].astype(F32))).astype(F32).astype(BF)
    out[...] = (after[...] + nn(placing, returned[...])).astype(BF)


def cols_at(j, size=256):
    return pl.ds(pl.multiple_of(size * j, size), size)


def fill_halves(
    turned, query_grad, context_grad, weight, gain, bias, proj_part, terms_two, tally,
    out, gain_wide, bias_wide, gain_sum, bias_sum,
):
    gain_wide[...] = jnp.broadcast_to(row(gain), (256, 768)).T
    bias_wide[...] = jnp.broadcast_to(row(bias), (256, 768)).T

    def finish(block, both):
        body, sums = both[0:768], both[768:769]
        half, step = block // 6, block % 6
        out[half, 768 * step : 768 * (step + 1), :] = (
            gain_wide[...] * body + bias_wide[...] * sums
        ).astype(BF)
        wide = weight[:, 256 * block : 256 * (block + 1)].astype(F32)
        if block == 0:
            gain_sum[...] = wide * body
            bias_sum[...] = wide * sums
        else:
            gain_sum[...] += wide * body
            bias_sum[...] += wide * sums

    for j in range(3):
        finish(j, nn(turned[:, 0:512], query_grad[:, 256 * j : 256 * (j + 1)]))
        out[1, 768 * (3 + j) : 768 * (4 + j), :] = proj_part[j]
    for j in range(6):
        finish(3 + j, nn(turned[...], context_grad[:, 256 * j : 256 * (j + 1)]))

    columns = jnp.concatenate(
        [
            jnp.broadcast_to(jnp.sum(gain_sum[...], axis=1, keepdims=True), (768, 128)),
            jnp.broadcast_to(jnp.sum(bias_sum[...], axis=1, keepdims=True), (768, 128)),
        ],
        axis=1,
    ).T
    out[:, GEMM_ROWS:, :] = jnp.zeros((2, HALF_ROWS - GEMM_ROWS, 256), BF)
    for t in range(3):
        lanes = slice(256 * t, 256 * (t + 1))
        block = jnp.concatenate(
            [columns[0:1, lanes], columns[128:129, lanes], terms_two[:, lanes], jnp.zeros((12, 256), F32)],
            axis=0,
        )
        out[0, GEMM_ROWS + 16 * t : GEMM_ROWS + 16 * t + 16, :] = block.astype(BF)
    out[0, GEMM_ROWS + 48 : GEMM_ROWS + 64, 0:128] = tally[...].astype(BF)


def backward_kernel(
    place, lengths, gain_two, gain, bias, target, turn, log_total, tally,
    back, after, grad, proj, attended, query, context, turned, weight,
    after_grad, query_grad, own_grad, input_two, input_one, keep, away,
    bk, af, gr, wp, att, q, ctx, tu, w, ag, do, dq, cg, pp, ip, out,
    gain_wide, bias_wide, gain_sum, bias_sum, terms, in_sems, out_sems,
):
    loads = copies(
        [back, after, grad, proj, attended, query, context, turned, weight],
        [bk, af, gr, wp, att, q, ctx, tu, w],
        in_sems,
    )
    scales = head_masks(HEAD_SIZE ** (-0.5))
    ones = head_masks(1.0)
    placing = (iota((512, 1024), 1).astype(F32) == column(target[0:1, :].astype(F32))).astype(F32).astype(BF)
    live = column(flat_line(turn))
    loads[0].wait()
    normed_grad = nn(placing, bk[...])
    loads[1].wait()
    unit, inverse = norm_parts(af[...])
    terms[0:1, :] = jnp.sum(normed_grad * unit, axis=0, keepdims=True)
    terms[1:2, :] = jnp.sum(normed_grad, axis=0, keepdims=True)
    loads[2].wait()
    total = gr[...].astype(F32) * live + norm_back(normed_grad, row(gain_two), unit, inverse)
    ag[...] = total
    stores = [pltpu.make_async_copy(ag, after_grad, out_sems.at[0])]
    stores[0].start()
    low = total.astype(BF)
    loads[3].wait()
    do[...] = nt(low, wp[...]).astype(BF).reshape(4, 128, 768)
    loads[4].wait()
    mixed = nn(att[...].T, low).astype(BF)
    for j in range(3):
        pp[j] = mixed[:, 256 * j : 256 * (j + 1)]
    loads[5].wait()
    loads[6].wait()

    def one_row(r, carry):
        mask = window_bias(place, lengths, r)
        pairs = range(PAIRS)
        stacked = [stack_heads(q[r, :, lanes_of(p)], scales) for p in pairs]
        grads = [stack_heads(do[r, :, lanes_of(p)], ones) for p in pairs]
        scores = [nt(ctx[r, :, lanes_of(p)], stacked[p]) for p in pairs]
        share_grads = [nt(ctx[r, :, lanes_of(p, 768)], grads[p]) for p in pairs]
        shares = [jnp.exp(scores[p] + mask - log_total[r, p : p + 1, :]) for p in pairs]
        sums = [jnp.sum(a * b, axis=0, keepdims=True) for a, b in zip(shares, share_grads)]
        score_grads = [(a * (b - c)).astype(BF) for a, b, c in zip(shares, share_grads, sums)]
        key_grads = [nn(score_grads[p], stacked[p]).astype(BF) for p in pairs]
        value_grads = [nn(shares[p].astype(BF), grads[p]).astype(BF) for p in pairs]
        turned_grads = [tn(ctx[r, :, lanes_of(p)], score_grads[p]) for p in pairs]
        halo = pl.ds(pl.multiple_of(512 + r * 256, 256), 256)
        own = pl.ds(pl.multiple_of(r * 128, 128), 128)
        for p in pairs:
            cg[halo, lanes_of(p)] = key_grads[p][:256]
            cg[own, lanes_of(p)] = key_grads[p][256:]
            cg[halo, lanes_of(p, 768)] = value_grads[p][:256]
            cg[own, lanes_of(p, 768)] = value_grads[p][256:]
            dq[own, lanes_of(p)] = (join_heads(turned_grads[p]) * HEAD_SIZE ** (-0.5)).astype(BF)
        return carry

    lax.fori_loop(0, 4, one_row, 0)
    loads[7].wait()
    loads[8].wait()

    def store(source, target):
        stores.append(pltpu.make_async_copy(source, target, out_sems.at[len(stores)]))
        stores[-1].start()

    store(dq, query_grad)
    store(cg.at[0:512], own_grad)
    ip[...] = nt(cg[512:1536, :], w[:, 768:]).astype(BF).reshape(4, 256, 768)
    store(ip.at[:, 0:128], input_two)
    store(ip.at[:, 128:256], input_one)
    fill_halves(
        tu, dq, cg, w, gain, bias, pp, terms, tally, out, gain_wide, bias_wide, gain_sum, bias_sum
    )
    core = place[0] % 2

    @pl.when(core == 0)
    def _():
        pltpu.make_async_copy(out.at[0], keep, out_sems.at[5]).start()
        pltpu.make_async_copy(out.at[1], away, out_sems.at[6]).start()

    @pl.when(core == 1)
    def _():
        pltpu.make_async_copy(out.at[1], keep, out_sems.at[5]).start()
        pltpu.make_async_copy(out.at[0], away, out_sems.at[6]).start()

    for copy in stores:
        copy.wait()
    pltpu.make_async_copy(out.at[0], keep, out_sems.at[5]).wait()
    pltpu.make_async_copy(out.at[1], away, out_sems.at[6]).wait()


def place_half(half, bits, pieces, qkv, proj, whole, stage, in_sems, sems):
    loads = []
    for i in range(2):
        for j in range(2):
            first = pl.multiple_of((2 * i + (bits[i] + j) % 2) * PIECE, PIECE)
            target = whole.at[pl.ds(first, PIECE)]
            loads.append(pltpu.make_async_copy(pieces[2 * i + j], target, in_sems.at[2 * i + j]))
            loads[-1].start()
    for copy in loads:
        copy.wait()
    for j in range(6):
        stage[j] = whole[768 * j : 768 * (j + 1), :].astype(F32)
        lanes = slice(256 * (j % 3), 256 * (j % 3 + 1))

        @pl.when(half == 0)
        def _():
            pltpu.make_async_copy(stage.at[j], qkv.at[:, 256 * j : 256 * (j + 1)], sems.at[j]).start()

        @pl.when(half == 1)
        def _():
            target = qkv.at[:, 1536 + 256 * j : 1792 + 256 * j] if j < 3 else proj.at[:, lanes]
            pltpu.make_async_copy(stage.at[j], target, sems.at[j]).start()

    for j in range(6):
        pltpu.make_async_copy(stage.at[j], proj.at[:, 0:256], sems.at[j]).wait()


def finish_mine_kernel(place, a, b, c, d, qkv, proj, tail, whole, stage, in_sems, sems):
    place_half(place[2], (place[3], place[4]), (a, b, c, d), qkv, proj, whole, stage, in_sems, sems)
    tail[...] = whole[GEMM_ROWS : GEMM_ROWS + 64, :]


def finish_other_kernel(
    place, tail, a, b, c, d, qkv_in, proj_in, qkv, proj, gain_one, bias_one, gain_two, bias_two, counts, received,
    whole, stage, in_sems, sems,
):
    place_half(1 - place[2], (place[5], place[6]), (a, b, c, d), qkv, proj, whole, stage, in_sems, sems)
    both = tail[...].astype(F32) + whole[GEMM_ROWS : GEMM_ROWS + 64, :].astype(F32)
    for i, out in enumerate([gain_one, bias_one, gain_two, bias_two]):
        line = jnp.concatenate([both[16 * t + i : 16 * t + i + 1, :] for t in range(3)], axis=1)
        out[...] = line.reshape(768)
    every = both[48:64, 0:128]
    counts[...] = nt(jnp.ones((8, 128), BF), every.astype(BF))[0:1, :].astype(I32).reshape(16)
    chosen = (iota((16, 128), 0) == place[1]) & ((iota((16, 128), 1) >> 4) == place[0])
    mine = jnp.where(chosen, every, 0.0).astype(BF)
    fold = ((iota((128, 16), 0) & 15) == iota((128, 16), 1)).astype(F32).astype(BF)
    received[0] = jnp.sum(nn(mine, fold), axis=0, keepdims=True).astype(I32)


def chunk_of(a, b):
    return 2 * b + (a + b) % 2


def add_chunks(plan, buffer, in_sems):
    loads = []
    for n, picks in enumerate(plan):
        for m, pick_ref in enumerate(picks):
            loads.append(pltpu.make_async_copy(pick_ref, buffer.at[n, m], in_sems.at[n, m]))
            loads[-1].start()
    return loads


def summed(buffer, n, count):
    total = buffer[n, 0].astype(F32)
    for m in range(1, count):
        total = total + buffer[n, m].astype(F32)
    return total


def expert_first_kernel(spots, own, got, one, two, buffer, made, in_sems, out_sems):
    a, b = spots[7], spots[8]
    wanted = [(chunk_of(1 - a, k), 0) for k in range(2)] + [(chunk_of(k, 1 - b), 1) for k in range(2)]
    plan = [[own.at[c, t], got.at[c, t]] for c, t in wanted]
    loads = add_chunks(plan, buffer, in_sems)
    stores = []
    for n in range(4):
        loads[2 * n].wait()
        loads[2 * n + 1].wait()
        made[n] = summed(buffer, n, 2).astype(BF)
        stores.append(pltpu.make_async_copy(made.at[n], (one, two)[n // 2].at[n % 2], out_sems.at[n]))
        stores[-1].start()
    for copy in stores:
        copy.wait()


def expert_second_kernel(spots, own, got, first, second, one, two, buffer, made, in_sems, out_sems):
    a, b = spots[7], spots[8]
    c, d = chunk_of(a, 1 - b), chunk_of(1 - a, b)
    plan = [
        [own.at[c, 0], got.at[c, 0], first.at[1 - b]],
        [own.at[d, 1], got.at[d, 1], second.at[1 - a]],
    ]
    loads = add_chunks(plan, buffer, in_sems)
    stores = []
    for n in range(2):
        for copy in loads[3 * n : 3 * n + 3]:
            copy.wait()
        made[n] = summed(buffer, n, 3).astype(BF)
        stores.append(pltpu.make_async_copy(made.at[n], (one, two)[n], out_sems.at[n]))
        stores[-1].start()
    for copy in stores:
        copy.wait()


def expert_last_kernel(spots, own, got, first, second, third, fourth, up, down, buffer, in_sems):
    a, b = spots[7], spots[8]
    c = chunk_of(a, b)
    plan = [
        [own.at[c, 0], got.at[c, 0], first.at[b], third],
        [own.at[c, 1], got.at[c, 1], second.at[a], fourth],
    ]
    loads = add_chunks(plan, buffer, in_sems)
    for copy in loads[:4]:
        copy.wait()
    up[0] = summed(buffer, 0, 4)
    for copy in loads[4:]:
        copy.wait()
    down[0] = summed(buffer, 1, 4).T


def input_own_kernel(query_grad, own_grad, weight, out, dq, og, w, in_sems):
    for copy in copies([weight, query_grad, own_grad], [w, dq, og], in_sems):
        copy.wait()
    out[...] = nt(dq[...], w[:, :768]) + nt(og[...], w[:, 768:])


def input_grad_kernel(
    even, gain, own, x, from_one, from_two, after_grad, out, ov, xv, one, two, ag, in_sems,
):
    loads = copies(
        [x, own, from_one, from_two, after_grad],
        [xv, ov, one, two, ag],
        in_sems,
    )
    loads[0].wait()
    unit, inverse = norm_parts(xv[...].astype(F32))
    for copy in loads[1:]:
        copy.wait()
    total = ov[...] + two[...].astype(F32) + even[0] * one[...].astype(F32)
    out[...] = ag[...] + norm_back(total, row(gain), unit, inverse)


PAIR_ONE = [b ^ 1 for b in range(4)]
PAIR_TWO = [b ^ 3 for b in range(4)]
PAIRS_OF = [PAIR_ONE, PAIR_TWO]
BOTH = ("batch", "seq")


def by_core(even_move, odd_move):
    pairs = []
    for b in range(16):
        for s in range(8):
            x, y = (even_move, odd_move)[s % 2](b & 3, b >> 2)
            pairs.append((b * 8 + s, (y * 4 + x) * 8 + s))
    return pairs


def first_pairs(pair):
    return by_core(lambda x, y: (pair[x], y), lambda x, y: (x, pair[y]))


def second_step(d):
    return by_core(lambda x, y: (x, (y + d) & 3), lambda x, y: ((x + d) & 3, y))


def along_z(d):
    return [(s, (s + 2 * d) & 7) for s in range(8)]


def pick(array, index):
    return lax.dynamic_index_in_dim(array, index, 0, keepdims=False)


def part_of(array, index):
    return lax.dynamic_index_in_dim(array, index % 4, 1, keepdims=False)


def bits_of(place):
    return [(place & 1) ^ (place >> 1), place >> 1]


def z_pairs(pair):
    return [(s, pair[s // 2] * 2 + s % 2) for s in range(8)]


def sum_start(bits, keep, got):
    def part(stream, bit, first=0, size=PIECE):
        at = (stream * 2 + bit) * PIECE + first
        return rows_at(keep, at, size).astype(F32) + rows_at(got, at, size).astype(F32)

    return part, [part(i, 1 - bits[i]).astype(BF) for i in range(2)]


def pair_moves(data, pairs):
    return [lax.ppermute(a, BOTH, first_pairs(pair)) for a, pair in zip(data, pairs)]


def rows_at(array, at, size):
    return lax.dynamic_slice(array, (at, 0), (size, array.shape[1]))


def sum_middle(bits, part, moved):
    size = PIECE // 2

    def rows_of(i, bit):
        return part(i, bits[i], bit * size, size) + rows_at(moved[i], bit * size, size).astype(F32)

    return [rows_of(i, bits[1 - i]) for i in range(2)], [rows_of(i, 1 - bits[1 - i]).astype(BF) for i in range(2)]


def group(chunks):
    size, lanes = chunks[0].shape
    return jnp.stack(chunks).reshape(2, 4, size // 4, lanes)


def sum_across(place, grouped):
    total = part_of(grouped, place).astype(F32)
    for d in (2, 1, 3):
        total = total + lax.ppermute(part_of(grouped, place + d), BOTH, second_step(d)).astype(F32)
    return total.astype(BF)


def sum_along(whole):
    total = whole.astype(F32)
    for d in (2, 1, 3):
        total = total + lax.ppermute(whole, "seq", along_z(d)).astype(F32)
    return total.astype(BF)


def gather_across(place, piece):
    size, lanes = PIECE // 2, piece.shape[-1]
    parts = [piece] + [lax.ppermute(piece, BOTH, second_step(d)) for d in (1, 2, 3)]
    stack = jnp.stack(parts, axis=1)
    ordered = jnp.stack([part_of(stack, place - p + 4) for p in range(4)], axis=1).reshape(2, size, lanes)
    return [ordered[0], ordered[1]]


def gather_pairs(bits, ordered):
    moved = pair_moves(ordered, PAIRS_OF[::-1])
    return [
        jnp.where(bit == 0, jnp.stack([a, b]), jnp.stack([b, a])).reshape(PIECE, a.shape[1])
        for bit, a, b in zip(bits[::-1], ordered, moved)
    ]


def hold(*values):
    return lax.optimization_barrier(values)


def exchange(array):
    return lax.all_to_all(
        array.reshape(16, CAP, 768), "batch", split_axis=0, concat_axis=0, tiled=True
    ).reshape(1024, 768)


def local(
    block_input, token_ids, hash_table, doc_lengths, turn_mask, attn_norm_gain, attn_norm_bias,
    qkv_weight, proj_weight, ffn_norm_gain, ffn_norm_bias, expert_up, expert_down, out_grad,
):
    seq = lax.axis_index("seq")
    owner = lax.axis_index("batch")
    odd = seq % 2
    flat = (512, 768)
    rows3 = (4, 128, 768)
    depth = seq // 2
    turn = jnp.where(odd == 0, owner // 4, owner % 4)
    bits = bits_of(jnp.where(odd == 0, owner % 4, owner // 4))
    place = jnp.stack([seq, owner, odd, *bits, *bits_of(turn), *bits_of(depth)]).astype(I32)
    spots = place
    up, down = expert_up[0], expert_down[0]

    behind_two = lax.ppermute(block_input, "seq", AHEAD_TWO)
    early = lax.ppermute(block_input, "seq", UP_ONE)

    table = jnp.pad(hash_table, (0, 8192 - 8008)).reshape(64, 128)
    target, tally, grad_sent, unit, query, keyval = kernel_call(
        entry_kernel,
        [
            shape((8, 512), I32), shape((16, 128), F32), shape((1024, 768)), shape(flat), shape(flat),
            shape((512, 1536)),
        ],
        [
            place, token_ids, table, turn_mask, attn_norm_gain, attn_norm_bias, block_input.reshape(flat),
            out_grad.reshape(flat), qkv_weight,
        ],
        "entry", 3 * 10**9,
        in_specs=[SM] + [VM] * 5 + [HB] * 3,
        out_specs=[VM] * 2 + [HB] * 4,
        scratch=[
            pltpu.VMEM(flat, BF), pltpu.VMEM(flat, BF), pltpu.VMEM((768, 2304), BF), pltpu.VMEM((1024, 768), BF),
            pltpu.VMEM(flat, BF), pltpu.VMEM(flat, BF), pltpu.VMEM((3, 512, 768), BF),
            pltpu.SemaphoreType.DMA((3,)), pltpu.SemaphoreType.DMA((5,)),
        ],
    )
    grad_rows = exchange(grad_sent)

    behind_two, query = hold(behind_two, query)
    late = lax.ppermute(behind_two, "seq", DOWN_ONE)
    query, keyval = query.reshape(rows3), keyval.reshape(4, 128, 1536)

    unit_halo, context, attended, log_total, after, rows_sent = kernel_call(
        forward_kernel,
        [
            shape((4, 256, 768)), shape((4, 384, 1536)), shape(rows3), shape((4, 8, 256), F32),
            shape(flat, F32), shape((1024, 768)),
        ],
        [
            place, doc_lengths, attn_norm_gain, attn_norm_bias, ffn_norm_gain, ffn_norm_bias, target,
            behind_two, early, late, qkv_weight, keyval, query, block_input, proj_weight,
        ],
        "forward", 10**9,
        in_specs=[SM] * 2 + [VM] * 5 + [HB] * 8,
        out_specs=[HB] * 3 + [VM] + [HB] * 2,
        scratch=[
            pltpu.VMEM(rows3, BF), pltpu.VMEM(rows3, BF), pltpu.VMEM(rows3, BF), pltpu.VMEM((768, 2304), BF),
            pltpu.VMEM(rows3, BF), pltpu.VMEM(rows3, BF), pltpu.VMEM((768, 768), BF),
            pltpu.VMEM((4, 256, 768), BF), pltpu.VMEM((4, 256, 768), BF), pltpu.VMEM((4, 384, 1536), BF),
            pltpu.VMEM(rows3, BF), pltpu.VMEM(flat, F32), pltpu.VMEM((1024, 768), BF),
            pltpu.SemaphoreType.DMA((8,)), pltpu.SemaphoreType.DMA((6,)),
        ],
    )
    rows = exchange(rows_sent)

    turned, grad_t = kernel_call(
        turn_kernel,
        [shape((784, 1536)), shape((768, 1024))],
        [unit, unit_halo.reshape(1024, 768), grad_rows],
        "turn", 10**6,
    )
    grad_rows, turned, grad_t = hold(grad_rows, turned, grad_t)
    tile = pl.BlockSpec((1, 1024, 768), lambda i: (i, 0, 0))
    tiled = shape((4, 1024, 768))
    whole = pl.BlockSpec((1024, 768), lambda i: (0, 0))
    raw = kernel_call(
        active_grad_kernel,
        [tiled],
        [grad_rows, down],
        "active_grad", 48 * 10**8,
        grid=(4,),
        in_specs=[whole, pl.BlockSpec((768, 768), lambda i: (i, 0))],
        out_specs=[tile],
    )[0]

    active, hidden_grad, back_sent = kernel_call(
        expert_kernel,
        [tiled, tiled, shape((1024, 768))],
        [rows, up, raw],
        "expert", 97 * 10**8,
        grid=(4,),
        in_specs=[whole, pl.BlockSpec((768, 768), lambda i: (0, i)), tile],
        out_specs=[tile, tile, whole],
        scratch=[pltpu.VMEM((1024, 768), F32)],
    )
    back = exchange(back_sent)

    result, parts, parts_away = kernel_call(
        weight_kernel,
        [shape((1024, 768)), shape((4, 2, 768, 384)), shape((4, 2, 768, 384))],
        [place, rows, grad_t, active, hidden_grad, down],
        "weights", 145 * 10**8,
        grid=(4,),
        in_specs=[
            SM,
            whole,
            pl.BlockSpec((768, 1024), lambda i: (0, 0)),
            tile,
            tile,
            pl.BlockSpec((768, 768), lambda i: (i, 0)),
        ],
        out_specs=[
            pl.BlockSpec((1024, 768), lambda i: (0, 0)),
            pl.BlockSpec((1, 2, 768, 384), lambda i: (i, 0, 0, 0)),
            pl.BlockSpec((1, 2, 768, 384), lambda i: (i, 0, 0, 0)),
        ],
        scratch=[pltpu.VMEM((768, 1024), BF), pltpu.VMEM((1024, 768), F32)],
    )
    returned = exchange(result)
    parts_away, back = hold(parts_away, back)
    parts_got = lax.ppermute(parts_away, "seq", SWAP)
    block = shape((768, 384))
    first_sent = kernel_call(
        expert_first_kernel, [shape((2, 768, 384))] * 2, [spots, parts, parts_got], "expert_first", 10**6,
        in_specs=[SM] + [HB] * 2, out_specs=[HB] * 2,
        scratch=[
            pltpu.VMEM((4, 2, 768, 384), BF), pltpu.VMEM((4, 768, 384), BF),
            pltpu.SemaphoreType.DMA((4, 2)), pltpu.SemaphoreType.DMA((4,)),
        ],
    )
    back, *first_sent = hold(back, *first_sent)
    routes = [z_pairs(pair) for pair in PAIRS_OF]
    first_got = [lax.ppermute(a, "seq", route) for a, route in zip(first_sent, routes)]

    after_grad, query_grad, own_grad, input_two, input_one, keep, away = kernel_call(
        backward_kernel,
        [
            shape(flat, F32), shape(flat), shape((512, 1536)), shape(rows3), shape(rows3),
            shape((HALF_ROWS, 256)), shape((HALF_ROWS, 256)),
        ],
        [
            place, doc_lengths, ffn_norm_gain, attn_norm_gain, attn_norm_bias, target, turn_mask, log_total, tally,
            back, after, out_grad.reshape(flat), proj_weight, attended.reshape(flat), query, context, turned,
            qkv_weight,
        ],
        "backward", 16 * 10**9,
        in_specs=[SM] * 2 + [VM] * 7 + [HB] * 9,
        out_specs=[HB] * 7,
        scratch=[
            pltpu.VMEM((1024, 768), BF), pltpu.VMEM(flat, F32), pltpu.VMEM(flat, BF), pltpu.VMEM((768, 768), BF),
            pltpu.VMEM(flat, BF), pltpu.VMEM(rows3, BF), pltpu.VMEM((4, 384, 1536), BF),
            pltpu.VMEM((784, 1536), BF), pltpu.VMEM((768, 2304), BF), pltpu.VMEM(flat, F32), pltpu.VMEM(rows3, BF),
            pltpu.VMEM(flat, BF), pltpu.VMEM((1536, 1536), BF), pltpu.VMEM((3, 768, 256), BF),
            pltpu.VMEM((4, 256, 768), BF), pltpu.VMEM((2, HALF_ROWS, 256), BF),
            pltpu.VMEM((768, 256), F32), pltpu.VMEM((768, 256), F32), pltpu.VMEM((768, 256), F32),
            pltpu.VMEM((768, 256), F32), pltpu.VMEM((2, 768), F32),
            pltpu.SemaphoreType.DMA((9,)), pltpu.SemaphoreType.DMA((7,)),
        ],
    )
    away, returned, *first_got = hold(away, returned, *first_got)
    got = lax.ppermute(away, "seq", SWAP)
    from_one = lax.ppermute(input_one, "seq", SWAP)
    second_sent = kernel_call(
        expert_second_kernel, [block] * 2, [spots, parts, parts_got, *first_got], "expert_second", 10**6,
        in_specs=[SM] + [HB] * 4, out_specs=[HB] * 2,
        scratch=[
            pltpu.VMEM((2, 3, 768, 384), BF), pltpu.VMEM((2, 768, 384), BF),
            pltpu.SemaphoreType.DMA((2, 3)), pltpu.SemaphoreType.DMA((2,)),
        ],
    )
    block_output = kernel_call(
        output_kernel, [shape(flat)], [after, target, returned], "output", 8 * 10**8
    )[0]
    got, from_one, block_output, *second_sent = hold(got, from_one, block_output, *second_sent)
    part, sent = sum_start(bits, keep, got)
    sent[0], sent[1], query_grad, *second_sent = hold(sent[0], sent[1], query_grad, *second_sent)

    moved = pair_moves(sent, PAIRS_OF)
    second_got = [lax.ppermute(second_sent[i], "seq", routes[1 - i]) for i in range(2)]
    own_part = kernel_call(
        input_own_kernel, [shape(flat, F32)], [query_grad, own_grad, qkv_weight], "input_own", 2 * 10**9,
        in_specs=[HB] * 3,
        scratch=[
            pltpu.VMEM(flat, BF), pltpu.VMEM((512, 1536), BF), pltpu.VMEM((768, 2304), BF),
            pltpu.SemaphoreType.DMA((3,)),
        ],
    )[0]
    moved[0], moved[1], own_part = hold(moved[0], moved[1], own_part)

    chunks, sent = sum_middle(bits, part, moved)
    sent[0], sent[1], from_one = hold(sent[0], sent[1], from_one)
    moved = pair_moves(sent, PAIRS_OF[::-1])
    passed = jnp.where(odd == 1, input_two + from_one, input_two)
    moved[0], moved[1], passed, *second_got = hold(moved[0], moved[1], passed, *second_got)
    chunks = [(a + b.astype(F32)).astype(BF) for a, b in zip(chunks, moved)]
    grouped = group(chunks)
    whole = sum_across(turn, grouped)
    piece = sum_along(whole)
    piece, passed = hold(piece, passed)
    from_two = lax.ppermute(passed, "seq", BACK_TWO)
    ordered = gather_across(turn, piece)
    ordered[0], ordered[1], *second_got = hold(ordered[0], ordered[1], *second_got)
    up_sum, down_sum = kernel_call(
        expert_last_kernel,
        [shape((1, 768, 384), F32), shape((1, 384, 768), F32)],
        [spots, parts, parts_got, *first_got, *second_got],
        "expert_last", 10**6,
        in_specs=[SM] + [HB] * 6,
        scratch=[pltpu.VMEM((2, 4, 768, 384), BF), pltpu.SemaphoreType.DMA((2, 4))],
    )
    chunks = gather_pairs(bits, ordered)
    chunks[0], chunks[1], up_sum, from_two = hold(chunks[0], chunks[1], up_sum, from_two)
    even = (1 - odd).astype(F32).reshape(1)
    input_grad = kernel_call(
        input_grad_kernel,
        [shape(flat, F32)],
        [
            even, attn_norm_gain, own_part, block_input.reshape(flat), from_one.reshape(flat),
            from_two.reshape(flat), after_grad,
        ],
        "input_grad", 10**7,
        in_specs=[SM, VM] + [HB] * 5,
        scratch=[
            pltpu.VMEM(flat, F32), pltpu.VMEM(flat, BF), pltpu.VMEM(flat, BF), pltpu.VMEM(flat, BF),
            pltpu.VMEM(flat, F32), pltpu.SemaphoreType.DMA((5,)),
        ],
    )[0]
    moved = pair_moves(chunks, PAIRS_OF)
    moved[0], moved[1], input_grad = hold(moved[0], moved[1], input_grad)
    mine = [chunks[0], moved[0], chunks[1], moved[1]]
    swapped = [lax.ppermute(a, "seq", SWAP) for a in mine]
    sums = [shape((768, 2304), F32), shape((768, 768), F32)]
    landing = [
        pltpu.VMEM((HALF_ROWS, 256), BF), pltpu.VMEM((6, 768, 256), F32),
        pltpu.SemaphoreType.DMA((4,)), pltpu.SemaphoreType.DMA((6,)),
    ]
    qkv_half, proj_half, tail = kernel_call(
        finish_mine_kernel, sums + [shape((64, 256))], [spots, *mine], "finish_mine", 10**6,
        in_specs=[SM] + [HB] * 4, out_specs=[HB, HB, VM], scratch=landing,
    )
    line = shape((768,), F32)
    qkv_sum, proj_sum, *rest = kernel_call(
        finish_other_kernel,
        sums + [line] * 4 + [shape((16,), I32), shape((1, 1, 16), I32)],
        [spots, tail, *swapped, qkv_half, proj_half],
        "finish_other", 10**6,
        in_specs=[SM, VM] + [HB] * 6, out_specs=[HB] * 2 + [VM] * 6, scratch=landing,
        aliases={6: 0, 7: 1},
    )
    return (
        block_output.reshape(rows3),
        input_grad.reshape(rows3),
        rest[0],
        rest[1],
        qkv_sum,
        proj_sum,
        rest[2],
        rest[3],
        up_sum,
        down_sum,
        rest[4],
        rest[5],
    )


def solution(mesh):
    placed = (
        P("batch", "seq", None),
        P("batch", "seq"),
        P(),
        P("batch", None),
        P("batch", "seq"),
        P(),
        P(),
        P(),
        P(),
        P(),
        P(),
        P("batch", None, None),
        P("batch", None, None),
        P("batch", "seq", None),
    )
    return jax.shard_map(
        local,
        mesh=mesh,
        in_specs=placed,
        out_specs=(
            P("batch", "seq", None),
            P("batch", "seq", None),
            P(),
            P(),
            P(),
            P(),
            P(),
            P(),
            P("batch", None, "seq"),
            P("batch", "seq", None),
            P(),
            P("batch", "seq", None),
        ),
        check_vma=False,
    )
```

```python
import jax
import jax.numpy as jnp
from jax import lax
from jax.experimental import pallas as pl
from jax.experimental.pallas import tpu as pltpu
from jax.sharding import PartitionSpec as P

BF = jnp.bfloat16
F32 = jnp.float32
I32 = jnp.int32
EPS = 1e-05
MASKED = -1e30
HEADS = 12
HEAD_SIZE = 64
PAIRS = 6
CAP = 64
SWAP = [(i, i ^ 1) for i in range(8)]
UP_ONE = [(i, i + 1) for i in range(0, 8, 2)]
DOWN_ONE = [(i + 1, i) for i in range(0, 8, 2)]
AHEAD_TWO = [(i, i + 2) for i in range(6)]
BACK_TWO = [(i + 2, i) for i in range(6)]
HALF_ROWS = 4864
PIECE = HALF_ROWS // 4
VMEM_BYTES = 63 * 1024 * 1024 + 640 * 1024
GEMM_ROWS = 4608
VM = pl.BlockSpec(memory_space=pltpu.VMEM)
HB = pl.BlockSpec(memory_space=pl.ANY)
SM = pl.BlockSpec(memory_space=pltpu.SMEM)


def shape(dims, kind=BF):
    return jax.ShapeDtypeStruct(dims, kind)


def kernel_call(body, outs, args, name, flops, grid=None, in_specs=None, out_specs=None, scratch=(), aliases=None):
    moved = sum(a.size * a.dtype.itemsize for a in args) + sum(
        o.size * o.dtype.itemsize for o in outs
    )
    extra = {} if grid is None else {"grid": grid}
    return pl.pallas_call(
        body,
        out_shape=outs,
        in_specs=in_specs or [VM] * len(args),
        out_specs=out_specs or [VM] * len(outs),
        scratch_shapes=list(scratch),
        compiler_params=pltpu.CompilerParams(vmem_limit_bytes=VMEM_BYTES),
        cost_estimate=pl.CostEstimate(flops=flops, bytes_accessed=moved, transcendentals=0),
        name=name,
        input_output_aliases=aliases or {},
        **extra,
    )(*args)


def nn(a, b):
    return jnp.dot(a, b, preferred_element_type=F32)


def nt(a, b):
    return lax.dot_general(a, b, (((1,), (1,)), ((), ())), preferred_element_type=F32)


def tn(a, b):
    return lax.dot_general(a, b, (((0,), (0,)), ((), ())), preferred_element_type=F32)


def iota(dims, axis):
    return lax.broadcasted_iota(I32, dims, axis)


def row(ref):
    return ref[...].reshape(1, 768)


def column(line):
    return jnp.broadcast_to(line, (128, line.shape[1])).T[:, 0:1]


def flat_line(ref):
    return jnp.concatenate([ref[i : i + 1, :] for i in range(4)], axis=1).astype(F32)


def norm_parts(values):
    centred = values - jnp.mean(values, axis=-1, keepdims=True)
    inverse = lax.rsqrt(jnp.mean(centred * centred, axis=-1, keepdims=True) + EPS)
    return centred * inverse, inverse


def norm_back(grad, gain, unit, inverse):
    t = grad * gain
    return inverse * (
        t - jnp.mean(t, axis=-1, keepdims=True) - unit * jnp.mean(t * unit, axis=-1, keepdims=True)
    )


def entry_kernel(
    place, tok, table, turn, gain, bias, x, grad, weight, target_out, tally, sent, unit_out, query, keyval,
    xv, gv, w, sv, uv, rv, kv, in_sems, out_sems,
):
    loads = copies([x, grad, weight], [xv, gv, w], in_sems)
    ids = jnp.concatenate([tok[i : i + 1, :] for i in range(4)], axis=1)
    live = flat_line(turn)
    high, low = ids >> 7, ids & 127
    picked = tn(table[...].astype(F32).astype(BF), (iota((64, 512), 0) == high).astype(F32).astype(BF))
    chosen = jnp.sum(jnp.where(iota((128, 512), 0) == low, picked, 0.0), axis=0, keepdims=True)
    member = (iota((16, 512), 0) == chosen.astype(I32)).astype(F32)
    earlier = (iota((512, 512), 0) < iota((512, 512), 1)).astype(F32).astype(BF)
    before = nn(member.astype(BF), earlier)
    slot = jnp.sum(before * member, axis=0, keepdims=True)
    target = (chosen * CAP + slot).astype(I32)
    target_out[...] = jnp.broadcast_to(target, (8, 512))
    counts = jnp.sum(member, axis=1, keepdims=True)
    tally[...] = jnp.where(iota((16, 128), 1) == place[0] * 16 + place[1], counts, 0.0)
    stores = []

    def store(source, goal):
        stores.append(pltpu.make_async_copy(source, goal, out_sems.at[len(stores)]))
        stores[-1].start()

    loads[0].wait()
    unit, _ = norm_parts(xv[...].astype(F32))
    uv[...] = unit.astype(BF)
    store(uv, unit_out)
    rows = (unit * row(gain) + row(bias)).astype(BF)
    loads[1].wait()
    for i in range(2):
        placing = jnp.where(iota((512, 512), 0) + 512 * i == target, live, 0.0).astype(BF)
        sv[512 * i : 512 * (i + 1), :] = nn(placing, gv[...]).astype(BF)
    store(sv, sent)
    loads[2].wait()
    rv[...] = rows

    def block(j, carry):
        kv[j] = nn(rv[...], w[:, cols_at(j, 768)]).astype(BF)
        return carry

    lax.fori_loop(0, 3, block, 0)
    store(kv.at[0], query)
    store(kv.at[1], keyval.at[:, 0:768])
    store(kv.at[2], keyval.at[:, 768:1536])
    for copy in stores:
        copy.wait()


def head_masks(scale):
    lane = iota((1, 128), 1)
    first = jnp.where(lane < 64, scale, 0.0).astype(BF)
    second = jnp.where(lane >= 64, scale, 0.0).astype(BF)
    return first, second


def stack_heads(pair, masks):
    return jnp.concatenate([pair * masks[0], pair * masks[1]], axis=0)


def window_bias(place, lengths, r):
    lane = iota((1, 128), 1) + place[0] * 128
    end, start = jnp.int32(0), jnp.zeros((1, 128), I32)
    for j in range(8):
        end = end + lengths[r, j]
        start = jnp.where(end <= lane, end, start)
    start = start - (place[0] - 2) * 128
    key = iota((384, 128), 0)
    allowed = (key >= start) & (key <= iota((384, 128), 1) + 256)
    half = jnp.where(allowed, 0.0, MASKED)
    return jnp.concatenate([half, half], axis=1)


def join_heads(both):
    one = jnp.where(iota((128, 128), 0) < 64, both[:, :128], both[:, 128:])
    return one.T


def copies(sources, targets, sems):
    out = [
        pltpu.make_async_copy(a, b, sems.at[i]) for i, (a, b) in enumerate(zip(sources, targets))
    ]
    for copy in out:
        copy.start()
    return out


def lanes_of(p, offset=0):
    return slice(offset + 128 * p, offset + 128 * (p + 1))


def forward_kernel(
    place, lengths, gain, bias, gain_two, bias_two, target,
    behind_two, early, late, weight, keyval, query, x, proj,
    unit_halo, context_out, attended, log_out, after_out, sent,
    b2, e1, l1, w, q, xv, wp, units, rows_in, context, att, aft, snd, in_sems, out_sems,
):
    loads = copies(
        [behind_two, early, late, weight, keyval, query, x, proj],
        [b2, e1, l1, w, context.at[:, 256:384, :], q, xv, wp],
        in_sems,
    )
    scales = head_masks(HEAD_SIZE ** (-0.5))
    for copy in loads[:3]:
        copy.wait()

    def norm_row(r, carry):
        halo = jnp.concatenate([b2[r], e1[r] + l1[r]], axis=0).astype(F32)
        unit, _ = norm_parts(halo)
        units[r] = unit.astype(BF)
        rows_in[r] = (unit * row(gain) + row(bias)).astype(BF)
        return carry

    lax.fori_loop(0, 4, norm_row, 0)
    unit_copy = pltpu.make_async_copy(units, unit_halo, out_sems.at[0])
    unit_copy.start()
    loads[3].wait()

    def keyval_block(j, carry):
        source = pl.ds(pl.multiple_of(768 + 512 * j, 256), 512)
        fresh = nn(rows_in[...].reshape(1024, 768), w[:, source])
        context[:, 0:256, cols_at(j, 512)] = fresh.astype(BF).reshape(4, 256, 512)
        return carry

    lax.fori_loop(0, 3, keyval_block, 0)
    for copy in loads[4:6]:
        copy.wait()
    context_copy = pltpu.make_async_copy(context, context_out, out_sems.at[1])
    context_copy.start()

    def one_row(r, carry):
        mask = window_bias(place, lengths, r)
        pairs = range(PAIRS)
        stacked = [stack_heads(q[r, :, lanes_of(p)], scales) for p in pairs]
        scores = [nt(context[r, :, lanes_of(p)], stacked[p]) + mask for p in pairs]
        tops = [jnp.max(a, axis=0, keepdims=True) for a in scores]
        weights = [jnp.exp(a - t) for a, t in zip(scores, tops)]
        totals = [jnp.sum(a, axis=0, keepdims=True) for a in weights]
        shares = [(a * (1.0 / t)).astype(BF) for a, t in zip(weights, totals)]
        mixed = [tn(context[r, :, lanes_of(p, 768)], shares[p]) for p in pairs]
        for p in pairs:
            log_out[r, p : p + 1, :] = tops[p] + jnp.log(totals[p])
            att[r, :, lanes_of(p)] = join_heads(mixed[p]).astype(BF)
        return carry

    lax.fori_loop(0, 4, one_row, 0)
    att_copy = pltpu.make_async_copy(att, attended, out_sems.at[2])
    att_copy.start()
    loads[6].wait()
    loads[7].wait()
    after = xv[...].reshape(512, 768).astype(F32) + nn(att[...].reshape(512, 768), wp[...])
    aft[...] = after
    after_copy = pltpu.make_async_copy(aft, after_out, out_sems.at[3])
    after_copy.start()
    unit, _ = norm_parts(after)
    rows = (unit * row(gain_two) + row(bias_two)).astype(BF)
    sends = []
    for i in range(2):
        part = slice(512 * i, 512 * (i + 1))
        placing = (iota((512, 512), 0) + 512 * i == target[0:1, :]).astype(F32).astype(BF)
        snd[part, :] = nn(placing, rows).astype(BF)
        sends.append(pltpu.make_async_copy(snd.at[part], sent.at[part], out_sems.at[4 + i]))
        sends[-1].start()
    for copy in [unit_copy, context_copy, att_copy, after_copy] + sends:
        copy.wait()


def active_grad_kernel(grad, down, out):
    out[0] = nt(grad[...], down[...]).astype(BF)


def gelu_both(v):
    c = 0.7978845608028654
    square = v * v
    p = c + (c * 0.044715) * square
    gate = 0.5 + 0.5 * jnp.tanh(v * p)
    value = v * gate
    return value, gate + value * (1.0 - gate) * (6.0 * p - 4.0 * c)


def expert_kernel(x, up, raw, active, hidden_grad, back, total):
    step = pl.program_id(0)

    @pl.when(step == 0)
    def _():
        total[...] = jnp.zeros_like(total)

    parts = [slice(256 * r, 256 * (r + 1)) for r in range(4)]
    hidden = [nn(x[rows, :], up[...]) for rows in parts]
    lows = []
    for rows, v in zip(parts, hidden):
        value, slope = gelu_both(v)
        active[0, rows, :] = value.astype(BF)
        low = (raw[0, rows, :].astype(F32) * slope).astype(BF)
        hidden_grad[0, rows, :] = low
        lows.append(low)
    for rows, low in zip(parts, lows):
        total[rows, :] += nt(low, up[...])

    @pl.when(step == pl.num_programs(0) - 1)
    def _():
        back[...] = total[...].astype(BF)


def turn_kernel(unit, unit_halo, grad, out, grad_t):
    out[0:768, 0:512] = unit[...].T
    out[0:768, 512:1536] = unit_halo[...].T
    out[768:784, :] = jnp.ones((16, 1536), BF)
    grad_t[...] = grad[...].T


def weight_kernel(
    place, x, grad_t, active, hidden_grad, down, out, mine, away, xv, gv, x_t, total, sems
):
    step = pl.program_id(0)
    loads = [pltpu.make_async_copy(x, xv, sems.at[0]), pltpu.make_async_copy(grad_t, gv, sems.at[1])]

    @pl.when(step == 0)
    def _():
        for copy in loads:
            copy.start()
        total[...] = nn(active[0], down[...])
        for copy in loads:
            copy.wait()
        x_t[...] = xv[...].T

    @pl.when(step > 0)
    def _():
        total[...] += nn(active[0], down[...])

    one = nn(x_t[...], hidden_grad[0])
    two = nn(gv[...], active[0])
    even = place[0] % 2 == 0
    for i, both in enumerate([one, two]):
        mine[0, i] = jnp.where(even, both[:, :384], both[:, 384:]).astype(BF)
        away[0, i] = jnp.where(even, both[:, 384:], both[:, :384]).astype(BF)

    @pl.when(step == pl.num_programs(0) - 1)
    def _():
        out[...] = total[...].astype(BF)


def output_kernel(after, target, returned, out):
    placing = (iota((512, 1024), 1).astype(F32) == column(target[0:1, :].astype(F32))).astype(F32).astype(BF)
    out[...] = (after[...] + nn(placing, returned[...])).astype(BF)


def cols_at(j, size=256):
    return pl.ds(pl.multiple_of(size * j, size), size)


def fill_halves(
    turned, query_grad, context_grad, weight, gain, bias, proj_part, terms_two, tally,
    out, gain_wide, bias_wide, gain_sum, bias_sum,
):
    gain_wide[...] = jnp.broadcast_to(row(gain), (256, 768)).T
    bias_wide[...] = jnp.broadcast_to(row(bias), (256, 768)).T

    def finish(block, both):
        body, sums = both[0:768], both[768:769]
        half, step = block // 6, block % 6
        out[half, 768 * step : 768 * (step + 1), :] = (
            gain_wide[...] * body + bias_wide[...] * sums
        ).astype(BF)
        wide = weight[:, 256 * block : 256 * (block + 1)].astype(F32)
        if block == 0:
            gain_sum[...] = wide * body
            bias_sum[...] = wide * sums
        else:
            gain_sum[...] += wide * body
            bias_sum[...] += wide * sums

    for j in range(3):
        finish(j, nn(turned[:, 0:512], query_grad[:, 256 * j : 256 * (j + 1)]))
        out[1, 768 * (3 + j) : 768 * (4 + j), :] = proj_part[j]
    for j in range(6):
        finish(3 + j, nn(turned[...], context_grad[:, 256 * j : 256 * (j + 1)]))

    columns = jnp.concatenate(
        [
            jnp.broadcast_to(jnp.sum(gain_sum[...], axis=1, keepdims=True), (768, 128)),
            jnp.broadcast_to(jnp.sum(bias_sum[...], axis=1, keepdims=True), (768, 128)),
        ],
        axis=1,
    ).T
    out[:, GEMM_ROWS:, :] = jnp.zeros((2, HALF_ROWS - GEMM_ROWS, 256), BF)
    for t in range(3):
        lanes = slice(256 * t, 256 * (t + 1))
        block = jnp.concatenate(
            [columns[0:1, lanes], columns[128:129, lanes], terms_two[:, lanes], jnp.zeros((12, 256), F32)],
            axis=0,
        )
        out[0, GEMM_ROWS + 16 * t : GEMM_ROWS + 16 * t + 16, :] = block.astype(BF)
    out[0, GEMM_ROWS + 48 : GEMM_ROWS + 64, 0:128] = tally[...].astype(BF)


def backward_kernel(
    place, lengths, gain_two, gain, bias, target, turn, log_total, tally,
    back, after, grad, proj, attended, query, context, turned, weight,
    after_grad, query_grad, own_grad, input_two, input_one, keep, away,
    bk, af, gr, wp, att, q, ctx, tu, w, ag, do, dq, cg, pp, ip, out,
    gain_wide, bias_wide, gain_sum, bias_sum, terms, in_sems, out_sems,
):
    loads = copies(
        [back, after, grad, proj, attended, query, context, turned, weight],
        [bk, af, gr, wp, att, q, ctx, tu, w],
        in_sems,
    )
    scales = head_masks(HEAD_SIZE ** (-0.5))
    ones = head_masks(1.0)
    placing = (iota((512, 1024), 1).astype(F32) == column(target[0:1, :].astype(F32))).astype(F32).astype(BF)
    live = column(flat_line(turn))
    loads[0].wait()
    normed_grad = nn(placing, bk[...])
    loads[1].wait()
    unit, inverse = norm_parts(af[...])
    terms[0:1, :] = jnp.sum(normed_grad * unit, axis=0, keepdims=True)
    terms[1:2, :] = jnp.sum(normed_grad, axis=0, keepdims=True)
    loads[2].wait()
    total = gr[...].astype(F32) * live + norm_back(normed_grad, row(gain_two), unit, inverse)
    ag[...] = total
    stores = [pltpu.make_async_copy(ag, after_grad, out_sems.at[0])]
    stores[0].start()
    low = total.astype(BF)
    loads[3].wait()
    do[...] = nt(low, wp[...]).astype(BF).reshape(4, 128, 768)
    loads[4].wait()
    mixed = nn(att[...].T, low).astype(BF)
    for j in range(3):
        pp[j] = mixed[:, 256 * j : 256 * (j + 1)]
    loads[5].wait()
    loads[6].wait()

    def one_row(r, carry):
        mask = window_bias(place, lengths, r)
        pairs = range(PAIRS)
        stacked = [stack_heads(q[r, :, lanes_of(p)], scales) for p in pairs]
        grads = [stack_heads(do[r, :, lanes_of(p)], ones) for p in pairs]
        scores = [nt(ctx[r, :, lanes_of(p)], stacked[p]) for p in pairs]
        share_grads = [nt(ctx[r, :, lanes_of(p, 768)], grads[p]) for p in pairs]
        shares = [jnp.exp(scores[p] + mask - log_total[r, p : p + 1, :]) for p in pairs]
        sums = [jnp.sum(a * b, axis=0, keepdims=True) for a, b in zip(shares, share_grads)]
        score_grads = [(a * (b - c)).astype(BF) for a, b, c in zip(shares, share_grads, sums)]
        key_grads = [nn(score_grads[p], stacked[p]).astype(BF) for p in pairs]
        value_grads = [nn(shares[p].astype(BF), grads[p]).astype(BF) for p in pairs]
        turned_grads = [tn(ctx[r, :, lanes_of(p)], score_grads[p]) for p in pairs]
        halo = pl.ds(pl.multiple_of(512 + r * 256, 256), 256)
        own = pl.ds(pl.multiple_of(r * 128, 128), 128)
        for p in pairs:
            cg[halo, lanes_of(p)] = key_grads[p][:256]
            cg[own, lanes_of(p)] = key_grads[p][256:]
            cg[halo, lanes_of(p, 768)] = value_grads[p][:256]
            cg[own, lanes_of(p, 768)] = value_grads[p][256:]
            dq[own, lanes_of(p)] = (join_heads(turned_grads[p]) * HEAD_SIZE ** (-0.5)).astype(BF)
        return carry

    lax.fori_loop(0, 4, one_row, 0)
    loads[7].wait()
    loads[8].wait()

    def store(source, target):
        stores.append(pltpu.make_async_copy(source, target, out_sems.at[len(stores)]))
        stores[-1].start()

    store(dq, query_grad)
    store(cg.at[0:512], own_grad)
    ip[...] = nt(cg[512:1536, :], w[:, 768:]).astype(BF).reshape(4, 256, 768)
    store(ip.at[:, 0:128], input_two)
    store(ip.at[:, 128:256], input_one)
    fill_halves(
        tu, dq, cg, w, gain, bias, pp, terms, tally, out, gain_wide, bias_wide, gain_sum, bias_sum
    )
    core = place[0] % 2

    @pl.when(core == 0)
    def _():
        pltpu.make_async_copy(out.at[0], keep, out_sems.at[5]).start()
        pltpu.make_async_copy(out.at[1], away, out_sems.at[6]).start()

    @pl.when(core == 1)
    def _():
        pltpu.make_async_copy(out.at[1], keep, out_sems.at[5]).start()
        pltpu.make_async_copy(out.at[0], away, out_sems.at[6]).start()

    for copy in stores:
        copy.wait()
    pltpu.make_async_copy(out.at[0], keep, out_sems.at[5]).wait()
    pltpu.make_async_copy(out.at[1], away, out_sems.at[6]).wait()


def place_half(half, bits, pieces, qkv, proj, whole, stage, in_sems, sems):
    loads = []
    for i in range(2):
        for j in range(2):
            first = pl.multiple_of((2 * i + (bits[i] + j) % 2) * PIECE, PIECE)
            target = whole.at[pl.ds(first, PIECE)]
            loads.append(pltpu.make_async_copy(pieces[2 * i + j], target, in_sems.at[2 * i + j]))
            loads[-1].start()
    for copy in loads:
        copy.wait()
    for j in range(6):
        stage[j] = whole[768 * j : 768 * (j + 1), :].astype(F32)
        lanes = slice(256 * (j % 3), 256 * (j % 3 + 1))

        @pl.when(half == 0)
        def _():
            pltpu.make_async_copy(stage.at[j], qkv.at[:, 256 * j : 256 * (j + 1)], sems.at[j]).start()

        @pl.when(half == 1)
        def _():
            target = qkv.at[:, 1536 + 256 * j : 1792 + 256 * j] if j < 3 else proj.at[:, lanes]
            pltpu.make_async_copy(stage.at[j], target, sems.at[j]).start()

    for j in range(6):
        pltpu.make_async_copy(stage.at[j], proj.at[:, 0:256], sems.at[j]).wait()


def finish_mine_kernel(place, a, b, c, d, qkv, proj, tail, whole, stage, in_sems, sems):
    place_half(place[2], (place[3], place[4]), (a, b, c, d), qkv, proj, whole, stage, in_sems, sems)
    tail[...] = whole[GEMM_ROWS : GEMM_ROWS + 64, :]


def finish_other_kernel(
    place, tail, a, b, c, d, qkv_in, proj_in, qkv, proj, gain_one, bias_one, gain_two, bias_two, counts, received,
    whole, stage, in_sems, sems,
):
    place_half(1 - place[2], (place[5], place[6]), (a, b, c, d), qkv, proj, whole, stage, in_sems, sems)
    both = tail[...].astype(F32) + whole[GEMM_ROWS : GEMM_ROWS + 64, :].astype(F32)
    for i, out in enumerate([gain_one, bias_one, gain_two, bias_two]):
        line = jnp.concatenate([both[16 * t + i : 16 * t + i + 1, :] for t in range(3)], axis=1)
        out[...] = line.reshape(768)
    every = both[48:64, 0:128]
    counts[...] = nt(jnp.ones((8, 128), BF), every.astype(BF))[0:1, :].astype(I32).reshape(16)
    chosen = (iota((16, 128), 0) == place[1]) & ((iota((16, 128), 1) >> 4) == place[0])
    mine = jnp.where(chosen, every, 0.0).astype(BF)
    fold = ((iota((128, 16), 0) & 15) == iota((128, 16), 1)).astype(F32).astype(BF)
    received[0] = jnp.sum(nn(mine, fold), axis=0, keepdims=True).astype(I32)


def chunk_of(a, b):
    return 2 * b + (a + b) % 2


def add_chunks(plan, buffer, in_sems):
    loads = []
    for n, picks in enumerate(plan):
        for m, pick_ref in enumerate(picks):
            loads.append(pltpu.make_async_copy(pick_ref, buffer.at[n, m], in_sems.at[n, m]))
            loads[-1].start()
    return loads


def summed(buffer, n, count):
    total = buffer[n, 0].astype(F32)
    for m in range(1, count):
        total = total + buffer[n, m].astype(F32)
    return total


def expert_first_kernel(spots, own, got, one, two, buffer, made, in_sems, out_sems):
    a, b = spots[7], spots[8]
    wanted = [(chunk_of(1 - a, k), 0) for k in range(2)] + [(chunk_of(k, 1 - b), 1) for k in range(2)]
    plan = [[own.at[c, t], got.at[c, t]] for c, t in wanted]
    loads = add_chunks(plan, buffer, in_sems)
    stores = []
    for n in range(4):
        loads[2 * n].wait()
        loads[2 * n + 1].wait()
        made[n] = summed(buffer, n, 2).astype(BF)
        stores.append(pltpu.make_async_copy(made.at[n], (one, two)[n // 2].at[n % 2], out_sems.at[n]))
        stores[-1].start()
    for copy in stores:
        copy.wait()


def expert_second_kernel(spots, own, got, first, second, one, two, buffer, made, in_sems, out_sems):
    a, b = spots[7], spots[8]
    c, d = chunk_of(a, 1 - b), chunk_of(1 - a, b)
    plan = [
        [own.at[c, 0], got.at[c, 0], first.at[1 - b]],
        [own.at[d, 1], got.at[d, 1], second.at[1 - a]],
    ]
    loads = add_chunks(plan, buffer, in_sems)
    stores = []
    for n in range(2):
        for copy in loads[3 * n : 3 * n + 3]:
            copy.wait()
        made[n] = summed(buffer, n, 3).astype(BF)
        stores.append(pltpu.make_async_copy(made.at[n], (one, two)[n], out_sems.at[n]))
        stores[-1].start()
    for copy in stores:
        copy.wait()


def expert_last_kernel(spots, own, got, first, second, third, fourth, up, down, buffer, in_sems):
    a, b = spots[7], spots[8]
    c = chunk_of(a, b)
    plan = [
        [own.at[c, 0], got.at[c, 0], first.at[b], third],
        [own.at[c, 1], got.at[c, 1], second.at[a], fourth],
    ]
    loads = add_chunks(plan, buffer, in_sems)
    for copy in loads[:4]:
        copy.wait()
    up[0] = summed(buffer, 0, 4)
    for copy in loads[4:]:
        copy.wait()
    down[0] = summed(buffer, 1, 4).T


def input_own_kernel(query_grad, own_grad, weight, out, dq, og, w, in_sems):
    for copy in copies([weight, query_grad, own_grad], [w, dq, og], in_sems):
        copy.wait()
    out[...] = nt(dq[...], w[:, :768]) + nt(og[...], w[:, 768:])


def input_grad_kernel(
    even, gain, own, x, from_one, from_two, after_grad, out, ov, xv, one, two, ag, in_sems,
):
    loads = copies(
        [x, own, from_one, from_two, after_grad],
        [xv, ov, one, two, ag],
        in_sems,
    )
    loads[0].wait()
    unit, inverse = norm_parts(xv[...].astype(F32))
    for copy in loads[1:]:
        copy.wait()
    total = ov[...] + two[...].astype(F32) + even[0] * one[...].astype(F32)
    out[...] = ag[...] + norm_back(total, row(gain), unit, inverse)


PAIR_ONE = [b ^ 1 for b in range(4)]
PAIR_TWO = [b ^ 3 for b in range(4)]
PAIRS_OF = [PAIR_ONE, PAIR_TWO]
BOTH = ("batch", "seq")


def by_core(even_move, odd_move):
    pairs = []
    for b in range(16):
        for s in range(8):
            x, y = (even_move, odd_move)[s % 2](b & 3, b >> 2)
            pairs.append((b * 8 + s, (y * 4 + x) * 8 + s))
    return pairs


def first_pairs(pair):
    return by_core(lambda x, y: (pair[x], y), lambda x, y: (x, pair[y]))


def second_step(d):
    return by_core(lambda x, y: (x, (y + d) & 3), lambda x, y: ((x + d) & 3, y))


def along_z(d):
    return [(s, (s + 2 * d) & 7) for s in range(8)]


def pick(array, index):
    return lax.dynamic_index_in_dim(array, index, 0, keepdims=False)


def part_of(array, index):
    return lax.dynamic_index_in_dim(array, index % 4, 1, keepdims=False)


def bits_of(place):
    return [(place & 1) ^ (place >> 1), place >> 1]


def z_pairs(pair):
    return [(s, pair[s // 2] * 2 + s % 2) for s in range(8)]


def sum_start(bits, keep, got):
    def part(stream, bit, first=0, size=PIECE):
        at = (stream * 2 + bit) * PIECE + first
        return rows_at(keep, at, size).astype(F32) + rows_at(got, at, size).astype(F32)

    return part, [part(i, 1 - bits[i]).astype(BF) for i in range(2)]


def pair_moves(data, pairs):
    return [lax.ppermute(a, BOTH, first_pairs(pair)) for a, pair in zip(data, pairs)]


def rows_at(array, at, size):
    return lax.dynamic_slice(array, (at, 0), (size, array.shape[1]))


def sum_middle(bits, part, moved):
    size = PIECE // 2

    def rows_of(i, bit):
        return part(i, bits[i], bit * size, size) + rows_at(moved[i], bit * size, size).astype(F32)

    return [rows_of(i, bits[1 - i]) for i in range(2)], [rows_of(i, 1 - bits[1 - i]).astype(BF) for i in range(2)]


def group(chunks):
    size, lanes = chunks[0].shape
    return jnp.stack(chunks).reshape(2, 4, size // 4, lanes)


def sum_across(place, grouped):
    total = part_of(grouped, place).astype(F32)
    for d in (2, 1, 3):
        total = total + lax.ppermute(part_of(grouped, place + d), BOTH, second_step(d)).astype(F32)
    return total.astype(BF)


def sum_along(whole):
    total = whole.astype(F32)
    for d in (2, 1, 3):
        total = total + lax.ppermute(whole, "seq", along_z(d)).astype(F32)
    return total.astype(BF)


def gather_across(place, piece):
    size, lanes = PIECE // 2, piece.shape[-1]
    parts = [piece] + [lax.ppermute(piece, BOTH, second_step(d)) for d in (1, 2, 3)]
    stack = jnp.stack(parts, axis=1)
    ordered = jnp.stack([part_of(stack, place - p + 4) for p in range(4)], axis=1).reshape(2, size, lanes)
    return [ordered[0], ordered[1]]


def gather_pairs(bits, ordered):
    moved = pair_moves(ordered, PAIRS_OF[::-1])
    return [
        jnp.where(bit == 0, jnp.stack([a, b]), jnp.stack([b, a])).reshape(PIECE, a.shape[1])
        for bit, a, b in zip(bits[::-1], ordered, moved)
    ]


def hold(*values):
    return lax.optimization_barrier(values)


def exchange(array):
    return lax.all_to_all(
        array.reshape(16, CAP, 768), "batch", split_axis=0, concat_axis=0, tiled=True
    ).reshape(1024, 768)


def local(
    block_input, token_ids, hash_table, doc_lengths, turn_mask, attn_norm_gain, attn_norm_bias,
    qkv_weight, proj_weight, ffn_norm_gain, ffn_norm_bias, expert_up, expert_down, out_grad,
):
    seq = lax.axis_index("seq")
    owner = lax.axis_index("batch")
    odd = seq % 2
    flat = (512, 768)
    rows3 = (4, 128, 768)
    depth = seq // 2
    turn = jnp.where(odd == 0, owner // 4, owner % 4)
    bits = bits_of(jnp.where(odd == 0, owner % 4, owner // 4))
    place = jnp.stack([seq, owner, odd, *bits, *bits_of(turn), *bits_of(depth)]).astype(I32)
    spots = place
    up, down = expert_up[0], expert_down[0]

    behind_two = lax.ppermute(block_input, "seq", AHEAD_TWO)
    early = lax.ppermute(block_input, "seq", UP_ONE)

    table = jnp.pad(hash_table, (0, 8192 - 8008)).reshape(64, 128)
    target, tally, grad_sent, unit, query, keyval = kernel_call(
        entry_kernel,
        [
            shape((8, 512), I32), shape((16, 128), F32), shape((1024, 768)), shape(flat), shape(flat),
            shape((512, 1536)),
        ],
        [
            place, token_ids, table, turn_mask, attn_norm_gain, attn_norm_bias, block_input.reshape(flat),
            out_grad.reshape(flat), qkv_weight,
        ],
        "entry", 3 * 10**9,
        in_specs=[SM] + [VM] * 5 + [HB] * 3,
        out_specs=[VM] * 2 + [HB] * 4,
        scratch=[
            pltpu.VMEM(flat, BF), pltpu.VMEM(flat, BF), pltpu.VMEM((768, 2304), BF), pltpu.VMEM((1024, 768), BF),
            pltpu.VMEM(flat, BF), pltpu.VMEM(flat, BF), pltpu.VMEM((3, 512, 768), BF),
            pltpu.SemaphoreType.DMA((3,)), pltpu.SemaphoreType.DMA((5,)),
        ],
    )
    grad_rows = exchange(grad_sent)

    behind_two, query = hold(behind_two, query)
    late = lax.ppermute(behind_two, "seq", DOWN_ONE)
    query, keyval = query.reshape(rows3), keyval.reshape(4, 128, 1536)

    unit_halo, context, attended, log_total, after, rows_sent = kernel_call(
        forward_kernel,
        [
            shape((4, 256, 768)), shape((4, 384, 1536)), shape(rows3), shape((4, 8, 256), F32),
            shape(flat, F32), shape((1024, 768)),
        ],
        [
            place, doc_lengths, attn_norm_gain, attn_norm_bias, ffn_norm_gain, ffn_norm_bias, target,
            behind_two, early, late, qkv_weight, keyval, query, block_input, proj_weight,
        ],
        "forward", 10**9,
        in_specs=[SM] * 2 + [VM] * 5 + [HB] * 8,
        out_specs=[HB] * 3 + [VM] + [HB] * 2,
        scratch=[
            pltpu.VMEM(rows3, BF), pltpu.VMEM(rows3, BF), pltpu.VMEM(rows3, BF), pltpu.VMEM((768, 2304), BF),
            pltpu.VMEM(rows3, BF), pltpu.VMEM(rows3, BF), pltpu.VMEM((768, 768), BF),
            pltpu.VMEM((4, 256, 768), BF), pltpu.VMEM((4, 256, 768), BF), pltpu.VMEM((4, 384, 1536), BF),
            pltpu.VMEM(rows3, BF), pltpu.VMEM(flat, F32), pltpu.VMEM((1024, 768), BF),
            pltpu.SemaphoreType.DMA((8,)), pltpu.SemaphoreType.DMA((6,)),
        ],
    )
    rows = exchange(rows_sent)

    turned, grad_t = kernel_call(
        turn_kernel,
        [shape((784, 1536)), shape((768, 1024))],
        [unit, unit_halo.reshape(1024, 768), grad_rows],
        "turn", 10**6,
    )
    grad_rows, turned, grad_t = hold(grad_rows, turned, grad_t)
    tile = pl.BlockSpec((1, 1024, 768), lambda i: (i, 0, 0))
    tiled = shape((4, 1024, 768))
    whole = pl.BlockSpec((1024, 768), lambda i: (0, 0))
    raw = kernel_call(
        active_grad_kernel,
        [tiled],
        [grad_rows, down],
        "active_grad", 48 * 10**8,
        grid=(4,),
        in_specs=[whole, pl.BlockSpec((768, 768), lambda i: (i, 0))],
        out_specs=[tile],
    )[0]

    active, hidden_grad, back_sent = kernel_call(
        expert_kernel,
        [tiled, tiled, shape((1024, 768))],
        [rows, up, raw],
        "expert", 97 * 10**8,
        grid=(4,),
        in_specs=[whole, pl.BlockSpec((768, 768), lambda i: (0, i)), tile],
        out_specs=[tile, tile, whole],
        scratch=[pltpu.VMEM((1024, 768), F32)],
    )
    back = exchange(back_sent)

    result, parts, parts_away = kernel_call(
        weight_kernel,
        [shape((1024, 768)), shape((4, 2, 768, 384)), shape((4, 2, 768, 384))],
        [place, rows, grad_t, active, hidden_grad, down],
        "weights", 145 * 10**8,
        grid=(4,),
        in_specs=[
            SM,
            HB,
            HB,
            tile,
            tile,
            pl.BlockSpec((768, 768), lambda i: (i, 0)),
        ],
        out_specs=[
            pl.BlockSpec((1024, 768), lambda i: (0, 0)),
            pl.BlockSpec((1, 2, 768, 384), lambda i: (i, 0, 0, 0)),
            pl.BlockSpec((1, 2, 768, 384), lambda i: (i, 0, 0, 0)),
        ],
        scratch=[
            pltpu.VMEM((1024, 768), BF), pltpu.VMEM((768, 1024), BF), pltpu.VMEM((768, 1024), BF),
            pltpu.VMEM((1024, 768), F32), pltpu.SemaphoreType.DMA((2,)),
        ],
    )
    returned = exchange(result)
    parts_away, back = hold(parts_away, back)
    parts_got = lax.ppermute(parts_away, "seq", SWAP)
    block = shape((768, 384))
    first_sent = kernel_call(
        expert_first_kernel, [shape((2, 768, 384))] * 2, [spots, parts, parts_got], "expert_first", 10**6,
        in_specs=[SM] + [HB] * 2, out_specs=[HB] * 2,
        scratch=[
            pltpu.VMEM((4, 2, 768, 384), BF), pltpu.VMEM((4, 768, 384), BF),
            pltpu.SemaphoreType.DMA((4, 2)), pltpu.SemaphoreType.DMA((4,)),
        ],
    )
    back, *first_sent = hold(back, *first_sent)
    routes = [z_pairs(pair) for pair in PAIRS_OF]
    first_got = [lax.ppermute(a, "seq", route) for a, route in zip(first_sent, routes)]

    after_grad, query_grad, own_grad, input_two, input_one, keep, away = kernel_call(
        backward_kernel,
        [
            shape(flat, F32), shape(flat), shape((512, 1536)), shape(rows3), shape(rows3),
            shape((HALF_ROWS, 256)), shape((HALF_ROWS, 256)),
        ],
        [
            place, doc_lengths, ffn_norm_gain, attn_norm_gain, attn_norm_bias, target, turn_mask, log_total, tally,
            back, after, out_grad.reshape(flat), proj_weight, attended.reshape(flat), query, context, turned,
            qkv_weight,
        ],
        "backward", 16 * 10**9,
        in_specs=[SM] * 2 + [VM] * 7 + [HB] * 9,
        out_specs=[HB] * 7,
        scratch=[
            pltpu.VMEM((1024, 768), BF), pltpu.VMEM(flat, F32), pltpu.VMEM(flat, BF), pltpu.VMEM((768, 768), BF),
            pltpu.VMEM(flat, BF), pltpu.VMEM(rows3, BF), pltpu.VMEM((4, 384, 1536), BF),
            pltpu.VMEM((784, 1536), BF), pltpu.VMEM((768, 2304), BF), pltpu.VMEM(flat, F32), pltpu.VMEM(rows3, BF),
            pltpu.VMEM(flat, BF), pltpu.VMEM((1536, 1536), BF), pltpu.VMEM((3, 768, 256), BF),
            pltpu.VMEM((4, 256, 768), BF), pltpu.VMEM((2, HALF_ROWS, 256), BF),
            pltpu.VMEM((768, 256), F32), pltpu.VMEM((768, 256), F32), pltpu.VMEM((768, 256), F32),
            pltpu.VMEM((768, 256), F32), pltpu.VMEM((2, 768), F32),
            pltpu.SemaphoreType.DMA((9,)), pltpu.SemaphoreType.DMA((7,)),
        ],
    )
    away, returned, *first_got = hold(away, returned, *first_got)
    got = lax.ppermute(away, "seq", SWAP)
    from_one = lax.ppermute(input_one, "seq", SWAP)
    second_sent = kernel_call(
        expert_second_kernel, [block] * 2, [spots, parts, parts_got, *first_got], "expert_second", 10**6,
        in_specs=[SM] + [HB] * 4, out_specs=[HB] * 2,
        scratch=[
            pltpu.VMEM((2, 3, 768, 384), BF), pltpu.VMEM((2, 768, 384), BF),
            pltpu.SemaphoreType.DMA((2, 3)), pltpu.SemaphoreType.DMA((2,)),
        ],
    )
    block_output = kernel_call(
        output_kernel, [shape(flat)], [after, target, returned], "output", 8 * 10**8
    )[0]
    got, from_one, block_output, *second_sent = hold(got, from_one, block_output, *second_sent)
    part, sent = sum_start(bits, keep, got)
    sent[0], sent[1], query_grad, *second_sent = hold(sent[0], sent[1], query_grad, *second_sent)

    moved = pair_moves(sent, PAIRS_OF)
    second_got = [lax.ppermute(second_sent[i], "seq", routes[1 - i]) for i in range(2)]
    own_part = kernel_call(
        input_own_kernel, [shape(flat, F32)], [query_grad, own_grad, qkv_weight], "input_own", 2 * 10**9,
        in_specs=[HB] * 3,
        scratch=[
            pltpu.VMEM(flat, BF), pltpu.VMEM((512, 1536), BF), pltpu.VMEM((768, 2304), BF),
            pltpu.SemaphoreType.DMA((3,)),
        ],
    )[0]
    moved[0], moved[1], own_part = hold(moved[0], moved[1], own_part)

    chunks, sent = sum_middle(bits, part, moved)
    sent[0], sent[1], from_one = hold(sent[0], sent[1], from_one)
    moved = pair_moves(sent, PAIRS_OF[::-1])
    passed = jnp.where(odd == 1, input_two + from_one, input_two)
    moved[0], moved[1], passed, *second_got = hold(moved[0], moved[1], passed, *second_got)
    chunks = [(a + b.astype(F32)).astype(BF) for a, b in zip(chunks, moved)]
    grouped = group(chunks)
    whole = sum_across(turn, grouped)
    piece = sum_along(whole)
    piece, passed = hold(piece, passed)
    from_two = lax.ppermute(passed, "seq", BACK_TWO)
    ordered = gather_across(turn, piece)
    ordered[0], ordered[1], *second_got = hold(ordered[0], ordered[1], *second_got)
    up_sum, down_sum = kernel_call(
        expert_last_kernel,
        [shape((1, 768, 384), F32), shape((1, 384, 768), F32)],
        [spots, parts, parts_got, *first_got, *second_got],
        "expert_last", 10**6,
        in_specs=[SM] + [HB] * 6,
        scratch=[pltpu.VMEM((2, 4, 768, 384), BF), pltpu.SemaphoreType.DMA((2, 4))],
    )
    chunks = gather_pairs(bits, ordered)
    chunks[0], chunks[1], up_sum, from_two = hold(chunks[0], chunks[1], up_sum, from_two)
    even = (1 - odd).astype(F32).reshape(1)
    input_grad = kernel_call(
        input_grad_kernel,
        [shape(flat, F32)],
        [
            even, attn_norm_gain, own_part, block_input.reshape(flat), from_one.reshape(flat),
            from_two.reshape(flat), after_grad,
        ],
        "input_grad", 10**7,
        in_specs=[SM, VM] + [HB] * 5,
        scratch=[
            pltpu.VMEM(flat, F32), pltpu.VMEM(flat, BF), pltpu.VMEM(flat, BF), pltpu.VMEM(flat, BF),
            pltpu.VMEM(flat, F32), pltpu.SemaphoreType.DMA((5,)),
        ],
    )[0]
    moved = pair_moves(chunks, PAIRS_OF)
    moved[0], moved[1], input_grad = hold(moved[0], moved[1], input_grad)
    mine = [chunks[0], moved[0], chunks[1], moved[1]]
    swapped = [lax.ppermute(a, "seq", SWAP) for a in mine]
    sums = [shape((768, 2304), F32), shape((768, 768), F32)]
    landing = [
        pltpu.VMEM((HALF_ROWS, 256), BF), pltpu.VMEM((6, 768, 256), F32),
        pltpu.SemaphoreType.DMA((4,)), pltpu.SemaphoreType.DMA((6,)),
    ]
    qkv_half, proj_half, tail = kernel_call(
        finish_mine_kernel, sums + [shape((64, 256))], [spots, *mine], "finish_mine", 10**6,
        in_specs=[SM] + [HB] * 4, out_specs=[HB, HB, VM], scratch=landing,
    )
    line = shape((768,), F32)
    qkv_sum, proj_sum, *rest = kernel_call(
        finish_other_kernel,
        sums + [line] * 4 + [shape((16,), I32), shape((1, 1, 16), I32)],
        [spots, tail, *swapped, qkv_half, proj_half],
        "finish_other", 10**6,
        in_specs=[SM, VM] + [HB] * 6, out_specs=[HB] * 2 + [VM] * 6, scratch=landing,
        aliases={6: 0, 7: 1},
    )
    return (
        block_output.reshape(rows3),
        input_grad.reshape(rows3),
        rest[0],
        rest[1],
        qkv_sum,
        proj_sum,
        rest[2],
        rest[3],
        up_sum,
        down_sum,
        rest[4],
        rest[5],
    )


def solution(mesh):
    placed = (
        P("batch", "seq", None),
        P("batch", "seq"),
        P(),
        P("batch", None),
        P("batch", "seq"),
        P(),
        P(),
        P(),
        P(),
        P(),
        P(),
        P("batch", None, None),
        P("batch", None, None),
        P("batch", "seq", None),
    )
    return jax.shard_map(
        local,
        mesh=mesh,
        in_specs=placed,
        out_specs=(
            P("batch", "seq", None),
            P("batch", "seq", None),
            P(),
            P(),
            P(),
            P(),
            P(),
            P(),
            P("batch", None, "seq"),
            P("batch", "seq", None),
            P(),
            P("batch", "seq", None),
        ),
        check_vma=False,
    )
```
